128 devices in a mesh: enc: 8 (over y, core), seq: 16 (over x, z).
Axes of the slice: x: 4, y: 4, z: 4, core: 2. Of those that a mesh axis runs over, the one named last changes fastest.
Arguments:
- frame_tiles: bfloat16 [8, 16, 2, 16, 32, 768], P('enc', 'seq'), may hold values from -6 to 6
- tile_ids: int32 [8, 16, 2], P('enc', 'seq'), may hold values from 0 to 15, as said below
- partner_slot: int32 [8, 16, 2], P('enc', 'seq'), may hold values from 0 to 15, as said below
- mix_kernel: bfloat16 [7, 7, 768], replicated, may hold values from -0.875 to 0.875
- mix_bias: float32 [768], replicated, may hold values from -3 to 3
- down_weight: bfloat16 [3072, 1536], replicated, may hold values from -0.109375 to 0.109375
- down_bias: float32 [1536], replicated, may hold values from -3 to 3
- token_pos: int32 [8, 16, 2, 128], P('enc', 'seq'), may hold values from 0 to 32767, as said below
- grad_rows: bfloat16 [32768, 1536], P(('enc', 'seq')), may hold values from -6 to 6
Outputs:
- llm_rows: bfloat16 [32768, 1536], P(('enc', 'seq'))
- grad_tiles: bfloat16 [8, 16, 2, 16, 32, 768], P('enc', 'seq')
The draws below stay inside these ranges and needn't reach their ends.
Inputs may be any that keep to these rules, and one draw needn't show every extreme that they name: `tile_ids`: for every index j of seq, the 16 slots (e, j, k) hold each tile number of that group once; tiles 2 f and 2 f + 1 are the upper and lower half of frame f of the group. partner_slot[e, j, k] = e2 * 2 + k2 where slot (e2, j, k2) holds the tile number tile_ids[e, j, k] + 1 - 2 (tile_ids[e, j, k] % 2). `token_pos`: every position occurs exactly once. Position p is owned by index p // 256 of enc+seq (enc slowest). The 256 rows of one device send at most 8 positions to any one owner, and exactly 8 to some owner.
All inputs are finite; a program needn't handle non-finite values.
Results may differ from the reference program's by a relative error of at most 0.0063.
Values may be sent and summed in bfloat16 or wider, within the bound.
A program may use at most 128 MiB of HBM per device.

```python
import jax
import jax.numpy as jnp
from jax import lax

C = 768
C2 = 1536
KS = 7
TH = 16
GW = 32
SLOTS = 2
TOK_TILE = 128
ROWS_DEV = 256
SEQ_ALL = 32768
N_ENC = 8
N_SEQ = 16


def packing_tables(key):
    slot_total = N_ENC * SLOTS
    key_list = jax.random.split(key, N_SEQ)
    slot_order = jax.vmap(lambda subkey: jax.random.permutation(subkey, slot_total))(key_list)
    where_tile = jnp.argsort(slot_order, axis=1)
    twin_tile = slot_order + 1 - 2 * (slot_order % 2)
    partner = jnp.take_along_axis(where_tile, twin_tile, axis=1)
    tile_table = slot_order.reshape(N_SEQ, N_ENC, SLOTS).transpose(1, 0, 2).astype(jnp.int32)
    partner_table = partner.reshape(N_SEQ, N_ENC, SLOTS).transpose(1, 0, 2).astype(jnp.int32)
    return (tile_table, partner_table)


def draw_tile_ids(key, part):
    tables = packing_tables(key)
    return tables[0]


def draw_partner_slot(key, part):
    tables = packing_tables(key)
    return tables[1]


def draw_token_pos(key, part):
    key = jax.random.fold_in(key, 17)
    owner_total = N_ENC * N_SEQ
    row_total = ROWS_DEV
    first_key, second_key, third_key = jax.random.split(key, 3)
    eighth = owner_total // 8
    pattern = jnp.concatenate([jnp.full((eighth,), 4 * row_total // owner_total, jnp.int32), jnp.full((owner_total // 4,), row_total // owner_total, jnp.int32), jnp.full((owner_total // 2,), row_total // (2 * owner_total), jnp.int32), jnp.zeros((eighth,), jnp.int32)])
    pattern = jax.random.permutation(first_key, pattern)
    source_idx = jnp.arange(owner_total, dtype=jnp.int32)[:, None]
    owner_idx = jnp.arange(owner_total, dtype=jnp.int32)[None, :]
    counts = pattern[(owner_idx - source_idx) % owner_total]
    bucket_end = jnp.cumsum(counts, axis=1)
    bucket_start = bucket_end - counts
    position_idx = jnp.arange(row_total, dtype=jnp.int32)
    owner_sorted = jnp.sum((bucket_end[:, None, :] <= position_idx[None, :, None]).astype(jnp.int32), axis=2)
    rank_sorted = position_idx[None, :] - jnp.take_along_axis(bucket_start, owner_sorted, axis=1)
    earlier = jnp.cumsum(counts, axis=0) - counts
    slot_in_owner = jnp.take_along_axis(earlier, owner_sorted, axis=1) + rank_sorted
    local_perm = jax.vmap(lambda subkey: jax.random.permutation(subkey, row_total))(jax.random.split(second_key, owner_total)).astype(jnp.int32)
    local_pos = local_perm[owner_sorted, slot_in_owner]
    global_pos = owner_sorted * row_total + local_pos
    shuffle = jax.vmap(lambda subkey: jax.random.permutation(subkey, row_total))(jax.random.split(third_key, owner_total))
    global_pos = jnp.take_along_axis(global_pos, shuffle, axis=1)
    return global_pos.reshape(N_ENC, N_SEQ, SLOTS, TOK_TILE).astype(jnp.int32)


def shard_levels(own_key, dims, shards, smallest, top_value):
    factor_of, own = 1.0, jax.random.fold_in(own_key, 6)
    for axis_at, blocks in shards:
        steps = jnp.exp(jax.random.uniform(jax.random.fold_in(own, axis_at), (blocks,), jnp.float32, smallest / len(shards), top_value / len(shards)))
        factor_of = factor_of * jnp.repeat(steps, dims[axis_at] // blocks).reshape([-1 if axis == axis_at else 1 for axis in range(len(dims))])
    return factor_of


def centred(stream_key, dims, scale, reach, shards=(), kind=jnp.bfloat16):
    result = jax.random.normal(stream_key, dims, jnp.float32) * scale
    if len(shards) > 0:
        result = shard_levels(stream_key, dims, shards, -0.22, 0.18) * result
    return jnp.clip(result, min=-reach, max=reach).astype(kind)


def setup_inputs(seed: int = 0) -> dict:
    seeds = jax.random.split(jax.random.key(seed), 10)
    return {
        "frame_tiles": centred(seeds[0], (N_ENC, N_SEQ, SLOTS, TH, GW, C), 1.0, 6.0, ((0, 8), (1, 16))),
        "tile_ids": draw_tile_ids(jax.random.fold_in(seeds[9], 71), 0),
        "partner_slot": draw_partner_slot(jax.random.fold_in(seeds[9], 71), 0),
        "mix_kernel": centred(seeds[3], (KS, KS, C), (KS * KS) ** -0.5, 0.875),
        "mix_bias": centred(seeds[4], (C,), 0.5, 3.0, (), jnp.float32),
        "down_weight": centred(seeds[5], (4 * C, C2), (4 * C) ** -0.5, 0.109375),
        "down_bias": centred(seeds[6], (C2,), 0.5, 3.0, (), jnp.float32),
        "token_pos": draw_token_pos(jax.random.fold_in(seeds[9], 71), 0),
        "grad_rows": centred(seeds[8], (SEQ_ALL, C2), 1.0, 6.0, ((0, 128),)),
    }


SQRT_HALF = 0.7071067811865476
INV_ROOT = 0.3989422804014327


def gelu_value(pre_act):
    return 0.5 * pre_act * (1.0 + jax.scipy.special.erf(pre_act * SQRT_HALF))


def gelu_slope(pre_act):
    return 0.5 * (1.0 + jax.scipy.special.erf(pre_act * SQRT_HALF)) + pre_act * INV_ROOT * jnp.exp(-0.5 * pre_act * pre_act)


def rim_of(fields, half_flag):
    upper_tile = (half_flag == 0)[:, None, None, None]
    return jnp.where(upper_tile, fields[:, -3:], fields[:, :3])


def depthwise(fields, rim_in, half_flag, kernel, offset):
    zeros_rim = jnp.zeros_like(rim_in)
    lower_tile = (half_flag == 1)[:, None, None, None]
    upper_rows = jnp.where(lower_tile, rim_in, zeros_rim)
    lower_rows = jnp.where(lower_tile, zeros_rim, rim_in)
    stacked = jnp.concatenate([upper_rows, fields, lower_rows], axis=1).astype(jnp.float32)
    padded = jnp.pad(stacked, ((0, 0), (0, 0), (3, 3), (0, 0)))
    tile_rows = fields.shape[1]
    tile_cols = fields.shape[2]
    weights = kernel.astype(jnp.float32)
    summed = fields.astype(jnp.float32) + offset
    for row_tap in range(KS):
        for col_tap in range(KS):
            summed = summed + weights[row_tap, col_tap] * padded[:, row_tap:row_tap + tile_rows, col_tap:col_tap + tile_cols]
    return summed


def to_patches(mixed_out):
    slot_count, tile_rows, tile_cols, channels = mixed_out.shape
    cell_grid = mixed_out.reshape(slot_count, tile_rows // 2, 2, tile_cols // 2, 2, channels).transpose(0, 1, 3, 2, 4, 5)
    return cell_grid.reshape(slot_count * (tile_rows // 2) * (tile_cols // 2), 4 * channels)


def from_patches(row_block, slot_count, tile_rows, tile_cols, channels):
    cell_grid = row_block.reshape(slot_count, tile_rows // 2, tile_cols // 2, 2, 2, channels).transpose(0, 1, 3, 2, 4, 5)
    return cell_grid.reshape(slot_count, tile_rows, tile_cols, channels)


def reference(frame_tiles, tile_ids, partner_slot, mix_kernel, mix_bias, down_weight, down_bias, token_pos, grad_rows):
    flipped = mix_kernel[::-1, ::-1]

    def one_group(group_items):
        tiles_group, ids_group, partner_group, pos_group = group_items
        fields = tiles_group.reshape(-1, TH, GW, C)
        slot_count = fields.shape[0]
        half_flag = ids_group.reshape(-1) % 2
        partner = partner_group.reshape(-1).astype(jnp.int32)
        rim_in = rim_of(fields, half_flag)[partner]
        mixed_out = depthwise(fields, rim_in, half_flag, mix_kernel, mix_bias).astype(jnp.bfloat16)
        pre_act = jnp.dot(to_patches(mixed_out), down_weight, preferred_element_type=jnp.float32) + down_bias
        tokens = gelu_value(pre_act).astype(jnp.bfloat16)
        back = grad_rows[pos_group.reshape(-1).astype(jnp.int32)]
        pre_grad = (back.astype(jnp.float32) * gelu_slope(pre_act)).astype(jnp.bfloat16)
        patch_grad = lax.dot_general(pre_grad, down_weight, (((1,), (1,)), ((), ())), preferred_element_type=jnp.float32)
        mixed_grad = from_patches(patch_grad, slot_count, TH, GW, C).astype(jnp.bfloat16)
        rim_grad = rim_of(mixed_grad, half_flag)[partner]
        grads = depthwise(mixed_grad, rim_grad, half_flag, flipped, jnp.float32(0.0)).astype(jnp.bfloat16)
        return tokens, grads.reshape(tiles_group.shape)

    tiles_swapped = jnp.swapaxes(frame_tiles, 0, 1)
    pos_swapped = jnp.swapaxes(token_pos, 0, 1)
    tokens, grads = lax.map(one_group, (tiles_swapped, jnp.swapaxes(tile_ids, 0, 1), jnp.swapaxes(partner_slot, 0, 1), pos_swapped))
    llm_rows = jnp.zeros((SEQ_ALL, C2), jnp.bfloat16).at[pos_swapped.reshape(-1).astype(jnp.int32)].set(tokens.reshape(-1, C2))
    grad_tiles = jnp.swapaxes(grads, 0, 1)
    return llm_rows, grad_tiles
```

```python
import functools

import jax
import jax.numpy as jnp
from jax import lax
from jax.experimental import pallas as pl
from jax.experimental.pallas import tpu as pltpu
from jax.sharding import PartitionSpec as P

C = 768
C2 = 1536
KS = 7
TH = 16
GW = 32
SLOTS = 2
ROWS = 256
N_ENC = 8
N_SEQ = 16
N_DEV = 128
CAP = 8
LT = C // 128
HALO = 3
XR = TH + 2 * HALO
SQRT_HALF = 0.7071067811865476
INV_ROOT = 0.3989422804014327
BF = jnp.bfloat16
F32 = jnp.float32
I32 = jnp.int32


def iota(shape, axis):
    return lax.broadcasted_iota(I32, shape, axis)


def dot(a, b):
    return jnp.dot(a, b, preferred_element_type=F32)


def kernel(
    tiles_hbm, half_ref, partner_ref, mixk_ref, mixb_ref, w_hbm, downb_ref, pos_ref, grad_hbm,
    llm_ref, gout_ref,
    tiles, w, grads, wb, X, F, A, slope, tok, pg, sel,
    msg, rmsg, gsend, grecv, tsend, trecv, rimf, rimb,
    lsem, msem, gsem, tsem, fsend, frecv, bsend, brecv,
):
    enc = lax.axis_index("enc")
    seq = lax.axis_index("seq")
    me = enc * N_SEQ + seq
    cy, core = enc // 2, enc % 2

    ld_tiles = pltpu.make_async_copy(tiles_hbm, tiles, lsem.at[0])
    ld_grads = pltpu.make_async_copy(grad_hbm, grads, lsem.at[1])
    ld_w = pltpu.make_async_copy(w_hbm, w, lsem.at[2])
    ld_tiles.start()
    ld_grads.start()
    ld_w.start()

    barrier = pltpu.get_barrier_semaphore()

    @pl.loop(1, N_DEV)
    def _(i):
        e = lax.rem(enc + i // N_SEQ, N_ENC)
        s = lax.rem(seq + i % N_SEQ, N_SEQ)
        pl.semaphore_signal(barrier, inc=1, device_id=(e, s), device_id_type=pl.DeviceIdType.MESH)

    pos = pos_ref[...]
    prow = jnp.concatenate([pos[0:1, :], pos[1:2, :]], axis=1)
    pcol = jnp.concatenate(
        [jnp.transpose(jnp.broadcast_to(pos[i : i + 1, :].astype(F32), (128, 128))) for i in range(2)], axis=0
    ).astype(I32)[:, 0:1]
    orow, ocol = prow // ROWS, pcol // ROWS
    lcol = pcol - ocol * ROWS
    same = jnp.broadcast_to(ocol, (ROWS, ROWS)) == jnp.broadcast_to(orow, (ROWS, ROWS))
    at0, at1 = iota((ROWS, ROWS), 0), iota((ROWS, ROWS), 1)
    rank_row = jnp.sum(jnp.where(same & (at0 < at1), 1.0, 0.0), axis=0, keepdims=True).astype(I32)
    rank_col = jnp.sum(jnp.where(same & (at1 < at0), 1.0, 0.0), axis=1, keepdims=True).astype(I32)
    slot_row = orow * CAP + rank_row
    to_owner = jnp.where(iota((N_DEV, ROWS), 0) == orow, 1.0, 0.0).astype(BF)
    ranked = jnp.where(iota((ROWS, 128), 1) == rank_col, (lcol + 1).astype(F32), 0.0).astype(BF)
    msg[...] = dot(to_owner, ranked).reshape(N_DEV, 1, 128)
    rmsg[pl.ds(me, 1)] = msg[pl.ds(me, 1)]

    for a in range(KS):
        for b in range(KS):
            row = mixk_ref[a, b : b + 1, :].astype(F32)
            if a == HALO and b == HALO:
                row = row + 1.0
            for t in range(LT):
                wb[t, a * KS + b] = jnp.broadcast_to(row[:, t * 128 : (t + 1) * 128], (8, 128))

    @pl.loop(0, SLOTS * LT)
    def _(i):
        X[i // LT, i % LT] = jnp.zeros((XR, 2, GW, 128), F32)

    q0, q1 = iota((128, 128), 0), iota((128, 128), 1)
    spread = jnp.where(q1 == (q0 // 32) * 32 + (q0 % 16) * 2 + (q0 % 32) // 16, 1.0, 0.0).astype(BF)
    gather = jnp.where(q0 == (q1 // 32) * 32 + (q1 % 16) * 2 + (q1 % 32) // 16, 1.0, 0.0).astype(BF)

    def fill(k, g):
        d = dot(spread, tiles[k, 4 * g : 4 * g + 4].reshape(128, C)).reshape(4, 2, 16, C)
        for t in range(LT):
            X[k, t, HALO + 4 * g : HALO + 4 * g + 4, :, 8:24, :] = d[..., t * 128 : (t + 1) * 128]

    def own_rims(rims):
        for k in range(SLOTS):
            low = X[k, :, HALO : 2 * HALO, :, 8:24, :]
            high = X[k, :, TH : TH + HALO, :, 8:24, :]
            rim = jnp.where(half_ref[k] == 0, high, low)
            rims[enc, k] = rim.astype(BF).reshape(LT, 96, 128)

    up = lax.rem(cy + 1, 4) * 2 + core
    down = lax.rem(cy + 3, 4) * 2 + core
    across = lax.rem(cy + 2, 4) * 2 + core
    sib = cy * 2 + 1 - core

    def rim_copies(rims, ssem, rsem):
        def copy(n, ref, to):
            return pltpu.make_async_remote_copy(
                src_ref=ref, dst_ref=ref, send_sem=ssem.at[n], recv_sem=rsem.at[n],
                device_id=(to, seq), device_id_type=pl.DeviceIdType.MESH,
            )

        def landed(n, ref):
            return pltpu.make_async_copy(ref, ref, rsem.at[n])

        sends = [
            copy(0, rims.at[enc], up),
            copy(1, rims.at[enc], down),
            copy(2, rims.at[enc], sib),
            copy(3, rims.at[down, 0], up),
            copy(4, rims.at[up, 1], down),
            copy(5, rims.at[down], sib),
            copy(6, rims.at[up], sib),
            copy(7, rims.at[across], sib),
        ]
        other = 1 - 2 * core
        arrivals = [
            landed(0, rims.at[down]),
            landed(1, rims.at[up]),
            landed(2, rims.at[sib]),
            landed(3, rims.at[across, 0]),
            landed(4, rims.at[across, 1]),
            landed(5, rims.at[down + other]),
            landed(6, rims.at[up + other]),
            landed(7, rims.at[across + other]),
        ]
        return sends, arrivals

    def place_rims(rims):
        for k in range(SLOTS):
            want = partner_ref[k]
            rim = jnp.zeros((LT, 96, 128), BF)
            for q in range(N_ENC * SLOTS):
                rim = jnp.where(want == q, rims[q // 2, q % 2], rim)
            rim = rim.astype(F32).reshape(LT, HALO, 2, 16, 128)
            lower = half_ref[k] == 1
            X[k, :, 0:HALO, :, 8:24, :] = jnp.where(lower, rim, 0.0)
            X[k, :, TH + HALO : XR, :, 8:24, :] = jnp.where(lower, 0.0, rim)

    def conv(flip, with_bias):
        @pl.loop(0, SLOTS * LT)
        def _(i):
            k, t = i // LT, i % LT
            lanes = pl.ds(pl.multiple_of(t * 128, 128), 128)
            for cb in range(2):
                first = jnp.zeros((TH, 8, 128), F32)
                if with_bias:
                    first = first + mixb_ref[:, lanes].reshape(1, 1, 128)
                acc = [first, first]
                for p in range(2):
                    for sh in range(-2, 3):
                        uses = [(dx, 2 * sh + p + 3 - dx) for dx in range(2)]
                        uses = [(dx, b) for dx, b in uses if 0 <= b < KS]
                        if not uses:
                            continue
                        xs = X[k, t, :, p, 8 + 8 * cb + sh : 16 + 8 * cb + sh, :]
                        for dx, b in uses:
                            for a in range(KS):
                                tap = a * KS + b
                                if flip:
                                    tap = KS * KS - 1 - tap
                                acc[dx] = acc[dx] + wb[t, tap][None] * xs[a : a + TH]
                for dx in range(2):
                    rows = acc[dx].reshape(TH // 2, 2, 8, 128)
                    for dy in range(2):
                        F[dy * 2 + dx, k, :, 8 * cb : 8 * cb + 8, lanes] = rows[:, dy]

    def send_rows(buf, got, sems, onehot, rows_ref):
        @pl.loop(0, N_ENC)
        def _(i):
            g = lax.rem(enc + i, N_ENC)
            hot = onehot(g)
            y0 = dot(hot, rows_ref[:, 0:C]).reshape(N_SEQ, CAP, C)
            y1 = dot(hot, rows_ref[:, C:C2]).reshape(N_SEQ, CAP, C)
            buf[pl.ds(g * N_SEQ, N_SEQ)] = jnp.concatenate([y0, y1], axis=1).astype(BF)

            @pl.loop(0, N_SEQ)
            def _(j):
                @pl.when(i + j > 0)
                def _():
                    s = lax.rem(seq + j, N_SEQ)
                    pltpu.make_async_remote_copy(
                        src_ref=buf.at[g * N_SEQ + s], dst_ref=got.at[me],
                        send_sem=sems.at[0], recv_sem=sems.at[1],
                        device_id=(g, s), device_id_type=pl.DeviceIdType.MESH,
                    ).start()

        got[pl.ds(me, 1)] = buf[pl.ds(me, 1)]

    def wait_rows(buf, sem):
        part = buf.at[pl.ds(0, N_DEV - 1)]
        pltpu.make_async_copy(part, part, sem).wait()

    ld_tiles.wait()
    for k in range(SLOTS):
        fill(k, 0)
        fill(k, 3)
    own_rims(rimf)
    pl.semaphore_wait(barrier, N_DEV - 1)

    @pl.loop(1, N_DEV)
    def _(i):
        e = lax.rem(enc + i // N_SEQ, N_ENC)
        s = lax.rem(seq + i % N_SEQ, N_SEQ)
        pltpu.make_async_remote_copy(
            src_ref=msg.at[e * N_SEQ + s], dst_ref=rmsg.at[me],
            send_sem=msem.at[0], recv_sem=msem.at[1],
            device_id=(e, s), device_id_type=pl.DeviceIdType.MESH,
        ).start()

    f_send, f_got = rim_copies(rimf, fsend, frecv)
    for n in range(3):
        f_send[n].start()
    for k in range(SLOTS):
        fill(k, 1)
        fill(k, 2)
    ld_grads.wait()
    wait_rows(rmsg, msem.at[1])

    asked = rmsg[...].reshape(N_DEV, 128)
    asked_t = jnp.transpose(asked)[0:CAP, :].astype(BF)
    asked = asked.astype(BF)

    def fetch(g):
        shape = (N_SEQ * CAP, 128)
        at = iota(shape, 0)
        rows = dot(jnp.where(iota(shape, 1) == g * N_SEQ + at // CAP, 1.0, 0.0).astype(BF), asked)
        want = jnp.sum(jnp.where(iota(shape, 1) == at % CAP, rows, 0.0), axis=1, keepdims=True).astype(I32)
        return jnp.where(iota((N_SEQ * CAP, ROWS), 1) == want - 1, 1.0, 0.0).astype(BF)

    send_rows(gsend, grecv, gsem, fetch, grads)

    f_got[0].wait()
    f_send[3].start()
    f_send[5].start()
    f_got[1].wait()
    f_send[4].start()
    f_send[6].start()
    f_got[3].wait()
    f_got[4].wait()
    f_send[7].start()
    for n in (2, 5, 6, 7):
        f_got[n].wait()
    place_rims(rimf)
    conv(False, True)

    @pl.loop(0, 4)
    def _(j):
        A[j] = F[j].reshape(ROWS, C).astype(BF)

    ld_w.wait()

    @pl.loop(0, C2 // 256)
    def _(n):
        cols = pl.ds(pl.multiple_of(n * 256, 256), 256)
        pre = jnp.zeros((ROWS, 256), F32) + downb_ref[:, cols]
        for j in range(4):
            pre = pre + dot(A[j], w[j * C : (j + 1) * C, cols])
        phi = 0.5 * (1.0 + lax.erf(pre * SQRT_HALF))
        tok[:, cols] = (pre * phi).astype(BF)
        slope[:, cols] = phi + pre * INV_ROOT * jnp.exp(-0.5 * pre * pre)

    def scatter(g):
        at = iota((N_SEQ * CAP, ROWS), 0) + g * (N_SEQ * CAP)
        return jnp.where(at == slot_row, 1.0, 0.0).astype(BF)

    send_rows(tsend, trecv, tsem, scatter, tok)

    back_at = ocol * (2 * CAP) + rank_col
    for h in range(2):
        sel[h] = jnp.where(iota((ROWS, 2 * CAP * N_DEV), 1) == back_at + h * CAP, 1.0, 0.0).astype(BF)
    wait_rows(grecv, gsem.at[1])

    def picked(got, h, c0):
        part = got[:, :, pl.ds(pl.multiple_of(c0, 256), 256)].reshape(2 * CAP * N_DEV, 256)
        return dot(sel[h], part)

    @pl.loop(0, C2 // 256)
    def _(n):
        h = n // 3
        cols = pl.ds(pl.multiple_of(n * 256, 256), 256)
        pg[:, cols] = (picked(grecv, h, (n - 3 * h) * 256) * slope[:, cols]).astype(BF)

    @pl.loop(0, 4 * (C // 256))
    def _(m):
        j, n = m // 3, lax.rem(m, 3)
        part = w[pl.ds(pl.multiple_of(m * 256, 256), 256), :]
        g = lax.dot_general(pg[...], part, (((1,), (1,)), ((), ())), preferred_element_type=F32)
        g = g.astype(BF).astype(F32).reshape(SLOTS, TH // 2, 16, 256)
        dy, dx = j // 2, lax.rem(j, 2)
        for y in range(TH // 2):
            for i in range(2):
                X[:, 2 * n + i, HALO + 2 * y + dy, dx, 8:24, :] = g[:, y, :, i * 128 : (i + 1) * 128]

    own_rims(rimb)
    b_send, b_got = rim_copies(rimb, bsend, brecv)
    for n in range(3):
        b_send[n].start()
    b_got[0].wait()
    b_send[3].start()
    b_send[5].start()
    b_got[1].wait()
    b_send[4].start()
    b_send[6].start()
    b_got[3].wait()
    b_got[4].wait()
    b_send[7].start()
    for n in (2, 5, 6, 7):
        b_got[n].wait()
    place_rims(rimb)
    conv(True, False)

    for k in range(SLOTS):
        for g in range(4):
            cells = jnp.concatenate(
                [F[dy * 2 + dx, k, 2 * g + y] for y in range(2) for dy in range(2) for dx in range(2)], axis=0
            ).astype(BF)
            gout_ref[k, 4 * g : 4 * g + 4] = dot(gather, cells).astype(BF).reshape(4, GW, C)

    for g in range(N_DEV // N_SEQ):
        shape = (N_DEV, 256)
        at1 = iota(shape, 1)
        over = jnp.where(iota(shape, 0) == g * N_SEQ + at1 // (2 * CAP), 1.0, 0.0).astype(BF)
        rows = dot(asked_t, over)
        k8 = iota((CAP, 256), 1)
        put = jnp.sum(jnp.where(iota((CAP, 256), 0) == k8 % CAP, rows, 0.0), axis=0, keepdims=True).astype(I32)
        hit = iota((ROWS, 256), 0) == put - 1
        part = (iota((ROWS, 256), 1) // CAP) % 2
        for h in range(2):
            sel[h, :, g * 256 : (g + 1) * 256] = jnp.where(hit & (part == h), 1.0, 0.0).astype(BF)
    wait_rows(trecv, tsem.at[1])

    @pl.loop(0, C2 // 256)
    def _(n):
        h = n // 3
        cols = pl.ds(pl.multiple_of(n * 256, 256), 256)
        llm_ref[:, cols] = picked(trecv, h, (n - 3 * h) * 256).astype(BF)

    for n in range(8):
        f_send[n].wait_send()
        b_send[n].wait_send()
    wait_rows(msg, msem.at[0])
    wait_rows(gsend, gsem.at[0])
    wait_rows(tsend, tsem.at[0])


def on_device(frame_tiles, tile_ids, partner_slot, mix_kernel, mix_bias, down_weight, down_bias, token_pos, grad_rows):
    vmem = pl.BlockSpec(memory_space=pltpu.VMEM)
    smem = pl.BlockSpec(memory_space=pltpu.SMEM)
    anyw = pl.BlockSpec(memory_space=pl.ANY)
    dma = pltpu.SemaphoreType.DMA
    llm, gout = pl.pallas_call(
        kernel,
        out_shape=(
            jax.ShapeDtypeStruct((ROWS, C2), BF),
            jax.ShapeDtypeStruct((SLOTS, TH, GW, C), BF),
        ),
        in_specs=[anyw, smem, smem, vmem, vmem, anyw, vmem, vmem, anyw],
        out_specs=(vmem, vmem),
        scratch_shapes=[
            pltpu.VMEM((SLOTS, TH, GW, C), BF),
            pltpu.VMEM((4 * C, C2), BF),
            pltpu.VMEM((ROWS, C2), BF),
            pltpu.VMEM((LT, KS * KS, 8, 128), F32),
            pltpu.VMEM((SLOTS, LT, XR, 2, GW, 128), F32),
            pltpu.VMEM((4, SLOTS, TH // 2, 16, C), F32),
            pltpu.VMEM((4, ROWS, C), BF),
            pltpu.VMEM((ROWS, C2), F32),
            pltpu.VMEM((ROWS, C2), BF),
            pltpu.VMEM((ROWS, C2), BF),
            pltpu.VMEM((2, ROWS, 2 * CAP * N_DEV), BF),
            pltpu.VMEM((N_DEV, 1, 128), F32),
            pltpu.VMEM((N_DEV, 1, 128), F32),
            pltpu.VMEM((N_DEV, 2 * CAP, C), BF),
            pltpu.VMEM((N_DEV, 2 * CAP, C), BF),
            pltpu.VMEM((N_DEV, 2 * CAP, C), BF),
            pltpu.VMEM((N_DEV, 2 * CAP, C), BF),
            pltpu.VMEM((N_ENC, SLOTS, LT, 96, 128), BF),
            pltpu.VMEM((N_ENC, SLOTS, LT, 96, 128), BF),
            dma((3,)),
            dma((2,)),
            dma((2,)),
            dma((2,)),
            dma((8,)),
            dma((8,)),
            dma((8,)),
            dma((8,)),
        ],
        compiler_params=pltpu.CompilerParams(
            collective_id=0, has_side_effects=True, vmem_limit_bytes=62 * 1024 * 1024
        ),
    )(
        frame_tiles[0, 0],
        tile_ids.reshape(SLOTS) % 2,
        partner_slot.reshape(SLOTS),
        mix_kernel,
        mix_bias.reshape(1, C),
        down_weight,
        down_bias.reshape(1, C2),
        token_pos.reshape(SLOTS, 128),
        grad_rows,
    )
    return llm, gout[None, None]


def solution(mesh):
    return jax.shard_map(
        on_device,
        mesh=mesh,
        in_specs=(
            P("enc", "seq", None, None, None, None),
            P("enc", "seq", None),
            P("enc", "seq", None),
            P(),
            P(),
            P(),
            P(),
            P("enc", "seq", None, None),
            P(("enc", "seq"), None),
        ),
        out_specs=(P(("enc", "seq"), None), P("enc", "seq", None, None, None, None)),
        check_vma=False,
    )
```

```python
import functools

import jax
import jax.numpy as jnp
from jax import lax
from jax.experimental import pallas as pl
from jax.experimental.pallas import tpu as pltpu
from jax.sharding import PartitionSpec as P

C = 768
C2 = 1536
KS = 7
TH = 16
GW = 32
SLOTS = 2
ROWS = 256
N_ENC = 8
N_SEQ = 16
N_DEV = 128
CAP = 8
GROUP = 16
GROUPS = 8
LT = C // 128
HALO = 3
XR = TH + 2 * HALO
SQRT_HALF = 0.7071067811865476
INV_ROOT = 0.3989422804014327
BF = jnp.bfloat16
F32 = jnp.float32
I32 = jnp.int32


def iota(shape, axis):
    return lax.broadcasted_iota(I32, shape, axis)


def dot(a, b):
    return jnp.dot(a, b, preferred_element_type=F32)


def kernel(
    tiles_hbm, ids_ref, partner_ref, mixk_ref, mixb_ref, w_hbm, downb_ref, pos_ref, grad_hbm,
    llm_ref, gout_ref,
    tiles, w, grads, mixb, downb, wb, X, F, A, slope, tok, pg, sel,
    msg, rmsg, gsend, grecv, tsend, trecv, rimf, rimb,
    lsem, msem, gsem, tsem, fsend, frecv, bsend, brecv,
):
    enc = lax.axis_index("enc")
    seq = lax.axis_index("seq")
    me = enc * N_SEQ + seq
    cy, core = enc // 2, enc % 2

    ld_tiles = pltpu.make_async_copy(tiles_hbm.at[0, 0], tiles, lsem.at[0])
    ld_grads = pltpu.make_async_copy(grad_hbm, grads, lsem.at[1])
    ld_w = pltpu.make_async_copy(w_hbm, w, lsem.at[2])
    ld_tiles.start()
    ld_grads.start()
    ld_w.start()

    barrier = pltpu.get_barrier_semaphore()

    @pl.loop(1, N_DEV)
    def _(i):
        e = lax.rem(enc + i // N_SEQ, N_ENC)
        s = lax.rem(seq + i % N_SEQ, N_SEQ)
        pl.semaphore_signal(barrier, inc=1, device_id=(e, s), device_id_type=pl.DeviceIdType.MESH)

    mixb[...] = mixb_ref[...].reshape(1, C)
    downb[...] = downb_ref[...].reshape(1, C2)

    pos = pos_ref[0, 0]
    prow = jnp.concatenate([pos[0:1, :], pos[1:2, :]], axis=1)
    pcol = jnp.concatenate(
        [jnp.transpose(jnp.broadcast_to(pos[i : i + 1, :].astype(F32), (128, 128))) for i in range(2)], axis=0
    ).astype(I32)[:, 0:1]
    orow, ocol = prow // ROWS, pcol // ROWS
    lcol = pcol - ocol * ROWS
    same = jnp.broadcast_to(ocol, (ROWS, ROWS)) == jnp.broadcast_to(orow, (ROWS, ROWS))
    at0, at1 = iota((ROWS, ROWS), 0), iota((ROWS, ROWS), 1)
    rank_row = jnp.sum(jnp.where(same & (at0 < at1), 1.0, 0.0), axis=0, keepdims=True).astype(I32)
    rank_col = jnp.sum(jnp.where(same & (at1 < at0), 1.0, 0.0), axis=1, keepdims=True).astype(I32)
    slot_row = orow * CAP + rank_row
    to_owner = jnp.where(iota((N_DEV, ROWS), 0) == orow, 1.0, 0.0).astype(BF)
    ranked = jnp.where(iota((ROWS, 128), 1) == rank_col, (lcol + 1).astype(F32), 0.0).astype(BF)
    msg[...] = dot(to_owner, ranked).reshape(N_DEV, 1, 128)
    rmsg[pl.ds(me, 1)] = msg[pl.ds(me, 1)]

    for a in range(KS):
        for b in range(KS):
            row = mixk_ref[a, b : b + 1, :].astype(F32)
            if a == HALO and b == HALO:
                row = row + 1.0
            for t in range(LT):
                wb[t, a * KS + b] = jnp.broadcast_to(row[:, t * 128 : (t + 1) * 128], (8, 128))

    @pl.loop(0, SLOTS * LT)
    def _(i):
        X[i // LT, i % LT] = jnp.zeros((XR, 2, GW, 128), F32)

    q0, q1 = iota((128, 128), 0), iota((128, 128), 1)
    spread = jnp.where(q1 == (q0 // 32) * 32 + (q0 % 16) * 2 + (q0 % 32) // 16, 1.0, 0.0).astype(BF)
    gather = jnp.where(q0 == (q1 // 32) * 32 + (q1 % 16) * 2 + (q1 % 32) // 16, 1.0, 0.0).astype(BF)

    def fill(k, g):
        d = dot(spread, tiles[k, 4 * g : 4 * g + 4].reshape(128, C)).reshape(4, 2, 16, C)
        for t in range(LT):
            X[k, t, HALO + 4 * g : HALO + 4 * g + 4, :, 8:24, :] = d[..., t * 128 : (t + 1) * 128]

    def own_rims(rims):
        for k in range(SLOTS):
            low = X[k, :, HALO : 2 * HALO, :, 8:24, :]
            high = X[k, :, TH : TH + HALO, :, 8:24, :]
            rim = jnp.where(lax.rem(ids_ref[0, 0, k], 2) == 0, high, low)
            rims[enc, k] = rim.astype(BF).reshape(LT, 96, 128)

    up = lax.rem(cy + 1, 4) * 2 + core
    down = lax.rem(cy + 3, 4) * 2 + core
    across = lax.rem(cy + 2, 4) * 2 + core
    sib = cy * 2 + 1 - core

    def rim_copies(rims, ssem, rsem):
        def copy(n, ref, to):
            return pltpu.make_async_remote_copy(
                src_ref=ref, dst_ref=ref, send_sem=ssem.at[n], recv_sem=rsem.at[n],
                device_id=(to, seq), device_id_type=pl.DeviceIdType.MESH,
            )

        def landed(n, ref):
            return pltpu.make_async_copy(ref, ref, rsem.at[n])

        sends = [
            copy(0, rims.at[enc], up),
            copy(1, rims.at[enc], down),
            copy(2, rims.at[enc], sib),
            copy(3, rims.at[down, 0], up),
            copy(4, rims.at[up, 1], down),
            copy(5, rims.at[down], sib),
            copy(6, rims.at[up], sib),
            copy(7, rims.at[across], sib),
        ]
        other = 1 - 2 * core
        arrivals = [
            landed(0, rims.at[down]),
            landed(1, rims.at[up]),
            landed(2, rims.at[sib]),
            landed(3, rims.at[across, 0]),
            landed(4, rims.at[across, 1]),
            landed(5, rims.at[down + other]),
            landed(6, rims.at[up + other]),
            landed(7, rims.at[across + other]),
        ]
        return sends, arrivals

    def place_rims(rims):
        for k in range(SLOTS):
            want = partner_ref[0, 0, k]
            rim = jnp.zeros((LT, 96, 128), BF)
            for q in range(N_ENC * SLOTS):
                rim = jnp.where(want == q, rims[q // 2, q % 2], rim)
            rim = rim.astype(F32).reshape(LT, HALO, 2, 16, 128)
            lower = lax.rem(ids_ref[0, 0, k], 2) == 1
            X[k, :, 0:HALO, :, 8:24, :] = jnp.where(lower, rim, 0.0)
            X[k, :, TH + HALO : XR, :, 8:24, :] = jnp.where(lower, 0.0, rim)

    def conv(flip, with_bias):
        @pl.loop(0, SLOTS * LT)
        def _(i):
            k, t = i // LT, i % LT
            lanes = pl.ds(pl.multiple_of(t * 128, 128), 128)
            for cb in range(2):
                first = jnp.zeros((TH, 8, 128), F32)
                if with_bias:
                    first = first + mixb[:, lanes].reshape(1, 1, 128)
                acc = [first, first]
                for p in range(2):
                    for sh in range(-2, 3):
                        uses = [(dx, 2 * sh + p + 3 - dx) for dx in range(2)]
                        uses = [(dx, b) for dx, b in uses if 0 <= b < KS]
                        if not uses:
                            continue
                        xs = X[k, t, :, p, 8 + 8 * cb + sh : 16 + 8 * cb + sh, :]
                        for dx, b in uses:
                            for a in range(KS):
                                tap = a * KS + b
                                if flip:
                                    tap = KS * KS - 1 - tap
                                acc[dx] = acc[dx] + wb[t, tap][None] * xs[a : a + TH]
                for dx in range(2):
                    rows = acc[dx].reshape(TH // 2, 2, 8, 128)
                    for dy in range(2):
                        F[dy * 2 + dx, k, :, 8 * cb : 8 * cb + 8, lanes] = rows[:, dy]

    def digit(values, i):
        code = sum(v * 4**n for n, v in enumerate(values))
        return lax.rem(jnp.right_shift(code, 2 * i), 4)

    def targets(i):
        x, z = seq // 4, lax.rem(seq, 4)
        first = lax.rem(x + digit((1, 0, 1, 1, 2, 1, 2, 2), i), 4) * 4 + lax.rem(z + digit((0, 1, 1, 3, 1, 2, 0, 2), i), 4)
        second = lax.rem(x + digit((3, 0, 3, 3, 2, 3, 0, 0), i), 4) * 4 + lax.rem(z + digit((0, 3, 3, 1, 3, 2, 2, 0), i), 4)
        return first, second

    def fill_rows(buf, onehot, rows_ref):
        @pl.loop(0, GROUPS)
        def _(i):
            first, second = targets(i)
            place = iota((GROUP * CAP, 1), 0) // CAP
            e = lax.rem(enc + 3 * (place // 2), N_ENC)
            hot = onehot(e * N_SEQ + jnp.where(place % 2 == 0, first, second))
            y0 = dot(hot, rows_ref[:, 0:C]).reshape(GROUP, CAP, C)
            y1 = dot(hot, rows_ref[:, C:C2]).reshape(GROUP, CAP, C)
            buf[pl.ds(i * GROUP, GROUP)] = jnp.concatenate([y0, y1], axis=1).astype(BF)

    def send_rows(buf, got, sems, begin, end):
        @pl.loop(begin, end)
        def _(i):
            first, second = targets(i)

            @pl.loop(0, GROUP)
            def _(n):
                @pl.when(jnp.logical_not((i == GROUPS - 1) & (n == 1)))
                def _():
                    e = lax.rem(enc + 3 * (n // 2), N_ENC)
                    s = jnp.where(n % 2 == 0, first, second)
                    pltpu.make_async_remote_copy(
                        src_ref=buf.at[i * GROUP + n], dst_ref=got.at[me],
                        send_sem=sems.at[0], recv_sem=sems.at[1],
                        device_id=(e, s), device_id_type=pl.DeviceIdType.MESH,
                    ).start()

    def keep_own(buf, got):
        got[pl.ds(me, 1)] = buf[pl.ds((GROUPS - 1) * GROUP + 1, 1)]

    def wait_rows(buf, sem):
        part = buf.at[pl.ds(0, N_DEV - 1)]
        pltpu.make_async_copy(part, part, sem).wait()

    ld_tiles.wait()
    for k in range(SLOTS):
        fill(k, 0)
        fill(k, 3)
    own_rims(rimf)
    pl.semaphore_wait(barrier, N_DEV - 1)

    @pl.loop(1, N_DEV)
    def _(i):
        e = lax.rem(enc + i // N_SEQ, N_ENC)
        s = lax.rem(seq + i % N_SEQ, N_SEQ)
        pltpu.make_async_remote_copy(
            src_ref=msg.at[e * N_SEQ + s], dst_ref=rmsg.at[me],
            send_sem=msem.at[0], recv_sem=msem.at[1],
            device_id=(e, s), device_id_type=pl.DeviceIdType.MESH,
        ).start()

    f_send, f_got = rim_copies(rimf, fsend, frecv)
    for n in range(3):
        f_send[n].start()
    for k in range(SLOTS):
        fill(k, 1)
        fill(k, 2)
    f_got[0].wait()
    f_send[3].start()
    f_send[5].start()
    f_got[1].wait()
    f_send[4].start()
    f_send[6].start()
    ld_grads.wait()
    wait_rows(rmsg, msem.at[1])

    asked = rmsg[...].reshape(N_DEV, 128)
    asked_t = jnp.transpose(asked)[0:CAP, :].astype(BF)
    asked = asked.astype(BF)

    def fetch(owner):
        shape = (GROUP * CAP, 128)
        at = iota(shape, 0)
        rows = dot(jnp.where(iota(shape, 1) == owner, 1.0, 0.0).astype(BF), asked)
        want = jnp.sum(jnp.where(iota(shape, 1) == at % CAP, rows, 0.0), axis=1, keepdims=True).astype(I32)
        return jnp.where(iota((GROUP * CAP, ROWS), 1) == want - 1, 1.0, 0.0).astype(BF)

    fill_rows(gsend, fetch, grads)
    send_rows(gsend, grecv, gsem, 0, GROUPS)
    keep_own(gsend, grecv)

    f_got[3].wait()
    f_got[4].wait()
    f_send[7].start()
    for n in (2, 5, 6, 7):
        f_got[n].wait()
    place_rims(rimf)
    conv(False, True)

    @pl.loop(0, 4)
    def _(j):
        A[j] = F[j].reshape(ROWS, C).astype(BF)

    ld_w.wait()

    @pl.loop(0, C2 // 256)
    def _(n):
        cols = pl.ds(pl.multiple_of(n * 256, 256), 256)
        pre = jnp.zeros((ROWS, 256), F32) + downb[:, cols]
        for j in range(4):
            pre = pre + dot(A[j], w[j * C : (j + 1) * C, cols])
        phi = 0.5 * (1.0 + lax.erf(pre * SQRT_HALF))
        tok[:, cols] = (pre * phi).astype(BF)
        slope[:, cols] = phi + pre * INV_ROOT * jnp.exp(-0.5 * pre * pre)

    def scatter(owner):
        at = owner * CAP + iota((GROUP * CAP, 1), 0) % CAP
        return jnp.where(at == slot_row, 1.0, 0.0).astype(BF)

    fill_rows(tsend, scatter, tok)
    send_rows(tsend, trecv, tsem, 0, GROUPS // 2)
    keep_own(tsend, trecv)

    back_at = ocol * (2 * CAP) + rank_col
    for h in range(2):
        sel[h] = jnp.where(iota((ROWS, 2 * CAP * N_DEV), 1) == back_at + h * CAP, 1.0, 0.0).astype(BF)
    wait_rows(grecv, gsem.at[1])

    def picked(got, h, c0):
        part = got[:, :, pl.ds(pl.multiple_of(c0, 256), 256)].reshape(2 * CAP * N_DEV, 256)
        return dot(sel[h], part)

    @pl.loop(0, C2 // 256)
    def _(n):
        h = n // 3
        cols = pl.ds(pl.multiple_of(n * 256, 256), 256)
        pg[:, cols] = (picked(grecv, h, (n - 3 * h) * 256) * slope[:, cols]).astype(BF)

    @pl.loop(0, 4 * (C // 256))
    def _(m):
        j, n = m // 3, lax.rem(m, 3)
        part = w[pl.ds(pl.multiple_of(m * 256, 256), 256), :]
        g = lax.dot_general(pg[...], part, (((1,), (1,)), ((), ())), preferred_element_type=F32)
        g = g.astype(BF).astype(F32).reshape(SLOTS, TH // 2, 16, 256)
        dy, dx = j // 2, lax.rem(j, 2)
        for y in range(TH // 2):
            for i in range(2):
                X[:, 2 * n + i, HALO + 2 * y + dy, dx, 8:24, :] = g[:, y, :, i * 128 : (i + 1) * 128]

    own_rims(rimb)
    b_send, b_got = rim_copies(rimb, bsend, brecv)
    for n in range(3):
        b_send[n].start()
    b_got[0].wait()
    b_send[3].start()
    b_send[5].start()
    b_got[1].wait()
    b_send[4].start()
    b_send[6].start()
    send_rows(tsend, trecv, tsem, GROUPS // 2, GROUPS)
    b_got[3].wait()
    b_got[4].wait()
    b_send[7].start()
    for n in (2, 5, 6, 7):
        b_got[n].wait()
    place_rims(rimb)
    conv(True, False)

    for k in range(SLOTS):
        for g in range(4):
            cells = jnp.concatenate(
                [F[dy * 2 + dx, k, 2 * g + y] for y in range(2) for dy in range(2) for dx in range(2)], axis=0
            ).astype(BF)
            gout_ref[k, 4 * g : 4 * g + 4] = dot(gather, cells).astype(BF).reshape(4, GW, C)

    for g in range(N_DEV // N_SEQ):
        shape = (N_DEV, 256)
        at1 = iota(shape, 1)
        over = jnp.where(iota(shape, 0) == g * N_SEQ + at1 // (2 * CAP), 1.0, 0.0).astype(BF)
        rows = dot(asked_t, over)
        k8 = iota((CAP, 256), 1)
        put = jnp.sum(jnp.where(iota((CAP, 256), 0) == k8 % CAP, rows, 0.0), axis=0, keepdims=True).astype(I32)
        hit = iota((ROWS, 256), 0) == put - 1
        part = (iota((ROWS, 256), 1) // CAP) % 2
        for h in range(2):
            sel[h, :, g * 256 : (g + 1) * 256] = jnp.where(hit & (part == h), 1.0, 0.0).astype(BF)
    wait_rows(trecv, tsem.at[1])

    @pl.loop(0, C2 // 256)
    def _(n):
        h = n // 3
        cols = pl.ds(pl.multiple_of(n * 256, 256), 256)
        llm_ref[:, cols] = picked(trecv, h, (n - 3 * h) * 256).astype(BF)

    for n in range(8):
        f_send[n].wait_send()
        b_send[n].wait_send()
    wait_rows(msg, msem.at[0])
    wait_rows(gsend, gsem.at[0])
    wait_rows(tsend, tsem.at[0])


def on_device(frame_tiles, tile_ids, partner_slot, mix_kernel, mix_bias, down_weight, down_bias, token_pos, grad_rows):
    vmem = pl.BlockSpec(memory_space=pltpu.VMEM)
    smem = pl.BlockSpec(memory_space=pltpu.SMEM)
    anyw = pl.BlockSpec(memory_space=pl.ANY)
    dma = pltpu.SemaphoreType.DMA
    llm, gout = pl.pallas_call(
        kernel,
        out_shape=(
            jax.ShapeDtypeStruct((ROWS, C2), BF),
            jax.ShapeDtypeStruct((SLOTS, TH, GW, C), BF),
        ),
        in_specs=[anyw, smem, smem, vmem, vmem, anyw, vmem, vmem, anyw],
        out_specs=(vmem, vmem),
        scratch_shapes=[
            pltpu.VMEM((SLOTS, TH, GW, C), BF),
            pltpu.VMEM((4 * C, C2), BF),
            pltpu.VMEM((ROWS, C2), BF),
            pltpu.VMEM((1, C), F32),
            pltpu.VMEM((1, C2), F32),
            pltpu.VMEM((LT, KS * KS, 8, 128), F32),
            pltpu.VMEM((SLOTS, LT, XR, 2, GW, 128), F32),
            pltpu.VMEM((4, SLOTS, TH // 2, 16, C), F32),
            pltpu.VMEM((4, ROWS, C), BF),
            pltpu.VMEM((ROWS, C2), F32),
            pltpu.VMEM((ROWS, C2), BF),
            pltpu.VMEM((ROWS, C2), BF),
            pltpu.VMEM((2, ROWS, 2 * CAP * N_DEV), BF),
            pltpu.VMEM((N_DEV, 1, 128), F32),
            pltpu.VMEM((N_DEV, 1, 128), F32),
            pltpu.VMEM((N_DEV, 2 * CAP, C), BF),
            pltpu.VMEM((N_DEV, 2 * CAP, C), BF),
            pltpu.VMEM((N_DEV, 2 * CAP, C), BF),
            pltpu.VMEM((N_DEV, 2 * CAP, C), BF),
            pltpu.VMEM((N_ENC, SLOTS, LT, 96, 128), BF),
            pltpu.VMEM((N_ENC, SLOTS, LT, 96, 128), BF),
            dma((3,)),
            dma((2,)),
            dma((2,)),
            dma((2,)),
            dma((8,)),
            dma((8,)),
            dma((8,)),
            dma((8,)),
        ],
        compiler_params=pltpu.CompilerParams(
            collective_id=0, has_side_effects=True, vmem_limit_bytes=62 * 1024 * 1024
        ),
    )(
        frame_tiles,
        tile_ids,
        partner_slot,
        mix_kernel,
        mix_bias,
        down_weight,
        down_bias,
        token_pos,
        grad_rows,
    )
    return llm, gout[None, None]


def solution(mesh):
    return jax.shard_map(
        on_device,
        mesh=mesh,
        in_specs=(
            P("enc", "seq", None, None, None, None),
            P("enc", "seq", None),
            P("enc", "seq", None),
            P(),
            P(),
            P(),
            P(),
            P("enc", "seq", None, None),
            P(("enc", "seq"), None),
        ),
        out_specs=(P(("enc", "seq"), None), P("enc", "seq", None, None, None, None)),
        check_vma=False,
    )
```

```python
import functools

import itertools

import jax
import jax.numpy as jnp
from jax import lax
from jax.experimental import pallas as pl
from jax.experimental.pallas import tpu as pltpu
from jax.sharding import PartitionSpec as P

C = 768
C2 = 1536
KS = 7
TH = 16
GW = 32
SLOTS = 2
ROWS = 256
N_ENC = 8
N_SEQ = 16
N_DEV = 128
CAP = 8
HOOK = 7
GROUP = 16
GROUPS = 8

OFFSETS = sorted(itertools.product((1, 3, 2, 0), repeat=3), key=lambda o: (2 not in o, o == (0, 0, 0)))
N_FAR = 2 * sum(2 in o for o in OFFSETS)
OWN = 2 * OFFSETS.index((0, 0, 0))


def packed(axis):
    words = []
    for n in range(0, 64, 16):
        word = sum(o[axis] << (2 * i) for i, o in enumerate(OFFSETS[n : n + 16]))
        words.append(word - (1 << 32) if word >> 31 else word)
    return words


WORDS = [packed(axis) for axis in range(3)]
LT = C // 128
HALO = 3
XR = TH + 2 * HALO
SQRT_HALF = 0.7071067811865476
INV_ROOT = 0.3989422804014327
BF = jnp.bfloat16
F32 = jnp.float32
I32 = jnp.int32


def iota(shape, axis):
    return lax.broadcasted_iota(I32, shape, axis)


def dot(a, b):
    return jnp.dot(a, b, preferred_element_type=F32)


def kernel(
    tiles_hbm, ids_ref, partner_ref, mixk_ref, mixb_ref, w_hbm, downb_ref, pos_ref, grad_hbm,
    llm_ref, gout_ref,
    tiles, w, grads, mixb, downb, wb, X, F, A, slope, tok, pg, sel,
    msg, rmsg, gsend, grecv, grel, tsend, trecv, trel, rimf, rimb,
    lsem, msem, gsem, tsem, fsend, frecv, bsend, brecv,
):
    enc = lax.axis_index("enc")
    seq = lax.axis_index("seq")
    me = enc * N_SEQ + seq
    cy, core = enc // 2, enc % 2

    ld_tiles = pltpu.make_async_copy(tiles_hbm.at[0, 0], tiles, lsem.at[0])
    ld_grads = pltpu.make_async_copy(grad_hbm, grads, lsem.at[1])
    ld_w = pltpu.make_async_copy(w_hbm, w, lsem.at[2])
    ld_tiles.start()
    ld_grads.start()
    ld_w.start()

    barrier = pltpu.get_barrier_semaphore()

    @pl.loop(1, N_DEV)
    def _(i):
        e = lax.rem(enc + i // N_SEQ, N_ENC)
        s = lax.rem(seq + i % N_SEQ, N_SEQ)
        pl.semaphore_signal(barrier, inc=1, device_id=(e, s), device_id_type=pl.DeviceIdType.MESH)

    mixb[...] = mixb_ref[...].reshape(1, C)
    downb[...] = downb_ref[...].reshape(1, C2)

    pos = pos_ref[0, 0]
    prow = jnp.concatenate([pos[0:1, :], pos[1:2, :]], axis=1)
    pcol = jnp.concatenate(
        [jnp.transpose(jnp.broadcast_to(pos[i : i + 1, :].astype(F32), (128, 128))) for i in range(2)], axis=0
    ).astype(I32)[:, 0:1]
    orow, ocol = prow // ROWS, pcol // ROWS
    lcol = pcol - ocol * ROWS
    same = jnp.broadcast_to(ocol, (ROWS, ROWS)) == jnp.broadcast_to(orow, (ROWS, ROWS))
    at0, at1 = iota((ROWS, ROWS), 0), iota((ROWS, ROWS), 1)
    rank_row = jnp.sum(jnp.where(same & (at0 < at1), 1.0, 0.0), axis=0, keepdims=True).astype(I32)
    rank_col = jnp.sum(jnp.where(same & (at1 < at0), 1.0, 0.0), axis=1, keepdims=True).astype(I32)
    slot_row = orow * CAP + rank_row
    to_owner = jnp.where(iota((N_DEV, ROWS), 0) == orow, 1.0, 0.0).astype(BF)
    ranked = jnp.where(iota((ROWS, 128), 1) == rank_col, (lcol + 1).astype(F32), 0.0).astype(BF)
    msg[...] = dot(to_owner, ranked).reshape(N_DEV, 1, 128)
    rmsg[pl.ds(me, 1)] = msg[pl.ds(me, 1)]

    for a in range(KS):
        for b in range(KS):
            row = mixk_ref[a, b : b + 1, :].astype(F32)
            if a == HALO and b == HALO:
                row = row + 1.0
            for t in range(LT):
                wb[t, a * KS + b] = jnp.broadcast_to(row[:, t * 128 : (t + 1) * 128], (8, 128))

    @pl.loop(0, SLOTS * LT)
    def _(i):
        X[i // LT, i % LT] = jnp.zeros((XR, 2, GW, 128), F32)

    q0, q1 = iota((128, 128), 0), iota((128, 128), 1)
    spread = jnp.where(q1 == (q0 // 32) * 32 + (q0 % 16) * 2 + (q0 % 32) // 16, 1.0, 0.0).astype(BF)
    gather = jnp.where(q0 == (q1 // 32) * 32 + (q1 % 16) * 2 + (q1 % 32) // 16, 1.0, 0.0).astype(BF)

    def fill(k, g):
        d = dot(spread, tiles[k, 4 * g : 4 * g + 4].reshape(128, C)).reshape(4, 2, 16, C)
        for t in range(LT):
            X[k, t, HALO + 4 * g : HALO + 4 * g + 4, :, 8:24, :] = d[..., t * 128 : (t + 1) * 128]

    def own_rims(rims):
        for k in range(SLOTS):
            low = X[k, :, HALO : 2 * HALO, :, 8:24, :]
            high = X[k, :, TH : TH + HALO, :, 8:24, :]
            rim = jnp.where(lax.rem(ids_ref[0, 0, k], 2) == 0, high, low)
            rims[enc, k] = rim.astype(BF).reshape(LT, 96, 128)

    up = lax.rem(cy + 1, 4) * 2 + core
    down = lax.rem(cy + 3, 4) * 2 + core
    across = lax.rem(cy + 2, 4) * 2 + core
    sib = cy * 2 + 1 - core

    def rim_copies(rims, ssem, rsem):
        def copy(n, ref, to):
            return pltpu.make_async_remote_copy(
                src_ref=ref, dst_ref=ref, send_sem=ssem.at[n], recv_sem=rsem.at[n],
                device_id=(to, seq), device_id_type=pl.DeviceIdType.MESH,
            )

        def landed(n, ref):
            return pltpu.make_async_copy(ref, ref, rsem.at[n])

        sends = [
            copy(0, rims.at[enc], up),
            copy(1, rims.at[enc], down),
            copy(2, rims.at[enc], sib),
            copy(3, rims.at[down, 0], up),
            copy(4, rims.at[up, 1], down),
            copy(5, rims.at[down], sib),
            copy(6, rims.at[up], sib),
            copy(7, rims.at[across], sib),
        ]
        other = 1 - 2 * core
        arrivals = [
            landed(0, rims.at[down]),
            landed(1, rims.at[up]),
            landed(2, rims.at[sib]),
            landed(3, rims.at[across, 0]),
            landed(4, rims.at[across, 1]),
            landed(5, rims.at[down + other]),
            landed(6, rims.at[up + other]),
            landed(7, rims.at[across + other]),
        ]
        return sends, arrivals

    def place_rims(rims):
        for k in range(SLOTS):
            want = partner_ref[0, 0, k]
            rim = jnp.zeros((LT, 96, 128), BF)
            for q in range(N_ENC * SLOTS):
                rim = jnp.where(want == q, rims[q // 2, q % 2], rim)
            rim = rim.astype(F32).reshape(LT, HALO, 2, 16, 128)
            lower = lax.rem(ids_ref[0, 0, k], 2) == 1
            X[k, :, 0:HALO, :, 8:24, :] = jnp.where(lower, rim, 0.0)
            X[k, :, TH + HALO : XR, :, 8:24, :] = jnp.where(lower, 0.0, rim)

    def conv(flip, with_bias, hook=None):
        @pl.loop(0, SLOTS * LT)
        def _(i):
            if hook is not None:
                pl.when(i == HOOK)(hook)
            k, t = i // LT, i % LT
            lanes = pl.ds(pl.multiple_of(t * 128, 128), 128)
            for cb in range(2):
                first = jnp.zeros((TH, 8, 128), F32)
                if with_bias:
                    first = first + mixb[:, lanes].reshape(1, 1, 128)
                acc = [first, first]
                for p in range(2):
                    for sh in range(-2, 3):
                        uses = [(dx, 2 * sh + p + 3 - dx) for dx in range(2)]
                        uses = [(dx, b) for dx, b in uses if 0 <= b < KS]
                        if not uses:
                            continue
                        xs = X[k, t, :, p, 8 + 8 * cb + sh : 16 + 8 * cb + sh, :]
                        for dx, b in uses:
                            for a in range(KS):
                                tap = a * KS + b
                                if flip:
                                    tap = KS * KS - 1 - tap
                                acc[dx] = acc[dx] + wb[t, tap][None] * xs[a : a + TH]
                for dx in range(2):
                    rows = acc[dx].reshape(TH // 2, 2, 8, 128)
                    for dy in range(2):
                        F[dy * 2 + dx, k, :, 8 * cb : 8 * cb + 8, lanes] = rows[:, dy]

    cx, cz = seq // 4, lax.rem(seq, 4)

    def word(axis, block):
        w0, w1, w2, w3 = WORDS[axis]
        return jnp.where(block < 2, jnp.where(block == 0, w0, w1), jnp.where(block == 2, w2, w3))

    def offset(n):
        return [jnp.right_shift(word(axis, n // 16), 2 * (n % 16)) & 3 for axis in range(3)]

    def step(off, f):
        ways = (1 + 2 * f, 3 - 2 * f, 1 + 2 * f)
        return [jnp.where(d == 2, way, 0) for d, way in zip(off, ways)]

    def device(dx, dy, dz, f):
        c = core + f - 2 * core * f
        return ((cy + dy) & 3) * 2 + c, ((cx + dx) & 3) * 4 + ((cz + dz) & 3)

    def fill_rows(buf, onehot, rows_ref):
        @pl.loop(0, GROUPS)
        def _(i):
            place = iota((GROUP * CAP, 1), 0) // CAP
            shift = 2 * ((i % 2) * CAP + place // 2)
            dx, dy, dz = [jnp.right_shift(jnp.full(place.shape, word(axis, i // 2)), shift) & 3 for axis in range(3)]
            e, s = device(dx, dy, dz, place % 2)
            hot = onehot(e * N_SEQ + s)
            y0 = dot(hot, rows_ref[:, 0:C]).reshape(GROUP, CAP, C)
            y1 = dot(hot, rows_ref[:, C:C2]).reshape(GROUP, CAP, C)
            buf[pl.ds(i * GROUP, GROUP)] = jnp.concatenate([y0, y1], axis=1).astype(BF)

    def send_far(buf, rel, sems):
        @pl.loop(0, N_FAR)
        def _(q):
            f = q % 2
            e, s = device(*step(offset(q // 2), f), 0)
            pltpu.make_async_remote_copy(
                src_ref=buf.at[q], dst_ref=rel.at[q],
                send_sem=sems.at[0], recv_sem=sems.at[2],
                device_id=(e, s), device_id_type=pl.DeviceIdType.MESH,
            ).start()

    def send_near(buf, got, sems):
        @pl.loop(N_FAR, N_DEV)
        def _(q):
            @pl.when(q != OWN)
            def _():
                e, s = device(*offset(q // 2), q % 2)
                pltpu.make_async_remote_copy(
                    src_ref=buf.at[q], dst_ref=got.at[me],
                    send_sem=sems.at[0], recv_sem=sems.at[1],
                    device_id=(e, s), device_id_type=pl.DeviceIdType.MESH,
                ).start()

    def forward(rel, got, sems):
        part = rel.at[pl.ds(0, N_FAR)]
        pltpu.make_async_copy(part, part, sems.at[2]).wait()

        @pl.loop(0, N_FAR)
        def _(q):
            f = q % 2
            off = offset(q // 2)
            leg = step(off, f)
            e0, s0 = device(*[4 - d for d in leg], 0)
            e, s = device(*[o + 4 - d for o, d in zip(off, leg)], f)
            pltpu.make_async_remote_copy(
                src_ref=rel.at[q], dst_ref=got.at[e0 * N_SEQ + s0],
                send_sem=sems.at[3], recv_sem=sems.at[1],
                device_id=(e, s), device_id_type=pl.DeviceIdType.MESH,
            ).start()

    def keep_own(buf, got):
        got[pl.ds(me, 1)] = buf[pl.ds(OWN, 1)]

    def wait_rows(buf, sem):
        part = buf.at[pl.ds(0, N_DEV - 1)]
        pltpu.make_async_copy(part, part, sem).wait()

    ld_tiles.wait()
    for k in range(SLOTS):
        fill(k, 0)
        fill(k, 3)
    own_rims(rimf)
    pl.semaphore_wait(barrier, N_DEV - 1)

    @pl.loop(1, N_DEV)
    def _(i):
        e = lax.rem(enc + i // N_SEQ, N_ENC)
        s = lax.rem(seq + i % N_SEQ, N_SEQ)
        pltpu.make_async_remote_copy(
            src_ref=msg.at[e * N_SEQ + s], dst_ref=rmsg.at[me],
            send_sem=msem.at[0], recv_sem=msem.at[1],
            device_id=(e, s), device_id_type=pl.DeviceIdType.MESH,
        ).start()

    f_send, f_got = rim_copies(rimf, fsend, frecv)
    for n in range(3):
        f_send[n].start()
    for k in range(SLOTS):
        fill(k, 1)
        fill(k, 2)
    f_got[0].wait()
    f_send[3].start()
    f_send[5].start()
    f_got[1].wait()
    f_send[4].start()
    f_send[6].start()
    ld_grads.wait()
    wait_rows(rmsg, msem.at[1])

    asked = rmsg[...].reshape(N_DEV, 128)
    asked_t = jnp.transpose(asked)[0:CAP, :].astype(BF)
    asked = asked.astype(BF)

    def fetch(owner):
        shape = (GROUP * CAP, 128)
        at = iota(shape, 0)
        rows = dot(jnp.where(iota(shape, 1) == owner, 1.0, 0.0).astype(BF), asked)
        want = jnp.sum(jnp.where(iota(shape, 1) == at % CAP, rows, 0.0), axis=1, keepdims=True).astype(I32)
        return jnp.where(iota((GROUP * CAP, ROWS), 1) == want - 1, 1.0, 0.0).astype(BF)

    fill_rows(gsend, fetch, grads)
    send_far(gsend, grel, gsem)
    send_near(gsend, grecv, gsem)
    keep_own(gsend, grecv)

    f_got[3].wait()
    f_got[4].wait()
    f_send[7].start()
    for n in (2, 5, 6, 7):
        f_got[n].wait()
    place_rims(rimf)
    conv(False, True, lambda: forward(grel, grecv, gsem))

    @pl.loop(0, 4)
    def _(j):
        A[j] = F[j].reshape(ROWS, C).astype(BF)

    ld_w.wait()

    @pl.loop(0, C2 // 256)
    def _(n):
        cols = pl.ds(pl.multiple_of(n * 256, 256), 256)
        pre = jnp.zeros((ROWS, 256), F32) + downb[:, cols]
        for j in range(4):
            pre = pre + dot(A[j], w[j * C : (j + 1) * C, cols])
        phi = 0.5 * (1.0 + lax.erf(pre * SQRT_HALF))
        tok[:, cols] = (pre * phi).astype(BF)
        slope[:, cols] = phi + pre * INV_ROOT * jnp.exp(-0.5 * pre * pre)

    def scatter(owner):
        at = owner * CAP + iota((GROUP * CAP, 1), 0) % CAP
        return jnp.where(at == slot_row, 1.0, 0.0).astype(BF)

    fill_rows(tsend, scatter, tok)
    send_far(tsend, trel, tsem)
    send_near(tsend, trecv, tsem)
    keep_own(tsend, trecv)

    back_at = ocol * (2 * CAP) + rank_col
    for h in range(2):
        sel[h] = jnp.where(iota((ROWS, 2 * CAP * N_DEV), 1) == back_at + h * CAP, 1.0, 0.0).astype(BF)
    wait_rows(grecv, gsem.at[1])

    def picked(got, h, c0):
        part = got[:, :, pl.ds(pl.multiple_of(c0, 256), 256)].reshape(2 * CAP * N_DEV, 256)
        return dot(sel[h], part)

    @pl.loop(0, C2 // 256)
    def _(n):
        h = n // 3
        cols = pl.ds(pl.multiple_of(n * 256, 256), 256)
        pg[:, cols] = (picked(grecv, h, (n - 3 * h) * 256) * slope[:, cols]).astype(BF)

    @pl.loop(0, 4 * (C // 256))
    def _(m):
        j, n = m // 3, lax.rem(m, 3)
        part = w[pl.ds(pl.multiple_of(m * 256, 256), 256), :]
        g = lax.dot_general(pg[...], part, (((1,), (1,)), ((), ())), preferred_element_type=F32)
        g = g.astype(BF).astype(F32).reshape(SLOTS, TH // 2, 16, 256)
        dy, dx = j // 2, lax.rem(j, 2)
        for y in range(TH // 2):
            for i in range(2):
                X[:, 2 * n + i, HALO + 2 * y + dy, dx, 8:24, :] = g[:, y, :, i * 128 : (i + 1) * 128]

    own_rims(rimb)
    b_send, b_got = rim_copies(rimb, bsend, brecv)
    for n in range(3):
        b_send[n].start()
    b_got[0].wait()
    b_send[3].start()
    b_send[5].start()
    b_got[1].wait()
    b_send[4].start()
    b_send[6].start()
    forward(trel, trecv, tsem)
    b_got[3].wait()
    b_got[4].wait()
    b_send[7].start()
    for n in (2, 5, 6, 7):
        b_got[n].wait()
    place_rims(rimb)
    conv(True, False)

    for k in range(SLOTS):
        for g in range(4):
            cells = jnp.concatenate(
                [F[dy * 2 + dx, k, 2 * g + y] for y in range(2) for dy in range(2) for dx in range(2)], axis=0
            ).astype(BF)
            gout_ref[k, 4 * g : 4 * g + 4] = dot(gather, cells).astype(BF).reshape(4, GW, C)

    for g in range(N_DEV // N_SEQ):
        shape = (N_DEV, 256)
        at1 = iota(shape, 1)
        over = jnp.where(iota(shape, 0) == g * N_SEQ + at1 // (2 * CAP), 1.0, 0.0).astype(BF)
        rows = dot(asked_t, over)
        k8 = iota((CAP, 256), 1)
        put = jnp.sum(jnp.where(iota((CAP, 256), 0) == k8 % CAP, rows, 0.0), axis=0, keepdims=True).astype(I32)
        hit = iota((ROWS, 256), 0) == put - 1
        part = (iota((ROWS, 256), 1) // CAP) % 2
        for h in range(2):
            sel[h, :, g * 256 : (g + 1) * 256] = jnp.where(hit & (part == h), 1.0, 0.0).astype(BF)
    wait_rows(trecv, tsem.at[1])

    @pl.loop(0, C2 // 256)
    def _(n):
        h = n // 3
        cols = pl.ds(pl.multiple_of(n * 256, 256), 256)
        llm_ref[:, cols] = picked(trecv, h, (n - 3 * h) * 256).astype(BF)

    for n in range(8):
        f_send[n].wait_send()
        b_send[n].wait_send()
    wait_rows(msg, msem.at[0])
    for buf, rel, sems in ((gsend, grel, gsem), (tsend, trel, tsem)):
        wait_rows(buf, sems.at[0])
        part = rel.at[pl.ds(0, N_FAR)]
        pltpu.make_async_copy(part, part, sems.at[3]).wait()


def on_device(frame_tiles, tile_ids, partner_slot, mix_kernel, mix_bias, down_weight, down_bias, token_pos, grad_rows):
    vmem = pl.BlockSpec(memory_space=pltpu.VMEM)
    smem = pl.BlockSpec(memory_space=pltpu.SMEM)
    anyw = pl.BlockSpec(memory_space=pl.ANY)
    dma = pltpu.SemaphoreType.DMA
    llm, gout = pl.pallas_call(
        kernel,
        out_shape=(
            jax.ShapeDtypeStruct((ROWS, C2), BF),
            jax.ShapeDtypeStruct((SLOTS, TH, GW, C), BF),
        ),
        in_specs=[anyw, smem, smem, vmem, vmem, anyw, vmem, vmem, anyw],
        out_specs=(vmem, vmem),
        scratch_shapes=[
            pltpu.VMEM((SLOTS, TH, GW, C), BF),
            pltpu.VMEM((4 * C, C2), BF),
            pltpu.VMEM((ROWS, C2), BF),
            pltpu.VMEM((1, C), F32),
            pltpu.VMEM((1, C2), F32),
            pltpu.VMEM((LT, KS * KS, 8, 128), F32),
            pltpu.VMEM((SLOTS, LT, XR, 2, GW, 128), F32),
            pltpu.VMEM((4, SLOTS, TH // 2, 16, C), F32),
            pltpu.VMEM((4, ROWS, C), BF),
            pltpu.VMEM((ROWS, C2), F32),
            pltpu.VMEM((ROWS, C2), BF),
            pltpu.VMEM((ROWS, C2), BF),
            pltpu.VMEM((2, ROWS, 2 * CAP * N_DEV), BF),
            pltpu.VMEM((N_DEV, 1, 128), F32),
            pltpu.VMEM((N_DEV, 1, 128), F32),
            pltpu.VMEM((N_DEV, 2 * CAP, C), BF),
            pltpu.VMEM((N_DEV, 2 * CAP, C), BF),
            pltpu.VMEM((N_FAR, 2 * CAP, C), BF),
            pltpu.VMEM((N_DEV, 2 * CAP, C), BF),
            pltpu.VMEM((N_DEV, 2 * CAP, C), BF),
            pltpu.VMEM((N_FAR, 2 * CAP, C), BF),
            pltpu.VMEM((N_ENC, SLOTS, LT, 96, 128), BF),
            pltpu.VMEM((N_ENC, SLOTS, LT, 96, 128), BF),
            dma((3,)),
            dma((2,)),
            dma((4,)),
            dma((4,)),
            dma((8,)),
            dma((8,)),
            dma((8,)),
            dma((8,)),
        ],
        compiler_params=pltpu.CompilerParams(
            collective_id=0, has_side_effects=True, vmem_limit_bytes=62 * 1024 * 1024
        ),
    )(
        frame_tiles,
        tile_ids,
        partner_slot,
        mix_kernel,
        mix_bias,
        down_weight,
        down_bias,
        token_pos,
        grad_rows,
    )
    return llm, gout[None, None]


def solution(mesh):
    return jax.shard_map(
        on_device,
        mesh=mesh,
        in_specs=(
            P("enc", "seq", None, None, None, None),
            P("enc", "seq", None),
            P("enc", "seq", None),
            P(),
            P(),
            P(),
            P(),
            P("enc", "seq", None, None),
            P(("enc", "seq"), None),
        ),
        out_specs=(P(("enc", "seq"), None), P("enc", "seq", None, None, None, None)),
        check_vma=False,
    )
```

```python
import functools

import itertools

import jax
import jax.numpy as jnp
from jax import lax
from jax.experimental import pallas as pl
from jax.experimental.pallas import tpu as pltpu
from jax.sharding import PartitionSpec as P

C = 768
C2 = 1536
KS = 7
TH = 16
GW = 32
SLOTS = 2
ROWS = 256
N_ENC = 8
N_SEQ = 16
N_DEV = 128
CAP = 8
SLOT_ROWS = CAP * N_DEV

ALL_OFFSETS = list(itertools.product(range(4), repeat=3))
FAR = [o for o in ALL_OFFSETS if 2 in o]
NEAR = [o for o in ALL_OFFSETS if 2 not in o and any(o)]
OFFSETS = (
    [FAR[16 * i % len(FAR)] for i in range(len(FAR))]
    + [NEAR[11 * i % len(NEAR)] for i in range(len(NEAR))]
    + [(0, 0, 0)]
)
N_FAR = 2 * len(FAR)
OWN = N_DEV - 2


def packed(axis):
    words = []
    for n in range(0, 64, 16):
        word = sum(o[axis] << (2 * i) for i, o in enumerate(OFFSETS[n : n + 16]))
        words.append(word - (1 << 32) if word >> 31 else word)
    return words


WORDS = [packed(axis) for axis in range(3)]
LT = C // 128
HALO = 3
XR = TH + 2 * HALO
SQRT_HALF = 0.7071067811865476
INV_ROOT = 0.3989422804014327
BF = jnp.bfloat16
F32 = jnp.float32
I32 = jnp.int32


def iota(shape, axis):
    return lax.broadcasted_iota(I32, shape, axis)


def dot(a, b):
    return jnp.dot(a, b, preferred_element_type=F32)


def kernel(
    tiles_hbm, ids_ref, partner_ref, mixk_ref, mixb_ref, w_hbm, downb_ref, pos_ref, grad_hbm,
    llm_ref, gout_ref,
    tiles, w, grads, mixb, downb, wb, X, F, A, slope, tok, pg, sel, hot, owner,
    msg, rmsg, gsend, grecv, grel, tsend, trecv, trel, rimf, rimb,
    lsem, msem, gsem, tsem, fsend, frecv, bsend, brecv,
):
    enc = lax.axis_index("enc")
    seq = lax.axis_index("seq")
    me = enc * N_SEQ + seq
    cy, core = enc // 2, enc % 2

    ld_tiles = pltpu.make_async_copy(tiles_hbm.at[0, 0], tiles, lsem.at[0])
    ld_grads = pltpu.make_async_copy(grad_hbm, grads, lsem.at[1])
    ld_w = pltpu.make_async_copy(w_hbm, w, lsem.at[2])
    ld_tiles.start()
    ld_grads.start()
    ld_w.start()

    barrier = pltpu.get_barrier_semaphore()

    @pl.loop(1, N_DEV)
    def _(i):
        e, s = (enc + (i >> 4)) & (N_ENC - 1), (seq + i) & (N_SEQ - 1)
        pl.semaphore_signal(barrier, inc=1, device_id=(e, s), device_id_type=pl.DeviceIdType.MESH)

    mixb[...] = mixb_ref[...].reshape(1, C)
    downb[...] = downb_ref[...].reshape(1, C2)

    pos = pos_ref[0, 0]
    prow = jnp.concatenate([pos[0:1, :], pos[1:2, :]], axis=1)
    pcol = jnp.concatenate(
        [jnp.transpose(jnp.broadcast_to(pos[i : i + 1, :].astype(F32), (128, 128))) for i in range(2)], axis=0
    ).astype(I32)[:, 0:1]
    orow, ocol = prow // ROWS, pcol // ROWS
    lcol = pcol - ocol * ROWS
    same = jnp.broadcast_to(ocol, (ROWS, ROWS)) == jnp.broadcast_to(orow, (ROWS, ROWS))
    at0, at1 = iota((ROWS, ROWS), 0), iota((ROWS, ROWS), 1)
    rank_row = jnp.sum(jnp.where(same & (at0 < at1), 1.0, 0.0), axis=0, keepdims=True).astype(I32)
    rank_col = jnp.sum(jnp.where(same & (at1 < at0), 1.0, 0.0), axis=1, keepdims=True).astype(I32)
    slot_row = orow * CAP + rank_row
    to_owner = jnp.where(iota((N_DEV, ROWS), 0) == orow, 1.0, 0.0).astype(BF)
    ranked = jnp.where(iota((ROWS, 128), 1) == rank_col, (lcol + 1).astype(F32), 0.0).astype(BF)
    msg[...] = dot(to_owner, ranked).reshape(N_DEV, 1, 128)
    rmsg[pl.ds(me, 1)] = msg[pl.ds(me, 1)]

    for a in range(KS):
        for b in range(KS):
            row = mixk_ref[a, b : b + 1, :].astype(F32)
            if a == HALO and b == HALO:
                row = row + 1.0
            for t in range(LT):
                wb[t, a * KS + b] = jnp.broadcast_to(row[:, t * 128 : (t + 1) * 128], (8, 128))

    @pl.loop(0, SLOTS * LT)
    def _(i):
        k, t = i // LT, lax.rem(i, LT)
        X[k, t, :, :, 0:8, :] = jnp.zeros((XR, 2, 8, 128), F32)
        X[k, t, :, :, 24:32, :] = jnp.zeros((XR, 2, 8, 128), F32)
        X[k, t, 0:HALO] = jnp.zeros((HALO, 2, GW, 128), F32)
        X[k, t, XR - HALO : XR] = jnp.zeros((HALO, 2, GW, 128), F32)

    q0, q1 = iota((128, 128), 0), iota((128, 128), 1)
    spread = jnp.where(q1 == (q0 // 32) * 32 + (q0 % 16) * 2 + (q0 % 32) // 16, 1.0, 0.0).astype(BF)
    gather = jnp.where(q0 == (q1 // 32) * 32 + (q1 % 16) * 2 + (q1 % 32) // 16, 1.0, 0.0).astype(BF)

    def fill(k, g):
        d = dot(spread, tiles[k, 4 * g : 4 * g + 4].reshape(128, C)).reshape(4, 2, 16, C)
        for t in range(LT):
            X[k, t, HALO + 4 * g : HALO + 4 * g + 4, :, 8:24, :] = d[..., t * 128 : (t + 1) * 128]

    def own_rims(rims):
        for k in range(SLOTS):
            low = X[k, :, HALO : 2 * HALO, :, 8:24, :]
            high = X[k, :, TH : TH + HALO, :, 8:24, :]
            rim = jnp.where(lax.rem(ids_ref[0, 0, k], 2) == 0, high, low)
            rims[enc, k] = rim.astype(BF).reshape(LT, 96, 128)

    up = lax.rem(cy + 1, 4) * 2 + core
    down = lax.rem(cy + 3, 4) * 2 + core
    across = lax.rem(cy + 2, 4) * 2 + core
    sib = cy * 2 + 1 - core

    def rim_copies(rims, ssem, rsem):
        def copy(n, ref, to):
            return pltpu.make_async_remote_copy(
                src_ref=ref, dst_ref=ref, send_sem=ssem.at[n], recv_sem=rsem.at[n],
                device_id=(to, seq), device_id_type=pl.DeviceIdType.MESH,
            )

        def landed(n, ref):
            return pltpu.make_async_copy(ref, ref, rsem.at[n])

        sends = [
            copy(0, rims.at[enc], up),
            copy(1, rims.at[enc], down),
            copy(2, rims.at[enc], sib),
            copy(3, rims.at[down, 0], up),
            copy(4, rims.at[up, 1], down),
            copy(5, rims.at[down], sib),
            copy(6, rims.at[up], sib),
            copy(7, rims.at[across], sib),
        ]
        other = 1 - 2 * core
        arrivals = [
            landed(0, rims.at[down]),
            landed(1, rims.at[up]),
            landed(2, rims.at[sib]),
            landed(3, rims.at[across, 0]),
            landed(4, rims.at[across, 1]),
            landed(5, rims.at[down + other]),
            landed(6, rims.at[up + other]),
            landed(7, rims.at[across + other]),
        ]
        return sends, arrivals

    def place_rims(rims):
        for k in range(SLOTS):
            want = partner_ref[0, 0, k]
            rim = jnp.zeros((LT, 96, 128), BF)
            for q in range(N_ENC * SLOTS):
                rim = jnp.where(want == q, rims[q // 2, q % 2], rim)
            rim = rim.astype(F32).reshape(LT, HALO, 2, 16, 128)
            is_lower = lax.rem(ids_ref[0, 0, k], 2) == 1
            X[k, :, 0:HALO, :, 8:24, :] = jnp.where(is_lower, rim, 0.0)
            X[k, :, TH + HALO : XR, :, 8:24, :] = jnp.where(is_lower, 0.0, rim)

    def lower(k):
        return lax.rem(ids_ref[0, 0, k], 2)

    def conv(flip, with_bias, part):
        @pl.loop(0, SLOTS * LT)
        def _(i):
            k, t = i // LT, lax.rem(i, LT)
            lanes = pl.ds(pl.multiple_of(t * 128, 128), 128)
            below = lower(k)
            start = 8 * (below if part == 0 else 1 - below)
            for cb in range(2):
                first = jnp.zeros((TH // 2, 8, 128), F32)
                if with_bias:
                    first = first + mixb[:, lanes].reshape(1, 1, 128)
                acc = [first, first]
                for p in range(2):
                    for sh in range(-2, 3):
                        uses = [(dx, 2 * sh + p + 3 - dx) for dx in range(2)]
                        uses = [(dx, b) for dx, b in uses if 0 <= b < KS]
                        if not uses:
                            continue
                        xs = X[k, t, pl.ds(start, TH // 2 + 2 * HALO), p, 8 + 8 * cb + sh : 16 + 8 * cb + sh, :]
                        for dx, b in uses:
                            for a in range(KS):
                                tap = a * KS + b
                                if flip:
                                    tap = KS * KS - 1 - tap
                                acc[dx] = acc[dx] + wb[t, tap][None] * xs[a : a + TH // 2]
                for dx in range(2):
                    rows = acc[dx].reshape(TH // 4, 2, 8, 128)
                    for dy in range(2):
                        F[part, dy * 2 + dx, k, :, 8 * cb : 8 * cb + 8, lanes] = rows[:, dy]

    cx, cz = seq >> 2, seq & 3
    at_x = [((cx + d) & 3) * 4 for d in range(4)]
    at_y = [((cy + d) & 3) * 2 for d in range(4)]
    at_z = [(cz + d) & 3 for d in range(4)]
    at_core = [core, 1 - core]

    def step(off, f):
        return [way if d == 2 else 0 for d, way in zip(off, (1 + 2 * f, 3 - 2 * f, 1 + 2 * f))]

    def device(off, f):
        return at_y[off[1]] + at_core[f], at_x[off[0]] + at_z[off[2]]

    def owner_of_row():
        place = iota((SLOT_ROWS, 1), 0) // CAP
        block, shift = place // 32, 2 * ((place // 2) % 16)
        d = []
        for w0, w1, w2, w3 in WORDS:
            word = jnp.where(block < 2, jnp.where(block == 0, w0, w1), jnp.where(block == 2, w2, w3))
            d.append(jnp.right_shift(word, shift) & 3)
        c = core + place % 2 - 2 * core * (place % 2)
        return (((cy + d[1]) & 3) * 2 + c) * N_SEQ + ((cx + d[0]) & 3) * 4 + ((cz + d[2]) & 3)

    def fill_rows(buf, rows_ref):
        @pl.loop(0, C // 256)
        def _(n):
            c0 = pl.multiple_of(n * 256, 256)
            y0 = dot(hot[...], rows_ref[:, pl.ds(c0, 256)]).reshape(N_DEV, CAP, 256)
            y1 = dot(hot[...], rows_ref[:, pl.ds(c0 + C, 256)]).reshape(N_DEV, CAP, 256)
            buf[:, :, pl.ds(c0, 256)] = jnp.concatenate([y0, y1], axis=1).astype(BF)

    def send_far(buf, rel, sems):
        for q in range(N_FAR):
            pltpu.make_async_remote_copy(
                src_ref=buf.at[q], dst_ref=rel.at[q],
                send_sem=sems.at[0], recv_sem=sems.at[2],
                device_id=device(step(OFFSETS[q // 2], q % 2), 0), device_id_type=pl.DeviceIdType.MESH,
            ).start()

    def send_near(buf, got, sems):
        for q in range(N_FAR, N_DEV):
            if q != OWN:
                pltpu.make_async_remote_copy(
                    src_ref=buf.at[q], dst_ref=got.at[me],
                    send_sem=sems.at[0], recv_sem=sems.at[1],
                    device_id=device(OFFSETS[q // 2], q % 2), device_id_type=pl.DeviceIdType.MESH,
                ).start()

    def forward(rel, got, sems):
        part = rel.at[pl.ds(0, N_FAR)]
        pltpu.make_async_copy(part, part, sems.at[2]).wait()
        for q in range(N_FAR):
            off = OFFSETS[q // 2]
            leg = step(off, q % 2)
            e0, s0 = device([(4 - d) % 4 for d in leg], 0)
            rest = [(o + 4 - d) % 4 for o, d in zip(off, leg)]
            pltpu.make_async_remote_copy(
                src_ref=rel.at[q], dst_ref=got.at[e0 * N_SEQ + s0],
                send_sem=sems.at[3], recv_sem=sems.at[1],
                device_id=device(rest, q % 2), device_id_type=pl.DeviceIdType.MESH,
            ).start()

    def keep_own(buf, got):
        got[pl.ds(me, 1)] = buf[OWN : OWN + 1]

    def wait_rows(buf, sem):
        part = buf.at[pl.ds(0, N_DEV - 1)]
        pltpu.make_async_copy(part, part, sem).wait()

    ld_tiles.wait()
    for k in range(SLOTS):
        for g in (0, 3, 1, 2):
            fill(k, g)
    own_rims(rimf)
    owner[...] = owner_of_row()
    pl.semaphore_wait(barrier, N_DEV - 1)

    f_send, f_got = rim_copies(rimf, fsend, frecv)
    for n in range(3):
        f_send[n].start()

    @pl.loop(1, N_DEV)
    def _(i):
        e, s = (enc + (i >> 4)) & (N_ENC - 1), (seq + i) & (N_SEQ - 1)
        pltpu.make_async_remote_copy(
            src_ref=msg.at[e * N_SEQ + s], dst_ref=rmsg.at[me],
            send_sem=msem.at[0], recv_sem=msem.at[1],
            device_id=(e, s), device_id_type=pl.DeviceIdType.MESH,
        ).start()

    conv(False, True, 0)
    ld_grads.wait()
    wait_rows(rmsg, msem.at[1])

    asked = rmsg[...].reshape(N_DEV, 128)
    asked_t = jnp.transpose(asked)[0:CAP, :].astype(BF)
    asked = asked.astype(BF)

    shape = (SLOT_ROWS, 128)
    rows = dot(jnp.where(iota(shape, 1) == owner[...], 1.0, 0.0).astype(BF), asked)
    want = jnp.sum(jnp.where(iota(shape, 1) == iota(shape, 0) % CAP, rows, 0.0), axis=1, keepdims=True).astype(I32)
    hot[...] = jnp.where(iota((SLOT_ROWS, ROWS), 1) == want - 1, 1.0, 0.0).astype(BF)
    fill_rows(gsend, grads)
    f_got[0].wait()
    f_send[3].start()
    f_send[5].start()
    f_got[1].wait()
    f_send[4].start()
    f_send[6].start()
    send_far(gsend, grel, gsem)
    send_near(gsend, grecv, gsem)
    keep_own(gsend, grecv)

    f_got[3].wait()
    f_got[4].wait()
    f_send[7].start()
    for n in (2, 5, 6, 7):
        f_got[n].wait()
    place_rims(rimf)
    conv(False, True, 1)

    def half_rows(j, k, y):
        below = lower(k)
        return F[below if y == 0 else 1 - below, j, k]

    @pl.loop(0, 4)
    def _(j):
        for k in range(SLOTS):
            for y in range(2):
                A[j, k * 128 + y * 64 : k * 128 + y * 64 + 64] = half_rows(j, k, y).reshape(64, C).astype(BF)

    forward(grel, grecv, gsem)
    ld_w.wait()

    @pl.loop(0, C2 // 256)
    def _(n):
        cols = pl.ds(pl.multiple_of(n * 256, 256), 256)
        pre = jnp.zeros((ROWS, 256), F32) + downb[:, cols]
        for j in range(4):
            pre = pre + dot(A[j], w[j * C : (j + 1) * C, cols])
        phi = 0.5 * (1.0 + lax.erf(pre * SQRT_HALF))
        tok[:, cols] = (pre * phi).astype(BF)
        slope[:, cols] = phi + pre * INV_ROOT * jnp.exp(-0.5 * pre * pre)

    at = owner[...] * CAP + iota((SLOT_ROWS, 1), 0) % CAP
    hot[...] = jnp.where(at == slot_row, 1.0, 0.0).astype(BF)
    fill_rows(tsend, tok)
    send_far(tsend, trel, tsem)
    send_near(tsend, trecv, tsem)
    keep_own(tsend, trecv)

    back_at = ocol * (2 * CAP) + rank_col
    for h in range(2):
        sel[h] = jnp.where(iota((ROWS, 2 * CAP * N_DEV), 1) == back_at + h * CAP, 1.0, 0.0).astype(BF)
    wait_rows(grecv, gsem.at[1])

    def picked(got, h, c0):
        part = got[:, :, pl.ds(pl.multiple_of(c0, 256), 256)].reshape(2 * CAP * N_DEV, 256)
        return dot(sel[h], part)

    @pl.loop(0, C2 // 256)
    def _(n):
        h = n // 3
        cols = pl.ds(pl.multiple_of(n * 256, 256), 256)
        pg[:, cols] = (picked(grecv, h, (n - 3 * h) * 256) * slope[:, cols]).astype(BF)

    @pl.loop(0, 4 * (C // 256))
    def _(m):
        j, n = m // 3, lax.rem(m, 3)
        part = w[pl.ds(pl.multiple_of(m * 256, 256), 256), :]
        g = lax.dot_general(pg[...], part, (((1,), (1,)), ((), ())), preferred_element_type=F32)
        g = g.astype(BF).astype(F32).reshape(SLOTS, TH // 2, 16, 256)
        dy, dx = j // 2, lax.rem(j, 2)
        for y in range(TH // 2):
            for i in range(2):
                X[:, 2 * n + i, HALO + 2 * y + dy, dx, 8:24, :] = g[:, y, :, i * 128 : (i + 1) * 128]

    own_rims(rimb)
    b_send, b_got = rim_copies(rimb, bsend, brecv)
    for n in range(3):
        b_send[n].start()
    conv(True, False, 0)
    b_got[0].wait()
    b_send[3].start()
    b_send[5].start()
    b_got[1].wait()
    b_send[4].start()
    b_send[6].start()
    forward(trel, trecv, tsem)
    b_got[3].wait()
    b_got[4].wait()
    b_send[7].start()
    for n in (2, 5, 6, 7):
        b_got[n].wait()
    place_rims(rimb)
    conv(True, False, 1)

    for k in range(SLOTS):
        for g in range(4):
            cells = jnp.concatenate(
                [
                    F[lower(k) if g < 2 else 1 - lower(k), dy * 2 + dx, k, 2 * (g % 2) + y]
                    for y in range(2) for dy in range(2) for dx in range(2)
                ],
                axis=0,
            ).astype(BF)
            gout_ref[k, 4 * g : 4 * g + 4] = dot(gather, cells).astype(BF).reshape(4, GW, C)

    for g in range(N_DEV // N_SEQ):
        shape = (N_DEV, 256)
        at1 = iota(shape, 1)
        over = jnp.where(iota(shape, 0) == g * N_SEQ + at1 // (2 * CAP), 1.0, 0.0).astype(BF)
        rows = dot(asked_t, over)
        k8 = iota((CAP, 256), 1)
        put = jnp.sum(jnp.where(iota((CAP, 256), 0) == k8 % CAP, rows, 0.0), axis=0, keepdims=True).astype(I32)
        hit = iota((ROWS, 256), 0) == put - 1
        part = (iota((ROWS, 256), 1) // CAP) % 2
        for h in range(2):
            sel[h, :, g * 256 : (g + 1) * 256] = jnp.where(hit & (part == h), 1.0, 0.0).astype(BF)
    wait_rows(trecv, tsem.at[1])

    @pl.loop(0, C2 // 256)
    def _(n):
        h = n // 3
        cols = pl.ds(pl.multiple_of(n * 256, 256), 256)
        llm_ref[:, cols] = picked(trecv, h, (n - 3 * h) * 256).astype(BF)

    for n in range(8):
        f_send[n].wait_send()
        b_send[n].wait_send()
    wait_rows(msg, msem.at[0])
    for buf, rel, sems in ((gsend, grel, gsem), (tsend, trel, tsem)):
        wait_rows(buf, sems.at[0])
        part = rel.at[pl.ds(0, N_FAR)]
        pltpu.make_async_copy(part, part, sems.at[3]).wait()


def on_device(frame_tiles, tile_ids, partner_slot, mix_kernel, mix_bias, down_weight, down_bias, token_pos, grad_rows):
    vmem = pl.BlockSpec(memory_space=pltpu.VMEM)
    smem = pl.BlockSpec(memory_space=pltpu.SMEM)
    anyw = pl.BlockSpec(memory_space=pl.ANY)
    dma = pltpu.SemaphoreType.DMA
    llm, gout = pl.pallas_call(
        kernel,
        out_shape=(
            jax.ShapeDtypeStruct((ROWS, C2), BF),
            jax.ShapeDtypeStruct((SLOTS, TH, GW, C), BF),
        ),
        in_specs=[anyw, smem, smem, vmem, vmem, anyw, vmem, vmem, anyw],
        out_specs=(vmem, vmem),
        scratch_shapes=[
            pltpu.VMEM((SLOTS, TH, GW, C), BF),
            pltpu.VMEM((4 * C, C2), BF),
            pltpu.VMEM((ROWS, C2), BF),
            pltpu.VMEM((1, C), F32),
            pltpu.VMEM((1, C2), F32),
            pltpu.VMEM((LT, KS * KS, 8, 128), F32),
            pltpu.VMEM((SLOTS, LT, XR, 2, GW, 128), F32),
            pltpu.VMEM((2, 4, SLOTS, TH // 4, 16, C), F32),
            pltpu.VMEM((4, ROWS, C), BF),
            pltpu.VMEM((ROWS, C2), F32),
            pltpu.VMEM((ROWS, C2), BF),
            pltpu.VMEM((ROWS, C2), BF),
            pltpu.VMEM((2, ROWS, 2 * CAP * N_DEV), BF),
            pltpu.VMEM((SLOT_ROWS, ROWS), BF),
            pltpu.VMEM((SLOT_ROWS, 1), I32),
            pltpu.VMEM((N_DEV, 1, 128), F32),
            pltpu.VMEM((N_DEV, 1, 128), F32),
            pltpu.VMEM((N_DEV, 2 * CAP, C), BF),
            pltpu.VMEM((N_DEV, 2 * CAP, C), BF),
            pltpu.VMEM((N_FAR, 2 * CAP, C), BF),
            pltpu.VMEM((N_DEV, 2 * CAP, C), BF),
            pltpu.VMEM((N_DEV, 2 * CAP, C), BF),
            pltpu.VMEM((N_FAR, 2 * CAP, C), BF),
            pltpu.VMEM((N_ENC, SLOTS, LT, 96, 128), BF),
            pltpu.VMEM((N_ENC, SLOTS, LT, 96, 128), BF),
            dma((3,)),
            dma((2,)),
            dma((4,)),
            dma((4,)),
            dma((8,)),
            dma((8,)),
            dma((8,)),
            dma((8,)),
        ],
        compiler_params=pltpu.CompilerParams(
            collective_id=0, has_side_effects=True, vmem_limit_bytes=62 * 1024 * 1024
        ),
    )(
        frame_tiles,
        tile_ids,
        partner_slot,
        mix_kernel,
        mix_bias,
        down_weight,
        down_bias,
        token_pos,
        grad_rows,
    )
    return llm, gout[None, None]


def solution(mesh):
    return jax.shard_map(
        on_device,
        mesh=mesh,
        in_specs=(
            P("enc", "seq", None, None, None, None),
            P("enc", "seq", None),
            P("enc", "seq", None),
            P(),
            P(),
            P(),
            P(),
            P("enc", "seq", None, None),
            P(("enc", "seq"), None),
        ),
        out_specs=(P(("enc", "seq"), None), P("enc", "seq", None, None, None, None)),
        check_vma=False,
    )
```

```python
import functools

import itertools

import jax
import jax.numpy as jnp
from jax import lax
from jax.experimental import pallas as pl
from jax.experimental.pallas import tpu as pltpu
from jax.sharding import PartitionSpec as P

C = 768
C2 = 1536
KS = 7
TH = 16
GW = 32
SLOTS = 2
ROWS = 256
N_ENC = 8
N_SEQ = 16
N_DEV = 128
CAP = 8
SLOT_ROWS = CAP * N_DEV

ALL_OFFSETS = list(itertools.product(range(4), repeat=3))
FAR = [o for o in ALL_OFFSETS if 2 in o]
NEAR = [o for o in ALL_OFFSETS if 2 not in o and any(o)]
OFFSETS = (
    [FAR[16 * i % len(FAR)] for i in range(len(FAR))]
    + [NEAR[11 * i % len(NEAR)] for i in range(len(NEAR))]
    + [(0, 0, 0)]
)
N_FAR = 2 * len(FAR)
OWN = N_DEV - 2


def packed(axis):
    words = []
    for n in range(0, 64, 16):
        word = sum(o[axis] << (2 * i) for i, o in enumerate(OFFSETS[n : n + 16]))
        words.append(word - (1 << 32) if word >> 31 else word)
    return words


WORDS = [packed(axis) for axis in range(3)]
LT = C // 128
HALO = 3
XR = TH + 2 * HALO
SQRT_HALF = 0.7071067811865476
INV_ROOT = 0.3989422804014327
BF = jnp.bfloat16
F32 = jnp.float32
I32 = jnp.int32


def iota(shape, axis):
    return lax.broadcasted_iota(I32, shape, axis)


def dot(a, b):
    return jnp.dot(a, b, preferred_element_type=F32)


def kernel(
    tiles_hbm, ids_ref, partner_ref, mixk_ref, mixb_ref, w_hbm, downb_ref, pos_ref, grad_hbm,
    llm_ref, gout_ref,
    tiles, w, grads, mixb, downb, wb, X, F, A, slope, tok, pg, sel, hot, owner,
    msg, rmsg, gsend, grecv, grel, tsend, trecv, trel, rimf, rimb,
    lsem, msem, gsem, tsem, fsend, frecv, bsend, brecv,
):
    enc = lax.axis_index("enc")
    seq = lax.axis_index("seq")
    me = enc * N_SEQ + seq
    cy, core = enc // 2, enc % 2

    ld_tiles = pltpu.make_async_copy(tiles_hbm.at[0, 0], tiles, lsem.at[0])
    ld_grads = pltpu.make_async_copy(grad_hbm, grads, lsem.at[1])
    ld_w = pltpu.make_async_copy(w_hbm, w, lsem.at[2])
    ld_tiles.start()
    ld_grads.start()
    ld_w.start()

    barrier = pltpu.get_barrier_semaphore()

    @pl.loop(1, N_DEV)
    def _(i):
        e, s = (enc + (i >> 4)) & (N_ENC - 1), (seq + i) & (N_SEQ - 1)
        pl.semaphore_signal(barrier, inc=1, device_id=(e, s), device_id_type=pl.DeviceIdType.MESH)

    mixb[...] = mixb_ref[...].reshape(1, C)
    downb[...] = downb_ref[...].reshape(1, C2)

    pos = pos_ref[0, 0]
    prow = jnp.concatenate([pos[0:1, :], pos[1:2, :]], axis=1)
    pcol = jnp.concatenate(
        [jnp.transpose(jnp.broadcast_to(pos[i : i + 1, :].astype(F32), (128, 128))) for i in range(2)], axis=0
    ).astype(I32)[:, 0:1]
    orow, ocol = prow // ROWS, pcol // ROWS
    lcol = pcol - ocol * ROWS
    same = jnp.broadcast_to(ocol, (ROWS, ROWS)) == jnp.broadcast_to(orow, (ROWS, ROWS))
    at0, at1 = iota((ROWS, ROWS), 0), iota((ROWS, ROWS), 1)
    rank_row = jnp.sum(jnp.where(same & (at0 < at1), 1.0, 0.0), axis=0, keepdims=True).astype(I32)
    rank_col = jnp.sum(jnp.where(same & (at1 < at0), 1.0, 0.0), axis=1, keepdims=True).astype(I32)
    slot_row = orow * CAP + rank_row
    to_owner = jnp.where(iota((N_DEV, ROWS), 0) == orow, 1.0, 0.0).astype(BF)
    ranked = jnp.where(iota((ROWS, 128), 1) == rank_col, (lcol + 1).astype(F32), 0.0).astype(BF)
    msg[...] = dot(to_owner, ranked).reshape(N_DEV, 1, 128)
    rmsg[pl.ds(me, 1)] = msg[pl.ds(me, 1)]

    for a in range(KS):
        for b in range(KS):
            row = mixk_ref[a, b : b + 1, :].astype(F32)
            if a == HALO and b == HALO:
                row = row + 1.0
            for t in range(LT):
                wb[t, a * KS + b] = jnp.broadcast_to(row[:, t * 128 : (t + 1) * 128], (8, 128))

    @pl.loop(0, SLOTS * LT)
    def _(i):
        k, t = i // LT, lax.rem(i, LT)
        X[k, t, :, :, 0:8, :] = jnp.zeros((XR, 2, 8, 128), F32)
        X[k, t, :, :, 24:32, :] = jnp.zeros((XR, 2, 8, 128), F32)
        X[k, t, 0:HALO] = jnp.zeros((HALO, 2, GW, 128), F32)
        X[k, t, XR - HALO : XR] = jnp.zeros((HALO, 2, GW, 128), F32)

    q0, q1 = iota((128, 128), 0), iota((128, 128), 1)
    spread = jnp.where(q1 == (q0 // 32) * 32 + (q0 % 16) * 2 + (q0 % 32) // 16, 1.0, 0.0).astype(BF)
    gather = jnp.where(q0 == (q1 // 32) * 32 + (q1 % 16) * 2 + (q1 % 32) // 16, 1.0, 0.0).astype(BF)

    def fill(k, g):
        d = dot(spread, tiles[k, 4 * g : 4 * g + 4].reshape(128, C)).reshape(4, 2, 16, C)
        for t in range(LT):
            X[k, t, HALO + 4 * g : HALO + 4 * g + 4, :, 8:24, :] = d[..., t * 128 : (t + 1) * 128]

    def own_rims(rims):
        for k in range(SLOTS):
            low = X[k, :, HALO : 2 * HALO, :, 8:24, :]
            high = X[k, :, TH : TH + HALO, :, 8:24, :]
            rim = jnp.where(lax.rem(ids_ref[0, 0, k], 2) == 0, high, low)
            rims[enc, k] = rim.astype(BF).reshape(LT, 96, 128)

    up = lax.rem(cy + 1, 4) * 2 + core
    down = lax.rem(cy + 3, 4) * 2 + core
    across = lax.rem(cy + 2, 4) * 2 + core
    sib = cy * 2 + 1 - core

    def rim_copies(rims, ssem, rsem):
        def copy(n, ref, to):
            return pltpu.make_async_remote_copy(
                src_ref=ref, dst_ref=ref, send_sem=ssem.at[n], recv_sem=rsem.at[n],
                device_id=(to, seq), device_id_type=pl.DeviceIdType.MESH,
            )

        def landed(n, ref):
            return pltpu.make_async_copy(ref, ref, rsem.at[n])

        sends = [
            copy(0, rims.at[enc], up),
            copy(1, rims.at[enc], down),
            copy(2, rims.at[enc], sib),
            copy(3, rims.at[down, 0], up),
            copy(4, rims.at[up, 1], down),
            copy(5, rims.at[down], sib),
            copy(6, rims.at[up], sib),
            copy(7, rims.at[across], sib),
        ]
        other = 1 - 2 * core
        arrivals = [
            landed(0, rims.at[down]),
            landed(1, rims.at[up]),
            landed(2, rims.at[sib]),
            landed(3, rims.at[across, 0]),
            landed(4, rims.at[across, 1]),
            landed(5, rims.at[down + other]),
            landed(6, rims.at[up + other]),
            landed(7, rims.at[across + other]),
        ]
        return sends, arrivals

    def place_rims(rims):
        for k in range(SLOTS):
            want = partner_ref[0, 0, k]
            rim = jnp.zeros((LT, 96, 128), BF)
            for q in range(N_ENC * SLOTS):
                rim = jnp.where(want == q, rims[q // 2, q % 2], rim)
            rim = rim.astype(F32).reshape(LT, HALO, 2, 16, 128)
            is_lower = lax.rem(ids_ref[0, 0, k], 2) == 1
            X[k, :, 0:HALO, :, 8:24, :] = jnp.where(is_lower, rim, 0.0)
            X[k, :, TH + HALO : XR, :, 8:24, :] = jnp.where(is_lower, 0.0, rim)

    def lower(k):
        return lax.rem(ids_ref[0, 0, k], 2)

    def conv(flip, with_bias, part):
        @pl.loop(0, SLOTS * LT)
        def _(i):
            k, t = i // LT, lax.rem(i, LT)
            lanes = pl.ds(pl.multiple_of(t * 128, 128), 128)
            below = lower(k)
            start = 8 * (below if part == 0 else 1 - below)
            for cb in range(2):
                first = jnp.zeros((TH // 2, 8, 128), F32)
                if with_bias:
                    first = first + mixb[:, lanes].reshape(1, 1, 128)
                acc = [first, first]
                for p in range(2):
                    for sh in range(-2, 3):
                        uses = [(dx, 2 * sh + p + 3 - dx) for dx in range(2)]
                        uses = [(dx, b) for dx, b in uses if 0 <= b < KS]
                        if not uses:
                            continue
                        rows = pl.ds(start, TH // 2 + 2 * HALO)
                        c0 = 8 * cb if sh < 0 else 8 * cb + 8
                        if sh == 0:
                            xs = X[k, t, rows, p, c0 : c0 + 8, :]
                        else:
                            xs = X[k, t, rows, p, c0 : c0 + 16, :]
                            xs = pltpu.roll(xs, 8 - sh if sh < 0 else 16 - sh, 1)[:, 0:8]
                        for dx, b in uses:
                            for a in range(KS):
                                tap = a * KS + b
                                if flip:
                                    tap = KS * KS - 1 - tap
                                acc[dx] = acc[dx] + wb[t, tap][None] * xs[a : a + TH // 2]
                for dx in range(2):
                    rows = acc[dx].reshape(TH // 4, 2, 8, 128)
                    for dy in range(2):
                        F[part, dy * 2 + dx, k, :, 8 * cb : 8 * cb + 8, lanes] = rows[:, dy]

    cx, cz = seq >> 2, seq & 3
    at_x = [((cx + d) & 3) * 4 for d in range(4)]
    at_y = [((cy + d) & 3) * 2 for d in range(4)]
    at_z = [(cz + d) & 3 for d in range(4)]
    at_core = [core, 1 - core]

    def step(off, f):
        return [way if d == 2 else 0 for d, way in zip(off, (1 + 2 * f, 3 - 2 * f, 1 + 2 * f))]

    def device(off, f):
        return at_y[off[1]] + at_core[f], at_x[off[0]] + at_z[off[2]]

    def owner_of_row():
        place = iota((SLOT_ROWS, 1), 0) // CAP
        block, shift = place // 32, 2 * ((place // 2) % 16)
        d = []
        for w0, w1, w2, w3 in WORDS:
            word = jnp.where(block < 2, jnp.where(block == 0, w0, w1), jnp.where(block == 2, w2, w3))
            d.append(jnp.right_shift(word, shift) & 3)
        c = core + place % 2 - 2 * core * (place % 2)
        return (((cy + d[1]) & 3) * 2 + c) * N_SEQ + ((cx + d[0]) & 3) * 4 + ((cz + d[2]) & 3)

    def fill_rows(buf, rows_ref):
        @pl.loop(0, C // 256)
        def _(n):
            c0 = pl.multiple_of(n * 256, 256)
            y0 = dot(hot[...], rows_ref[:, pl.ds(c0, 256)]).reshape(N_DEV, CAP, 256)
            y1 = dot(hot[...], rows_ref[:, pl.ds(c0 + C, 256)]).reshape(N_DEV, CAP, 256)
            buf[:, :, pl.ds(c0, 256)] = jnp.concatenate([y0, y1], axis=1).astype(BF)

    def send_far(buf, rel, sems):
        for q in range(N_FAR):
            pltpu.make_async_remote_copy(
                src_ref=buf.at[q], dst_ref=rel.at[q],
                send_sem=sems.at[0], recv_sem=sems.at[2],
                device_id=device(step(OFFSETS[q // 2], q % 2), 0), device_id_type=pl.DeviceIdType.MESH,
            ).start()

    def send_near(buf, got, sems):
        for q in range(N_FAR, N_DEV):
            if q != OWN:
                pltpu.make_async_remote_copy(
                    src_ref=buf.at[q], dst_ref=got.at[me],
                    send_sem=sems.at[0], recv_sem=sems.at[1],
                    device_id=device(OFFSETS[q // 2], q % 2), device_id_type=pl.DeviceIdType.MESH,
                ).start()

    def forward(rel, got, sems):
        part = rel.at[pl.ds(0, N_FAR)]
        pltpu.make_async_copy(part, part, sems.at[2]).wait()
        for q in range(N_FAR):
            off = OFFSETS[q // 2]
            leg = step(off, q % 2)
            e0, s0 = device([(4 - d) % 4 for d in leg], 0)
            rest = [(o + 4 - d) % 4 for o, d in zip(off, leg)]
            pltpu.make_async_remote_copy(
                src_ref=rel.at[q], dst_ref=got.at[e0 * N_SEQ + s0],
                send_sem=sems.at[3], recv_sem=sems.at[1],
                device_id=device(rest, q % 2), device_id_type=pl.DeviceIdType.MESH,
            ).start()

    def keep_own(buf, got):
        got[pl.ds(me, 1)] = buf[OWN : OWN + 1]

    def wait_rows(buf, sem):
        part = buf.at[pl.ds(0, N_DEV - 1)]
        pltpu.make_async_copy(part, part, sem).wait()

    ld_tiles.wait()
    for k in range(SLOTS):
        for g in (0, 3, 1, 2):
            fill(k, g)
    own_rims(rimf)
    owner[...] = owner_of_row()
    pl.semaphore_wait(barrier, N_DEV - 1)

    f_send, f_got = rim_copies(rimf, fsend, frecv)
    for n in range(3):
        f_send[n].start()

    @pl.loop(1, N_DEV)
    def _(i):
        e, s = (enc + (i >> 4)) & (N_ENC - 1), (seq + i) & (N_SEQ - 1)
        pltpu.make_async_remote_copy(
            src_ref=msg.at[e * N_SEQ + s], dst_ref=rmsg.at[me],
            send_sem=msem.at[0], recv_sem=msem.at[1],
            device_id=(e, s), device_id_type=pl.DeviceIdType.MESH,
        ).start()

    ld_grads.wait()
    wait_rows(rmsg, msem.at[1])

    asked = rmsg[...].reshape(N_DEV, 128)
    asked_t = jnp.transpose(asked)[0:CAP, :].astype(BF)
    asked = asked.astype(BF)

    shape = (SLOT_ROWS, 128)
    rows = dot(jnp.where(iota(shape, 1) == owner[...], 1.0, 0.0).astype(BF), asked)
    want = jnp.sum(jnp.where(iota(shape, 1) == iota(shape, 0) % CAP, rows, 0.0), axis=1, keepdims=True).astype(I32)
    hot[...] = jnp.where(iota((SLOT_ROWS, ROWS), 1) == want - 1, 1.0, 0.0).astype(BF)
    fill_rows(gsend, grads)
    f_got[0].wait()
    f_send[3].start()
    f_send[5].start()
    f_got[1].wait()
    f_send[4].start()
    f_send[6].start()
    send_far(gsend, grel, gsem)
    send_near(gsend, grecv, gsem)
    keep_own(gsend, grecv)
    conv(False, True, 0)

    f_got[3].wait()
    f_got[4].wait()
    f_send[7].start()
    for n in (2, 5, 6, 7):
        f_got[n].wait()
    place_rims(rimf)
    conv(False, True, 1)

    def half_rows(j, k, y):
        below = lower(k)
        return F[below if y == 0 else 1 - below, j, k]

    @pl.loop(0, 4)
    def _(j):
        for k in range(SLOTS):
            for y in range(2):
                A[j, k * 128 + y * 64 : k * 128 + y * 64 + 64] = half_rows(j, k, y).reshape(64, C).astype(BF)

    forward(grel, grecv, gsem)
    ld_w.wait()

    @pl.loop(0, C2 // 256)
    def _(n):
        cols = pl.ds(pl.multiple_of(n * 256, 256), 256)
        pre = jnp.zeros((ROWS, 256), F32) + downb[:, cols]
        for j in range(4):
            pre = pre + dot(A[j], w[j * C : (j + 1) * C, cols])
        phi = 0.5 * (1.0 + lax.erf(pre * SQRT_HALF))
        tok[:, cols] = (pre * phi).astype(BF)
        slope[:, cols] = phi + pre * INV_ROOT * jnp.exp(-0.5 * pre * pre)

    at = owner[...] * CAP + iota((SLOT_ROWS, 1), 0) % CAP
    hot[...] = jnp.where(at == slot_row, 1.0, 0.0).astype(BF)
    fill_rows(tsend, tok)
    send_far(tsend, trel, tsem)
    send_near(tsend, trecv, tsem)
    keep_own(tsend, trecv)

    back_at = ocol * (2 * CAP) + rank_col
    for h in range(2):
        sel[h] = jnp.where(iota((ROWS, 2 * CAP * N_DEV), 1) == back_at + h * CAP, 1.0, 0.0).astype(BF)
    wait_rows(grecv, gsem.at[1])

    def picked(got, h, c0):
        part = got[:, :, pl.ds(pl.multiple_of(c0, 256), 256)].reshape(2 * CAP * N_DEV, 256)
        return dot(sel[h], part)

    @pl.loop(0, C2 // 256)
    def _(n):
        h = n // 3
        cols = pl.ds(pl.multiple_of(n * 256, 256), 256)
        pg[:, cols] = (picked(grecv, h, (n - 3 * h) * 256) * slope[:, cols]).astype(BF)

    forward(trel, trecv, tsem)

    @pl.loop(0, 4 * (C // 256))
    def _(m):
        j, n = m // 3, lax.rem(m, 3)
        part = w[pl.ds(pl.multiple_of(m * 256, 256), 256), :]
        g = lax.dot_general(pg[...], part, (((1,), (1,)), ((), ())), preferred_element_type=F32)
        g = g.astype(BF).astype(F32).reshape(SLOTS, TH // 2, 16, 256)
        dy, dx = j // 2, lax.rem(j, 2)
        for y in range(TH // 2):
            for i in range(2):
                X[:, 2 * n + i, HALO + 2 * y + dy, dx, 8:24, :] = g[:, y, :, i * 128 : (i + 1) * 128]

    own_rims(rimb)
    b_send, b_got = rim_copies(rimb, bsend, brecv)
    for n in range(3):
        b_send[n].start()
    conv(True, False, 0)
    b_got[0].wait()
    b_send[3].start()
    b_send[5].start()
    b_got[1].wait()
    b_send[4].start()
    b_send[6].start()
    b_got[3].wait()
    b_got[4].wait()
    b_send[7].start()
    for n in (2, 5, 6, 7):
        b_got[n].wait()
    place_rims(rimb)
    conv(True, False, 1)

    for k in range(SLOTS):
        for g in range(4):
            cells = jnp.concatenate(
                [
                    F[lower(k) if g < 2 else 1 - lower(k), dy * 2 + dx, k, 2 * (g % 2) + y]
                    for y in range(2) for dy in range(2) for dx in range(2)
                ],
                axis=0,
            ).astype(BF)
            gout_ref[k, 4 * g : 4 * g + 4] = dot(gather, cells).astype(BF).reshape(4, GW, C)

    for g in range(N_DEV // N_SEQ):
        shape = (N_DEV, 256)
        at1 = iota(shape, 1)
        over = jnp.where(iota(shape, 0) == g * N_SEQ + at1 // (2 * CAP), 1.0, 0.0).astype(BF)
        rows = dot(asked_t, over)
        k8 = iota((CAP, 256), 1)
        put = jnp.sum(jnp.where(iota((CAP, 256), 0) == k8 % CAP, rows, 0.0), axis=0, keepdims=True).astype(I32)
        hit = iota((ROWS, 256), 0) == put - 1
        part = (iota((ROWS, 256), 1) // CAP) % 2
        for h in range(2):
            sel[h, :, g * 256 : (g + 1) * 256] = jnp.where(hit & (part == h), 1.0, 0.0).astype(BF)
    wait_rows(trecv, tsem.at[1])

    @pl.loop(0, C2 // 256)
    def _(n):
        h = n // 3
        cols = pl.ds(pl.multiple_of(n * 256, 256), 256)
        llm_ref[:, cols] = picked(trecv, h, (n - 3 * h) * 256).astype(BF)

    for n in range(8):
        f_send[n].wait_send()
        b_send[n].wait_send()
    wait_rows(msg, msem.at[0])
    for buf, rel, sems in ((gsend, grel, gsem), (tsend, trel, tsem)):
        wait_rows(buf, sems.at[0])
        part = rel.at[pl.ds(0, N_FAR)]
        pltpu.make_async_copy(part, part, sems.at[3]).wait()


def on_device(frame_tiles, tile_ids, partner_slot, mix_kernel, mix_bias, down_weight, down_bias, token_pos, grad_rows):
    vmem = pl.BlockSpec(memory_space=pltpu.VMEM)
    smem = pl.BlockSpec(memory_space=pltpu.SMEM)
    anyw = pl.BlockSpec(memory_space=pl.ANY)
    dma = pltpu.SemaphoreType.DMA
    llm, gout = pl.pallas_call(
        kernel,
        out_shape=(
            jax.ShapeDtypeStruct((ROWS, C2), BF),
            jax.ShapeDtypeStruct((SLOTS, TH, GW, C), BF),
        ),
        in_specs=[anyw, smem, smem, vmem, vmem, anyw, vmem, vmem, anyw],
        out_specs=(vmem, vmem),
        scratch_shapes=[
            pltpu.VMEM((SLOTS, TH, GW, C), BF),
            pltpu.VMEM((4 * C, C2), BF),
            pltpu.VMEM((ROWS, C2), BF),
            pltpu.VMEM((1, C), F32),
            pltpu.VMEM((1, C2), F32),
            pltpu.VMEM((LT, KS * KS, 8, 128), F32),
            pltpu.VMEM((SLOTS, LT, XR, 2, GW, 128), F32),
            pltpu.VMEM((2, 4, SLOTS, TH // 4, 16, C), F32),
            pltpu.VMEM((4, ROWS, C), BF),
            pltpu.VMEM((ROWS, C2), F32),
            pltpu.VMEM((ROWS, C2), BF),
            pltpu.VMEM((ROWS, C2), BF),
            pltpu.VMEM((2, ROWS, 2 * CAP * N_DEV), BF),
            pltpu.VMEM((SLOT_ROWS, ROWS), BF),
            pltpu.VMEM((SLOT_ROWS, 1), I32),
            pltpu.VMEM((N_DEV, 1, 128), F32),
            pltpu.VMEM((N_DEV, 1, 128), F32),
            pltpu.VMEM((N_DEV, 2 * CAP, C), BF),
            pltpu.VMEM((N_DEV, 2 * CAP, C), BF),
            pltpu.VMEM((N_FAR, 2 * CAP, C), BF),
            pltpu.VMEM((N_DEV, 2 * CAP, C), BF),
            pltpu.VMEM((N_DEV, 2 * CAP, C), BF),
            pltpu.VMEM((N_FAR, 2 * CAP, C), BF),
            pltpu.VMEM((N_ENC, SLOTS, LT, 96, 128), BF),
            pltpu.VMEM((N_ENC, SLOTS, LT, 96, 128), BF),
            dma((3,)),
            dma((2,)),
            dma((4,)),
            dma((4,)),
            dma((8,)),
            dma((8,)),
            dma((8,)),
            dma((8,)),
        ],
        compiler_params=pltpu.CompilerParams(
            collective_id=0, has_side_effects=True, vmem_limit_bytes=62 * 1024 * 1024
        ),
    )(
        frame_tiles,
        tile_ids,
        partner_slot,
        mix_kernel,
        mix_bias,
        down_weight,
        down_bias,
        token_pos,
        grad_rows,
    )
    return llm, gout[None, None]


def solution(mesh):
    return jax.shard_map(
        on_device,
        mesh=mesh,
        in_specs=(
            P("enc", "seq", None, None, None, None),
            P("enc", "seq", None),
            P("enc", "seq", None),
            P(),
            P(),
            P(),
            P(),
            P("enc", "seq", None, None),
            P(("enc", "seq"), None),
        ),
        out_specs=(P(("enc", "seq"), None), P("enc", "seq", None, None, None, None)),
        check_vma=False,
    )
```

```python
import functools

import itertools

import jax
import jax.numpy as jnp
from jax import lax
from jax.experimental import pallas as pl
from jax.experimental.pallas import tpu as pltpu
from jax.sharding import PartitionSpec as P

C = 768
C2 = 1536
KS = 7
TH = 16
GW = 32
SLOTS = 2
ROWS = 256
N_ENC = 8
N_SEQ = 16
N_DEV = 128
CAP = 8
SLOT_ROWS = CAP * N_DEV

def orbit(o):
    turned = [o, o[2:] + o[:2], o[1:] + o[:1]]
    return [p for q in turned for p in (q, tuple(-d % 4 for d in q))]


ALL_OFFSETS = sorted(itertools.product((0, 1, 3, 2), repeat=3), key=lambda o: -sum(min(d, 4 - d) for d in o))
ORDERED = list(dict.fromkeys(p for o in ALL_OFFSETS for p in orbit(o)))
FAR = [o for o in ORDERED if 2 in o]
OFFSETS = FAR + [o for o in ORDERED if 2 not in o]
N_FAR = 2 * len(FAR)
OWN = N_DEV - 2


def packed(axis):
    words = []
    for n in range(0, 64, 16):
        word = sum(o[axis] << (2 * i) for i, o in enumerate(OFFSETS[n : n + 16]))
        words.append(word - (1 << 32) if word >> 31 else word)
    return words


WORDS = [packed(axis) for axis in range(3)]
LT = C // 128
HALO = 3
XR = TH + 2 * HALO
SQRT_HALF = 0.7071067811865476
INV_ROOT = 0.3989422804014327
BF = jnp.bfloat16
F32 = jnp.float32
I32 = jnp.int32


def iota(shape, axis):
    return lax.broadcasted_iota(I32, shape, axis)


def dot(a, b):
    return jnp.dot(a, b, preferred_element_type=F32)


def kernel(
    tiles_hbm, ids_ref, partner_ref, mixk_ref, mixb_ref, w_hbm, downb_ref, pos_ref, grad_hbm,
    llm_ref, gout_ref,
    tiles, w, grads, mixb, downb, wb, X, F, A, slope, tok, pg, sel, hot, owner,
    msg, rmsg, gsend, grecv, grel, tsend, trecv, trel, rimf, rimb,
    lsem, msem, gsem, tsem, fsend, frecv, bsend, brecv,
):
    enc = lax.axis_index("enc")
    seq = lax.axis_index("seq")
    me = enc * N_SEQ + seq
    cy, core = enc // 2, enc % 2

    ld_tiles = pltpu.make_async_copy(tiles_hbm.at[0, 0], tiles, lsem.at[0])
    ld_grads = pltpu.make_async_copy(grad_hbm, grads, lsem.at[1])
    ld_w = pltpu.make_async_copy(w_hbm, w, lsem.at[2])
    ld_tiles.start()
    ld_grads.start()
    ld_w.start()

    barrier = pltpu.get_barrier_semaphore()

    @pl.loop(1, N_DEV)
    def _(i):
        e, s = (enc + (i >> 4)) & (N_ENC - 1), (seq + i) & (N_SEQ - 1)
        pl.semaphore_signal(barrier, inc=1, device_id=(e, s), device_id_type=pl.DeviceIdType.MESH)

    mixb[...] = mixb_ref[...].reshape(1, C)
    downb[...] = downb_ref[...].reshape(1, C2)

    pos = pos_ref[0, 0]
    prow = jnp.concatenate([pos[0:1, :], pos[1:2, :]], axis=1)
    pcol = jnp.concatenate(
        [jnp.transpose(jnp.broadcast_to(pos[i : i + 1, :].astype(F32), (128, 128))) for i in range(2)], axis=0
    ).astype(I32)[:, 0:1]
    orow, ocol = prow // ROWS, pcol // ROWS
    lcol = pcol - ocol * ROWS
    same = jnp.broadcast_to(ocol, (ROWS, ROWS)) == jnp.broadcast_to(orow, (ROWS, ROWS))
    at0, at1 = iota((ROWS, ROWS), 0), iota((ROWS, ROWS), 1)
    rank_row = jnp.sum(jnp.where(same & (at0 < at1), 1.0, 0.0), axis=0, keepdims=True).astype(I32)
    rank_col = jnp.sum(jnp.where(same & (at1 < at0), 1.0, 0.0), axis=1, keepdims=True).astype(I32)
    slot_row = orow * CAP + rank_row
    to_owner = jnp.where(iota((N_DEV, ROWS), 0) == orow, 1.0, 0.0).astype(BF)
    ranked = jnp.where(iota((ROWS, 128), 1) == rank_col, (lcol + 1).astype(F32), 0.0).astype(BF)
    msg[...] = dot(to_owner, ranked).reshape(N_DEV, 1, 128)
    rmsg[pl.ds(me, 1)] = msg[pl.ds(me, 1)]

    for a in range(KS):
        for b in range(KS):
            row = mixk_ref[a, b : b + 1, :].astype(F32)
            if a == HALO and b == HALO:
                row = row + 1.0
            for t in range(LT):
                wb[t, a * KS + b] = jnp.broadcast_to(row[:, t * 128 : (t + 1) * 128], (8, 128))

    @pl.loop(0, SLOTS * LT)
    def _(i):
        k, t = i // LT, lax.rem(i, LT)
        X[k, t, :, :, 0:8, :] = jnp.zeros((XR, 2, 8, 128), F32)
        X[k, t, :, :, 24:32, :] = jnp.zeros((XR, 2, 8, 128), F32)
        X[k, t, 0:HALO] = jnp.zeros((HALO, 2, GW, 128), F32)
        X[k, t, XR - HALO : XR] = jnp.zeros((HALO, 2, GW, 128), F32)

    q0, q1 = iota((128, 128), 0), iota((128, 128), 1)
    spread = jnp.where(q1 == (q0 // 32) * 32 + (q0 % 16) * 2 + (q0 % 32) // 16, 1.0, 0.0).astype(BF)
    gather = jnp.where(q0 == (q1 // 32) * 32 + (q1 % 16) * 2 + (q1 % 32) // 16, 1.0, 0.0).astype(BF)

    def fill(k, g):
        d = dot(spread, tiles[k, 4 * g : 4 * g + 4].reshape(128, C)).reshape(4, 2, 16, C)
        for t in range(LT):
            X[k, t, HALO + 4 * g : HALO + 4 * g + 4, :, 8:24, :] = d[..., t * 128 : (t + 1) * 128]

    def own_rims(rims):
        for k in range(SLOTS):
            low = X[k, :, HALO : 2 * HALO, :, 8:24, :]
            high = X[k, :, TH : TH + HALO, :, 8:24, :]
            rim = jnp.where(lax.rem(ids_ref[0, 0, k], 2) == 0, high, low)
            rims[enc, k] = rim.astype(BF).reshape(LT, 96, 128)

    up = lax.rem(cy + 1, 4) * 2 + core
    down = lax.rem(cy + 3, 4) * 2 + core
    across = lax.rem(cy + 2, 4) * 2 + core
    sib = cy * 2 + 1 - core

    def rim_copies(rims, ssem, rsem):
        def copy(n, ref, to):
            return pltpu.make_async_remote_copy(
                src_ref=ref, dst_ref=ref, send_sem=ssem.at[n], recv_sem=rsem.at[n],
                device_id=(to, seq), device_id_type=pl.DeviceIdType.MESH,
            )

        def landed(n, ref):
            return pltpu.make_async_copy(ref, ref, rsem.at[n])

        sends = [
            copy(0, rims.at[enc], up),
            copy(1, rims.at[enc], down),
            copy(2, rims.at[enc], sib),
            copy(3, rims.at[down, 0], up),
            copy(4, rims.at[up, 1], down),
            copy(5, rims.at[down], sib),
            copy(6, rims.at[up], sib),
            copy(7, rims.at[across], sib),
        ]
        other = 1 - 2 * core
        arrivals = [
            landed(0, rims.at[down]),
            landed(1, rims.at[up]),
            landed(2, rims.at[sib]),
            landed(3, rims.at[across, 0]),
            landed(4, rims.at[across, 1]),
            landed(5, rims.at[down + other]),
            landed(6, rims.at[up + other]),
            landed(7, rims.at[across + other]),
        ]
        return sends, arrivals

    def place_rims(rims):
        for k in range(SLOTS):
            want = partner_ref[0, 0, k]
            rim = jnp.zeros((LT, 96, 128), BF)
            for q in range(N_ENC * SLOTS):
                rim = jnp.where(want == q, rims[q // 2, q % 2], rim)
            rim = rim.astype(F32).reshape(LT, HALO, 2, 16, 128)
            is_lower = lax.rem(ids_ref[0, 0, k], 2) == 1
            X[k, :, 0:HALO, :, 8:24, :] = jnp.where(is_lower, rim, 0.0)
            X[k, :, TH + HALO : XR, :, 8:24, :] = jnp.where(is_lower, 0.0, rim)

    def lower(k):
        return lax.rem(ids_ref[0, 0, k], 2)

    def conv(flip, with_bias, part):
        @pl.loop(0, SLOTS * LT)
        def _(i):
            k, t = i // LT, lax.rem(i, LT)
            lanes = pl.ds(pl.multiple_of(t * 128, 128), 128)
            below = lower(k)
            start = 8 * (below if part == 0 else 1 - below)
            for cb in range(2):
                first = jnp.zeros((TH // 2, 8, 128), F32)
                if with_bias:
                    first = first + mixb[:, lanes].reshape(1, 1, 128)
                acc = [first, first]
                for p in range(2):
                    for sh in range(-2, 3):
                        uses = [(dx, 2 * sh + p + 3 - dx) for dx in range(2)]
                        uses = [(dx, b) for dx, b in uses if 0 <= b < KS]
                        if not uses:
                            continue
                        rows = pl.ds(start, TH // 2 + 2 * HALO)
                        c0 = 8 * cb if sh < 0 else 8 * cb + 8
                        if sh == 0:
                            xs = X[k, t, rows, p, c0 : c0 + 8, :]
                        else:
                            xs = X[k, t, rows, p, c0 : c0 + 16, :]
                            xs = pltpu.roll(xs, 8 - sh if sh < 0 else 16 - sh, 1)[:, 0:8]
                        for dx, b in uses:
                            for a in range(KS):
                                tap = a * KS + b
                                if flip:
                                    tap = KS * KS - 1 - tap
                                acc[dx] = acc[dx] + wb[t, tap][None] * xs[a : a + TH // 2]
                for dx in range(2):
                    rows = acc[dx].reshape(TH // 4, 2, 8, 128)
                    for dy in range(2):
                        F[part, dy * 2 + dx, k, :, 8 * cb : 8 * cb + 8, lanes] = rows[:, dy]

    cx, cz = seq >> 2, seq & 3
    at_x = [((cx + d) & 3) * 4 for d in range(4)]
    at_y = [((cy + d) & 3) * 2 for d in range(4)]
    at_z = [(cz + d) & 3 for d in range(4)]
    at_core = [core, 1 - core]

    def step(off, f):
        return [way if d == 2 else 0 for d, way in zip(off, (1 + 2 * f, 3 - 2 * f, 1 + 2 * f))]

    def device(off, f):
        return at_y[off[1]] + at_core[f], at_x[off[0]] + at_z[off[2]]

    def owner_of_row():
        place = iota((SLOT_ROWS, 1), 0) // CAP
        block, shift = place // 32, 2 * ((place // 2) % 16)
        d = []
        for w0, w1, w2, w3 in WORDS:
            word = jnp.where(block < 2, jnp.where(block == 0, w0, w1), jnp.where(block == 2, w2, w3))
            d.append(jnp.right_shift(word, shift) & 3)
        c = core + place % 2 - 2 * core * (place % 2)
        return (((cy + d[1]) & 3) * 2 + c) * N_SEQ + ((cx + d[0]) & 3) * 4 + ((cz + d[2]) & 3)

    def fill_rows(buf, rows_ref):
        @pl.loop(0, C // 256)
        def _(n):
            c0 = pl.multiple_of(n * 256, 256)
            y0 = dot(hot[...], rows_ref[:, pl.ds(c0, 256)]).reshape(N_DEV, CAP, 256)
            y1 = dot(hot[...], rows_ref[:, pl.ds(c0 + C, 256)]).reshape(N_DEV, CAP, 256)
            buf[:, :, pl.ds(c0, 256)] = jnp.concatenate([y0, y1], axis=1).astype(BF)

    def send_far(buf, rel, sems):
        for q in range(N_FAR):
            pltpu.make_async_remote_copy(
                src_ref=buf.at[q], dst_ref=rel.at[q],
                send_sem=sems.at[0], recv_sem=sems.at[2],
                device_id=device(step(OFFSETS[q // 2], q % 2), 0), device_id_type=pl.DeviceIdType.MESH,
            ).start()

    def send_near(buf, got, sems):
        for q in range(N_FAR, N_DEV):
            if q != OWN:
                pltpu.make_async_remote_copy(
                    src_ref=buf.at[q], dst_ref=got.at[me],
                    send_sem=sems.at[0], recv_sem=sems.at[1],
                    device_id=device(OFFSETS[q // 2], q % 2), device_id_type=pl.DeviceIdType.MESH,
                ).start()

    def forward(rel, got, sems):
        part = rel.at[pl.ds(0, N_FAR)]
        pltpu.make_async_copy(part, part, sems.at[2]).wait()
        for q in range(N_FAR):
            off = OFFSETS[q // 2]
            leg = step(off, q % 2)
            e0, s0 = device([(4 - d) % 4 for d in leg], 0)
            rest = [(o + 4 - d) % 4 for o, d in zip(off, leg)]
            pltpu.make_async_remote_copy(
                src_ref=rel.at[q], dst_ref=got.at[e0 * N_SEQ + s0],
                send_sem=sems.at[3], recv_sem=sems.at[1],
                device_id=device(rest, q % 2), device_id_type=pl.DeviceIdType.MESH,
            ).start()

    def keep_own(buf, got):
        got[pl.ds(me, 1)] = buf[OWN : OWN + 1]

    def wait_rows(buf, sem):
        part = buf.at[pl.ds(0, N_DEV - 1)]
        pltpu.make_async_copy(part, part, sem).wait()

    ld_tiles.wait()
    for k in range(SLOTS):
        for g in (0, 3, 1, 2):
            fill(k, g)
    own_rims(rimf)
    owner[...] = owner_of_row()
    pl.semaphore_wait(barrier, N_DEV - 1)

    f_send, f_got = rim_copies(rimf, fsend, frecv)
    for n in range(3):
        f_send[n].start()

    @pl.loop(1, N_DEV)
    def _(i):
        e, s = (enc + (i >> 4)) & (N_ENC - 1), (seq + i) & (N_SEQ - 1)
        pltpu.make_async_remote_copy(
            src_ref=msg.at[e * N_SEQ + s], dst_ref=rmsg.at[me],
            send_sem=msem.at[0], recv_sem=msem.at[1],
            device_id=(e, s), device_id_type=pl.DeviceIdType.MESH,
        ).start()

    ld_grads.wait()
    wait_rows(rmsg, msem.at[1])

    asked = rmsg[...].reshape(N_DEV, 128)
    asked_t = jnp.transpose(asked)[0:CAP, :].astype(BF)
    asked = asked.astype(BF)

    shape = (SLOT_ROWS, 128)
    rows = dot(jnp.where(iota(shape, 1) == owner[...], 1.0, 0.0).astype(BF), asked)
    want = jnp.sum(jnp.where(iota(shape, 1) == iota(shape, 0) % CAP, rows, 0.0), axis=1, keepdims=True).astype(I32)
    hot[...] = jnp.where(iota((SLOT_ROWS, ROWS), 1) == want - 1, 1.0, 0.0).astype(BF)
    fill_rows(gsend, grads)
    f_got[0].wait()
    f_send[3].start()
    f_send[5].start()
    f_got[1].wait()
    f_send[4].start()
    f_send[6].start()
    send_far(gsend, grel, gsem)
    send_near(gsend, grecv, gsem)
    keep_own(gsend, grecv)
    conv(False, True, 0)
    forward(grel, grecv, gsem)

    f_got[3].wait()
    f_got[4].wait()
    f_send[7].start()
    for n in (2, 5, 6, 7):
        f_got[n].wait()
    place_rims(rimf)
    conv(False, True, 1)

    def half_rows(j, k, y):
        below = lower(k)
        return F[below if y == 0 else 1 - below, j, k]

    @pl.loop(0, 4)
    def _(j):
        for k in range(SLOTS):
            for y in range(2):
                A[j, k * 128 + y * 64 : k * 128 + y * 64 + 64] = half_rows(j, k, y).reshape(64, C).astype(BF)

    ld_w.wait()

    @pl.loop(0, C2 // 256)
    def _(n):
        cols = pl.ds(pl.multiple_of(n * 256, 256), 256)
        pre = jnp.zeros((ROWS, 256), F32) + downb[:, cols]
        for j in range(4):
            pre = pre + dot(A[j], w[j * C : (j + 1) * C, cols])
        phi = 0.5 * (1.0 + lax.erf(pre * SQRT_HALF))
        tok[:, cols] = (pre * phi).astype(BF)
        slope[:, cols] = phi + pre * INV_ROOT * jnp.exp(-0.5 * pre * pre)

    at = owner[...] * CAP + iota((SLOT_ROWS, 1), 0) % CAP
    hot[...] = jnp.where(at == slot_row, 1.0, 0.0).astype(BF)
    fill_rows(tsend, tok)
    send_far(tsend, trel, tsem)
    send_near(tsend, trecv, tsem)
    keep_own(tsend, trecv)

    back_at = ocol * (2 * CAP) + rank_col
    for h in range(2):
        sel[h] = jnp.where(iota((ROWS, 2 * CAP * N_DEV), 1) == back_at + h * CAP, 1.0, 0.0).astype(BF)
    wait_rows(grecv, gsem.at[1])

    def picked(got, h, c0):
        part = got[:, :, pl.ds(pl.multiple_of(c0, 256), 256)].reshape(2 * CAP * N_DEV, 256)
        return dot(sel[h], part)

    @pl.loop(0, C2 // 256)
    def _(n):
        h = n // 3
        cols = pl.ds(pl.multiple_of(n * 256, 256), 256)
        pg[:, cols] = (picked(grecv, h, (n - 3 * h) * 256) * slope[:, cols]).astype(BF)

    forward(trel, trecv, tsem)

    @pl.loop(0, 4 * (C // 256))
    def _(m):
        j, n = m // 3, lax.rem(m, 3)
        part = w[pl.ds(pl.multiple_of(m * 256, 256), 256), :]
        g = lax.dot_general(pg[...], part, (((1,), (1,)), ((), ())), preferred_element_type=F32)
        g = g.astype(BF).astype(F32).reshape(SLOTS, TH // 2, 16, 256)
        dy, dx = j // 2, lax.rem(j, 2)
        for y in range(TH // 2):
            for i in range(2):
                X[:, 2 * n + i, HALO + 2 * y + dy, dx, 8:24, :] = g[:, y, :, i * 128 : (i + 1) * 128]

    own_rims(rimb)
    b_send, b_got = rim_copies(rimb, bsend, brecv)
    for n in range(3):
        b_send[n].start()
    conv(True, False, 0)
    b_got[0].wait()
    b_send[3].start()
    b_send[5].start()
    b_got[1].wait()
    b_send[4].start()
    b_send[6].start()
    b_got[3].wait()
    b_got[4].wait()
    b_send[7].start()
    for n in (2, 5, 6, 7):
        b_got[n].wait()
    place_rims(rimb)
    conv(True, False, 1)

    for k in range(SLOTS):
        for g in range(4):
            cells = jnp.concatenate(
                [
                    F[lower(k) if g < 2 else 1 - lower(k), dy * 2 + dx, k, 2 * (g % 2) + y]
                    for y in range(2) for dy in range(2) for dx in range(2)
                ],
                axis=0,
            ).astype(BF)
            gout_ref[k, 4 * g : 4 * g + 4] = dot(gather, cells).astype(BF).reshape(4, GW, C)

    for g in range(N_DEV // N_SEQ):
        shape = (N_DEV, 256)
        at1 = iota(shape, 1)
        over = jnp.where(iota(shape, 0) == g * N_SEQ + at1 // (2 * CAP), 1.0, 0.0).astype(BF)
        rows = dot(asked_t, over)
        k8 = iota((CAP, 256), 1)
        put = jnp.sum(jnp.where(iota((CAP, 256), 0) == k8 % CAP, rows, 0.0), axis=0, keepdims=True).astype(I32)
        hit = iota((ROWS, 256), 0) == put - 1
        part = (iota((ROWS, 256), 1) // CAP) % 2
        for h in range(2):
            sel[h, :, g * 256 : (g + 1) * 256] = jnp.where(hit & (part == h), 1.0, 0.0).astype(BF)
    wait_rows(trecv, tsem.at[1])

    @pl.loop(0, C2 // 256)
    def _(n):
        h = n // 3
        cols = pl.ds(pl.multiple_of(n * 256, 256), 256)
        llm_ref[:, cols] = picked(trecv, h, (n - 3 * h) * 256).astype(BF)

    for n in range(8):
        f_send[n].wait_send()
        b_send[n].wait_send()
    wait_rows(msg, msem.at[0])
    for buf, rel, sems in ((gsend, grel, gsem), (tsend, trel, tsem)):
        wait_rows(buf, sems.at[0])
        part = rel.at[pl.ds(0, N_FAR)]
        pltpu.make_async_copy(part, part, sems.at[3]).wait()


def on_device(frame_tiles, tile_ids, partner_slot, mix_kernel, mix_bias, down_weight, down_bias, token_pos, grad_rows):
    vmem = pl.BlockSpec(memory_space=pltpu.VMEM)
    smem = pl.BlockSpec(memory_space=pltpu.SMEM)
    anyw = pl.BlockSpec(memory_space=pl.ANY)
    dma = pltpu.SemaphoreType.DMA
    llm, gout = pl.pallas_call(
        kernel,
        out_shape=(
            jax.ShapeDtypeStruct((ROWS, C2), BF),
            jax.ShapeDtypeStruct((SLOTS, TH, GW, C), BF),
        ),
        in_specs=[anyw, smem, smem, vmem, vmem, anyw, vmem, vmem, anyw],
        out_specs=(vmem, vmem),
        scratch_shapes=[
            pltpu.VMEM((SLOTS, TH, GW, C), BF),
            pltpu.VMEM((4 * C, C2), BF),
            pltpu.VMEM((ROWS, C2), BF),
            pltpu.VMEM((1, C), F32),
            pltpu.VMEM((1, C2), F32),
            pltpu.VMEM((LT, KS * KS, 8, 128), F32),
            pltpu.VMEM((SLOTS, LT, XR, 2, GW, 128), F32),
            pltpu.VMEM((2, 4, SLOTS, TH // 4, 16, C), F32),
            pltpu.VMEM((4, ROWS, C), BF),
            pltpu.VMEM((ROWS, C2), F32),
            pltpu.VMEM((ROWS, C2), BF),
            pltpu.VMEM((ROWS, C2), BF),
            pltpu.VMEM((2, ROWS, 2 * CAP * N_DEV), BF),
            pltpu.VMEM((SLOT_ROWS, ROWS), BF),
            pltpu.VMEM((SLOT_ROWS, 1), I32),
            pltpu.VMEM((N_DEV, 1, 128), F32),
            pltpu.VMEM((N_DEV, 1, 128), F32),
            pltpu.VMEM((N_DEV, 2 * CAP, C), BF),
            pltpu.VMEM((N_DEV, 2 * CAP, C), BF),
            pltpu.VMEM((N_FAR, 2 * CAP, C), BF),
            pltpu.VMEM((N_DEV, 2 * CAP, C), BF),
            pltpu.VMEM((N_DEV, 2 * CAP, C), BF),
            pltpu.VMEM((N_FAR, 2 * CAP, C), BF),
            pltpu.VMEM((N_ENC, SLOTS, LT, 96, 128), BF),
            pltpu.VMEM((N_ENC, SLOTS, LT, 96, 128), BF),
            dma((3,)),
            dma((2,)),
            dma((4,)),
            dma((4,)),
            dma((8,)),
            dma((8,)),
            dma((8,)),
            dma((8,)),
        ],
        compiler_params=pltpu.CompilerParams(
            collective_id=0, has_side_effects=True, vmem_limit_bytes=62 * 1024 * 1024
        ),
    )(
        frame_tiles,
        tile_ids,
        partner_slot,
        mix_kernel,
        mix_bias,
        down_weight,
        down_bias,
        token_pos,
        grad_rows,
    )
    return llm, gout[None, None]


def solution(mesh):
    return jax.shard_map(
        on_device,
        mesh=mesh,
        in_specs=(
            P("enc", "seq", None, None, None, None),
            P("enc", "seq", None),
            P("enc", "seq", None),
            P(),
            P(),
            P(),
            P(),
            P("enc", "seq", None, None),
            P(("enc", "seq"), None),
        ),
        out_specs=(P(("enc", "seq"), None), P("enc", "seq", None, None, None, None)),
        check_vma=False,
    )
```

```python
import functools

import itertools

import jax
import jax.numpy as jnp
import numpy as np
from jax import lax
from jax.experimental import pallas as pl
from jax.experimental.pallas import tpu as pltpu
from jax.sharding import PartitionSpec as P

C = 768
C2 = 1536
KS = 7
TH = 16
GW = 32
SLOTS = 2
ROWS = 256
N_ENC = 8
N_SEQ = 16
N_DEV = 128
CAP = 8
SLOT_ROWS = CAP * N_DEV

def orbit(o):
    turned = [o, o[2:] + o[:2], o[1:] + o[:1]]
    return [p for q in turned for p in (q, tuple(-d % 4 for d in q))]


ALL_OFFSETS = sorted(itertools.product((0, 1, 3, 2), repeat=3), key=lambda o: -sum(min(d, 4 - d) for d in o))
ORDERED = list(dict.fromkeys(p for o in ALL_OFFSETS for p in orbit(o)))
FAR = [o for o in ORDERED if 2 in o]
OFFSETS = FAR + [o for o in ORDERED if 2 not in o]
N_FAR = 2 * len(FAR)
OWN = N_DEV - 2


def packed(axis):
    words = []
    for n in range(0, 64, 16):
        word = sum(o[axis] << (2 * i) for i, o in enumerate(OFFSETS[n : n + 16]))
        words.append(word - (1 << 32) if word >> 31 else word)
    return words


WORDS = [packed(axis) for axis in range(3)]
HALO = 3
CELLS = TH * GW
RIM = HALO * GW
FR, FC = TH + 2 * HALO, GW + HALO
N_FREQ = FR * (FC // 2 + 1)
HALF_F = 400
ALL_F = 2 * HALF_F
TAPS = 8 * KS
SQRT_HALF = 0.7071067811865476
INV_ROOT = 0.3989422804014327
BF = jnp.bfloat16
F32 = jnp.float32
I32 = jnp.int32


def transforms():
    kr, kc = [v.reshape(-1, 1) for v in np.meshgrid(np.arange(FR), np.arange(FC // 2 + 1), indexing="ij")]

    def wave(r, c):
        return np.exp(2j * np.pi * (kr * r / FR + kc * c / FC))

    def rows_of(z):
        out = np.zeros((ALL_F, z.shape[1]))
        out[:N_FREQ], out[HALF_F : HALF_F + N_FREQ] = z.real, z.imag
        return out

    r, c = [v.ravel() for v in np.meshgrid(np.arange(TH), np.arange(GW), indexing="ij")]
    by_patch = np.argsort(((r % 2) * 2 + c % 2) * 128 + (r // 2) * 16 + c // 2)
    rr, rc = [v.ravel() for v in np.meshgrid(np.arange(HALO), np.arange(GW), indexing="ij")]
    rim_patch = np.argsort(rr * GW + (rc % 2) * 16 + rc // 2)
    there = rows_of(np.conj(wave(r, c)))
    rims = [rows_of(np.conj(wave(rr + at, rc))) for at in (-HALO, TH)]
    rim_cells = np.concatenate(rims, axis=1)
    rim_patches = np.concatenate([m[:, rim_patch] for m in rims], axis=1)
    share = np.where(kc == 0, 1.0, 2.0) / (FR * FC)
    back = wave(r, c) * share
    back = (rows_of(np.conj(back))).T
    a, b = np.arange(TAPS) // 8, np.arange(TAPS) % 8
    taps = rows_of(wave(a - HALO, b - HALO) * (b < KS))
    high = taps.astype(BF)
    low = (taps - high.astype(np.float64)).astype(BF)
    return [
        m.astype(BF)
        for m in (there, there[:, by_patch], rim_cells, rim_patches, back[by_patch], back, high, low)
    ]


def iota(shape, axis):
    return lax.broadcasted_iota(I32, shape, axis)


def dot(a, b):
    return jnp.dot(a, b, preferred_element_type=F32)


def kernel(
    tiles_hbm, ids_ref, partner_ref, mixk_ref, mixb_ref, w_hbm, downb_ref, pos_ref, grad_hbm,
    to_f_hbm, to_b_hbm, rim_f_hbm, rim_b_hbm, from_f_hbm, from_b_hbm, tap_high, tap_low,
    llm_ref, gout_ref,
    to_f, to_b, rim_f, rim_b, from_f, from_b, taps, wave, field, edge, mg, to_patch, to_cell,
    tiles, w, grads, mixb, downb, A, slope, tok, pg, sel, hot, owner,
    msg, rmsg, gsend, grecv, grel, tsend, trecv, trel, rimf, rimb,
    lsem, msem, gsem, tsem, fsend, frecv, bsend, brecv,
):
    enc = lax.axis_index("enc")
    seq = lax.axis_index("seq")
    me = enc * N_SEQ + seq
    cy, core = enc // 2, enc % 2

    ld_tiles = pltpu.make_async_copy(tiles_hbm.at[0, 0], tiles, lsem.at[0])
    ld_grads = pltpu.make_async_copy(grad_hbm, grads, lsem.at[1])
    ld_w = pltpu.make_async_copy(w_hbm, w, lsem.at[2])
    ld_tiles.start()
    ld_grads.start()
    ld_consts = [
        pltpu.make_async_copy(src, dst, lsem.at[3 + n])
        for n, (src, dst) in enumerate(
            ((to_f_hbm, to_f), (rim_f_hbm, rim_f), (from_f_hbm, from_f), (to_b_hbm, to_b), (rim_b_hbm, rim_b), (from_b_hbm, from_b))
        )
    ]
    for n in range(3):
        ld_consts[n].start()
    ld_w.start()
    for n in range(3, 6):
        ld_consts[n].start()

    barrier = pltpu.get_barrier_semaphore()

    @pl.loop(1, N_DEV)
    def _(i):
        e, s = (enc + (i >> 4)) & (N_ENC - 1), (seq + i) & (N_SEQ - 1)
        pl.semaphore_signal(barrier, inc=1, device_id=(e, s), device_id_type=pl.DeviceIdType.MESH)

    mixb[...] = mixb_ref[...].reshape(1, C)
    downb[...] = downb_ref[...].reshape(1, C2)

    pos = pos_ref[0, 0]
    prow = jnp.concatenate([pos[0:1, :], pos[1:2, :]], axis=1)
    pcol = jnp.concatenate(
        [jnp.transpose(jnp.broadcast_to(pos[i : i + 1, :].astype(F32), (128, 128))) for i in range(2)], axis=0
    ).astype(I32)[:, 0:1]
    orow, ocol = prow // ROWS, pcol // ROWS
    lcol = pcol - ocol * ROWS
    same = jnp.broadcast_to(ocol, (ROWS, ROWS)) == jnp.broadcast_to(orow, (ROWS, ROWS))
    at0, at1 = iota((ROWS, ROWS), 0), iota((ROWS, ROWS), 1)
    rank_row = jnp.sum(jnp.where(same & (at0 < at1), 1.0, 0.0), axis=0, keepdims=True).astype(I32)
    rank_col = jnp.sum(jnp.where(same & (at1 < at0), 1.0, 0.0), axis=1, keepdims=True).astype(I32)
    slot_row = orow * CAP + rank_row
    to_owner = jnp.where(iota((N_DEV, ROWS), 0) == orow, 1.0, 0.0).astype(BF)
    ranked = jnp.where(iota((ROWS, 128), 1) == rank_col, (lcol + 1).astype(F32), 0.0).astype(BF)
    msg[...] = dot(to_owner, ranked).reshape(N_DEV, 1, 128)
    rmsg[pl.ds(me, 1)] = msg[pl.ds(me, 1)]

    def cell_of(m):
        return ((m % 128) // 16 * 2 + m // 256) * GW + m % 16 * 2 + m // 128 % 2

    p0, p1 = iota((CELLS, CELLS), 0), iota((CELLS, CELLS), 1)
    to_patch[...] = jnp.where(p1 == cell_of(p0), 1.0, 0.0).astype(BF)
    to_cell[...] = jnp.where(p0 == cell_of(p1), 1.0, 0.0).astype(BF)

    taps[...] = jnp.zeros((TAPS, C), F32)
    for a in range(KS):
        taps[8 * a : 8 * a + KS, :] = mixk_ref[a].astype(F32)
    flat_taps = taps[...].astype(BF)
    wave[...] = dot(tap_high[...], flat_taps) + dot(tap_low[...], flat_taps)

    def lower(k):
        return lax.rem(ids_ref[0, 0, k], 2)

    up = lax.rem(cy + 1, 4) * 2 + core
    down = lax.rem(cy + 3, 4) * 2 + core
    across = lax.rem(cy + 2, 4) * 2 + core
    sib = cy * 2 + 1 - core

    def rim_copies(rims, ssem, rsem):
        def copy(n, ref, to):
            return pltpu.make_async_remote_copy(
                src_ref=ref, dst_ref=ref, send_sem=ssem.at[n], recv_sem=rsem.at[n],
                device_id=(to, seq), device_id_type=pl.DeviceIdType.MESH,
            )

        def landed(n, ref):
            return pltpu.make_async_copy(ref, ref, rsem.at[n])

        sends = [
            copy(0, rims.at[enc], up),
            copy(1, rims.at[enc], down),
            copy(2, rims.at[enc], sib),
            copy(3, rims.at[down, 0], up),
            copy(4, rims.at[up, 1], down),
            copy(5, rims.at[down], sib),
            copy(6, rims.at[up], sib),
            copy(7, rims.at[across], sib),
        ]
        other = 1 - 2 * core
        arrivals = [
            landed(0, rims.at[down]),
            landed(1, rims.at[up]),
            landed(2, rims.at[sib]),
            landed(3, rims.at[across, 0]),
            landed(4, rims.at[across, 1]),
            landed(5, rims.at[down + other]),
            landed(6, rims.at[up + other]),
            landed(7, rims.at[across + other]),
        ]
        return sends, arrivals

    def place_rims(rims):
        for k in range(SLOTS):
            want = partner_ref[0, 0, k]
            rim = jnp.zeros((RIM, C), BF)
            for q in range(N_ENC * SLOTS):
                rim = jnp.where(want == q, rims[q // 2, q % 2], rim)
            none = jnp.zeros((RIM, C), BF)
            below = lower(k) == 1
            edge[k, 0:RIM, :] = jnp.where(below, rim, none)
            edge[k, RIM : 2 * RIM, :] = jnp.where(below, none, rim)

    def columns(n):
        return pl.ds(pl.multiple_of(n * 256, 256), 256)

    def spectrum(there, cells):
        @pl.loop(0, SLOTS * 3)
        def _(i):
            k, cols = i // 3, columns(lax.rem(i, 3))
            field[k, :, cols] = dot(there, cells(k, cols))

    def depthwise(there, back, way, turn, cells, store):
        @pl.loop(0, SLOTS * 3)
        def _(i):
            k, cols = i // 3, columns(lax.rem(i, 3))
            z = field[k, :, cols] + dot(there[...], edge[k, :, cols])
            re, im = z[0:HALF_F], z[HALF_F:ALL_F]
            wr, wi = wave[0:HALF_F, cols], way * wave[HALF_F:ALL_F, cols]
            product = jnp.concatenate([re * wr - im * wi, re * wi + im * wr], axis=0).astype(BF)
            store(k, cols, dot(turn[...], cells(k, cols)) + dot(back[...], product))

    cx, cz = seq >> 2, seq & 3
    at_x = [((cx + d) & 3) * 4 for d in range(4)]
    at_y = [((cy + d) & 3) * 2 for d in range(4)]
    at_z = [(cz + d) & 3 for d in range(4)]
    at_core = [core, 1 - core]

    def step(off, f):
        return [way if d == 2 else 0 for d, way in zip(off, (1 + 2 * f, 3 - 2 * f, 1 + 2 * f))]

    def device(off, f):
        return at_y[off[1]] + at_core[f], at_x[off[0]] + at_z[off[2]]

    def owner_of_row():
        place = iota((SLOT_ROWS, 1), 0) // CAP
        block, shift = place // 32, 2 * ((place // 2) % 16)
        d = []
        for w0, w1, w2, w3 in WORDS:
            word = jnp.where(block < 2, jnp.where(block == 0, w0, w1), jnp.where(block == 2, w2, w3))
            d.append(jnp.right_shift(word, shift) & 3)
        c = core + place % 2 - 2 * core * (place % 2)
        return (((cy + d[1]) & 3) * 2 + c) * N_SEQ + ((cx + d[0]) & 3) * 4 + ((cz + d[2]) & 3)

    def fill_rows(buf, rows_ref):
        @pl.loop(0, C // 256)
        def _(n):
            c0 = pl.multiple_of(n * 256, 256)
            y0 = dot(hot[...], rows_ref[:, pl.ds(c0, 256)]).reshape(N_DEV, CAP, 256)
            y1 = dot(hot[...], rows_ref[:, pl.ds(c0 + C, 256)]).reshape(N_DEV, CAP, 256)
            buf[:, :, pl.ds(c0, 256)] = jnp.concatenate([y0, y1], axis=1).astype(BF)

    def send_far(buf, rel, sems):
        for q in range(N_FAR):
            pltpu.make_async_remote_copy(
                src_ref=buf.at[q], dst_ref=rel.at[q],
                send_sem=sems.at[0], recv_sem=sems.at[2],
                device_id=device(step(OFFSETS[q // 2], q % 2), 0), device_id_type=pl.DeviceIdType.MESH,
            ).start()

    def send_near(buf, got, sems):
        for q in range(N_FAR, N_DEV):
            if q != OWN:
                pltpu.make_async_remote_copy(
                    src_ref=buf.at[q], dst_ref=got.at[me],
                    send_sem=sems.at[0], recv_sem=sems.at[1],
                    device_id=device(OFFSETS[q // 2], q % 2), device_id_type=pl.DeviceIdType.MESH,
                ).start()

    def forward(rel, got, sems):
        part = rel.at[pl.ds(0, N_FAR)]
        pltpu.make_async_copy(part, part, sems.at[2]).wait()
        for q in range(N_FAR):
            off = OFFSETS[q // 2]
            leg = step(off, q % 2)
            e0, s0 = device([(4 - d) % 4 for d in leg], 0)
            rest = [(o + 4 - d) % 4 for o, d in zip(off, leg)]
            pltpu.make_async_remote_copy(
                src_ref=rel.at[q], dst_ref=got.at[e0 * N_SEQ + s0],
                send_sem=sems.at[3], recv_sem=sems.at[1],
                device_id=device(rest, q % 2), device_id_type=pl.DeviceIdType.MESH,
            ).start()

    def keep_own(buf, got):
        got[pl.ds(me, 1)] = buf[OWN : OWN + 1]

    def wait_rows(buf, sem):
        part = buf.at[pl.ds(0, N_DEV - 1)]
        pltpu.make_async_copy(part, part, sem).wait()

    ld_tiles.wait()
    for k in range(SLOTS):
        high, low = tiles[k, TH - HALO : TH].reshape(RIM, C), tiles[k, 0:HALO].reshape(RIM, C)
        rimf[enc, k] = jnp.where(lower(k) == 0, high, low)
    owner[...] = owner_of_row()
    pl.semaphore_wait(barrier, N_DEV - 1)

    f_send, f_got = rim_copies(rimf, fsend, frecv)
    for n in range(3):
        f_send[n].start()

    @pl.loop(1, N_DEV)
    def _(i):
        e, s = (enc + (i >> 4)) & (N_ENC - 1), (seq + i) & (N_SEQ - 1)
        pltpu.make_async_remote_copy(
            src_ref=msg.at[e * N_SEQ + s], dst_ref=rmsg.at[me],
            send_sem=msem.at[0], recv_sem=msem.at[1],
            device_id=(e, s), device_id_type=pl.DeviceIdType.MESH,
        ).start()

    ld_consts[0].wait()

    def tile_cells(k, cols):
        return tiles[k, :, :, cols].reshape(CELLS, 256)

    def grad_cells(k, cols):
        return mg[k, :, cols]

    spectrum(to_f[...], tile_cells)
    ld_grads.wait()
    wait_rows(rmsg, msem.at[1])

    asked = rmsg[...].reshape(N_DEV, 128)
    asked_t = jnp.transpose(asked)[0:CAP, :].astype(BF)
    asked = asked.astype(BF)

    shape = (SLOT_ROWS, 128)
    rows = dot(jnp.where(iota(shape, 1) == owner[...], 1.0, 0.0).astype(BF), asked)
    want = jnp.sum(jnp.where(iota(shape, 1) == iota(shape, 0) % CAP, rows, 0.0), axis=1, keepdims=True).astype(I32)
    hot[...] = jnp.where(iota((SLOT_ROWS, ROWS), 1) == want - 1, 1.0, 0.0).astype(BF)
    fill_rows(gsend, grads)
    f_got[0].wait()
    f_send[3].start()
    f_send[5].start()
    f_got[1].wait()
    f_send[4].start()
    f_send[6].start()
    send_far(gsend, grel, gsem)
    send_near(gsend, grecv, gsem)
    keep_own(gsend, grecv)
    f_got[3].wait()
    f_got[4].wait()
    f_send[7].start()
    for n in (2, 5, 6, 7):
        f_got[n].wait()
    place_rims(rimf)
    ld_consts[1].wait()
    ld_consts[2].wait()

    def store_mixed(k, cols, cells):
        mixed = (cells + mixb[:, cols]).astype(BF)
        A[:, pl.ds(pl.multiple_of(k * 128, 128), 128), cols] = mixed.reshape(4, 128, 256)

    depthwise(rim_f, from_f, 1.0, to_patch, tile_cells, store_mixed)
    forward(grel, grecv, gsem)
    ld_w.wait()

    @pl.loop(0, C2 // 256)
    def _(n):
        cols = pl.ds(pl.multiple_of(n * 256, 256), 256)
        pre = jnp.zeros((ROWS, 256), F32) + downb[:, cols]
        for j in range(4):
            pre = pre + dot(A[j], w[j * C : (j + 1) * C, cols])
        phi = 0.5 * (1.0 + lax.erf(pre * SQRT_HALF))
        tok[:, cols] = (pre * phi).astype(BF)
        slope[:, cols] = phi + pre * INV_ROOT * jnp.exp(-0.5 * pre * pre)

    at = owner[...] * CAP + iota((SLOT_ROWS, 1), 0) % CAP
    hot[...] = jnp.where(at == slot_row, 1.0, 0.0).astype(BF)
    fill_rows(tsend, tok)
    send_far(tsend, trel, tsem)
    send_near(tsend, trecv, tsem)
    keep_own(tsend, trecv)

    back_at = ocol * (2 * CAP) + rank_col
    for h in range(2):
        sel[h] = jnp.where(iota((ROWS, 2 * CAP * N_DEV), 1) == back_at + h * CAP, 1.0, 0.0).astype(BF)
    wait_rows(grecv, gsem.at[1])

    def picked(got, h, c0):
        part = got[:, :, pl.ds(pl.multiple_of(c0, 256), 256)].reshape(2 * CAP * N_DEV, 256)
        return dot(sel[h], part)

    @pl.loop(0, C2 // 256)
    def _(n):
        h = n // 3
        cols = pl.ds(pl.multiple_of(n * 256, 256), 256)
        pg[:, cols] = (picked(grecv, h, (n - 3 * h) * 256) * slope[:, cols]).astype(BF)

    forward(trel, trecv, tsem)

    @pl.loop(0, 4 * (C // 256))
    def _(m):
        j, n = m // 3, lax.rem(m, 3)
        part = w[pl.ds(pl.multiple_of(m * 256, 256), 256), :]
        g = lax.dot_general(pg[...], part, (((1,), (1,)), ((), ())), preferred_element_type=F32)
        mg[:, pl.ds(pl.multiple_of(j * 128, 128), 128), columns(n)] = g.astype(BF).reshape(SLOTS, 128, 256)

    def rim_rows(k, rows):
        at = [((r % 2) * 2 + dx) * 128 + (r // 2) * 16 for r in rows for dx in range(2)]
        return jnp.concatenate([mg[k, a : a + 16, :] for a in at], axis=0)

    for k in range(SLOTS):
        rimb[enc, k] = jnp.where(lower(k) == 0, rim_rows(k, range(TH - HALO, TH)), rim_rows(k, range(HALO)))
    b_send, b_got = rim_copies(rimb, bsend, brecv)
    for n in range(3):
        b_send[n].start()
    ld_consts[3].wait()
    spectrum(to_b[...], grad_cells)
    b_got[0].wait()
    b_send[3].start()
    b_send[5].start()
    b_got[1].wait()
    b_send[4].start()
    b_send[6].start()
    b_got[3].wait()
    b_got[4].wait()
    b_send[7].start()
    for n in (2, 5, 6, 7):
        b_got[n].wait()
    place_rims(rimb)
    ld_consts[4].wait()
    ld_consts[5].wait()

    def store_grad(k, cols, cells):
        gout_ref[k, :, :, cols] = cells.astype(BF).reshape(TH, GW, 256)

    depthwise(rim_b, from_b, -1.0, to_cell, grad_cells, store_grad)

    for g in range(N_DEV // N_SEQ):
        shape = (N_DEV, 256)
        at1 = iota(shape, 1)
        over = jnp.where(iota(shape, 0) == g * N_SEQ + at1 // (2 * CAP), 1.0, 0.0).astype(BF)
        rows = dot(asked_t, over)
        k8 = iota((CAP, 256), 1)
        put = jnp.sum(jnp.where(iota((CAP, 256), 0) == k8 % CAP, rows, 0.0), axis=0, keepdims=True).astype(I32)
        hit = iota((ROWS, 256), 0) == put - 1
        part = (iota((ROWS, 256), 1) // CAP) % 2
        for h in range(2):
            sel[h, :, g * 256 : (g + 1) * 256] = jnp.where(hit & (part == h), 1.0, 0.0).astype(BF)
    wait_rows(trecv, tsem.at[1])

    @pl.loop(0, C2 // 256)
    def _(n):
        h = n // 3
        cols = pl.ds(pl.multiple_of(n * 256, 256), 256)
        llm_ref[:, cols] = picked(trecv, h, (n - 3 * h) * 256).astype(BF)

    for n in range(8):
        f_send[n].wait_send()
        b_send[n].wait_send()
    wait_rows(msg, msem.at[0])
    for buf, rel, sems in ((gsend, grel, gsem), (tsend, trel, tsem)):
        wait_rows(buf, sems.at[0])
        part = rel.at[pl.ds(0, N_FAR)]
        pltpu.make_async_copy(part, part, sems.at[3]).wait()


def on_device(frame_tiles, tile_ids, partner_slot, mix_kernel, mix_bias, down_weight, down_bias, token_pos, grad_rows):
    vmem = pl.BlockSpec(memory_space=pltpu.VMEM)
    smem = pl.BlockSpec(memory_space=pltpu.SMEM)
    anyw = pl.BlockSpec(memory_space=pl.ANY)
    dma = pltpu.SemaphoreType.DMA
    llm, gout = pl.pallas_call(
        kernel,
        out_shape=(
            jax.ShapeDtypeStruct((ROWS, C2), BF),
            jax.ShapeDtypeStruct((SLOTS, TH, GW, C), BF),
        ),
        in_specs=[anyw, smem, smem, vmem, vmem, anyw, vmem, vmem, anyw] + [anyw] * 6 + [vmem] * 2,
        out_specs=(vmem, vmem),
        scratch_shapes=[
            pltpu.VMEM((ALL_F, CELLS), BF),
            pltpu.VMEM((ALL_F, CELLS), BF),
            pltpu.VMEM((ALL_F, 2 * RIM), BF),
            pltpu.VMEM((ALL_F, 2 * RIM), BF),
            pltpu.VMEM((CELLS, ALL_F), BF),
            pltpu.VMEM((CELLS, ALL_F), BF),
            pltpu.VMEM((TAPS, C), F32),
            pltpu.VMEM((ALL_F, C), F32),
            pltpu.VMEM((SLOTS, ALL_F, C), F32),
            pltpu.VMEM((SLOTS, 2 * RIM, C), BF),
            pltpu.VMEM((SLOTS, CELLS, C), BF),
            pltpu.VMEM((CELLS, CELLS), BF),
            pltpu.VMEM((CELLS, CELLS), BF),
            pltpu.VMEM((SLOTS, TH, GW, C), BF),
            pltpu.VMEM((4 * C, C2), BF),
            pltpu.VMEM((ROWS, C2), BF),
            pltpu.VMEM((1, C), F32),
            pltpu.VMEM((1, C2), F32),
            pltpu.VMEM((4, ROWS, C), BF),
            pltpu.VMEM((ROWS, C2), F32),
            pltpu.VMEM((ROWS, C2), BF),
            pltpu.VMEM((ROWS, C2), BF),
            pltpu.VMEM((2, ROWS, 2 * CAP * N_DEV), BF),
            pltpu.VMEM((SLOT_ROWS, ROWS), BF),
            pltpu.VMEM((SLOT_ROWS, 1), I32),
            pltpu.VMEM((N_DEV, 1, 128), F32),
            pltpu.VMEM((N_DEV, 1, 128), F32),
            pltpu.VMEM((N_DEV, 2 * CAP, C), BF),
            pltpu.VMEM((N_DEV, 2 * CAP, C), BF),
            pltpu.VMEM((N_FAR, 2 * CAP, C), BF),
            pltpu.VMEM((N_DEV, 2 * CAP, C), BF),
            pltpu.VMEM((N_DEV, 2 * CAP, C), BF),
            pltpu.VMEM((N_FAR, 2 * CAP, C), BF),
            pltpu.VMEM((N_ENC, SLOTS, RIM, C), BF),
            pltpu.VMEM((N_ENC, SLOTS, RIM, C), BF),
            dma((9,)),
            dma((2,)),
            dma((4,)),
            dma((4,)),
            dma((8,)),
            dma((8,)),
            dma((8,)),
            dma((8,)),
        ],
        compiler_params=pltpu.CompilerParams(
            collective_id=0, has_side_effects=True, vmem_limit_bytes=62 * 1024 * 1024
        ),
    )(
        frame_tiles,
        tile_ids,
        partner_slot,
        mix_kernel,
        mix_bias,
        down_weight,
        down_bias,
        token_pos,
        grad_rows,
        *transforms(),
    )
    return llm, gout[None, None]


def solution(mesh):
    return jax.shard_map(
        on_device,
        mesh=mesh,
        in_specs=(
            P("enc", "seq", None, None, None, None),
            P("enc", "seq", None),
            P("enc", "seq", None),
            P(),
            P(),
            P(),
            P(),
            P("enc", "seq", None, None),
            P(("enc", "seq"), None),
        ),
        out_specs=(P(("enc", "seq"), None), P("enc", "seq", None, None, None, None)),
        check_vma=False,
    )
```

```python
import functools

import itertools

import jax
import jax.numpy as jnp
import numpy as np
from jax import lax
from jax.experimental import pallas as pl
from jax.experimental.pallas import tpu as pltpu
from jax.sharding import PartitionSpec as P

C = 768
C2 = 1536
KS = 7
TH = 16
GW = 32
SLOTS = 2
ROWS = 256
N_ENC = 8
N_SEQ = 16
N_DEV = 128
CAP = 8
SLOT_ROWS = CAP * N_DEV

def orbit(o):
    turned = [o, o[2:] + o[:2], o[1:] + o[:1]]
    return [p for q in turned for p in (q, tuple(-d % 4 for d in q))]


ALL_OFFSETS = sorted(itertools.product((0, 1, 3, 2), repeat=3), key=lambda o: -sum(min(d, 4 - d) for d in o))
ORDERED = list(dict.fromkeys(p for o in ALL_OFFSETS for p in orbit(o)))
OFFSETS = ORDERED
HALF_DEV = N_DEV // 2
OWN = N_DEV - 2


def packed(axis):
    words = []
    for n in range(0, 64, 16):
        word = sum(o[axis] << (2 * i) for i, o in enumerate(OFFSETS[n : n + 16]))
        words.append(word - (1 << 32) if word >> 31 else word)
    return words


WORDS = [packed(axis) for axis in range(3)]
HALO = 3
CELLS = TH * GW
RIM = HALO * GW
FR, FC = TH + 2 * HALO, GW + HALO
N_FREQ = FR * (FC // 2 + 1)
HALF_F = 400
ALL_F = 2 * HALF_F
TAPS = 8 * KS
SQRT_HALF = 0.7071067811865476
INV_ROOT = 0.3989422804014327
BF = jnp.bfloat16
F32 = jnp.float32
I32 = jnp.int32


def transforms():
    kr, kc = [v.reshape(-1, 1) for v in np.meshgrid(np.arange(FR), np.arange(FC // 2 + 1), indexing="ij")]

    def wave(r, c):
        return np.exp(2j * np.pi * (kr * r / FR + kc * c / FC))

    def rows_of(z):
        out = np.zeros((ALL_F, z.shape[1]))
        out[:N_FREQ], out[HALF_F : HALF_F + N_FREQ] = z.real, z.imag
        return out

    r, c = [v.ravel() for v in np.meshgrid(np.arange(TH), np.arange(GW), indexing="ij")]
    by_patch = np.argsort(((r % 2) * 2 + c % 2) * 128 + (r // 2) * 16 + c // 2)
    rr, rc = [v.ravel() for v in np.meshgrid(np.arange(HALO), np.arange(GW), indexing="ij")]
    rim_patch = np.argsort(rr * GW + (rc % 2) * 16 + rc // 2)
    there = rows_of(np.conj(wave(r, c)))
    rims = [rows_of(np.conj(wave(rr + at, rc))) for at in (-HALO, TH)]
    rim_cells = np.concatenate(rims, axis=1)
    rim_patches = np.concatenate([m[:, rim_patch] for m in rims], axis=1)
    share = np.where(kc == 0, 1.0, 2.0) / (FR * FC)
    back = wave(r, c) * share
    back = (rows_of(np.conj(back))).T
    a, b = np.arange(TAPS) // 8, np.arange(TAPS) % 8
    taps = rows_of(wave(a - HALO, b - HALO) * (b < KS))
    high = taps.astype(BF)
    low = (taps - high.astype(np.float64)).astype(BF)
    return [
        m.astype(BF)
        for m in (there, there[:, by_patch], rim_cells, rim_patches, back[by_patch], back, high, low)
    ]


def iota(shape, axis):
    return lax.broadcasted_iota(I32, shape, axis)


def dot(a, b):
    return jnp.dot(a, b, preferred_element_type=F32)


def kernel(
    tiles_hbm, ids_ref, partner_ref, mixk_ref, mixb_ref, w_hbm, downb_ref, pos_ref, grad_hbm,
    to_f_hbm, to_b_hbm, rim_f_hbm, rim_b_hbm, from_f_hbm, from_b_hbm, tap_high, tap_low,
    llm_ref, gout_ref,
    to_f, to_b, rim_f, rim_b, from_f, from_b, taps, wave, field, edge, mg, to_patch, to_cell,
    tiles, w, grads, mixb, downb, A, slope, tok, pg, sel, hot, owner,
    msg, rmsg, gsend, grecv, tsend, trecv, rimf, rimb,
    lsem, msem, gsem, tsem, fsend, frecv, bsend, brecv,
):
    enc = lax.axis_index("enc")
    seq = lax.axis_index("seq")
    me = enc * N_SEQ + seq
    cy, core = enc // 2, enc % 2

    ld_tiles = pltpu.make_async_copy(tiles_hbm.at[0, 0], tiles, lsem.at[0])
    ld_grads = pltpu.make_async_copy(grad_hbm, grads, lsem.at[1])
    ld_w = pltpu.make_async_copy(w_hbm, w, lsem.at[2])
    ld_tiles.start()
    ld_grads.start()
    ld_consts = [
        pltpu.make_async_copy(src, dst, lsem.at[3 + n])
        for n, (src, dst) in enumerate(
            ((to_f_hbm, to_f), (rim_f_hbm, rim_f), (from_f_hbm, from_f), (to_b_hbm, to_b), (rim_b_hbm, rim_b), (from_b_hbm, from_b))
        )
    ]
    for n in range(3):
        ld_consts[n].start()
    ld_w.start()
    for n in range(3, 6):
        ld_consts[n].start()

    cx, cz = seq >> 2, seq & 3
    at_x = [((cx + d) & 3) * 4 for d in range(4)]
    at_y = [((cy + d) & 3) * 2 for d in range(4)]
    at_z = [(cz + d) & 3 for d in range(4)]
    at_core = [core, 1 - core]

    def device(q):
        dx, dy, dz = OFFSETS[q // 2]
        return at_y[dy] + at_core[q % 2], at_x[dx] + at_z[dz]

    others = [q for q in range(N_DEV) if q != OWN]
    barrier = pltpu.get_barrier_semaphore()
    for q in others:
        pl.semaphore_signal(barrier, inc=1, device_id=device(q), device_id_type=pl.DeviceIdType.MESH)


    pos = pos_ref[0, 0]
    prow = jnp.concatenate([pos[0:1, :], pos[1:2, :]], axis=1)
    pcol = jnp.concatenate(
        [jnp.transpose(jnp.broadcast_to(pos[i : i + 1, :].astype(F32), (128, 128))) for i in range(2)], axis=0
    ).astype(I32)[:, 0:1]
    orow, ocol = prow // ROWS, pcol // ROWS
    lcol = pcol - ocol * ROWS
    same = jnp.broadcast_to(ocol, (ROWS, ROWS)) == jnp.broadcast_to(orow, (ROWS, ROWS))
    at0, at1 = iota((ROWS, ROWS), 0), iota((ROWS, ROWS), 1)
    rank_row = jnp.sum(jnp.where(same & (at0 < at1), 1.0, 0.0), axis=0, keepdims=True).astype(I32)
    rank_col = jnp.sum(jnp.where(same & (at1 < at0), 1.0, 0.0), axis=1, keepdims=True).astype(I32)
    slot_row = orow * CAP + rank_row
    to_owner = jnp.where(iota((N_DEV, ROWS), 0) == orow, 1.0, 0.0).astype(BF)
    ranked = jnp.where(iota((ROWS, 128), 1) == rank_col, (lcol + 1).astype(F32), 0.0).astype(BF)
    msg[...] = dot(to_owner, ranked).reshape(N_DEV, 1, 128)
    rmsg[pl.ds(me, 1)] = msg[pl.ds(me, 1)]

    def lower(k):
        return lax.rem(ids_ref[0, 0, k], 2)

    up = lax.rem(cy + 1, 4) * 2 + core
    down = lax.rem(cy + 3, 4) * 2 + core
    across = lax.rem(cy + 2, 4) * 2 + core
    sib = cy * 2 + 1 - core

    def rim_copies(rims, ssem, rsem):
        def copy(n, ref, to):
            return pltpu.make_async_remote_copy(
                src_ref=ref, dst_ref=ref, send_sem=ssem.at[n], recv_sem=rsem.at[n],
                device_id=(to, seq), device_id_type=pl.DeviceIdType.MESH,
            )

        def landed(n, ref):
            return pltpu.make_async_copy(ref, ref, rsem.at[n])

        sends = [
            copy(0, rims.at[enc], up),
            copy(1, rims.at[enc], down),
            copy(2, rims.at[enc], sib),
            copy(3, rims.at[down, 0], up),
            copy(4, rims.at[up, 1], down),
            copy(5, rims.at[down], sib),
            copy(6, rims.at[up], sib),
            copy(7, rims.at[across], sib),
        ]
        other = 1 - 2 * core
        arrivals = [
            landed(0, rims.at[down]),
            landed(1, rims.at[up]),
            landed(2, rims.at[sib]),
            landed(3, rims.at[across, 0]),
            landed(4, rims.at[across, 1]),
            landed(5, rims.at[down + other]),
            landed(6, rims.at[up + other]),
            landed(7, rims.at[across + other]),
        ]
        return sends, arrivals

    def place_rims(rims):
        for k in range(SLOTS):
            want = partner_ref[0, 0, k]
            rim = jnp.zeros((RIM, C), BF)
            for q in range(N_ENC * SLOTS):
                rim = jnp.where(want == q, rims[q // 2, q % 2], rim)
            none = jnp.zeros((RIM, C), BF)
            below = lower(k) == 1
            edge[k, 0:RIM, :] = jnp.where(below, rim, none)
            edge[k, RIM : 2 * RIM, :] = jnp.where(below, none, rim)

    def columns(n):
        return pl.ds(pl.multiple_of(n * 256, 256), 256)

    def spectrum(there, cells):
        @pl.loop(0, SLOTS * 3)
        def _(i):
            k, cols = i // 3, columns(lax.rem(i, 3))
            field[k, :, cols] = dot(there, cells(k, cols))

    def depthwise(there, back, way, turn, cells, store):
        @pl.loop(0, SLOTS * 3)
        def _(i):
            k, cols = i // 3, columns(lax.rem(i, 3))
            z = field[k, :, cols] + dot(there[...], edge[k, :, cols])
            re, im = z[0:HALF_F], z[HALF_F:ALL_F]
            wr, wi = wave[0:HALF_F, cols], way * wave[HALF_F:ALL_F, cols]
            product = jnp.concatenate([re * wr - im * wi, re * wi + im * wr], axis=0).astype(BF)
            store(k, cols, dot(turn[...], cells(k, cols)) + dot(back[...], product))

    def owner_of_row():
        place = iota((SLOT_ROWS, 1), 0) // CAP
        block, shift = place // 32, 2 * ((place // 2) % 16)
        d = []
        for w0, w1, w2, w3 in WORDS:
            word = jnp.where(block < 2, jnp.where(block == 0, w0, w1), jnp.where(block == 2, w2, w3))
            d.append(jnp.right_shift(word, shift) & 3)
        c = core + place % 2 - 2 * core * (place % 2)
        return (((cy + d[1]) & 3) * 2 + c) * N_SEQ + ((cx + d[0]) & 3) * 4 + ((cz + d[2]) & 3)

    def fill_rows(buf, rows_ref, part):
        slots = slice(part * SLOT_ROWS // 2, (part + 1) * SLOT_ROWS // 2)
        dests = slice(part * HALF_DEV, (part + 1) * HALF_DEV)

        @pl.loop(0, C // 256)
        def _(n):
            c0 = pl.multiple_of(n * 256, 256)
            y0 = dot(hot[slots, :], rows_ref[:, pl.ds(c0, 256)]).reshape(HALF_DEV, CAP, 256)
            y1 = dot(hot[slots, :], rows_ref[:, pl.ds(c0 + C, 256)]).reshape(HALF_DEV, CAP, 256)
            buf[dests, :, pl.ds(c0, 256)] = jnp.concatenate([y0, y1], axis=1).astype(BF)

    def send_rows(buf, got, sems, part):
        for q in others:
            if q // HALF_DEV == part:
                pltpu.make_async_remote_copy(
                    src_ref=buf.at[q], dst_ref=got.at[me],
                    send_sem=sems.at[0], recv_sem=sems.at[1],
                    device_id=device(q), device_id_type=pl.DeviceIdType.MESH,
                ).start()

    def keep_own(buf, got):
        got[pl.ds(me, 1)] = buf[OWN : OWN + 1]

    def wait_rows(buf, sem):
        part = buf.at[pl.ds(0, N_DEV - 1)]
        pltpu.make_async_copy(part, part, sem).wait()

    ld_tiles.wait()
    for k in range(SLOTS):
        high, low = tiles[k, TH - HALO : TH].reshape(RIM, C), tiles[k, 0:HALO].reshape(RIM, C)
        rimf[enc, k] = jnp.where(lower(k) == 0, high, low)
    pl.semaphore_wait(barrier, N_DEV - 1)
    for q in others:
        e, s = device(q)
        pltpu.make_async_remote_copy(
            src_ref=msg.at[e * N_SEQ + s], dst_ref=rmsg.at[me],
            send_sem=msem.at[0], recv_sem=msem.at[1],
            device_id=(e, s), device_id_type=pl.DeviceIdType.MESH,
        ).start()
    f_send, f_got = rim_copies(rimf, fsend, frecv)
    for n in range(3):
        f_send[n].start()
    owner[...] = owner_of_row()

    def tile_cells(k, cols):
        return tiles[k, :, :, cols].reshape(CELLS, 256)

    def grad_cells(k, cols):
        return mg[k, :, cols]

    ld_grads.wait()
    wait_rows(rmsg, msem.at[1])

    asked = rmsg[...].reshape(N_DEV, 128)
    asked_t = jnp.transpose(asked)[0:CAP, :].astype(BF)
    asked = asked.astype(BF)

    shape = (SLOT_ROWS, 128)
    rows = dot(jnp.where(iota(shape, 1) == owner[...], 1.0, 0.0).astype(BF), asked)
    want = jnp.sum(jnp.where(iota(shape, 1) == iota(shape, 0) % CAP, rows, 0.0), axis=1, keepdims=True).astype(I32)
    hot[...] = jnp.where(iota((SLOT_ROWS, ROWS), 1) == want - 1, 1.0, 0.0).astype(BF)
    for part in range(2):
        fill_rows(gsend, grads, part)
        send_rows(gsend, grecv, gsem, part)
        if part == 0:
            f_got[0].wait()
            f_send[3].start()
            f_send[5].start()
            f_got[1].wait()
            f_send[4].start()
            f_send[6].start()
    keep_own(gsend, grecv)

    mixb[...] = mixb_ref[...].reshape(1, C)
    downb[...] = downb_ref[...].reshape(1, C2)

    def cell_of(m):
        return ((m % 128) // 16 * 2 + m // 256) * GW + m % 16 * 2 + m // 128 % 2

    p0, p1 = iota((CELLS, CELLS), 0), iota((CELLS, CELLS), 1)
    to_patch[...] = jnp.where(p1 == cell_of(p0), 1.0, 0.0).astype(BF)
    to_cell[...] = jnp.where(p0 == cell_of(p1), 1.0, 0.0).astype(BF)

    taps[...] = jnp.zeros((TAPS, C), F32)
    for a in range(KS):
        taps[8 * a : 8 * a + KS, :] = mixk_ref[a].astype(F32)
    flat_taps = taps[...].astype(BF)
    wave[...] = dot(tap_high[...], flat_taps) + dot(tap_low[...], flat_taps)

    ld_consts[0].wait()
    spectrum(to_f[...], tile_cells)
    f_got[3].wait()
    f_got[4].wait()
    f_send[7].start()
    for n in (2, 5, 6, 7):
        f_got[n].wait()
    place_rims(rimf)
    ld_consts[1].wait()
    ld_consts[2].wait()

    def store_mixed(k, cols, cells):
        mixed = (cells + mixb[:, cols]).astype(BF)
        A[:, pl.ds(pl.multiple_of(k * 128, 128), 128), cols] = mixed.reshape(4, 128, 256)

    depthwise(rim_f, from_f, 1.0, to_patch, tile_cells, store_mixed)
    ld_w.wait()

    @pl.loop(0, C2 // 256)
    def _(n):
        cols = pl.ds(pl.multiple_of(n * 256, 256), 256)
        pre = jnp.zeros((ROWS, 256), F32) + downb[:, cols]
        for j in range(4):
            pre = pre + dot(A[j], w[j * C : (j + 1) * C, cols])
        phi = 0.5 * (1.0 + lax.erf(pre * SQRT_HALF))
        tok[:, cols] = (pre * phi).astype(BF)
        slope[:, cols] = phi + pre * INV_ROOT * jnp.exp(-0.5 * pre * pre)

    at = owner[...] * CAP + iota((SLOT_ROWS, 1), 0) % CAP
    hot[...] = jnp.where(at == slot_row, 1.0, 0.0).astype(BF)
    fill_rows(tsend, tok, 0)
    send_rows(tsend, trecv, tsem, 0)
    fill_rows(tsend, tok, 1)
    keep_own(tsend, trecv)

    back_at = ocol * (2 * CAP) + rank_col
    for h in range(2):
        sel[h] = jnp.where(iota((ROWS, 2 * CAP * N_DEV), 1) == back_at + h * CAP, 1.0, 0.0).astype(BF)
    wait_rows(grecv, gsem.at[1])

    def picked(got, h, c0):
        part = got[:, :, pl.ds(pl.multiple_of(c0, 256), 256)].reshape(2 * CAP * N_DEV, 256)
        return dot(sel[h], part)

    @pl.loop(0, C2 // 256)
    def _(n):
        h = n // 3
        cols = pl.ds(pl.multiple_of(n * 256, 256), 256)
        pg[:, cols] = (picked(grecv, h, (n - 3 * h) * 256) * slope[:, cols]).astype(BF)

    @pl.loop(0, 4 * (C // 256))
    def _(m):
        j, n = m // 3, lax.rem(m, 3)
        part = w[pl.ds(pl.multiple_of(m * 256, 256), 256), :]
        g = lax.dot_general(pg[...], part, (((1,), (1,)), ((), ())), preferred_element_type=F32)
        mg[:, pl.ds(pl.multiple_of(j * 128, 128), 128), columns(n)] = g.astype(BF).reshape(SLOTS, 128, 256)

    def rim_rows(k, rows):
        at = [((r % 2) * 2 + dx) * 128 + (r // 2) * 16 for r in rows for dx in range(2)]
        return jnp.concatenate([mg[k, a : a + 16, :] for a in at], axis=0)

    for k in range(SLOTS):
        rimb[enc, k] = jnp.where(lower(k) == 0, rim_rows(k, range(TH - HALO, TH)), rim_rows(k, range(HALO)))
    b_send, b_got = rim_copies(rimb, bsend, brecv)
    for n in range(3):
        b_send[n].start()
    ld_consts[3].wait()
    spectrum(to_b[...], grad_cells)
    b_got[0].wait()
    b_send[3].start()
    b_send[5].start()
    b_got[1].wait()
    b_send[4].start()
    b_send[6].start()
    send_rows(tsend, trecv, tsem, 1)
    b_got[3].wait()
    b_got[4].wait()
    b_send[7].start()
    for n in (2, 5, 6, 7):
        b_got[n].wait()
    place_rims(rimb)
    ld_consts[4].wait()
    ld_consts[5].wait()

    def store_grad(k, cols, cells):
        gout_ref[k, :, :, cols] = cells.astype(BF).reshape(TH, GW, 256)

    depthwise(rim_b, from_b, -1.0, to_cell, grad_cells, store_grad)

    for g in range(N_DEV // N_SEQ):
        shape = (N_DEV, 256)
        at1 = iota(shape, 1)
        over = jnp.where(iota(shape, 0) == g * N_SEQ + at1 // (2 * CAP), 1.0, 0.0).astype(BF)
        rows = dot(asked_t, over)
        k8 = iota((CAP, 256), 1)
        put = jnp.sum(jnp.where(iota((CAP, 256), 0) == k8 % CAP, rows, 0.0), axis=0, keepdims=True).astype(I32)
        hit = iota((ROWS, 256), 0) == put - 1
        part = (iota((ROWS, 256), 1) // CAP) % 2
        for h in range(2):
            sel[h, :, g * 256 : (g + 1) * 256] = jnp.where(hit & (part == h), 1.0, 0.0).astype(BF)
    wait_rows(trecv, tsem.at[1])

    @pl.loop(0, C2 // 256)
    def _(n):
        h = n // 3
        cols = pl.ds(pl.multiple_of(n * 256, 256), 256)
        llm_ref[:, cols] = picked(trecv, h, (n - 3 * h) * 256).astype(BF)

    for n in range(8):
        f_send[n].wait_send()
        b_send[n].wait_send()
    wait_rows(msg, msem.at[0])
    wait_rows(gsend, gsem.at[0])
    wait_rows(tsend, tsem.at[0])


def hand_over(llm_ref, gout_ref, llm_out, gout_out, sems):
    copies = [
        pltpu.make_async_copy(llm_ref.at[pl.ds(n * 64, 64)], llm_out.at[pl.ds(n * 64, 64)], sems.at[n]) for n in range(4)
    ] + [
        pltpu.make_async_copy(
            gout_ref.at[n // 4, pl.ds(n % 4 * 4, 4)], gout_out.at[n // 4, pl.ds(n % 4 * 4, 4)], sems.at[4 + n]
        )
        for n in range(8)
    ]
    for copy in copies:
        copy.start()
    for copy in copies:
        copy.wait()


def on_device(frame_tiles, tile_ids, partner_slot, mix_kernel, mix_bias, down_weight, down_bias, token_pos, grad_rows):
    vmem = pl.BlockSpec(memory_space=pltpu.VMEM)
    smem = pl.BlockSpec(memory_space=pltpu.SMEM)
    anyw = pl.BlockSpec(memory_space=pl.ANY)
    dma = pltpu.SemaphoreType.DMA
    llm, gout = pl.pallas_call(
        kernel,
        out_shape=(
            jax.ShapeDtypeStruct((ROWS, C2), BF),
            jax.ShapeDtypeStruct((SLOTS, TH, GW, C), BF),
        ),
        in_specs=[anyw, smem, smem, vmem, vmem, anyw, vmem, vmem, anyw] + [anyw] * 6 + [vmem] * 2,
        out_specs=(vmem, vmem),
        scratch_shapes=[
            pltpu.VMEM((ALL_F, CELLS), BF),
            pltpu.VMEM((ALL_F, CELLS), BF),
            pltpu.VMEM((ALL_F, 2 * RIM), BF),
            pltpu.VMEM((ALL_F, 2 * RIM), BF),
            pltpu.VMEM((CELLS, ALL_F), BF),
            pltpu.VMEM((CELLS, ALL_F), BF),
            pltpu.VMEM((TAPS, C), F32),
            pltpu.VMEM((ALL_F, C), F32),
            pltpu.VMEM((SLOTS, ALL_F, C), F32),
            pltpu.VMEM((SLOTS, 2 * RIM, C), BF),
            pltpu.VMEM((SLOTS, CELLS, C), BF),
            pltpu.VMEM((CELLS, CELLS), BF),
            pltpu.VMEM((CELLS, CELLS), BF),
            pltpu.VMEM((SLOTS, TH, GW, C), BF),
            pltpu.VMEM((4 * C, C2), BF),
            pltpu.VMEM((ROWS, C2), BF),
            pltpu.VMEM((1, C), F32),
            pltpu.VMEM((1, C2), F32),
            pltpu.VMEM((4, ROWS, C), BF),
            pltpu.VMEM((ROWS, C2), F32),
            pltpu.VMEM((ROWS, C2), BF),
            pltpu.VMEM((ROWS, C2), BF),
            pltpu.VMEM((2, ROWS, 2 * CAP * N_DEV), BF),
            pltpu.VMEM((SLOT_ROWS, ROWS), BF),
            pltpu.VMEM((SLOT_ROWS, 1), I32),
            pltpu.VMEM((N_DEV, 1, 128), F32),
            pltpu.VMEM((N_DEV, 1, 128), F32),
            pltpu.VMEM((N_DEV, 2 * CAP, C), BF),
            pltpu.VMEM((N_DEV, 2 * CAP, C), BF),
            pltpu.VMEM((N_DEV, 2 * CAP, C), BF),
            pltpu.VMEM((N_DEV, 2 * CAP, C), BF),
            pltpu.VMEM((N_ENC, SLOTS, RIM, C), BF),
            pltpu.VMEM((N_ENC, SLOTS, RIM, C), BF),
            dma((9,)),
            dma((2,)),
            dma((2,)),
            dma((2,)),
            dma((8,)),
            dma((8,)),
            dma((8,)),
            dma((8,)),
        ],
        compiler_params=pltpu.CompilerParams(
            collective_id=0, has_side_effects=True, vmem_limit_bytes=62 * 1024 * 1024
        ),
    )(
        frame_tiles,
        tile_ids,
        partner_slot,
        mix_kernel,
        mix_bias,
        down_weight,
        down_bias,
        token_pos,
        grad_rows,
        *transforms(),
    )
    llm, gout = pl.pallas_call(
        hand_over,
        out_shape=(
            jax.ShapeDtypeStruct((ROWS, C2), BF),
            jax.ShapeDtypeStruct((SLOTS, TH, GW, C), BF),
        ),
        in_specs=[anyw, anyw],
        out_specs=(anyw, anyw),
        scratch_shapes=[dma((12,))],
    )(llm, gout)
    return llm, gout[None, None]


def solution(mesh):
    return jax.shard_map(
        on_device,
        mesh=mesh,
        in_specs=(
            P("enc", "seq", None, None, None, None),
            P("enc", "seq", None),
            P("enc", "seq", None),
            P(),
            P(),
            P(),
            P(),
            P("enc", "seq", None, None),
            P(("enc", "seq"), None),
        ),
        out_specs=(P(("enc", "seq"), None), P("enc", "seq", None, None, None, None)),
        check_vma=False,
    )
```

```python
import functools

import itertools

import jax
import jax.numpy as jnp
import numpy as np
from jax import lax
from jax.experimental import pallas as pl
from jax.experimental.pallas import tpu as pltpu
from jax.sharding import PartitionSpec as P

C = 768
C2 = 1536
KS = 7
TH = 16
GW = 32
SLOTS = 2
ROWS = 256
N_ENC = 8
N_SEQ = 16
N_DEV = 128
CAP = 8
SLOT_ROWS = CAP * N_DEV

def orbit(o):
    turned = [o, o[2:] + o[:2], o[1:] + o[:1]]
    return [p for q in turned for p in (q, tuple(-d % 4 for d in q))]


ALL_OFFSETS = sorted(itertools.product((0, 1, 3, 2), repeat=3), key=lambda o: -sum(min(d, 4 - d) for d in o))
ORDERED = list(dict.fromkeys(p for o in ALL_OFFSETS for p in orbit(o)))


def relayed(off, f):
    return 2 in off


def first_leg(off, f):
    return tuple(way if d == 2 else 0 for d, way in zip(off, (1 + 2 * f, 3 - 2 * f, 1 + 2 * f)))


PLACES = [(o, f) for o in ORDERED for f in (0, 1) if any(o)] + [((0, 0, 0), 1), ((0, 0, 0), 0)]
DESTS = [p for p in PLACES if relayed(*p)] + [p for p in PLACES if not relayed(*p)]
N_FAR = sum(relayed(*p) for p in PLACES)
OWN = N_DEV - 1
HALF_DEV = N_DEV // 2


def packed(values):
    words = []
    for n in range(0, N_DEV, 16):
        word = sum(v << (2 * i) for i, v in enumerate(values[n : n + 16]))
        words.append(word - (1 << 32) if word >> 31 else word)
    return words


WORDS = [packed([o[axis] for o, f in DESTS]) for axis in range(3)] + [packed([f for o, f in DESTS])]
HALO = 3
CELLS = TH * GW
RIM = HALO * GW
FR, FC = TH + 2 * HALO, GW + HALO
N_FREQ = FR * (FC // 2 + 1)
HALF_F = 400
ALL_F = 2 * HALF_F
TAPS = 8 * KS
SQRT_HALF = 0.7071067811865476
INV_ROOT = 0.3989422804014327
BF = jnp.bfloat16
F32 = jnp.float32
I32 = jnp.int32


def transforms():
    kr, kc = [v.reshape(-1, 1) for v in np.meshgrid(np.arange(FR), np.arange(FC // 2 + 1), indexing="ij")]

    def wave(r, c):
        return np.exp(2j * np.pi * (kr * r / FR + kc * c / FC))

    def rows_of(z):
        out = np.zeros((ALL_F, z.shape[1]))
        out[:N_FREQ], out[HALF_F : HALF_F + N_FREQ] = z.real, z.imag
        return out

    r, c = [v.ravel() for v in np.meshgrid(np.arange(TH), np.arange(GW), indexing="ij")]
    by_patch = np.argsort(((r % 2) * 2 + c % 2) * 128 + (r // 2) * 16 + c // 2)
    rr, rc = [v.ravel() for v in np.meshgrid(np.arange(HALO), np.arange(GW), indexing="ij")]
    rim_patch = np.argsort(rr * GW + (rc % 2) * 16 + rc // 2)
    there = rows_of(np.conj(wave(r, c)))
    rims = [rows_of(np.conj(wave(rr + at, rc))) for at in (-HALO, TH)]
    rim_cells = np.concatenate(rims, axis=1)
    rim_patches = np.concatenate([m[:, rim_patch] for m in rims], axis=1)
    share = np.where(kc == 0, 1.0, 2.0) / (FR * FC)
    back = wave(r, c) * share
    back = (rows_of(np.conj(back))).T
    a, b = np.arange(TAPS) // 8, np.arange(TAPS) % 8
    taps = rows_of(wave(a - HALO, b - HALO) * (b < KS))
    high = taps.astype(BF)
    low = (taps - high.astype(np.float64)).astype(BF)
    return [
        m.astype(BF)
        for m in (there, there[:, by_patch], rim_cells, rim_patches, back[by_patch], back, high, low)
    ]


def iota(shape, axis):
    return lax.broadcasted_iota(I32, shape, axis)


def dot(a, b):
    return jnp.dot(a, b, preferred_element_type=F32)


def kernel(
    tiles_hbm, ids_ref, partner_ref, mixk_ref, mixb_ref, w_hbm, downb_ref, pos_ref, grad_hbm,
    to_f_hbm, to_b_hbm, rim_f_hbm, rim_b_hbm, from_f_hbm, from_b_hbm, tap_high, tap_low,
    llm_ref, gout_ref,
    to_f, to_b, rim_f, rim_b, from_f, from_b, taps, wave, field, edge, mg, to_patch, to_cell,
    tiles, w, grads, mixb, downb, A, slope, tok, pg, sel, hot, owner,
    msg, rmsg, gsend, grecv, grel, tsend, trecv, trel, rimf, rimb,
    lsem, msem, gsem, tsem, fsend, frecv, bsend, brecv,
):
    enc = lax.axis_index("enc")
    seq = lax.axis_index("seq")
    me = enc * N_SEQ + seq
    cy, core = enc // 2, enc % 2

    ld_tiles = pltpu.make_async_copy(tiles_hbm.at[0, 0], tiles, lsem.at[0])
    ld_grads = pltpu.make_async_copy(grad_hbm, grads, lsem.at[1])
    ld_w = pltpu.make_async_copy(w_hbm, w, lsem.at[2])
    ld_tiles.start()
    ld_grads.start()
    ld_consts = [
        pltpu.make_async_copy(src, dst, lsem.at[3 + n])
        for n, (src, dst) in enumerate(
            ((to_f_hbm, to_f), (rim_f_hbm, rim_f), (from_f_hbm, from_f), (to_b_hbm, to_b), (rim_b_hbm, rim_b), (from_b_hbm, from_b))
        )
    ]
    for n in range(3):
        ld_consts[n].start()
    ld_w.start()
    for n in range(3, 6):
        ld_consts[n].start()

    cx, cz = seq >> 2, seq & 3
    at_x = [((cx + d) & 3) * 4 for d in range(4)]
    at_y = [((cy + d) & 3) * 2 for d in range(4)]
    at_z = [(cz + d) & 3 for d in range(4)]
    at_core = [core, 1 - core]

    def device(off, f):
        dx, dy, dz = off
        return at_y[dy] + at_core[f], at_x[dx] + at_z[dz]

    others = range(OWN)
    barrier = pltpu.get_barrier_semaphore()
    for q in others:
        pl.semaphore_signal(barrier, inc=1, device_id=device(*DESTS[q]), device_id_type=pl.DeviceIdType.MESH)


    pos = pos_ref[0, 0]
    prow = jnp.concatenate([pos[0:1, :], pos[1:2, :]], axis=1)
    pcol = jnp.concatenate(
        [jnp.transpose(jnp.broadcast_to(pos[i : i + 1, :].astype(F32), (128, 128))) for i in range(2)], axis=0
    ).astype(I32)[:, 0:1]
    orow, ocol = prow // ROWS, pcol // ROWS
    lcol = pcol - ocol * ROWS
    same = jnp.broadcast_to(ocol, (ROWS, ROWS)) == jnp.broadcast_to(orow, (ROWS, ROWS))
    at0, at1 = iota((ROWS, ROWS), 0), iota((ROWS, ROWS), 1)
    rank_row = jnp.sum(jnp.where(same & (at0 < at1), 1.0, 0.0), axis=0, keepdims=True).astype(I32)
    rank_col = jnp.sum(jnp.where(same & (at1 < at0), 1.0, 0.0), axis=1, keepdims=True).astype(I32)
    slot_row = orow * CAP + rank_row
    to_owner = jnp.where(iota((N_DEV, ROWS), 0) == orow, 1.0, 0.0).astype(BF)
    ranked = jnp.where(iota((ROWS, 128), 1) == rank_col, (lcol + 1).astype(F32), 0.0).astype(BF)
    msg[...] = dot(to_owner, ranked).reshape(N_DEV, 1, 128)
    rmsg[pl.ds(me, 1)] = msg[pl.ds(me, 1)]

    def lower(k):
        return lax.rem(ids_ref[0, 0, k], 2)

    up = lax.rem(cy + 1, 4) * 2 + core
    down = lax.rem(cy + 3, 4) * 2 + core
    across = lax.rem(cy + 2, 4) * 2 + core
    sib = cy * 2 + 1 - core

    def rim_copies(rims, ssem, rsem):
        def copy(n, ref, to):
            return pltpu.make_async_remote_copy(
                src_ref=ref, dst_ref=ref, send_sem=ssem.at[n], recv_sem=rsem.at[n],
                device_id=(to, seq), device_id_type=pl.DeviceIdType.MESH,
            )

        def landed(n, ref):
            return pltpu.make_async_copy(ref, ref, rsem.at[n])

        sends = [
            copy(0, rims.at[enc], up),
            copy(1, rims.at[enc], down),
            copy(2, rims.at[enc], sib),
            copy(3, rims.at[down, 0], up),
            copy(4, rims.at[up, 1], down),
            copy(5, rims.at[down], sib),
            copy(6, rims.at[up], sib),
            copy(7, rims.at[across], sib),
        ]
        other = 1 - 2 * core
        arrivals = [
            landed(0, rims.at[down]),
            landed(1, rims.at[up]),
            landed(2, rims.at[sib]),
            landed(3, rims.at[across, 0]),
            landed(4, rims.at[across, 1]),
            landed(5, rims.at[down + other]),
            landed(6, rims.at[up + other]),
            landed(7, rims.at[across + other]),
        ]
        return sends, arrivals

    def place_rims(rims):
        for k in range(SLOTS):
            want = partner_ref[0, 0, k]
            rim = jnp.zeros((RIM, C), BF)
            for q in range(N_ENC * SLOTS):
                rim = jnp.where(want == q, rims[q // 2, q % 2], rim)
            none = jnp.zeros((RIM, C), BF)
            below = lower(k) == 1
            edge[k, 0:RIM, :] = jnp.where(below, rim, none)
            edge[k, RIM : 2 * RIM, :] = jnp.where(below, none, rim)

    def columns(n):
        return pl.ds(pl.multiple_of(n * 256, 256), 256)

    def spectrum(there, cells):
        @pl.loop(0, SLOTS * 3)
        def _(i):
            k, cols = i // 3, columns(lax.rem(i, 3))
            field[k, :, cols] = dot(there, cells(k, cols))

    def depthwise(there, back, way, turn, cells, store):
        @pl.loop(0, SLOTS * 3)
        def _(i):
            k, cols = i // 3, columns(lax.rem(i, 3))
            z = field[k, :, cols] + dot(there[...], edge[k, :, cols])
            re, im = z[0:HALF_F], z[HALF_F:ALL_F]
            wr, wi = wave[0:HALF_F, cols], way * wave[HALF_F:ALL_F, cols]
            product = jnp.concatenate([re * wr - im * wi, re * wi + im * wr], axis=0).astype(BF)
            store(k, cols, dot(turn[...], cells(k, cols)) + dot(back[...], product))

    def owner_of_row():
        place = iota((SLOT_ROWS, 1), 0) // CAP
        block, shift = place // 16, 2 * (place % 16)
        d = []
        for words in WORDS:
            word = jnp.full(place.shape, words[0])
            for n in range(1, 8):
                word = jnp.where(block == n, words[n], word)
            d.append(jnp.right_shift(word, shift) & 3)
        c = core + d[3] - 2 * core * d[3]
        return (((cy + d[1]) & 3) * 2 + c) * N_SEQ + ((cx + d[0]) & 3) * 4 + ((cz + d[2]) & 3)

    def fill_rows(buf, rows_ref, part):
        slots = slice(part * SLOT_ROWS // 2, (part + 1) * SLOT_ROWS // 2)
        dests = slice(part * HALF_DEV, (part + 1) * HALF_DEV)

        @pl.loop(0, C // 256)
        def _(n):
            c0 = pl.multiple_of(n * 256, 256)
            y0 = dot(hot[slots, :], rows_ref[:, pl.ds(c0, 256)]).reshape(HALF_DEV, CAP, 256)
            y1 = dot(hot[slots, :], rows_ref[:, pl.ds(c0 + C, 256)]).reshape(HALF_DEV, CAP, 256)
            buf[dests, :, pl.ds(c0, 256)] = jnp.concatenate([y0, y1], axis=1).astype(BF)

    def send_rows(buf, rel, got, sems, part):
        for q in others:
            if q // HALF_DEV == part:
                off, f = DESTS[q]
                far = q < N_FAR
                pltpu.make_async_remote_copy(
                    src_ref=buf.at[q], dst_ref=rel.at[q] if far else got.at[me],
                    send_sem=sems.at[0], recv_sem=sems.at[2 if far else 1],
                    device_id=device(first_leg(off, f), 0) if far else device(off, f),
                    device_id_type=pl.DeviceIdType.MESH,
                ).start()

    def forward(rel, got, sems):
        part = rel.at[pl.ds(0, N_FAR)]
        pltpu.make_async_copy(part, part, sems.at[2]).wait()
        for q in range(N_FAR):
            off, f = DESTS[q]
            leg = first_leg(off, f)
            e0, s0 = device([-d % 4 for d in leg], 0)
            pltpu.make_async_remote_copy(
                src_ref=rel.at[q], dst_ref=got.at[e0 * N_SEQ + s0],
                send_sem=sems.at[3], recv_sem=sems.at[1],
                device_id=device([(o - d) % 4 for o, d in zip(off, leg)], f), device_id_type=pl.DeviceIdType.MESH,
            ).start()

    def keep_own(buf, got):
        got[pl.ds(me, 1)] = buf[OWN : OWN + 1]

    def wait_rows(buf, sem):
        part = buf.at[pl.ds(0, N_DEV - 1)]
        pltpu.make_async_copy(part, part, sem).wait()

    ld_tiles.wait()
    for k in range(SLOTS):
        high, low = tiles[k, TH - HALO : TH].reshape(RIM, C), tiles[k, 0:HALO].reshape(RIM, C)
        rimf[enc, k] = jnp.where(lower(k) == 0, high, low)
    pl.semaphore_wait(barrier, N_DEV - 1)
    for q in others:
        e, s = device(*DESTS[q])
        pltpu.make_async_remote_copy(
            src_ref=msg.at[e * N_SEQ + s], dst_ref=rmsg.at[me],
            send_sem=msem.at[0], recv_sem=msem.at[1],
            device_id=(e, s), device_id_type=pl.DeviceIdType.MESH,
        ).start()
    f_send, f_got = rim_copies(rimf, fsend, frecv)
    for n in range(3):
        f_send[n].start()
    owner[...] = owner_of_row()

    def tile_cells(k, cols):
        return tiles[k, :, :, cols].reshape(CELLS, 256)

    def grad_cells(k, cols):
        return mg[k, :, cols]

    ld_grads.wait()
    wait_rows(rmsg, msem.at[1])

    asked = rmsg[...].reshape(N_DEV, 128)
    asked_t = jnp.transpose(asked)[0:CAP, :].astype(BF)
    asked = asked.astype(BF)

    shape = (SLOT_ROWS, 128)
    rows = dot(jnp.where(iota(shape, 1) == owner[...], 1.0, 0.0).astype(BF), asked)
    want = jnp.sum(jnp.where(iota(shape, 1) == iota(shape, 0) % CAP, rows, 0.0), axis=1, keepdims=True).astype(I32)
    hot[...] = jnp.where(iota((SLOT_ROWS, ROWS), 1) == want - 1, 1.0, 0.0).astype(BF)
    for part in range(2):
        fill_rows(gsend, grads, part)
        send_rows(gsend, grel, grecv, gsem, part)
        if part == 0:
            f_got[0].wait()
            f_send[3].start()
            f_send[5].start()
            f_got[1].wait()
            f_send[4].start()
            f_send[6].start()
    keep_own(gsend, grecv)

    mixb[...] = mixb_ref[...].reshape(1, C)
    downb[...] = downb_ref[...].reshape(1, C2)

    def cell_of(m):
        return ((m % 128) // 16 * 2 + m // 256) * GW + m % 16 * 2 + m // 128 % 2

    p0, p1 = iota((CELLS, CELLS), 0), iota((CELLS, CELLS), 1)
    to_patch[...] = jnp.where(p1 == cell_of(p0), 1.0, 0.0).astype(BF)
    to_cell[...] = jnp.where(p0 == cell_of(p1), 1.0, 0.0).astype(BF)

    taps[...] = jnp.zeros((TAPS, C), F32)
    for a in range(KS):
        taps[8 * a : 8 * a + KS, :] = mixk_ref[a].astype(F32)
    flat_taps = taps[...].astype(BF)
    wave[...] = dot(tap_high[...], flat_taps) + dot(tap_low[...], flat_taps)

    ld_consts[0].wait()
    spectrum(to_f[...], tile_cells)
    f_got[3].wait()
    f_got[4].wait()
    f_send[7].start()
    for n in (2, 5, 6, 7):
        f_got[n].wait()
    place_rims(rimf)
    ld_consts[1].wait()
    ld_consts[2].wait()

    def store_mixed(k, cols, cells):
        mixed = (cells + mixb[:, cols]).astype(BF)
        A[:, pl.ds(pl.multiple_of(k * 128, 128), 128), cols] = mixed.reshape(4, 128, 256)

    depthwise(rim_f, from_f, 1.0, to_patch, tile_cells, store_mixed)
    forward(grel, grecv, gsem)
    ld_w.wait()

    @pl.loop(0, C2 // 256)
    def _(n):
        cols = pl.ds(pl.multiple_of(n * 256, 256), 256)
        pre = jnp.zeros((ROWS, 256), F32) + downb[:, cols]
        for j in range(4):
            pre = pre + dot(A[j], w[j * C : (j + 1) * C, cols])
        phi = 0.5 * (1.0 + lax.erf(pre * SQRT_HALF))
        tok[:, cols] = (pre * phi).astype(BF)
        slope[:, cols] = phi + pre * INV_ROOT * jnp.exp(-0.5 * pre * pre)

    at = owner[...] * CAP + iota((SLOT_ROWS, 1), 0) % CAP
    hot[...] = jnp.where(at == slot_row, 1.0, 0.0).astype(BF)
    for part in range(2):
        fill_rows(tsend, tok, part)
        send_rows(tsend, trel, trecv, tsem, part)
    keep_own(tsend, trecv)

    back_at = ocol * (2 * CAP) + rank_col
    for h in range(2):
        sel[h] = jnp.where(iota((ROWS, 2 * CAP * N_DEV), 1) == back_at + h * CAP, 1.0, 0.0).astype(BF)
    wait_rows(grecv, gsem.at[1])

    def picked(got, h, c0):
        part = got[:, :, pl.ds(pl.multiple_of(c0, 256), 256)].reshape(2 * CAP * N_DEV, 256)
        return dot(sel[h], part)

    @pl.loop(0, C2 // 256)
    def _(n):
        h = n // 3
        cols = pl.ds(pl.multiple_of(n * 256, 256), 256)
        pg[:, cols] = (picked(grecv, h, (n - 3 * h) * 256) * slope[:, cols]).astype(BF)

    @pl.loop(0, 4 * (C // 256))
    def _(m):
        j, n = m // 3, lax.rem(m, 3)
        part = w[pl.ds(pl.multiple_of(m * 256, 256), 256), :]
        g = lax.dot_general(pg[...], part, (((1,), (1,)), ((), ())), preferred_element_type=F32)
        mg[:, pl.ds(pl.multiple_of(j * 128, 128), 128), columns(n)] = g.astype(BF).reshape(SLOTS, 128, 256)

    def rim_rows(k, rows):
        at = [((r % 2) * 2 + dx) * 128 + (r // 2) * 16 for r in rows for dx in range(2)]
        return jnp.concatenate([mg[k, a : a + 16, :] for a in at], axis=0)

    for k in range(SLOTS):
        rimb[enc, k] = jnp.where(lower(k) == 0, rim_rows(k, range(TH - HALO, TH)), rim_rows(k, range(HALO)))
    b_send, b_got = rim_copies(rimb, bsend, brecv)
    for n in range(3):
        b_send[n].start()
    ld_consts[3].wait()
    spectrum(to_b[...], grad_cells)
    b_got[0].wait()
    b_send[3].start()
    b_send[5].start()
    b_got[1].wait()
    b_send[4].start()
    b_send[6].start()
    forward(trel, trecv, tsem)
    b_got[3].wait()
    b_got[4].wait()
    b_send[7].start()
    for n in (2, 5, 6, 7):
        b_got[n].wait()
    place_rims(rimb)
    ld_consts[4].wait()
    ld_consts[5].wait()

    def store_grad(k, cols, cells):
        gout_ref[k, :, :, cols] = cells.astype(BF).reshape(TH, GW, 256)

    depthwise(rim_b, from_b, -1.0, to_cell, grad_cells, store_grad)

    for g in range(N_DEV // N_SEQ):
        shape = (N_DEV, 256)
        at1 = iota(shape, 1)
        over = jnp.where(iota(shape, 0) == g * N_SEQ + at1 // (2 * CAP), 1.0, 0.0).astype(BF)
        rows = dot(asked_t, over)
        k8 = iota((CAP, 256), 1)
        put = jnp.sum(jnp.where(iota((CAP, 256), 0) == k8 % CAP, rows, 0.0), axis=0, keepdims=True).astype(I32)
        hit = iota((ROWS, 256), 0) == put - 1
        part = (iota((ROWS, 256), 1) // CAP) % 2
        for h in range(2):
            sel[h, :, g * 256 : (g + 1) * 256] = jnp.where(hit & (part == h), 1.0, 0.0).astype(BF)
    wait_rows(trecv, tsem.at[1])

    @pl.loop(0, C2 // 256)
    def _(n):
        h = n // 3
        cols = pl.ds(pl.multiple_of(n * 256, 256), 256)
        llm_ref[:, cols] = picked(trecv, h, (n - 3 * h) * 256).astype(BF)

    for n in range(8):
        f_send[n].wait_send()
        b_send[n].wait_send()
    wait_rows(msg, msem.at[0])
    for buf, rel, sems in ((gsend, grel, gsem), (tsend, trel, tsem)):
        wait_rows(buf, sems.at[0])
        part = rel.at[pl.ds(0, N_FAR)]
        pltpu.make_async_copy(part, part, sems.at[3]).wait()


def hand_over(llm_ref, gout_ref, llm_out, gout_out):
    llm_out[...] = llm_ref[...]
    gout_out[...] = gout_ref[...]


def on_device(frame_tiles, tile_ids, partner_slot, mix_kernel, mix_bias, down_weight, down_bias, token_pos, grad_rows):
    vmem = pl.BlockSpec(memory_space=pltpu.VMEM)
    smem = pl.BlockSpec(memory_space=pltpu.SMEM)
    anyw = pl.BlockSpec(memory_space=pl.ANY)
    dma = pltpu.SemaphoreType.DMA
    llm, gout = pl.pallas_call(
        kernel,
        out_shape=(
            jax.ShapeDtypeStruct((ROWS, C2), BF),
            jax.ShapeDtypeStruct((SLOTS, TH, GW, C), BF),
        ),
        in_specs=[anyw, smem, smem, vmem, vmem, anyw, vmem, vmem, anyw] + [anyw] * 6 + [vmem] * 2,
        out_specs=(vmem, vmem),
        scratch_shapes=[
            pltpu.VMEM((ALL_F, CELLS), BF),
            pltpu.VMEM((ALL_F, CELLS), BF),
            pltpu.VMEM((ALL_F, 2 * RIM), BF),
            pltpu.VMEM((ALL_F, 2 * RIM), BF),
            pltpu.VMEM((CELLS, ALL_F), BF),
            pltpu.VMEM((CELLS, ALL_F), BF),
            pltpu.VMEM((TAPS, C), F32),
            pltpu.VMEM((ALL_F, C), F32),
            pltpu.VMEM((SLOTS, ALL_F, C), F32),
            pltpu.VMEM((SLOTS, 2 * RIM, C), BF),
            pltpu.VMEM((SLOTS, CELLS, C), BF),
            pltpu.VMEM((CELLS, CELLS), BF),
            pltpu.VMEM((CELLS, CELLS), BF),
            pltpu.VMEM((SLOTS, TH, GW, C), BF),
            pltpu.VMEM((4 * C, C2), BF),
            pltpu.VMEM((ROWS, C2), BF),
            pltpu.VMEM((1, C), F32),
            pltpu.VMEM((1, C2), F32),
            pltpu.VMEM((4, ROWS, C), BF),
            pltpu.VMEM((ROWS, C2), F32),
            pltpu.VMEM((ROWS, C2), BF),
            pltpu.VMEM((ROWS, C2), BF),
            pltpu.VMEM((2, ROWS, 2 * CAP * N_DEV), BF),
            pltpu.VMEM((SLOT_ROWS, ROWS), BF),
            pltpu.VMEM((SLOT_ROWS, 1), I32),
            pltpu.VMEM((N_DEV, 1, 128), F32),
            pltpu.VMEM((N_DEV, 1, 128), F32),
            pltpu.VMEM((N_DEV, 2 * CAP, C), BF),
            pltpu.VMEM((N_DEV, 2 * CAP, C), BF),
            pltpu.VMEM((N_FAR, 2 * CAP, C), BF),
            pltpu.VMEM((N_DEV, 2 * CAP, C), BF),
            pltpu.VMEM((N_DEV, 2 * CAP, C), BF),
            pltpu.VMEM((N_FAR, 2 * CAP, C), BF),
            pltpu.VMEM((N_ENC, SLOTS, RIM, C), BF),
            pltpu.VMEM((N_ENC, SLOTS, RIM, C), BF),
            dma((9,)),
            dma((2,)),
            dma((4,)),
            dma((4,)),
            dma((8,)),
            dma((8,)),
            dma((8,)),
            dma((8,)),
        ],
        compiler_params=pltpu.CompilerParams(
            collective_id=0, has_side_effects=True, vmem_limit_bytes=62 * 1024 * 1024
        ),
    )(
        frame_tiles,
        tile_ids,
        partner_slot,
        mix_kernel,
        mix_bias,
        down_weight,
        down_bias,
        token_pos,
        grad_rows,
        *transforms(),
    )
    blocks = (
        pl.BlockSpec((ROWS // 4, C2), lambda n: (n, 0)),
        pl.BlockSpec((SLOTS, TH // 4, GW, C), lambda n: (0, n, 0, 0)),
    )
    llm, gout = pl.pallas_call(
        hand_over,
        out_shape=(
            jax.ShapeDtypeStruct((ROWS, C2), BF),
            jax.ShapeDtypeStruct((SLOTS, TH, GW, C), BF),
        ),
        grid=(4,),
        in_specs=list(blocks),
        out_specs=blocks,
    )(llm, gout)
    return llm, gout[None, None]


def solution(mesh):
    return jax.shard_map(
        on_device,
        mesh=mesh,
        in_specs=(
            P("enc", "seq", None, None, None, None),
            P("enc", "seq", None),
            P("enc", "seq", None),
            P(),
            P(),
            P(),
            P(),
            P("enc", "seq", None, None),
            P(("enc", "seq"), None),
        ),
        out_specs=(P(("enc", "seq"), None), P("enc", "seq", None, None, None, None)),
        check_vma=False,
    )
```

```python
import functools

import itertools

import jax
import jax.numpy as jnp
import numpy as np
from jax import lax
from jax.experimental import pallas as pl
from jax.experimental.pallas import tpu as pltpu
from jax.sharding import PartitionSpec as P

C = 768
C2 = 1536
KS = 7
TH = 16
GW = 32
SLOTS = 2
ROWS = 256
N_ENC = 8
N_SEQ = 16
N_DEV = 128
CAP = 8
SLOT_ROWS = CAP * N_DEV

def orbit(o):
    turned = [o, o[2:] + o[:2], o[1:] + o[:1]]
    return [p for q in turned for p in (q, tuple(-d % 4 for d in q))]


ALL_OFFSETS = sorted(itertools.product((0, 1, 3, 2), repeat=3), key=lambda o: -sum(min(d, 4 - d) for d in o))
ORDERED = list(dict.fromkeys(p for o in ALL_OFFSETS for p in orbit(o)))


def relayed(off, f):
    return 2 in off and f == 1


def first_leg(off, f):
    return tuple(3 if d == 2 else 0 for d in off)


PLACES = [(o, f) for o in ORDERED for f in (0, 1) if any(o)] + [((0, 0, 0), 1), ((0, 0, 0), 0)]
DESTS = [p for p in PLACES if relayed(*p)] + [p for p in PLACES if not relayed(*p)]
N_FAR = sum(relayed(*p) for p in PLACES)
OWN = N_DEV - 1
HALF_DEV = N_DEV // 2


def packed(values):
    words = []
    for n in range(0, N_DEV, 16):
        word = sum(v << (2 * i) for i, v in enumerate(values[n : n + 16]))
        words.append(word - (1 << 32) if word >> 31 else word)
    return words


WORDS = [packed([o[axis] for o, f in DESTS]) for axis in range(3)] + [packed([f for o, f in DESTS])]
HALO = 3
CELLS = TH * GW
RIM = HALO * GW
FR, FC = TH + 2 * HALO, GW + HALO
N_FREQ = FR * (FC // 2 + 1)
HALF_F = 400
ALL_F = 2 * HALF_F
TAPS = 8 * KS
SQRT_HALF = 0.7071067811865476
INV_ROOT = 0.3989422804014327
BF = jnp.bfloat16
F32 = jnp.float32
I32 = jnp.int32


def transforms():
    kr, kc = [v.reshape(-1, 1) for v in np.meshgrid(np.arange(FR), np.arange(FC // 2 + 1), indexing="ij")]

    def wave(r, c):
        return np.exp(2j * np.pi * (kr * r / FR + kc * c / FC))

    def rows_of(z):
        out = np.zeros((ALL_F, z.shape[1]))
        out[:N_FREQ], out[HALF_F : HALF_F + N_FREQ] = z.real, z.imag
        return out

    r, c = [v.ravel() for v in np.meshgrid(np.arange(TH), np.arange(GW), indexing="ij")]
    by_patch = np.argsort(((r % 2) * 2 + c % 2) * 128 + (r // 2) * 16 + c // 2)
    rr, rc = [v.ravel() for v in np.meshgrid(np.arange(HALO), np.arange(GW), indexing="ij")]
    rim_patch = np.argsort(rr * GW + (rc % 2) * 16 + rc // 2)
    there = rows_of(np.conj(wave(r, c)))
    rims = [rows_of(np.conj(wave(rr + at, rc))) for at in (-HALO, TH)]
    rim_cells = np.concatenate(rims, axis=1)
    rim_patches = np.concatenate([m[:, rim_patch] for m in rims], axis=1)
    share = np.where(kc == 0, 1.0, 2.0) / (FR * FC)
    back = wave(r, c) * share
    back = (rows_of(np.conj(back))).T
    a, b = np.arange(TAPS) // 8, np.arange(TAPS) % 8
    taps = rows_of(wave(a - HALO, b - HALO) * (b < KS))
    high = taps.astype(BF)
    low = (taps - high.astype(np.float64)).astype(BF)
    return [
        m.astype(BF)
        for m in (there, there[:, by_patch], rim_cells, rim_patches, back[by_patch], back, high, low)
    ]


def iota(shape, axis):
    return lax.broadcasted_iota(I32, shape, axis)


def dot(a, b):
    return jnp.dot(a, b, preferred_element_type=F32)


def kernel(
    tiles_hbm, ids_ref, partner_ref, mixk_ref, mixb_ref, w_hbm, downb_ref, pos_ref, grad_hbm,
    to_f_hbm, to_b_hbm, rim_f_hbm, rim_b_hbm, from_f_hbm, from_b_hbm, tap_high, tap_low,
    llm_ref, gout_ref,
    to_f, to_b, rim_f, rim_b, from_f, from_b, taps, wave, field, edge, mg, to_patch, to_cell,
    tiles, w, grads, mixb, downb, A, slope, tok, pg, sel, hot, owner,
    msg, rmsg, gsend, grecv, grel, tsend, trecv, trel, rimf, rimb,
    lsem, msem, gsem, tsem, fsend, frecv, bsend, brecv,
):
    enc = lax.axis_index("enc")
    seq = lax.axis_index("seq")
    me = enc * N_SEQ + seq
    cy, core = enc // 2, enc % 2

    ld_tiles = pltpu.make_async_copy(tiles_hbm.at[0, 0], tiles, lsem.at[0])
    ld_grads = pltpu.make_async_copy(grad_hbm, grads, lsem.at[1])
    ld_w = pltpu.make_async_copy(w_hbm, w, lsem.at[2])
    ld_tiles.start()
    ld_grads.start()
    ld_consts = [
        pltpu.make_async_copy(src, dst, lsem.at[3 + n])
        for n, (src, dst) in enumerate(
            ((to_f_hbm, to_f), (rim_f_hbm, rim_f), (from_f_hbm, from_f), (to_b_hbm, to_b), (rim_b_hbm, rim_b), (from_b_hbm, from_b))
        )
    ]
    for n in range(3):
        ld_consts[n].start()
    ld_w.start()
    for n in range(3, 6):
        ld_consts[n].start()

    cx, cz = seq >> 2, seq & 3
    at_x = [((cx + d) & 3) * 4 for d in range(4)]
    at_y = [((cy + d) & 3) * 2 for d in range(4)]
    at_z = [(cz + d) & 3 for d in range(4)]
    at_core = [core, 1 - core]

    def device(off, f):
        dx, dy, dz = off
        return at_y[dy] + at_core[f], at_x[dx] + at_z[dz]

    others = range(OWN)
    barrier = pltpu.get_barrier_semaphore()
    for q in others:
        pl.semaphore_signal(barrier, inc=1, device_id=device(*DESTS[q]), device_id_type=pl.DeviceIdType.MESH)


    pos = pos_ref[0, 0]
    prow = jnp.concatenate([pos[0:1, :], pos[1:2, :]], axis=1)
    pcol = jnp.concatenate(
        [jnp.transpose(jnp.broadcast_to(pos[i : i + 1, :].astype(F32), (128, 128))) for i in range(2)], axis=0
    ).astype(I32)[:, 0:1]
    orow, ocol = prow // ROWS, pcol // ROWS
    lcol = pcol - ocol * ROWS
    same = jnp.broadcast_to(ocol, (ROWS, ROWS)) == jnp.broadcast_to(orow, (ROWS, ROWS))
    at0, at1 = iota((ROWS, ROWS), 0), iota((ROWS, ROWS), 1)
    rank_row = jnp.sum(jnp.where(same & (at0 < at1), 1.0, 0.0), axis=0, keepdims=True).astype(I32)
    rank_col = jnp.sum(jnp.where(same & (at1 < at0), 1.0, 0.0), axis=1, keepdims=True).astype(I32)
    slot_row = orow * CAP + rank_row
    to_owner = jnp.where(iota((N_DEV, ROWS), 0) == orow, 1.0, 0.0).astype(BF)
    ranked = jnp.where(iota((ROWS, 128), 1) == rank_col, (lcol + 1).astype(F32), 0.0).astype(BF)
    msg[...] = dot(to_owner, ranked).reshape(N_DEV, 1, 128)
    rmsg[pl.ds(me, 1)] = msg[pl.ds(me, 1)]

    def lower(k):
        return lax.rem(ids_ref[0, 0, k], 2)

    up = lax.rem(cy + 1, 4) * 2 + core
    down = lax.rem(cy + 3, 4) * 2 + core
    across = lax.rem(cy + 2, 4) * 2 + core
    sib = cy * 2 + 1 - core

    def rim_copies(rims, ssem, rsem):
        def copy(n, ref, to):
            return pltpu.make_async_remote_copy(
                src_ref=ref, dst_ref=ref, send_sem=ssem.at[n], recv_sem=rsem.at[n],
                device_id=(to, seq), device_id_type=pl.DeviceIdType.MESH,
            )

        def landed(n, ref):
            return pltpu.make_async_copy(ref, ref, rsem.at[n])

        sends = [
            copy(0, rims.at[enc], up),
            copy(1, rims.at[enc], down),
            copy(2, rims.at[enc], sib),
            copy(3, rims.at[down, 0], up),
            copy(4, rims.at[up, 1], down),
            copy(5, rims.at[down], sib),
            copy(6, rims.at[up], sib),
            copy(7, rims.at[across], sib),
        ]
        other = 1 - 2 * core
        arrivals = [
            landed(0, rims.at[down]),
            landed(1, rims.at[up]),
            landed(2, rims.at[sib]),
            landed(3, rims.at[across, 0]),
            landed(4, rims.at[across, 1]),
            landed(5, rims.at[down + other]),
            landed(6, rims.at[up + other]),
            landed(7, rims.at[across + other]),
        ]
        return sends, arrivals

    def place_rims(rims):
        for k in range(SLOTS):
            want = partner_ref[0, 0, k]
            rim = jnp.zeros((RIM, C), BF)
            for q in range(N_ENC * SLOTS):
                rim = jnp.where(want == q, rims[q // 2, q % 2], rim)
            none = jnp.zeros((RIM, C), BF)
            below = lower(k) == 1
            edge[k, 0:RIM, :] = jnp.where(below, rim, none)
            edge[k, RIM : 2 * RIM, :] = jnp.where(below, none, rim)

    def columns(n):
        return pl.ds(pl.multiple_of(n * 256, 256), 256)

    def spectrum(there, cells):
        @pl.loop(0, SLOTS * 3)
        def _(i):
            k, cols = i // 3, columns(lax.rem(i, 3))
            field[k, :, cols] = dot(there, cells(k, cols))

    def depthwise(there, back, way, turn, cells, store):
        @pl.loop(0, SLOTS * 3)
        def _(i):
            k, cols = i // 3, columns(lax.rem(i, 3))
            z = field[k, :, cols] + dot(there[...], edge[k, :, cols])
            re, im = z[0:HALF_F], z[HALF_F:ALL_F]
            wr, wi = wave[0:HALF_F, cols], way * wave[HALF_F:ALL_F, cols]
            product = jnp.concatenate([re * wr - im * wi, re * wi + im * wr], axis=0).astype(BF)
            store(k, cols, dot(turn[...], cells(k, cols)) + dot(back[...], product))

    def owner_of_row():
        place = iota((SLOT_ROWS, 1), 0) // CAP
        block, shift = place // 16, 2 * (place % 16)
        d = []
        for words in WORDS:
            word = jnp.full(place.shape, words[0])
            for n in range(1, 8):
                word = jnp.where(block == n, words[n], word)
            d.append(jnp.right_shift(word, shift) & 3)
        c = core + d[3] - 2 * core * d[3]
        return (((cy + d[1]) & 3) * 2 + c) * N_SEQ + ((cx + d[0]) & 3) * 4 + ((cz + d[2]) & 3)

    def fill_rows(buf, rows_ref, part):
        slots = slice(part * SLOT_ROWS // 2, (part + 1) * SLOT_ROWS // 2)
        dests = slice(part * HALF_DEV, (part + 1) * HALF_DEV)

        @pl.loop(0, C // 256)
        def _(n):
            c0 = pl.multiple_of(n * 256, 256)
            y0 = dot(hot[slots, :], rows_ref[:, pl.ds(c0, 256)]).reshape(HALF_DEV, CAP, 256)
            y1 = dot(hot[slots, :], rows_ref[:, pl.ds(c0 + C, 256)]).reshape(HALF_DEV, CAP, 256)
            buf[dests, :, pl.ds(c0, 256)] = jnp.concatenate([y0, y1], axis=1).astype(BF)

    def send_rows(buf, rel, got, sems, part):
        for q in others:
            if q // HALF_DEV == part:
                off, f = DESTS[q]
                far = q < N_FAR
                pltpu.make_async_remote_copy(
                    src_ref=buf.at[q], dst_ref=rel.at[q] if far else got.at[me],
                    send_sem=sems.at[0], recv_sem=sems.at[2 if far else 1],
                    device_id=device(first_leg(off, f), 0) if far else device(off, f),
                    device_id_type=pl.DeviceIdType.MESH,
                ).start()

    def forward(rel, got, sems):
        part = rel.at[pl.ds(0, N_FAR)]
        pltpu.make_async_copy(part, part, sems.at[2]).wait()
        for q in range(N_FAR):
            off, f = DESTS[q]
            leg = first_leg(off, f)
            e0, s0 = device([-d % 4 for d in leg], 0)
            pltpu.make_async_remote_copy(
                src_ref=rel.at[q], dst_ref=got.at[e0 * N_SEQ + s0],
                send_sem=sems.at[3], recv_sem=sems.at[1],
                device_id=device([(o - d) % 4 for o, d in zip(off, leg)], f), device_id_type=pl.DeviceIdType.MESH,
            ).start()

    def keep_own(buf, got):
        got[pl.ds(me, 1)] = buf[OWN : OWN + 1]

    def wait_rows(buf, sem):
        part = buf.at[pl.ds(0, N_DEV - 1)]
        pltpu.make_async_copy(part, part, sem).wait()

    ld_tiles.wait()
    for k in range(SLOTS):
        high, low = tiles[k, TH - HALO : TH].reshape(RIM, C), tiles[k, 0:HALO].reshape(RIM, C)
        rimf[enc, k] = jnp.where(lower(k) == 0, high, low)
    pl.semaphore_wait(barrier, N_DEV - 1)
    for q in others:
        e, s = device(*DESTS[q])
        pltpu.make_async_remote_copy(
            src_ref=msg.at[e * N_SEQ + s], dst_ref=rmsg.at[me],
            send_sem=msem.at[0], recv_sem=msem.at[1],
            device_id=(e, s), device_id_type=pl.DeviceIdType.MESH,
        ).start()
    f_send, f_got = rim_copies(rimf, fsend, frecv)
    for n in range(3):
        f_send[n].start()
    owner[...] = owner_of_row()

    def tile_cells(k, cols):
        return tiles[k, :, :, cols].reshape(CELLS, 256)

    def grad_cells(k, cols):
        return mg[k, :, cols]

    ld_grads.wait()
    wait_rows(rmsg, msem.at[1])

    asked = rmsg[...].reshape(N_DEV, 128)
    asked_t = jnp.transpose(asked)[0:CAP, :].astype(BF)
    asked = asked.astype(BF)

    shape = (SLOT_ROWS, 128)
    rows = dot(jnp.where(iota(shape, 1) == owner[...], 1.0, 0.0).astype(BF), asked)
    want = jnp.sum(jnp.where(iota(shape, 1) == iota(shape, 0) % CAP, rows, 0.0), axis=1, keepdims=True).astype(I32)
    hot[...] = jnp.where(iota((SLOT_ROWS, ROWS), 1) == want - 1, 1.0, 0.0).astype(BF)
    for part in range(2):
        fill_rows(gsend, grads, part)
    f_got[0].wait()
    f_send[3].start()
    f_send[5].start()
    f_got[1].wait()
    f_send[4].start()
    f_send[6].start()
    for part in range(2):
        send_rows(gsend, grel, grecv, gsem, part)
    keep_own(gsend, grecv)

    mixb[...] = mixb_ref[...].reshape(1, C)
    downb[...] = downb_ref[...].reshape(1, C2)

    def cell_of(m):
        return ((m % 128) // 16 * 2 + m // 256) * GW + m % 16 * 2 + m // 128 % 2

    p0, p1 = iota((CELLS, CELLS), 0), iota((CELLS, CELLS), 1)
    to_patch[...] = jnp.where(p1 == cell_of(p0), 1.0, 0.0).astype(BF)
    to_cell[...] = jnp.where(p0 == cell_of(p1), 1.0, 0.0).astype(BF)

    taps[...] = jnp.zeros((TAPS, C), F32)
    for a in range(KS):
        taps[8 * a : 8 * a + KS, :] = mixk_ref[a].astype(F32)
    flat_taps = taps[...].astype(BF)
    wave[...] = dot(tap_high[...], flat_taps) + dot(tap_low[...], flat_taps)

    ld_consts[0].wait()
    spectrum(to_f[...], tile_cells)
    forward(grel, grecv, gsem)
    f_got[3].wait()
    f_got[4].wait()
    f_send[7].start()
    for n in (2, 5, 6, 7):
        f_got[n].wait()
    place_rims(rimf)
    ld_consts[1].wait()
    ld_consts[2].wait()

    def store_mixed(k, cols, cells):
        mixed = (cells + mixb[:, cols]).astype(BF)
        A[:, pl.ds(pl.multiple_of(k * 128, 128), 128), cols] = mixed.reshape(4, 128, 256)

    depthwise(rim_f, from_f, 1.0, to_patch, tile_cells, store_mixed)
    ld_w.wait()

    @pl.loop(0, C2 // 256)
    def _(n):
        cols = pl.ds(pl.multiple_of(n * 256, 256), 256)
        pre = jnp.zeros((ROWS, 256), F32) + downb[:, cols]
        for j in range(4):
            pre = pre + dot(A[j], w[j * C : (j + 1) * C, cols])
        phi = 0.5 * (1.0 + lax.erf(pre * SQRT_HALF))
        tok[:, cols] = (pre * phi).astype(BF)
        slope[:, cols] = phi + pre * INV_ROOT * jnp.exp(-0.5 * pre * pre)

    at = owner[...] * CAP + iota((SLOT_ROWS, 1), 0) % CAP
    hot[...] = jnp.where(at == slot_row, 1.0, 0.0).astype(BF)
    for part in range(2):
        fill_rows(tsend, tok, part)
        send_rows(tsend, trel, trecv, tsem, part)
    keep_own(tsend, trecv)

    back_at = ocol * (2 * CAP) + rank_col
    for h in range(2):
        sel[h] = jnp.where(iota((ROWS, 2 * CAP * N_DEV), 1) == back_at + h * CAP, 1.0, 0.0).astype(BF)
    wait_rows(grecv, gsem.at[1])

    def picked(got, h, c0):
        part = got[:, :, pl.ds(pl.multiple_of(c0, 256), 256)].reshape(2 * CAP * N_DEV, 256)
        return dot(sel[h], part)

    @pl.loop(0, C2 // 256)
    def _(n):
        h = n // 3
        cols = pl.ds(pl.multiple_of(n * 256, 256), 256)
        pg[:, cols] = (picked(grecv, h, (n - 3 * h) * 256) * slope[:, cols]).astype(BF)

    forward(trel, trecv, tsem)

    @pl.loop(0, 4 * (C // 256))
    def _(m):
        j, n = m // 3, lax.rem(m, 3)
        part = w[pl.ds(pl.multiple_of(m * 256, 256), 256), :]
        g = lax.dot_general(pg[...], part, (((1,), (1,)), ((), ())), preferred_element_type=F32)
        mg[:, pl.ds(pl.multiple_of(j * 128, 128), 128), columns(n)] = g.astype(BF).reshape(SLOTS, 128, 256)

    def rim_rows(k, rows):
        at = [((r % 2) * 2 + dx) * 128 + (r // 2) * 16 for r in rows for dx in range(2)]
        return jnp.concatenate([mg[k, a : a + 16, :] for a in at], axis=0)

    for k in range(SLOTS):
        rimb[enc, k] = jnp.where(lower(k) == 0, rim_rows(k, range(TH - HALO, TH)), rim_rows(k, range(HALO)))
    b_send, b_got = rim_copies(rimb, bsend, brecv)
    for n in range(3):
        b_send[n].start()
    ld_consts[3].wait()
    spectrum(to_b[...], grad_cells)
    b_got[0].wait()
    b_send[3].start()
    b_send[5].start()
    b_got[1].wait()
    b_send[4].start()
    b_send[6].start()
    b_got[3].wait()
    b_got[4].wait()
    b_send[7].start()
    for n in (2, 5, 6, 7):
        b_got[n].wait()
    place_rims(rimb)
    ld_consts[4].wait()
    ld_consts[5].wait()

    def store_grad(k, cols, cells):
        gout_ref[k, :, :, cols] = cells.astype(BF).reshape(TH, GW, 256)

    depthwise(rim_b, from_b, -1.0, to_cell, grad_cells, store_grad)

    for g in range(N_DEV // N_SEQ):
        shape = (N_DEV, 256)
        at1 = iota(shape, 1)
        over = jnp.where(iota(shape, 0) == g * N_SEQ + at1 // (2 * CAP), 1.0, 0.0).astype(BF)
        rows = dot(asked_t, over)
        k8 = iota((CAP, 256), 1)
        put = jnp.sum(jnp.where(iota((CAP, 256), 0) == k8 % CAP, rows, 0.0), axis=0, keepdims=True).astype(I32)
        hit = iota((ROWS, 256), 0) == put - 1
        part = (iota((ROWS, 256), 1) // CAP) % 2
        for h in range(2):
            sel[h, :, g * 256 : (g + 1) * 256] = jnp.where(hit & (part == h), 1.0, 0.0).astype(BF)
    wait_rows(trecv, tsem.at[1])

    @pl.loop(0, C2 // 256)
    def _(n):
        h = n // 3
        cols = pl.ds(pl.multiple_of(n * 256, 256), 256)
        llm_ref[:, cols] = picked(trecv, h, (n - 3 * h) * 256).astype(BF)

    for n in range(8):
        f_send[n].wait_send()
        b_send[n].wait_send()
    wait_rows(msg, msem.at[0])
    for buf, rel, sems in ((gsend, grel, gsem), (tsend, trel, tsem)):
        wait_rows(buf, sems.at[0])
        part = rel.at[pl.ds(0, N_FAR)]
        pltpu.make_async_copy(part, part, sems.at[3]).wait()


def on_device(frame_tiles, tile_ids, partner_slot, mix_kernel, mix_bias, down_weight, down_bias, token_pos, grad_rows):
    vmem = pl.BlockSpec(memory_space=pltpu.VMEM)
    smem = pl.BlockSpec(memory_space=pltpu.SMEM)
    anyw = pl.BlockSpec(memory_space=pl.ANY)
    dma = pltpu.SemaphoreType.DMA
    llm, gout = pl.pallas_call(
        kernel,
        out_shape=(
            jax.ShapeDtypeStruct((ROWS, C2), BF),
            jax.ShapeDtypeStruct((SLOTS, TH, GW, C), BF),
        ),
        in_specs=[anyw, smem, smem, vmem, vmem, anyw, vmem, vmem, anyw] + [anyw] * 6 + [vmem] * 2,
        out_specs=(vmem, vmem),
        scratch_shapes=[
            pltpu.VMEM((ALL_F, CELLS), BF),
            pltpu.VMEM((ALL_F, CELLS), BF),
            pltpu.VMEM((ALL_F, 2 * RIM), BF),
            pltpu.VMEM((ALL_F, 2 * RIM), BF),
            pltpu.VMEM((CELLS, ALL_F), BF),
            pltpu.VMEM((CELLS, ALL_F), BF),
            pltpu.VMEM((TAPS, C), F32),
            pltpu.VMEM((ALL_F, C), F32),
            pltpu.VMEM((SLOTS, ALL_F, C), F32),
            pltpu.VMEM((SLOTS, 2 * RIM, C), BF),
            pltpu.VMEM((SLOTS, CELLS, C), BF),
            pltpu.VMEM((CELLS, CELLS), BF),
            pltpu.VMEM((CELLS, CELLS), BF),
            pltpu.VMEM((SLOTS, TH, GW, C), BF),
            pltpu.VMEM((4 * C, C2), BF),
            pltpu.VMEM((ROWS, C2), BF),
            pltpu.VMEM((1, C), F32),
            pltpu.VMEM((1, C2), F32),
            pltpu.VMEM((4, ROWS, C), BF),
            pltpu.VMEM((ROWS, C2), F32),
            pltpu.VMEM((ROWS, C2), BF),
            pltpu.VMEM((ROWS, C2), BF),
            pltpu.VMEM((2, ROWS, 2 * CAP * N_DEV), BF),
            pltpu.VMEM((SLOT_ROWS, ROWS), BF),
            pltpu.VMEM((SLOT_ROWS, 1), I32),
            pltpu.VMEM((N_DEV, 1, 128), F32),
            pltpu.VMEM((N_DEV, 1, 128), F32),
            pltpu.VMEM((N_DEV, 2 * CAP, C), BF),
            pltpu.VMEM((N_DEV, 2 * CAP, C), BF),
            pltpu.VMEM((N_FAR, 2 * CAP, C), BF),
            pltpu.VMEM((N_DEV, 2 * CAP, C), BF),
            pltpu.VMEM((N_DEV, 2 * CAP, C), BF),
            pltpu.VMEM((N_FAR, 2 * CAP, C), BF),
            pltpu.VMEM((N_ENC, SLOTS, RIM, C), BF),
            pltpu.VMEM((N_ENC, SLOTS, RIM, C), BF),
            dma((9,)),
            dma((2,)),
            dma((4,)),
            dma((4,)),
            dma((8,)),
            dma((8,)),
            dma((8,)),
            dma((8,)),
        ],
        compiler_params=pltpu.CompilerParams(
            collective_id=0, has_side_effects=True, vmem_limit_bytes=62 * 1024 * 1024
        ),
    )(
        frame_tiles,
        tile_ids,
        partner_slot,
        mix_kernel,
        mix_bias,
        down_weight,
        down_bias,
        token_pos,
        grad_rows,
        *transforms(),
    )
    return llm, gout[None, None]


def solution(mesh):
    return jax.shard_map(
        on_device,
        mesh=mesh,
        in_specs=(
            P("enc", "seq", None, None, None, None),
            P("enc", "seq", None),
            P("enc", "seq", None),
            P(),
            P(),
            P(),
            P(),
            P("enc", "seq", None, None),
            P(("enc", "seq"), None),
        ),
        out_specs=(P(("enc", "seq"), None), P("enc", "seq", None, None, None, None)),
        check_vma=False,
    )
```

```python
import functools

import itertools

import jax
import jax.numpy as jnp
import numpy as np
from jax import lax
from jax.experimental import pallas as pl
from jax.experimental.pallas import tpu as pltpu
from jax.sharding import PartitionSpec as P

C = 768
C2 = 1536
KS = 7
TH = 16
GW = 32
SLOTS = 2
ROWS = 256
N_ENC = 8
N_SEQ = 16
N_DEV = 128
CAP = 8
SLOT_ROWS = CAP * N_DEV

def orbit(o):
    turned = [o, o[2:] + o[:2], o[1:] + o[:1]]
    return [p for q in turned for p in (q, tuple(-d % 4 for d in q))]


ALL_OFFSETS = sorted(itertools.product((0, 1, 3, 2), repeat=3), key=lambda o: -sum(min(d, 4 - d) for d in o))
ORDERED = list(dict.fromkeys(p for o in ALL_OFFSETS for p in orbit(o)))


def relayed(off, f):
    return 2 in off and f == 1


def first_leg(off, f):
    return tuple(1 if d == 2 else 0 for d in off)


PLACES = [(o, f) for o in ORDERED for f in (0, 1) if any(o)] + [((0, 0, 0), 1), ((0, 0, 0), 0)]
DESTS = [p for p in PLACES if relayed(*p)] + [p for p in PLACES if not relayed(*p)]
N_FAR = sum(relayed(*p) for p in PLACES)
OWN = N_DEV - 1
HALF_DEV = N_DEV // 2


def packed(values):
    words = []
    for n in range(0, N_DEV, 16):
        word = sum(v << (2 * i) for i, v in enumerate(values[n : n + 16]))
        words.append(word - (1 << 32) if word >> 31 else word)
    return words


WORDS = [packed([o[axis] for o, f in DESTS]) for axis in range(3)] + [packed([f for o, f in DESTS])]
HALO = 3
CELLS = TH * GW
RIM = HALO * GW
FR, FC = TH + 2 * HALO, GW + HALO
N_FREQ = FR * (FC // 2 + 1)
HALF_F = 400
ALL_F = 2 * HALF_F
TAPS = 8 * KS
SQRT_HALF = 0.7071067811865476
INV_ROOT = 0.3989422804014327
BF = jnp.bfloat16
F32 = jnp.float32
I32 = jnp.int32


def transforms():
    kr, kc = [v.reshape(-1, 1) for v in np.meshgrid(np.arange(FR), np.arange(FC // 2 + 1), indexing="ij")]

    def wave(r, c):
        return np.exp(2j * np.pi * (kr * r / FR + kc * c / FC))

    def rows_of(z):
        out = np.zeros((ALL_F, z.shape[1]))
        out[:N_FREQ], out[HALF_F : HALF_F + N_FREQ] = z.real, z.imag
        return out

    r, c = [v.ravel() for v in np.meshgrid(np.arange(TH), np.arange(GW), indexing="ij")]
    by_patch = np.argsort(((r % 2) * 2 + c % 2) * 128 + (r // 2) * 16 + c // 2)
    rr, rc = [v.ravel() for v in np.meshgrid(np.arange(HALO), np.arange(GW), indexing="ij")]
    rim_patch = np.argsort(rr * GW + (rc % 2) * 16 + rc // 2)
    there = rows_of(np.conj(wave(r, c)))
    rims = [rows_of(np.conj(wave(rr + at, rc))) for at in (-HALO, TH)]
    rim_cells = np.concatenate(rims, axis=1)
    rim_patches = np.concatenate([m[:, rim_patch] for m in rims], axis=1)
    share = np.where(kc == 0, 1.0, 2.0) / (FR * FC)
    back = wave(r, c) * share
    back = (rows_of(np.conj(back))).T
    a, b = np.arange(TAPS) // 8, np.arange(TAPS) % 8
    taps = rows_of(wave(a - HALO, b - HALO) * (b < KS))
    high = taps.astype(BF)
    low = (taps - high.astype(np.float64)).astype(BF)
    return [
        m.astype(BF)
        for m in (there, there[:, by_patch], rim_cells, rim_patches, back[by_patch], back, high, low)
    ]


def iota(shape, axis):
    return lax.broadcasted_iota(I32, shape, axis)


def dot(a, b):
    return jnp.dot(a, b, preferred_element_type=F32)


def kernel(
    tiles_hbm, ids_ref, partner_ref, mixk_ref, mixb_ref, w_hbm, downb_ref, pos_ref, grad_hbm,
    to_f_hbm, to_b_hbm, rim_f_hbm, rim_b_hbm, from_f_hbm, from_b_hbm, tap_high, tap_low,
    llm_ref, gout_ref,
    to_f, to_b, rim_f, rim_b, from_f, from_b, taps, wave, field, edge, mg, to_patch, to_cell,
    tiles, w, grads, mixb, downb, A, slope, tok, pg, sel, hot, owner,
    msg, rmsg, gsend, grecv, grel, tsend, trecv, trel, rimf, rimb,
    lsem, msem, gsem, tsem, fsend, frecv, bsend, brecv,
):
    enc = lax.axis_index("enc")
    seq = lax.axis_index("seq")
    me = enc * N_SEQ + seq
    cy, core = enc // 2, enc % 2

    ld_tiles = pltpu.make_async_copy(tiles_hbm.at[0, 0], tiles, lsem.at[0])
    ld_grads = pltpu.make_async_copy(grad_hbm, grads, lsem.at[1])
    ld_w = pltpu.make_async_copy(w_hbm, w, lsem.at[2])
    ld_tiles.start()
    ld_grads.start()
    ld_consts = [
        pltpu.make_async_copy(src, dst, lsem.at[3 + n])
        for n, (src, dst) in enumerate(
            ((to_f_hbm, to_f), (rim_f_hbm, rim_f), (from_f_hbm, from_f), (to_b_hbm, to_b), (rim_b_hbm, rim_b), (from_b_hbm, from_b))
        )
    ]
    for n in range(3):
        ld_consts[n].start()
    ld_w.start()
    for n in range(3, 6):
        ld_consts[n].start()

    cx, cz = seq >> 2, seq & 3
    at_x = [((cx + d) & 3) * 4 for d in range(4)]
    at_y = [((cy + d) & 3) * 2 for d in range(4)]
    at_z = [(cz + d) & 3 for d in range(4)]
    at_core = [core, 1 - core]

    def device(off, f):
        dx, dy, dz = off
        return at_y[dy] + at_core[f], at_x[dx] + at_z[dz]

    others = range(OWN)
    barrier = pltpu.get_barrier_semaphore()
    for q in others:
        pl.semaphore_signal(barrier, inc=1, device_id=device(*DESTS[q]), device_id_type=pl.DeviceIdType.MESH)


    pos = pos_ref[0, 0]
    prow = jnp.concatenate([pos[0:1, :], pos[1:2, :]], axis=1)
    pcol = jnp.concatenate(
        [jnp.transpose(jnp.broadcast_to(pos[i : i + 1, :].astype(F32), (128, 128))) for i in range(2)], axis=0
    ).astype(I32)[:, 0:1]
    orow, ocol = prow // ROWS, pcol // ROWS
    lcol = pcol - ocol * ROWS
    same = jnp.broadcast_to(ocol, (ROWS, ROWS)) == jnp.broadcast_to(orow, (ROWS, ROWS))
    at0, at1 = iota((ROWS, ROWS), 0), iota((ROWS, ROWS), 1)
    rank_row = jnp.sum(jnp.where(same & (at0 < at1), 1.0, 0.0), axis=0, keepdims=True).astype(I32)
    rank_col = jnp.sum(jnp.where(same & (at1 < at0), 1.0, 0.0), axis=1, keepdims=True).astype(I32)
    slot_row = orow * CAP + rank_row
    to_owner = jnp.where(iota((N_DEV, ROWS), 0) == orow, 1.0, 0.0).astype(BF)
    ranked = jnp.where(iota((ROWS, 128), 1) == rank_col, (lcol + 1).astype(F32), 0.0).astype(BF)
    msg[...] = dot(to_owner, ranked).reshape(N_DEV, 1, 128)
    rmsg[pl.ds(me, 1)] = msg[pl.ds(me, 1)]

    def lower(k):
        return lax.rem(ids_ref[0, 0, k], 2)

    up = lax.rem(cy + 1, 4) * 2 + core
    down = lax.rem(cy + 3, 4) * 2 + core
    across = lax.rem(cy + 2, 4) * 2 + core
    sib = cy * 2 + 1 - core

    def rim_copies(rims, ssem, rsem):
        def copy(n, ref, to):
            return pltpu.make_async_remote_copy(
                src_ref=ref, dst_ref=ref, send_sem=ssem.at[n], recv_sem=rsem.at[n],
                device_id=(to, seq), device_id_type=pl.DeviceIdType.MESH,
            )

        def landed(n, ref):
            return pltpu.make_async_copy(ref, ref, rsem.at[n])

        sends = [
            copy(0, rims.at[enc], up),
            copy(1, rims.at[enc], down),
            copy(2, rims.at[enc], sib),
            copy(3, rims.at[down, 0], up),
            copy(4, rims.at[up, 1], down),
            copy(5, rims.at[down], sib),
            copy(6, rims.at[up], sib),
            copy(7, rims.at[across], sib),
        ]
        other = 1 - 2 * core
        arrivals = [
            landed(0, rims.at[down]),
            landed(1, rims.at[up]),
            landed(2, rims.at[sib]),
            landed(3, rims.at[across, 0]),
            landed(4, rims.at[across, 1]),
            landed(5, rims.at[down + other]),
            landed(6, rims.at[up + other]),
            landed(7, rims.at[across + other]),
        ]
        return sends, arrivals

    def place_rims(rims):
        for k in range(SLOTS):
            want = partner_ref[0, 0, k]
            rim = jnp.zeros((RIM, C), BF)
            for q in range(N_ENC * SLOTS):
                rim = jnp.where(want == q, rims[q // 2, q % 2], rim)
            none = jnp.zeros((RIM, C), BF)
            below = lower(k) == 1
            edge[k, 0:RIM, :] = jnp.where(below, rim, none)
            edge[k, RIM : 2 * RIM, :] = jnp.where(below, none, rim)

    def columns(n):
        return pl.ds(pl.multiple_of(n * 256, 256), 256)

    def spectrum(there, cells):
        @pl.loop(0, SLOTS * 3)
        def _(i):
            k, cols = i // 3, columns(lax.rem(i, 3))
            field[k, :, cols] = dot(there, cells(k, cols))

    def depthwise(there, back, way, turn, cells, store):
        @pl.loop(0, SLOTS * 3)
        def _(i):
            k, cols = i // 3, columns(lax.rem(i, 3))
            z = field[k, :, cols] + dot(there[...], edge[k, :, cols])
            re, im = z[0:HALF_F], z[HALF_F:ALL_F]
            wr, wi = wave[0:HALF_F, cols], way * wave[HALF_F:ALL_F, cols]
            product = jnp.concatenate([re * wr - im * wi, re * wi + im * wr], axis=0).astype(BF)
            store(k, cols, dot(turn[...], cells(k, cols)) + dot(back[...], product))

    def owner_of_row():
        place = iota((SLOT_ROWS, 1), 0) // CAP
        block, shift = place // 16, 2 * (place % 16)
        d = []
        for words in WORDS:
            word = jnp.full(place.shape, words[0])
            for n in range(1, 8):
                word = jnp.where(block == n, words[n], word)
            d.append(jnp.right_shift(word, shift) & 3)
        c = core + d[3] - 2 * core * d[3]
        return (((cy + d[1]) & 3) * 2 + c) * N_SEQ + ((cx + d[0]) & 3) * 4 + ((cz + d[2]) & 3)

    def fill_rows(buf, rows_ref, part):
        slots = slice(part * SLOT_ROWS // 2, (part + 1) * SLOT_ROWS // 2)
        dests = slice(part * HALF_DEV, (part + 1) * HALF_DEV)

        @pl.loop(0, C // 256)
        def _(n):
            c0 = pl.multiple_of(n * 256, 256)
            y0 = dot(hot[slots, :], rows_ref[:, pl.ds(c0, 256)]).reshape(HALF_DEV, CAP, 256)
            y1 = dot(hot[slots, :], rows_ref[:, pl.ds(c0 + C, 256)]).reshape(HALF_DEV, CAP, 256)
            buf[dests, :, pl.ds(c0, 256)] = jnp.concatenate([y0, y1], axis=1).astype(BF)

    def send_rows(buf, rel, got, sems, part):
        for q in others:
            if q // HALF_DEV == part:
                off, f = DESTS[q]
                far = q < N_FAR
                pltpu.make_async_remote_copy(
                    src_ref=buf.at[q], dst_ref=rel.at[q] if far else got.at[me],
                    send_sem=sems.at[0], recv_sem=sems.at[2 if far else 1],
                    device_id=device(first_leg(off, f), 0) if far else device(off, f),
                    device_id_type=pl.DeviceIdType.MESH,
                ).start()

    def forward(rel, got, sems):
        part = rel.at[pl.ds(0, N_FAR)]
        pltpu.make_async_copy(part, part, sems.at[2]).wait()
        for q in range(N_FAR):
            off, f = DESTS[q]
            leg = first_leg(off, f)
            e0, s0 = device([-d % 4 for d in leg], 0)
            pltpu.make_async_remote_copy(
                src_ref=rel.at[q], dst_ref=got.at[e0 * N_SEQ + s0],
                send_sem=sems.at[3], recv_sem=sems.at[1],
                device_id=device([(o - d) % 4 for o, d in zip(off, leg)], f), device_id_type=pl.DeviceIdType.MESH,
            ).start()

    def keep_own(buf, got):
        got[pl.ds(me, 1)] = buf[OWN : OWN + 1]

    def wait_rows(buf, sem):
        part = buf.at[pl.ds(0, N_DEV - 1)]
        pltpu.make_async_copy(part, part, sem).wait()

    ld_tiles.wait()
    for k in range(SLOTS):
        high, low = tiles[k, TH - HALO : TH].reshape(RIM, C), tiles[k, 0:HALO].reshape(RIM, C)
        rimf[enc, k] = jnp.where(lower(k) == 0, high, low)
    pl.semaphore_wait(barrier, N_DEV - 1)
    for q in others:
        e, s = device(*DESTS[q])
        pltpu.make_async_remote_copy(
            src_ref=msg.at[e * N_SEQ + s], dst_ref=rmsg.at[me],
            send_sem=msem.at[0], recv_sem=msem.at[1],
            device_id=(e, s), device_id_type=pl.DeviceIdType.MESH,
        ).start()
    f_send, f_got = rim_copies(rimf, fsend, frecv)
    for n in range(3):
        f_send[n].start()
    owner[...] = owner_of_row()

    def tile_cells(k, cols):
        return tiles[k, :, :, cols].reshape(CELLS, 256)

    def grad_cells(k, cols):
        return mg[k, :, cols]

    ld_grads.wait()
    wait_rows(rmsg, msem.at[1])

    asked = rmsg[...].reshape(N_DEV, 128)
    asked_t = jnp.transpose(asked)[0:CAP, :].astype(BF)
    asked = asked.astype(BF)

    shape = (SLOT_ROWS, 128)
    rows = dot(jnp.where(iota(shape, 1) == owner[...], 1.0, 0.0).astype(BF), asked)
    want = jnp.sum(jnp.where(iota(shape, 1) == iota(shape, 0) % CAP, rows, 0.0), axis=1, keepdims=True).astype(I32)
    hot[...] = jnp.where(iota((SLOT_ROWS, ROWS), 1) == want - 1, 1.0, 0.0).astype(BF)
    for part in range(2):
        fill_rows(gsend, grads, part)
    f_got[0].wait()
    f_send[3].start()
    f_send[5].start()
    f_got[1].wait()
    f_send[4].start()
    f_send[6].start()
    for part in range(2):
        send_rows(gsend, grel, grecv, gsem, part)
    keep_own(gsend, grecv)

    mixb[...] = mixb_ref[...].reshape(1, C)
    downb[...] = downb_ref[...].reshape(1, C2)

    def cell_of(m):
        return ((m % 128) // 16 * 2 + m // 256) * GW + m % 16 * 2 + m // 128 % 2

    p0, p1 = iota((CELLS, CELLS), 0), iota((CELLS, CELLS), 1)
    to_patch[...] = jnp.where(p1 == cell_of(p0), 1.0, 0.0).astype(BF)
    to_cell[...] = jnp.where(p0 == cell_of(p1), 1.0, 0.0).astype(BF)

    taps[...] = jnp.zeros((TAPS, C), F32)
    for a in range(KS):
        taps[8 * a : 8 * a + KS, :] = mixk_ref[a].astype(F32)
    flat_taps = taps[...].astype(BF)
    wave[...] = dot(tap_high[...], flat_taps) + dot(tap_low[...], flat_taps)

    ld_consts[0].wait()
    spectrum(to_f[...], tile_cells)
    forward(grel, grecv, gsem)
    f_got[3].wait()
    f_got[4].wait()
    f_send[7].start()
    for n in (2, 5, 6, 7):
        f_got[n].wait()
    place_rims(rimf)
    ld_consts[1].wait()
    ld_consts[2].wait()

    def store_mixed(k, cols, cells):
        mixed = (cells + mixb[:, cols]).astype(BF)
        A[:, pl.ds(pl.multiple_of(k * 128, 128), 128), cols] = mixed.reshape(4, 128, 256)

    depthwise(rim_f, from_f, 1.0, to_patch, tile_cells, store_mixed)
    ld_w.wait()

    @pl.loop(0, C2 // 256)
    def _(n):
        cols = pl.ds(pl.multiple_of(n * 256, 256), 256)
        pre = jnp.zeros((ROWS, 256), F32) + downb[:, cols]
        for j in range(4):
            pre = pre + dot(A[j], w[j * C : (j + 1) * C, cols])
        phi = 0.5 * (1.0 + lax.erf(pre * SQRT_HALF))
        tok[:, cols] = (pre * phi).astype(BF)
        slope[:, cols] = phi + pre * INV_ROOT * jnp.exp(-0.5 * pre * pre)

    at = owner[...] * CAP + iota((SLOT_ROWS, 1), 0) % CAP
    hot[...] = jnp.where(at == slot_row, 1.0, 0.0).astype(BF)
    for part in range(2):
        fill_rows(tsend, tok, part)
        send_rows(tsend, trel, trecv, tsem, part)
    keep_own(tsend, trecv)

    back_at = ocol * (2 * CAP) + rank_col
    for h in range(2):
        sel[h] = jnp.where(iota((ROWS, 2 * CAP * N_DEV), 1) == back_at + h * CAP, 1.0, 0.0).astype(BF)
    wait_rows(grecv, gsem.at[1])

    def picked(got, h, c0):
        part = got[:, :, pl.ds(pl.multiple_of(c0, 256), 256)].reshape(2 * CAP * N_DEV, 256)
        return dot(sel[h], part)

    @pl.loop(0, C2 // 256)
    def _(n):
        h = n // 3
        cols = pl.ds(pl.multiple_of(n * 256, 256), 256)
        pg[:, cols] = (picked(grecv, h, (n - 3 * h) * 256) * slope[:, cols]).astype(BF)

    forward(trel, trecv, tsem)

    @pl.loop(0, 4 * (C // 256))
    def _(m):
        j, n = m // 3, lax.rem(m, 3)
        part = w[pl.ds(pl.multiple_of(m * 256, 256), 256), :]
        g = lax.dot_general(pg[...], part, (((1,), (1,)), ((), ())), preferred_element_type=F32)
        mg[:, pl.ds(pl.multiple_of(j * 128, 128), 128), columns(n)] = g.astype(BF).reshape(SLOTS, 128, 256)

    def rim_rows(k, rows):
        at = [((r % 2) * 2 + dx) * 128 + (r // 2) * 16 for r in rows for dx in range(2)]
        return jnp.concatenate([mg[k, a : a + 16, :] for a in at], axis=0)

    for k in range(SLOTS):
        rimb[enc, k] = jnp.where(lower(k) == 0, rim_rows(k, range(TH - HALO, TH)), rim_rows(k, range(HALO)))
    b_send, b_got = rim_copies(rimb, bsend, brecv)
    for n in range(3):
        b_send[n].start()
    ld_consts[3].wait()
    spectrum(to_b[...], grad_cells)
    b_got[0].wait()
    b_send[3].start()
    b_send[5].start()
    b_got[1].wait()
    b_send[4].start()
    b_send[6].start()
    b_got[3].wait()
    b_got[4].wait()
    b_send[7].start()
    for n in (2, 5, 6, 7):
        b_got[n].wait()
    place_rims(rimb)
    ld_consts[4].wait()
    ld_consts[5].wait()

    def store_grad(k, cols, cells):
        gout_ref[k, :, :, cols] = cells.astype(BF).reshape(TH, GW, 256)

    depthwise(rim_b, from_b, -1.0, to_cell, grad_cells, store_grad)

    for g in range(N_DEV // N_SEQ):
        shape = (N_DEV, 256)
        at1 = iota(shape, 1)
        over = jnp.where(iota(shape, 0) == g * N_SEQ + at1 // (2 * CAP), 1.0, 0.0).astype(BF)
        rows = dot(asked_t, over)
        k8 = iota((CAP, 256), 1)
        put = jnp.sum(jnp.where(iota((CAP, 256), 0) == k8 % CAP, rows, 0.0), axis=0, keepdims=True).astype(I32)
        hit = iota((ROWS, 256), 0) == put - 1
        part = (iota((ROWS, 256), 1) // CAP) % 2
        for h in range(2):
            sel[h, :, g * 256 : (g + 1) * 256] = jnp.where(hit & (part == h), 1.0, 0.0).astype(BF)
    wait_rows(trecv, tsem.at[1])

    @pl.loop(0, C2 // 256)
    def _(n):
        h = n // 3
        cols = pl.ds(pl.multiple_of(n * 256, 256), 256)
        llm_ref[:, cols] = picked(trecv, h, (n - 3 * h) * 256).astype(BF)

    for n in range(8):
        f_send[n].wait_send()
        b_send[n].wait_send()
    wait_rows(msg, msem.at[0])
    for buf, rel, sems in ((gsend, grel, gsem), (tsend, trel, tsem)):
        wait_rows(buf, sems.at[0])
        part = rel.at[pl.ds(0, N_FAR)]
        pltpu.make_async_copy(part, part, sems.at[3]).wait()


def on_device(frame_tiles, tile_ids, partner_slot, mix_kernel, mix_bias, down_weight, down_bias, token_pos, grad_rows):
    vmem = pl.BlockSpec(memory_space=pltpu.VMEM)
    smem = pl.BlockSpec(memory_space=pltpu.SMEM)
    anyw = pl.BlockSpec(memory_space=pl.ANY)
    dma = pltpu.SemaphoreType.DMA
    llm, gout = pl.pallas_call(
        kernel,
        out_shape=(
            jax.ShapeDtypeStruct((ROWS, C2), BF),
            jax.ShapeDtypeStruct((SLOTS, TH, GW, C), BF),
        ),
        in_specs=[anyw, smem, smem, vmem, vmem, anyw, vmem, vmem, anyw] + [anyw] * 6 + [vmem] * 2,
        out_specs=(vmem, vmem),
        scratch_shapes=[
            pltpu.VMEM((ALL_F, CELLS), BF),
            pltpu.VMEM((ALL_F, CELLS), BF),
            pltpu.VMEM((ALL_F, 2 * RIM), BF),
            pltpu.VMEM((ALL_F, 2 * RIM), BF),
            pltpu.VMEM((CELLS, ALL_F), BF),
            pltpu.VMEM((CELLS, ALL_F), BF),
            pltpu.VMEM((TAPS, C), F32),
            pltpu.VMEM((ALL_F, C), F32),
            pltpu.VMEM((SLOTS, ALL_F, C), F32),
            pltpu.VMEM((SLOTS, 2 * RIM, C), BF),
            pltpu.VMEM((SLOTS, CELLS, C), BF),
            pltpu.VMEM((CELLS, CELLS), BF),
            pltpu.VMEM((CELLS, CELLS), BF),
            pltpu.VMEM((SLOTS, TH, GW, C), BF),
            pltpu.VMEM((4 * C, C2), BF),
            pltpu.VMEM((ROWS, C2), BF),
            pltpu.VMEM((1, C), F32),
            pltpu.VMEM((1, C2), F32),
            pltpu.VMEM((4, ROWS, C), BF),
            pltpu.VMEM((ROWS, C2), F32),
            pltpu.VMEM((ROWS, C2), BF),
            pltpu.VMEM((ROWS, C2), BF),
            pltpu.VMEM((2, ROWS, 2 * CAP * N_DEV), BF),
            pltpu.VMEM((SLOT_ROWS, ROWS), BF),
            pltpu.VMEM((SLOT_ROWS, 1), I32),
            pltpu.VMEM((N_DEV, 1, 128), F32),
            pltpu.VMEM((N_DEV, 1, 128), F32),
            pltpu.VMEM((N_DEV, 2 * CAP, C), BF),
            pltpu.VMEM((N_DEV, 2 * CAP, C), BF),
            pltpu.VMEM((N_FAR, 2 * CAP, C), BF),
            pltpu.VMEM((N_DEV, 2 * CAP, C), BF),
            pltpu.VMEM((N_DEV, 2 * CAP, C), BF),
            pltpu.VMEM((N_FAR, 2 * CAP, C), BF),
            pltpu.VMEM((N_ENC, SLOTS, RIM, C), BF),
            pltpu.VMEM((N_ENC, SLOTS, RIM, C), BF),
            dma((9,)),
            dma((2,)),
            dma((4,)),
            dma((4,)),
            dma((8,)),
            dma((8,)),
            dma((8,)),
            dma((8,)),
        ],
        compiler_params=pltpu.CompilerParams(
            collective_id=0, has_side_effects=True, vmem_limit_bytes=62 * 1024 * 1024
        ),
    )(
        frame_tiles,
        tile_ids,
        partner_slot,
        mix_kernel,
        mix_bias,
        down_weight,
        down_bias,
        token_pos,
        grad_rows,
        *transforms(),
    )
    return llm, gout[None, None]


def solution(mesh):
    return jax.shard_map(
        on_device,
        mesh=mesh,
        in_specs=(
            P("enc", "seq", None, None, None, None),
            P("enc", "seq", None),
            P("enc", "seq", None),
            P(),
            P(),
            P(),
            P(),
            P("enc", "seq", None, None),
            P(("enc", "seq"), None),
        ),
        out_specs=(P(("enc", "seq"), None), P("enc", "seq", None, None, None, None)),
        check_vma=False,
    )
```

```python
import functools

import itertools

import jax
import jax.numpy as jnp
import numpy as np
from jax import lax
from jax.experimental import pallas as pl
from jax.experimental.pallas import tpu as pltpu
from jax.sharding import PartitionSpec as P

C = 768
C2 = 1536
KS = 7
TH = 16
GW = 32
SLOTS = 2
ROWS = 256
N_ENC = 8
N_SEQ = 16
N_DEV = 128
CAP = 8
SLOT_ROWS = CAP * N_DEV

def orbit(o):
    turned = [o, o[2:] + o[:2], o[1:] + o[:1]]
    return [p for q in turned for p in (q, tuple(-d % 4 for d in q))]


ALL_OFFSETS = sorted(itertools.product((0, 1, 3, 2), repeat=3), key=lambda o: -sum(min(d, 4 - d) for d in o))
ORDERED = list(dict.fromkeys(p for o in ALL_OFFSETS for p in orbit(o)))


def relayed(off, f):
    return 2 in off


def first_leg(off, f):
    return tuple(way if d == 2 else 0 for d, way in zip(off, (1 + 2 * f, 3 - 2 * f, 1 + 2 * f)))


PLACES = [(o, f) for o in ORDERED for f in (0, 1) if any(o)] + [((0, 0, 0), 1), ((0, 0, 0), 0)]
DESTS = [p for p in PLACES if relayed(*p)] + [p for p in PLACES if not relayed(*p)]
N_FAR = sum(relayed(*p) for p in PLACES)
OWN = N_DEV - 1
HALF_DEV = N_DEV // 2


def packed(values):
    words = []
    for n in range(0, N_DEV, 16):
        word = sum(v << (2 * i) for i, v in enumerate(values[n : n + 16]))
        words.append(word - (1 << 32) if word >> 31 else word)
    return words


WORDS = [packed([o[axis] for o, f in DESTS]) for axis in range(3)] + [packed([f for o, f in DESTS])]
HALO = 3
CELLS = TH * GW
RIM = HALO * GW
FR, FC = TH + 2 * HALO, GW + HALO
N_FREQ = FR * (FC // 2 + 1)
HALF_F = 400
ALL_F = 2 * HALF_F
TAPS = 8 * KS
SQRT_HALF = 0.7071067811865476
INV_ROOT = 0.3989422804014327
BF = jnp.bfloat16
F32 = jnp.float32
I32 = jnp.int32


def transforms():
    kr, kc = [v.reshape(-1, 1) for v in np.meshgrid(np.arange(FR), np.arange(FC // 2 + 1), indexing="ij")]

    def wave(r, c):
        return np.exp(2j * np.pi * (kr * r / FR + kc * c / FC))

    def rows_of(z):
        out = np.zeros((ALL_F, z.shape[1]))
        out[:N_FREQ], out[HALF_F : HALF_F + N_FREQ] = z.real, z.imag
        return out

    r, c = [v.ravel() for v in np.meshgrid(np.arange(TH), np.arange(GW), indexing="ij")]
    by_patch = np.argsort(((r % 2) * 2 + c % 2) * 128 + (r // 2) * 16 + c // 2)
    rr, rc = [v.ravel() for v in np.meshgrid(np.arange(HALO), np.arange(GW), indexing="ij")]
    rim_patch = np.argsort(rr * GW + (rc % 2) * 16 + rc // 2)
    there = rows_of(np.conj(wave(r, c)))
    rims = [rows_of(np.conj(wave(rr + at, rc))) for at in (-HALO, TH)]
    rim_cells = np.concatenate(rims, axis=1)
    rim_patches = np.concatenate([m[:, rim_patch] for m in rims], axis=1)
    share = np.where(kc == 0, 1.0, 2.0) / (FR * FC)
    back = wave(r, c) * share
    back = (rows_of(np.conj(back))).T
    a, b = np.arange(TAPS) // 8, np.arange(TAPS) % 8
    taps = rows_of(wave(a - HALO, b - HALO) * (b < KS))
    high = taps.astype(BF)
    low = (taps - high.astype(np.float64)).astype(BF)
    return [
        m.astype(BF)
        for m in (there, there[:, by_patch], rim_cells, rim_patches, back[by_patch], back, high, low)
    ]


def iota(shape, axis):
    return lax.broadcasted_iota(I32, shape, axis)


def dot(a, b):
    return jnp.dot(a, b, preferred_element_type=F32)


def kernel(
    tiles_hbm, ids_ref, partner_ref, mixk_ref, mixb_ref, w_hbm, downb_ref, pos_ref, grad_hbm,
    to_f_hbm, to_b_hbm, rim_f_hbm, rim_b_hbm, from_f_hbm, from_b_hbm, tap_high, tap_low,
    llm_ref, gout_ref,
    to_f, to_b, rim_f, rim_b, from_f, from_b, taps, wave, field, edge, mg, to_patch, to_cell,
    tiles, w, grads, mixb, downb, A, slope, tok, pg, sel, hot, owner,
    msg, rmsg, gsend, grecv, grel, tsend, trecv, trel, rimf, rimb,
    lsem, msem, gsem, tsem, fsend, frecv, bsend, brecv,
):
    enc = lax.axis_index("enc")
    seq = lax.axis_index("seq")
    me = enc * N_SEQ + seq
    cy, core = enc // 2, enc % 2

    ld_tiles = pltpu.make_async_copy(tiles_hbm.at[0, 0], tiles, lsem.at[0])
    ld_grads = pltpu.make_async_copy(grad_hbm, grads, lsem.at[1])
    ld_w = pltpu.make_async_copy(w_hbm, w, lsem.at[2])
    ld_tiles.start()
    ld_grads.start()
    ld_consts = [
        pltpu.make_async_copy(src, dst, lsem.at[3 + n])
        for n, (src, dst) in enumerate(
            ((to_f_hbm, to_f), (rim_f_hbm, rim_f), (from_f_hbm, from_f), (to_b_hbm, to_b), (rim_b_hbm, rim_b), (from_b_hbm, from_b))
        )
    ]
    for n in range(3):
        ld_consts[n].start()
    ld_w.start()
    for n in range(3, 6):
        ld_consts[n].start()

    cx, cz = seq >> 2, seq & 3
    at_x = [((cx + d) & 3) * 4 for d in range(4)]
    at_y = [((cy + d) & 3) * 2 for d in range(4)]
    at_z = [(cz + d) & 3 for d in range(4)]
    at_core = [core, 1 - core]

    def device(off, f):
        dx, dy, dz = off
        return at_y[dy] + at_core[f], at_x[dx] + at_z[dz]

    others = range(OWN)
    barrier = pltpu.get_barrier_semaphore()
    for q in others:
        pl.semaphore_signal(barrier, inc=1, device_id=device(*DESTS[q]), device_id_type=pl.DeviceIdType.MESH)


    pos = pos_ref[0, 0]
    prow = jnp.concatenate([pos[0:1, :], pos[1:2, :]], axis=1)
    pcol = jnp.concatenate(
        [jnp.transpose(jnp.broadcast_to(pos[i : i + 1, :].astype(F32), (128, 128))) for i in range(2)], axis=0
    ).astype(I32)[:, 0:1]
    orow, ocol = prow // ROWS, pcol // ROWS
    lcol = pcol - ocol * ROWS
    same = jnp.broadcast_to(ocol, (ROWS, ROWS)) == jnp.broadcast_to(orow, (ROWS, ROWS))
    at0, at1 = iota((ROWS, ROWS), 0), iota((ROWS, ROWS), 1)
    rank_row = jnp.sum(jnp.where(same & (at0 < at1), 1.0, 0.0), axis=0, keepdims=True).astype(I32)
    rank_col = jnp.sum(jnp.where(same & (at1 < at0), 1.0, 0.0), axis=1, keepdims=True).astype(I32)
    slot_row = orow * CAP + rank_row
    to_owner = jnp.where(iota((N_DEV, ROWS), 0) == orow, 1.0, 0.0).astype(BF)
    ranked = jnp.where(iota((ROWS, 128), 1) == rank_col, (lcol + 1).astype(F32), 0.0).astype(BF)
    msg[...] = dot(to_owner, ranked).reshape(N_DEV, 1, 128)
    rmsg[pl.ds(me, 1)] = msg[pl.ds(me, 1)]

    def lower(k):
        return lax.rem(ids_ref[0, 0, k], 2)

    up = lax.rem(cy + 1, 4) * 2 + core
    down = lax.rem(cy + 3, 4) * 2 + core
    across = lax.rem(cy + 2, 4) * 2 + core
    sib = cy * 2 + 1 - core

    def rim_copies(rims, ssem, rsem):
        def copy(n, ref, to):
            return pltpu.make_async_remote_copy(
                src_ref=ref, dst_ref=ref, send_sem=ssem.at[n], recv_sem=rsem.at[n],
                device_id=(to, seq), device_id_type=pl.DeviceIdType.MESH,
            )

        def landed(n, ref):
            return pltpu.make_async_copy(ref, ref, rsem.at[n])

        sends = [
            copy(0, rims.at[enc], up),
            copy(1, rims.at[enc], down),
            copy(2, rims.at[enc], sib),
            copy(3, rims.at[down, 0], up),
            copy(4, rims.at[up, 1], down),
            copy(5, rims.at[down], sib),
            copy(6, rims.at[up], sib),
            copy(7, rims.at[across], sib),
        ]
        other = 1 - 2 * core
        arrivals = [
            landed(0, rims.at[down]),
            landed(1, rims.at[up]),
            landed(2, rims.at[sib]),
            landed(3, rims.at[across, 0]),
            landed(4, rims.at[across, 1]),
            landed(5, rims.at[down + other]),
            landed(6, rims.at[up + other]),
            landed(7, rims.at[across + other]),
        ]
        return sends, arrivals

    def place_rims(rims):
        for k in range(SLOTS):
            want = partner_ref[0, 0, k]
            rim = jnp.zeros((RIM, C), BF)
            for q in range(N_ENC * SLOTS):
                rim = jnp.where(want == q, rims[q // 2, q % 2], rim)
            none = jnp.zeros((RIM, C), BF)
            below = lower(k) == 1
            edge[k, 0:RIM, :] = jnp.where(below, rim, none)
            edge[k, RIM : 2 * RIM, :] = jnp.where(below, none, rim)

    def columns(n):
        return pl.ds(pl.multiple_of(n * 256, 256), 256)

    def spectrum(there, cells):
        @pl.loop(0, SLOTS * 3)
        def _(i):
            k, cols = i // 3, columns(lax.rem(i, 3))
            field[k, :, cols] = dot(there, cells(k, cols))

    def depthwise(there, back, way, turn, cells, store):
        @pl.loop(0, SLOTS * 3)
        def _(i):
            k, cols = i // 3, columns(lax.rem(i, 3))
            z = field[k, :, cols] + dot(there[...], edge[k, :, cols])
            re, im = z[0:HALF_F], z[HALF_F:ALL_F]
            wr, wi = wave[0:HALF_F, cols], way * wave[HALF_F:ALL_F, cols]
            product = jnp.concatenate([re * wr - im * wi, re * wi + im * wr], axis=0).astype(BF)
            store(k, cols, dot(turn[...], cells(k, cols)) + dot(back[...], product))

    def owner_of_row():
        place = iota((SLOT_ROWS, 1), 0) // CAP
        block, shift = place // 16, 2 * (place % 16)
        d = []
        for words in WORDS:
            word = jnp.full(place.shape, words[0])
            for n in range(1, 8):
                word = jnp.where(block == n, words[n], word)
            d.append(jnp.right_shift(word, shift) & 3)
        c = core + d[3] - 2 * core * d[3]
        return (((cy + d[1]) & 3) * 2 + c) * N_SEQ + ((cx + d[0]) & 3) * 4 + ((cz + d[2]) & 3)

    def fill_rows(buf, rows_ref, part):
        slots = slice(part * SLOT_ROWS // 2, (part + 1) * SLOT_ROWS // 2)
        dests = slice(part * HALF_DEV, (part + 1) * HALF_DEV)

        @pl.loop(0, C // 256)
        def _(n):
            c0 = pl.multiple_of(n * 256, 256)
            y0 = dot(hot[slots, :], rows_ref[:, pl.ds(c0, 256)]).reshape(HALF_DEV, CAP, 256)
            y1 = dot(hot[slots, :], rows_ref[:, pl.ds(c0 + C, 256)]).reshape(HALF_DEV, CAP, 256)
            buf[dests, :, pl.ds(c0, 256)] = jnp.concatenate([y0, y1], axis=1).astype(BF)

    def send_rows(buf, rel, got, sems, part):
        for q in others:
            if q // HALF_DEV == part:
                off, f = DESTS[q]
                far = q < N_FAR
                pltpu.make_async_remote_copy(
                    src_ref=buf.at[q], dst_ref=rel.at[q] if far else got.at[me],
                    send_sem=sems.at[0], recv_sem=sems.at[2 if far else 1],
                    device_id=device(first_leg(off, f), 0) if far else device(off, f),
                    device_id_type=pl.DeviceIdType.MESH,
                ).start()

    def forward(rel, got, sems):
        part = rel.at[pl.ds(0, N_FAR)]
        pltpu.make_async_copy(part, part, sems.at[2]).wait()
        for q in range(N_FAR):
            off, f = DESTS[q]
            leg = first_leg(off, f)
            e0, s0 = device([-d % 4 for d in leg], 0)
            pltpu.make_async_remote_copy(
                src_ref=rel.at[q], dst_ref=got.at[e0 * N_SEQ + s0],
                send_sem=sems.at[3], recv_sem=sems.at[1],
                device_id=device([(o - d) % 4 for o, d in zip(off, leg)], f), device_id_type=pl.DeviceIdType.MESH,
            ).start()

    def keep_own(buf, got):
        got[pl.ds(me, 1)] = buf[OWN : OWN + 1]

    def wait_rows(buf, sem):
        part = buf.at[pl.ds(0, N_DEV - 1)]
        pltpu.make_async_copy(part, part, sem).wait()

    ld_tiles.wait()
    for k in range(SLOTS):
        high, low = tiles[k, TH - HALO : TH].reshape(RIM, C), tiles[k, 0:HALO].reshape(RIM, C)
        rimf[enc, k] = jnp.where(lower(k) == 0, high, low)
    pl.semaphore_wait(barrier, N_DEV - 1)
    for q in others:
        e, s = device(*DESTS[q])
        pltpu.make_async_remote_copy(
            src_ref=msg.at[e * N_SEQ + s], dst_ref=rmsg.at[me],
            send_sem=msem.at[0], recv_sem=msem.at[1],
            device_id=(e, s), device_id_type=pl.DeviceIdType.MESH,
        ).start()
    f_send, f_got = rim_copies(rimf, fsend, frecv)
    for n in range(3):
        f_send[n].start()
    owner[...] = owner_of_row()

    def tile_cells(k, cols):
        return tiles[k, :, :, cols].reshape(CELLS, 256)

    def grad_cells(k, cols):
        return mg[k, :, cols]

    ld_grads.wait()
    wait_rows(rmsg, msem.at[1])

    asked = rmsg[...].reshape(N_DEV, 128)
    asked_t = jnp.transpose(asked)[0:CAP, :].astype(BF)
    asked = asked.astype(BF)

    shape = (SLOT_ROWS, 128)
    rows = dot(jnp.where(iota(shape, 1) == owner[...], 1.0, 0.0).astype(BF), asked)
    want = jnp.sum(jnp.where(iota(shape, 1) == iota(shape, 0) % CAP, rows, 0.0), axis=1, keepdims=True).astype(I32)
    hot[...] = jnp.where(iota((SLOT_ROWS, ROWS), 1) == want - 1, 1.0, 0.0).astype(BF)
    for part in range(2):
        fill_rows(gsend, grads, part)
    f_got[0].wait()
    f_send[3].start()
    f_send[5].start()
    f_got[1].wait()
    f_send[4].start()
    f_send[6].start()
    for part in range(2):
        send_rows(gsend, grel, grecv, gsem, part)
    keep_own(gsend, grecv)

    mixb[...] = mixb_ref[...].reshape(1, C)
    downb[...] = downb_ref[...].reshape(1, C2)

    def cell_of(m):
        return ((m % 128) // 16 * 2 + m // 256) * GW + m % 16 * 2 + m // 128 % 2

    p0, p1 = iota((CELLS, CELLS), 0), iota((CELLS, CELLS), 1)
    to_patch[...] = jnp.where(p1 == cell_of(p0), 1.0, 0.0).astype(BF)
    to_cell[...] = jnp.where(p0 == cell_of(p1), 1.0, 0.0).astype(BF)

    taps[...] = jnp.zeros((TAPS, C), F32)
    for a in range(KS):
        taps[8 * a : 8 * a + KS, :] = mixk_ref[a].astype(F32)
    flat_taps = taps[...].astype(BF)
    wave[...] = dot(tap_high[...], flat_taps) + dot(tap_low[...], flat_taps)

    ld_consts[0].wait()
    spectrum(to_f[...], tile_cells)
    forward(grel, grecv, gsem)
    f_got[3].wait()
    f_got[4].wait()
    f_send[7].start()
    for n in (2, 5, 6, 7):
        f_got[n].wait()
    place_rims(rimf)
    ld_consts[1].wait()
    ld_consts[2].wait()

    def store_mixed(k, cols, cells):
        mixed = (cells + mixb[:, cols]).astype(BF)
        A[:, pl.ds(pl.multiple_of(k * 128, 128), 128), cols] = mixed.reshape(4, 128, 256)

    depthwise(rim_f, from_f, 1.0, to_patch, tile_cells, store_mixed)
    ld_w.wait()

    @pl.loop(0, C2 // 256)
    def _(n):
        cols = pl.ds(pl.multiple_of(n * 256, 256), 256)
        pre = jnp.zeros((ROWS, 256), F32) + downb[:, cols]
        for j in range(4):
            pre = pre + dot(A[j], w[j * C : (j + 1) * C, cols])
        phi = 0.5 * (1.0 + lax.erf(pre * SQRT_HALF))
        tok[:, cols] = (pre * phi).astype(BF)
        slope[:, cols] = phi + pre * INV_ROOT * jnp.exp(-0.5 * pre * pre)

    at = owner[...] * CAP + iota((SLOT_ROWS, 1), 0) % CAP
    hot[...] = jnp.where(at == slot_row, 1.0, 0.0).astype(BF)
    for part in range(2):
        fill_rows(tsend, tok, part)
        send_rows(tsend, trel, trecv, tsem, part)
    keep_own(tsend, trecv)

    back_at = ocol * (2 * CAP) + rank_col
    for h in range(2):
        sel[h] = jnp.where(iota((ROWS, 2 * CAP * N_DEV), 1) == back_at + h * CAP, 1.0, 0.0).astype(BF)
    wait_rows(grecv, gsem.at[1])

    def picked(got, h, c0):
        part = got[:, :, pl.ds(pl.multiple_of(c0, 256), 256)].reshape(2 * CAP * N_DEV, 256)
        return dot(sel[h], part)

    @pl.loop(0, C2 // 256)
    def _(n):
        h = n // 3
        cols = pl.ds(pl.multiple_of(n * 256, 256), 256)
        pg[:, cols] = (picked(grecv, h, (n - 3 * h) * 256) * slope[:, cols]).astype(BF)

    forward(trel, trecv, tsem)

    @pl.loop(0, 4 * (C // 256))
    def _(m):
        j, n = m // 3, lax.rem(m, 3)
        part = w[pl.ds(pl.multiple_of(m * 256, 256), 256), :]
        g = lax.dot_general(pg[...], part, (((1,), (1,)), ((), ())), preferred_element_type=F32)
        mg[:, pl.ds(pl.multiple_of(j * 128, 128), 128), columns(n)] = g.astype(BF).reshape(SLOTS, 128, 256)

    def rim_rows(k, rows):
        at = [((r % 2) * 2 + dx) * 128 + (r // 2) * 16 for r in rows for dx in range(2)]
        return jnp.concatenate([mg[k, a : a + 16, :] for a in at], axis=0)

    for k in range(SLOTS):
        rimb[enc, k] = jnp.where(lower(k) == 0, rim_rows(k, range(TH - HALO, TH)), rim_rows(k, range(HALO)))
    b_send, b_got = rim_copies(rimb, bsend, brecv)
    for n in range(3):
        b_send[n].start()
    ld_consts[3].wait()
    spectrum(to_b[...], grad_cells)
    b_got[0].wait()
    b_send[3].start()
    b_send[5].start()
    b_got[1].wait()
    b_send[4].start()
    b_send[6].start()
    b_got[3].wait()
    b_got[4].wait()
    b_send[7].start()
    for n in (2, 5, 6, 7):
        b_got[n].wait()
    place_rims(rimb)
    ld_consts[4].wait()
    ld_consts[5].wait()

    def store_grad(k, cols, cells):
        gout_ref[k, :, :, cols] = cells.astype(BF).reshape(TH, GW, 256)

    depthwise(rim_b, from_b, -1.0, to_cell, grad_cells, store_grad)

    for g in range(N_DEV // N_SEQ):
        shape = (N_DEV, 256)
        at1 = iota(shape, 1)
        over = jnp.where(iota(shape, 0) == g * N_SEQ + at1 // (2 * CAP), 1.0, 0.0).astype(BF)
        rows = dot(asked_t, over)
        k8 = iota((CAP, 256), 1)
        put = jnp.sum(jnp.where(iota((CAP, 256), 0) == k8 % CAP, rows, 0.0), axis=0, keepdims=True).astype(I32)
        hit = iota((ROWS, 256), 0) == put - 1
        part = (iota((ROWS, 256), 1) // CAP) % 2
        for h in range(2):
            sel[h, :, g * 256 : (g + 1) * 256] = jnp.where(hit & (part == h), 1.0, 0.0).astype(BF)
    wait_rows(trecv, tsem.at[1])

    @pl.loop(0, C2 // 256)
    def _(n):
        h = n // 3
        cols = pl.ds(pl.multiple_of(n * 256, 256), 256)
        llm_ref[:, cols] = picked(trecv, h, (n - 3 * h) * 256).astype(BF)

    for n in range(8):
        f_send[n].wait_send()
        b_send[n].wait_send()
    wait_rows(msg, msem.at[0])
    for buf, rel, sems in ((gsend, grel, gsem), (tsend, trel, tsem)):
        wait_rows(buf, sems.at[0])
        part = rel.at[pl.ds(0, N_FAR)]
        pltpu.make_async_copy(part, part, sems.at[3]).wait()


def on_device(frame_tiles, tile_ids, partner_slot, mix_kernel, mix_bias, down_weight, down_bias, token_pos, grad_rows):
    vmem = pl.BlockSpec(memory_space=pltpu.VMEM)
    smem = pl.BlockSpec(memory_space=pltpu.SMEM)
    anyw = pl.BlockSpec(memory_space=pl.ANY)
    dma = pltpu.SemaphoreType.DMA
    llm, gout = pl.pallas_call(
        kernel,
        out_shape=(
            jax.ShapeDtypeStruct((ROWS, C2), BF),
            jax.ShapeDtypeStruct((SLOTS, TH, GW, C), BF),
        ),
        in_specs=[anyw, smem, smem, vmem, vmem, anyw, vmem, vmem, anyw] + [anyw] * 6 + [vmem] * 2,
        out_specs=(vmem, vmem),
        scratch_shapes=[
            pltpu.VMEM((ALL_F, CELLS), BF),
            pltpu.VMEM((ALL_F, CELLS), BF),
            pltpu.VMEM((ALL_F, 2 * RIM), BF),
            pltpu.VMEM((ALL_F, 2 * RIM), BF),
            pltpu.VMEM((CELLS, ALL_F), BF),
            pltpu.VMEM((CELLS, ALL_F), BF),
            pltpu.VMEM((TAPS, C), F32),
            pltpu.VMEM((ALL_F, C), F32),
            pltpu.VMEM((SLOTS, ALL_F, C), F32),
            pltpu.VMEM((SLOTS, 2 * RIM, C), BF),
            pltpu.VMEM((SLOTS, CELLS, C), BF),
            pltpu.VMEM((CELLS, CELLS), BF),
            pltpu.VMEM((CELLS, CELLS), BF),
            pltpu.VMEM((SLOTS, TH, GW, C), BF),
            pltpu.VMEM((4 * C, C2), BF),
            pltpu.VMEM((ROWS, C2), BF),
            pltpu.VMEM((1, C), F32),
            pltpu.VMEM((1, C2), F32),
            pltpu.VMEM((4, ROWS, C), BF),
            pltpu.VMEM((ROWS, C2), F32),
            pltpu.VMEM((ROWS, C2), BF),
            pltpu.VMEM((ROWS, C2), BF),
            pltpu.VMEM((2, ROWS, 2 * CAP * N_DEV), BF),
            pltpu.VMEM((SLOT_ROWS, ROWS), BF),
            pltpu.VMEM((SLOT_ROWS, 1), I32),
            pltpu.VMEM((N_DEV, 1, 128), F32),
            pltpu.VMEM((N_DEV, 1, 128), F32),
            pltpu.VMEM((N_DEV, 2 * CAP, C), BF),
            pltpu.VMEM((N_DEV, 2 * CAP, C), BF),
            pltpu.VMEM((N_FAR, 2 * CAP, C), BF),
            pltpu.VMEM((N_DEV, 2 * CAP, C), BF),
            pltpu.VMEM((N_DEV, 2 * CAP, C), BF),
            pltpu.VMEM((N_FAR, 2 * CAP, C), BF),
            pltpu.VMEM((N_ENC, SLOTS, RIM, C), BF),
            pltpu.VMEM((N_ENC, SLOTS, RIM, C), BF),
            dma((9,)),
            dma((2,)),
            dma((4,)),
            dma((4,)),
            dma((8,)),
            dma((8,)),
            dma((8,)),
            dma((8,)),
        ],
        compiler_params=pltpu.CompilerParams(
            collective_id=0, has_side_effects=True, vmem_limit_bytes=62 * 1024 * 1024
        ),
    )(
        frame_tiles,
        tile_ids,
        partner_slot,
        mix_kernel,
        mix_bias,
        down_weight,
        down_bias,
        token_pos,
        grad_rows,
        *transforms(),
    )
    return llm, gout[None, None]


def solution(mesh):
    return jax.shard_map(
        on_device,
        mesh=mesh,
        in_specs=(
            P("enc", "seq", None, None, None, None),
            P("enc", "seq", None),
            P("enc", "seq", None),
            P(),
            P(),
            P(),
            P(),
            P("enc", "seq", None, None),
            P(("enc", "seq"), None),
        ),
        out_specs=(P(("enc", "seq"), None), P("enc", "seq", None, None, None, None)),
        check_vma=False,
    )
```

```python
import functools

import itertools

import jax
import jax.numpy as jnp
import numpy as np
from jax import lax
from jax.experimental import pallas as pl
from jax.experimental.pallas import tpu as pltpu
from jax.sharding import PartitionSpec as P

C = 768
C2 = 1536
KS = 7
TH = 16
GW = 32
SLOTS = 2
ROWS = 256
N_ENC = 8
N_SEQ = 16
N_DEV = 128
CAP = 8
SLOT_ROWS = CAP * N_DEV

def orbit(o):
    turned = [o, o[2:] + o[:2], o[1:] + o[:1]]
    return [p for q in turned for p in (q, tuple(-d % 4 for d in q))]


ALL_OFFSETS = sorted(itertools.product((0, 1, 3, 2), repeat=3), key=lambda o: -sum(min(d, 4 - d) for d in o))
ORDERED = list(dict.fromkeys(p for o in ALL_OFFSETS for p in orbit(o)))


def relayed(off, f):
    return 2 in off


def first_leg(off, f):
    return tuple(way if d == 2 else 0 for d, way in zip(off, (1 + 2 * f, 3 - 2 * f, 1 + 2 * f)))


PLACES = [(o, f) for o in ORDERED for f in (0, 1) if any(o)] + [((0, 0, 0), 1), ((0, 0, 0), 0)]
DESTS = [p for p in PLACES if relayed(*p)] + [p for p in PLACES if not relayed(*p)]
N_FAR = sum(relayed(*p) for p in PLACES)
OWN = N_DEV - 1
HALF_DEV = N_DEV // 2


def packed(values):
    words = []
    for n in range(0, N_DEV, 16):
        word = sum(v << (2 * i) for i, v in enumerate(values[n : n + 16]))
        words.append(word - (1 << 32) if word >> 31 else word)
    return words


WORDS = [packed([o[axis] for o, f in DESTS]) for axis in range(3)] + [packed([f for o, f in DESTS])]
HALO = 3
CELLS = TH * GW
RIM = HALO * GW
FR, FC = TH + 2 * HALO, GW + HALO
N_FREQ = FR * (FC // 2 + 1)
HALF_F = 400
ALL_F = 2 * HALF_F
TAPS = 8 * KS
SQRT_HALF = 0.7071067811865476
INV_ROOT = 0.3989422804014327
BF = jnp.bfloat16
F32 = jnp.float32
I32 = jnp.int32


def transforms():
    kr, kc = [v.reshape(-1, 1) for v in np.meshgrid(np.arange(FR), np.arange(FC // 2 + 1), indexing="ij")]

    def wave(r, c):
        return np.exp(2j * np.pi * (kr * r / FR + kc * c / FC))

    def rows_of(z):
        out = np.zeros((ALL_F, z.shape[1]))
        out[:N_FREQ], out[HALF_F : HALF_F + N_FREQ] = z.real, z.imag
        return out

    r, c = [v.ravel() for v in np.meshgrid(np.arange(TH), np.arange(GW), indexing="ij")]
    by_patch = np.argsort(((r % 2) * 2 + c % 2) * 128 + (r // 2) * 16 + c // 2)
    rr, rc = [v.ravel() for v in np.meshgrid(np.arange(HALO), np.arange(GW), indexing="ij")]
    rim_patch = np.argsort(rr * GW + (rc % 2) * 16 + rc // 2)
    there = rows_of(np.conj(wave(r, c)))
    rims = [rows_of(np.conj(wave(rr + at, rc))) for at in (-HALO, TH)]
    rim_cells = np.concatenate(rims, axis=1)
    rim_patches = np.concatenate([m[:, rim_patch] for m in rims], axis=1)
    share = np.where(kc == 0, 1.0, 2.0) / (FR * FC)
    back = wave(r, c) * share
    back = (rows_of(np.conj(back))).T
    a, b = np.arange(TAPS) // 8, np.arange(TAPS) % 8
    taps = rows_of(wave(a - HALO, b - HALO) * (b < KS))
    high = taps.astype(BF)
    low = (taps - high.astype(np.float64)).astype(BF)
    return [
        m.astype(BF)
        for m in (there, there[:, by_patch], rim_cells, rim_patches, back[by_patch], back, high, low)
    ]


def iota(shape, axis):
    return lax.broadcasted_iota(I32, shape, axis)


def dot(a, b):
    return jnp.dot(a, b, preferred_element_type=F32)


def kernel(
    tiles_hbm, ids_ref, partner_ref, mixk_ref, mixb_ref, w_hbm, downb_ref, pos_ref, grad_hbm,
    to_f_hbm, to_b_hbm, rim_f_hbm, rim_b_hbm, from_f_hbm, from_b_hbm, tap_high, tap_low,
    llm_hbm, gout_hbm,
    to_f, to_b, rim_f, rim_b, from_f, from_b, taps, wave, field, edge, mg, to_patch, to_cell, llm_ref, gout_ref, osem,
    tiles, w, grads, mixb, downb, A, slope, tok, pg, sel, hot, owner,
    msg, rmsg, gsend, grecv, grel, tsend, trecv, trel, rimf, rimb,
    lsem, msem, gsem, tsem, fsend, frecv, bsend, brecv,
):
    enc = lax.axis_index("enc")
    seq = lax.axis_index("seq")
    me = enc * N_SEQ + seq
    cy, core = enc // 2, enc % 2

    ld_tiles = pltpu.make_async_copy(tiles_hbm.at[0, 0], tiles, lsem.at[0])
    ld_grads = pltpu.make_async_copy(grad_hbm, grads, lsem.at[1])
    ld_w = pltpu.make_async_copy(w_hbm, w, lsem.at[2])
    ld_tiles.start()
    ld_grads.start()
    ld_consts = [
        pltpu.make_async_copy(src, dst, lsem.at[3 + n])
        for n, (src, dst) in enumerate(
            ((to_f_hbm, to_f), (rim_f_hbm, rim_f), (from_f_hbm, from_f), (to_b_hbm, to_b), (rim_b_hbm, rim_b), (from_b_hbm, from_b))
        )
    ]
    for n in range(3):
        ld_consts[n].start()
    ld_w.start()
    for n in range(3, 6):
        ld_consts[n].start()

    cx, cz = seq >> 2, seq & 3
    at_x = [((cx + d) & 3) * 4 for d in range(4)]
    at_y = [((cy + d) & 3) * 2 for d in range(4)]
    at_z = [(cz + d) & 3 for d in range(4)]
    at_core = [core, 1 - core]

    def device(off, f):
        dx, dy, dz = off
        return at_y[dy] + at_core[f], at_x[dx] + at_z[dz]

    others = range(OWN)
    barrier = pltpu.get_barrier_semaphore()
    for q in others:
        pl.semaphore_signal(barrier, inc=1, device_id=device(*DESTS[q]), device_id_type=pl.DeviceIdType.MESH)


    pos = pos_ref[0, 0]
    prow = jnp.concatenate([pos[0:1, :], pos[1:2, :]], axis=1)
    pcol = jnp.concatenate(
        [jnp.transpose(jnp.broadcast_to(pos[i : i + 1, :].astype(F32), (128, 128))) for i in range(2)], axis=0
    ).astype(I32)[:, 0:1]
    orow, ocol = prow // ROWS, pcol // ROWS
    lcol = pcol - ocol * ROWS
    same = jnp.broadcast_to(ocol, (ROWS, ROWS)) == jnp.broadcast_to(orow, (ROWS, ROWS))
    at0, at1 = iota((ROWS, ROWS), 0), iota((ROWS, ROWS), 1)
    rank_row = jnp.sum(jnp.where(same & (at0 < at1), 1.0, 0.0), axis=0, keepdims=True).astype(I32)
    rank_col = jnp.sum(jnp.where(same & (at1 < at0), 1.0, 0.0), axis=1, keepdims=True).astype(I32)
    slot_row = orow * CAP + rank_row
    to_owner = jnp.where(iota((N_DEV, ROWS), 0) == orow, 1.0, 0.0).astype(BF)
    ranked = jnp.where(iota((ROWS, 128), 1) == rank_col, (lcol + 1).astype(F32), 0.0).astype(BF)
    msg[...] = dot(to_owner, ranked).reshape(N_DEV, 1, 128)
    rmsg[pl.ds(me, 1)] = msg[pl.ds(me, 1)]

    def lower(k):
        return lax.rem(ids_ref[0, 0, k], 2)

    up = lax.rem(cy + 1, 4) * 2 + core
    down = lax.rem(cy + 3, 4) * 2 + core
    across = lax.rem(cy + 2, 4) * 2 + core
    sib = cy * 2 + 1 - core

    def rim_copies(rims, ssem, rsem):
        def copy(n, ref, to):
            return pltpu.make_async_remote_copy(
                src_ref=ref, dst_ref=ref, send_sem=ssem.at[n], recv_sem=rsem.at[n],
                device_id=(to, seq), device_id_type=pl.DeviceIdType.MESH,
            )

        def landed(n, ref):
            return pltpu.make_async_copy(ref, ref, rsem.at[n])

        sends = [
            copy(0, rims.at[enc], up),
            copy(1, rims.at[enc], down),
            copy(2, rims.at[enc], sib),
            copy(3, rims.at[down, 0], up),
            copy(4, rims.at[up, 1], down),
            copy(5, rims.at[down], sib),
            copy(6, rims.at[up], sib),
            copy(7, rims.at[across], sib),
        ]
        other = 1 - 2 * core
        arrivals = [
            landed(0, rims.at[down]),
            landed(1, rims.at[up]),
            landed(2, rims.at[sib]),
            landed(3, rims.at[across, 0]),
            landed(4, rims.at[across, 1]),
            landed(5, rims.at[down + other]),
            landed(6, rims.at[up + other]),
            landed(7, rims.at[across + other]),
        ]
        return sends, arrivals

    def place_rims(rims):
        for k in range(SLOTS):
            want = partner_ref[0, 0, k]
            rim = jnp.zeros((RIM, C), BF)
            for q in range(N_ENC * SLOTS):
                rim = jnp.where(want == q, rims[q // 2, q % 2], rim)
            none = jnp.zeros((RIM, C), BF)
            below = lower(k) == 1
            edge[k, 0:RIM, :] = jnp.where(below, rim, none)
            edge[k, RIM : 2 * RIM, :] = jnp.where(below, none, rim)

    def columns(n):
        return pl.ds(pl.multiple_of(n * 256, 256), 256)

    def spectrum(there, cells):
        @pl.loop(0, SLOTS * 3)
        def _(i):
            k, cols = i // 3, columns(lax.rem(i, 3))
            field[k, :, cols] = dot(there, cells(k, cols))

    def depthwise(there, back, way, turn, cells, store):
        @pl.loop(0, SLOTS * 3)
        def _(i):
            k, cols = i // 3, columns(lax.rem(i, 3))
            z = field[k, :, cols] + dot(there[...], edge[k, :, cols])
            re, im = z[0:HALF_F], z[HALF_F:ALL_F]
            wr, wi = wave[0:HALF_F, cols], way * wave[HALF_F:ALL_F, cols]
            product = jnp.concatenate([re * wr - im * wi, re * wi + im * wr], axis=0).astype(BF)
            store(k, cols, dot(turn[...], cells(k, cols)) + dot(back[...], product))

    def owner_of_row():
        place = iota((SLOT_ROWS, 1), 0) // CAP
        block, shift = place // 16, 2 * (place % 16)
        d = []
        for words in WORDS:
            word = jnp.full(place.shape, words[0])
            for n in range(1, 8):
                word = jnp.where(block == n, words[n], word)
            d.append(jnp.right_shift(word, shift) & 3)
        c = core + d[3] - 2 * core * d[3]
        return (((cy + d[1]) & 3) * 2 + c) * N_SEQ + ((cx + d[0]) & 3) * 4 + ((cz + d[2]) & 3)

    def fill_rows(buf, rows_ref, part):
        slots = slice(part * SLOT_ROWS // 2, (part + 1) * SLOT_ROWS // 2)
        dests = slice(part * HALF_DEV, (part + 1) * HALF_DEV)

        @pl.loop(0, C // 256)
        def _(n):
            c0 = pl.multiple_of(n * 256, 256)
            y0 = dot(hot[slots, :], rows_ref[:, pl.ds(c0, 256)]).reshape(HALF_DEV, CAP, 256)
            y1 = dot(hot[slots, :], rows_ref[:, pl.ds(c0 + C, 256)]).reshape(HALF_DEV, CAP, 256)
            buf[dests, :, pl.ds(c0, 256)] = jnp.concatenate([y0, y1], axis=1).astype(BF)

    def send_rows(buf, rel, got, sems, chosen):
        for q in chosen:
            off, f = DESTS[q]
            far = q < N_FAR
            pltpu.make_async_remote_copy(
                src_ref=buf.at[q], dst_ref=rel.at[q] if far else got.at[me],
                send_sem=sems.at[0], recv_sem=sems.at[2 if far else 1],
                device_id=device(first_leg(off, f), 0) if far else device(off, f),
                device_id_type=pl.DeviceIdType.MESH,
            ).start()

    def forward(rel, got, sems):
        part = rel.at[pl.ds(0, N_FAR)]
        pltpu.make_async_copy(part, part, sems.at[2]).wait()
        for q in range(N_FAR):
            off, f = DESTS[q]
            leg = first_leg(off, f)
            e0, s0 = device([-d % 4 for d in leg], 0)
            pltpu.make_async_remote_copy(
                src_ref=rel.at[q], dst_ref=got.at[e0 * N_SEQ + s0],
                send_sem=sems.at[3], recv_sem=sems.at[1],
                device_id=device([(o - d) % 4 for o, d in zip(off, leg)], f), device_id_type=pl.DeviceIdType.MESH,
            ).start()

    def keep_own(buf, got):
        got[pl.ds(me, 1)] = buf[OWN : OWN + 1]

    def wait_rows(buf, sem):
        part = buf.at[pl.ds(0, N_DEV - 1)]
        pltpu.make_async_copy(part, part, sem).wait()

    ld_tiles.wait()
    for k in range(SLOTS):
        high, low = tiles[k, TH - HALO : TH].reshape(RIM, C), tiles[k, 0:HALO].reshape(RIM, C)
        rimf[enc, k] = jnp.where(lower(k) == 0, high, low)
    pl.semaphore_wait(barrier, N_DEV - 1)
    for q in others:
        e, s = device(*DESTS[q])
        pltpu.make_async_remote_copy(
            src_ref=msg.at[e * N_SEQ + s], dst_ref=rmsg.at[me],
            send_sem=msem.at[0], recv_sem=msem.at[1],
            device_id=(e, s), device_id_type=pl.DeviceIdType.MESH,
        ).start()
    f_send, f_got = rim_copies(rimf, fsend, frecv)
    for n in range(3):
        f_send[n].start()
    owner[...] = owner_of_row()

    def tile_cells(k, cols):
        return tiles[k, :, :, cols].reshape(CELLS, 256)

    def grad_cells(k, cols):
        return mg[k, :, cols]

    ld_grads.wait()
    wait_rows(rmsg, msem.at[1])

    asked = rmsg[...].reshape(N_DEV, 128)
    asked_t = jnp.transpose(asked)[0:CAP, :].astype(BF)
    asked = asked.astype(BF)

    shape = (SLOT_ROWS, 128)
    rows = dot(jnp.where(iota(shape, 1) == owner[...], 1.0, 0.0).astype(BF), asked)
    want = jnp.sum(jnp.where(iota(shape, 1) == iota(shape, 0) % CAP, rows, 0.0), axis=1, keepdims=True).astype(I32)
    hot[...] = jnp.where(iota((SLOT_ROWS, ROWS), 1) == want - 1, 1.0, 0.0).astype(BF)
    for part in range(2):
        fill_rows(gsend, grads, part)
    send_rows(gsend, grel, grecv, gsem, [q for q in others if DESTS[q][0][1] == 0])
    f_got[0].wait()
    f_send[3].start()
    f_send[5].start()
    f_got[1].wait()
    f_send[4].start()
    f_send[6].start()
    send_rows(gsend, grel, grecv, gsem, [q for q in others if DESTS[q][0][1] != 0])
    keep_own(gsend, grecv)

    mixb[...] = mixb_ref[...].reshape(1, C)
    downb[...] = downb_ref[...].reshape(1, C2)

    def cell_of(m):
        return ((m % 128) // 16 * 2 + m // 256) * GW + m % 16 * 2 + m // 128 % 2

    p0, p1 = iota((CELLS, CELLS), 0), iota((CELLS, CELLS), 1)
    to_patch[...] = jnp.where(p1 == cell_of(p0), 1.0, 0.0).astype(BF)
    to_cell[...] = jnp.where(p0 == cell_of(p1), 1.0, 0.0).astype(BF)

    taps[...] = jnp.zeros((TAPS, C), F32)
    for a in range(KS):
        taps[8 * a : 8 * a + KS, :] = mixk_ref[a].astype(F32)
    flat_taps = taps[...].astype(BF)
    wave[...] = dot(tap_high[...], flat_taps) + dot(tap_low[...], flat_taps)

    ld_consts[0].wait()
    spectrum(to_f[...], tile_cells)
    forward(grel, grecv, gsem)
    f_got[3].wait()
    f_got[4].wait()
    f_send[7].start()
    for n in (2, 5, 6, 7):
        f_got[n].wait()
    place_rims(rimf)
    ld_consts[1].wait()
    ld_consts[2].wait()

    def store_mixed(k, cols, cells):
        mixed = (cells + mixb[:, cols]).astype(BF)
        A[:, pl.ds(pl.multiple_of(k * 128, 128), 128), cols] = mixed.reshape(4, 128, 256)

    depthwise(rim_f, from_f, 1.0, to_patch, tile_cells, store_mixed)
    ld_w.wait()

    @pl.loop(0, C2 // 256)
    def _(n):
        cols = pl.ds(pl.multiple_of(n * 256, 256), 256)
        pre = jnp.zeros((ROWS, 256), F32) + downb[:, cols]
        for j in range(4):
            pre = pre + dot(A[j], w[j * C : (j + 1) * C, cols])
        phi = 0.5 * (1.0 + lax.erf(pre * SQRT_HALF))
        tok[:, cols] = (pre * phi).astype(BF)
        slope[:, cols] = phi + pre * INV_ROOT * jnp.exp(-0.5 * pre * pre)

    at = owner[...] * CAP + iota((SLOT_ROWS, 1), 0) % CAP
    hot[...] = jnp.where(at == slot_row, 1.0, 0.0).astype(BF)
    for part in range(2):
        fill_rows(tsend, tok, part)
        send_rows(tsend, trel, trecv, tsem, others[part * HALF_DEV : (part + 1) * HALF_DEV])
    keep_own(tsend, trecv)

    back_at = ocol * (2 * CAP) + rank_col
    for h in range(2):
        sel[h] = jnp.where(iota((ROWS, 2 * CAP * N_DEV), 1) == back_at + h * CAP, 1.0, 0.0).astype(BF)
    wait_rows(grecv, gsem.at[1])

    def picked(got, h, c0):
        part = got[:, :, pl.ds(pl.multiple_of(c0, 256), 256)].reshape(2 * CAP * N_DEV, 256)
        return dot(sel[h], part)

    @pl.loop(0, C2 // 256)
    def _(n):
        h = n // 3
        cols = pl.ds(pl.multiple_of(n * 256, 256), 256)
        pg[:, cols] = (picked(grecv, h, (n - 3 * h) * 256) * slope[:, cols]).astype(BF)

    @pl.loop(0, 4 * (C // 256))
    def _(m):
        j, n = m // 3, lax.rem(m, 3)
        part = w[pl.ds(pl.multiple_of(m * 256, 256), 256), :]
        g = lax.dot_general(pg[...], part, (((1,), (1,)), ((), ())), preferred_element_type=F32)
        mg[:, pl.ds(pl.multiple_of(j * 128, 128), 128), columns(n)] = g.astype(BF).reshape(SLOTS, 128, 256)

    def rim_rows(k, rows):
        at = [((r % 2) * 2 + dx) * 128 + (r // 2) * 16 for r in rows for dx in range(2)]
        return jnp.concatenate([mg[k, a : a + 16, :] for a in at], axis=0)

    for k in range(SLOTS):
        rimb[enc, k] = jnp.where(lower(k) == 0, rim_rows(k, range(TH - HALO, TH)), rim_rows(k, range(HALO)))
    b_send, b_got = rim_copies(rimb, bsend, brecv)
    for n in range(3):
        b_send[n].start()
    forward(trel, trecv, tsem)
    ld_consts[3].wait()
    spectrum(to_b[...], grad_cells)
    b_got[0].wait()
    b_send[3].start()
    b_send[5].start()
    b_got[1].wait()
    b_send[4].start()
    b_send[6].start()
    b_got[3].wait()
    b_got[4].wait()
    b_send[7].start()
    for n in (2, 5, 6, 7):
        b_got[n].wait()
    place_rims(rimb)
    ld_consts[4].wait()
    ld_consts[5].wait()

    def store_grad(k, cols, cells):
        gout_ref[k, :, :, cols] = cells.astype(BF).reshape(TH, GW, 256)

    depthwise(rim_b, from_b, -1.0, to_cell, grad_cells, store_grad)
    put_gout = pltpu.make_async_copy(gout_ref, gout_hbm, osem.at[6])
    put_gout.start()

    for g in range(N_DEV // N_SEQ):
        shape = (N_DEV, 256)
        at1 = iota(shape, 1)
        over = jnp.where(iota(shape, 0) == g * N_SEQ + at1 // (2 * CAP), 1.0, 0.0).astype(BF)
        rows = dot(asked_t, over)
        k8 = iota((CAP, 256), 1)
        put = jnp.sum(jnp.where(iota((CAP, 256), 0) == k8 % CAP, rows, 0.0), axis=0, keepdims=True).astype(I32)
        hit = iota((ROWS, 256), 0) == put - 1
        part = (iota((ROWS, 256), 1) // CAP) % 2
        for h in range(2):
            sel[h, :, g * 256 : (g + 1) * 256] = jnp.where(hit & (part == h), 1.0, 0.0).astype(BF)
    wait_rows(trecv, tsem.at[1])

    @pl.loop(0, C2 // 256)
    def _(n):
        h = n // 3
        cols = pl.ds(pl.multiple_of(n * 256, 256), 256)
        llm_ref[:, cols] = picked(trecv, h, (n - 3 * h) * 256).astype(BF)
        pltpu.make_async_copy(llm_ref.at[:, cols], llm_hbm.at[:, cols], osem.at[n]).start()

    for n in range(C2 // 256):
        cols = pl.ds(n * 256, 256)
        pltpu.make_async_copy(llm_ref.at[:, cols], llm_hbm.at[:, cols], osem.at[n]).wait()
    put_gout.wait()
    for n in range(8):
        f_send[n].wait_send()
        b_send[n].wait_send()
    wait_rows(msg, msem.at[0])
    for buf, rel, sems in ((gsend, grel, gsem), (tsend, trel, tsem)):
        wait_rows(buf, sems.at[0])
        part = rel.at[pl.ds(0, N_FAR)]
        pltpu.make_async_copy(part, part, sems.at[3]).wait()


def on_device(frame_tiles, tile_ids, partner_slot, mix_kernel, mix_bias, down_weight, down_bias, token_pos, grad_rows):
    vmem = pl.BlockSpec(memory_space=pltpu.VMEM)
    smem = pl.BlockSpec(memory_space=pltpu.SMEM)
    anyw = pl.BlockSpec(memory_space=pl.ANY)
    dma = pltpu.SemaphoreType.DMA
    llm, gout = pl.pallas_call(
        kernel,
        out_shape=(
            jax.ShapeDtypeStruct((ROWS, C2), BF),
            jax.ShapeDtypeStruct((SLOTS, TH, GW, C), BF),
        ),
        in_specs=[anyw, smem, smem, vmem, vmem, anyw, vmem, vmem, anyw] + [anyw] * 6 + [vmem] * 2,
        out_specs=(anyw, anyw),
        scratch_shapes=[
            pltpu.VMEM((ALL_F, CELLS), BF),
            pltpu.VMEM((ALL_F, CELLS), BF),
            pltpu.VMEM((ALL_F, 2 * RIM), BF),
            pltpu.VMEM((ALL_F, 2 * RIM), BF),
            pltpu.VMEM((CELLS, ALL_F), BF),
            pltpu.VMEM((CELLS, ALL_F), BF),
            pltpu.VMEM((TAPS, C), F32),
            pltpu.VMEM((ALL_F, C), F32),
            pltpu.VMEM((SLOTS, ALL_F, C), F32),
            pltpu.VMEM((SLOTS, 2 * RIM, C), BF),
            pltpu.VMEM((SLOTS, CELLS, C), BF),
            pltpu.VMEM((CELLS, CELLS), BF),
            pltpu.VMEM((CELLS, CELLS), BF),
            pltpu.VMEM((ROWS, C2), BF),
            pltpu.VMEM((SLOTS, TH, GW, C), BF),
            dma((7,)),
            pltpu.VMEM((SLOTS, TH, GW, C), BF),
            pltpu.VMEM((4 * C, C2), BF),
            pltpu.VMEM((ROWS, C2), BF),
            pltpu.VMEM((1, C), F32),
            pltpu.VMEM((1, C2), F32),
            pltpu.VMEM((4, ROWS, C), BF),
            pltpu.VMEM((ROWS, C2), F32),
            pltpu.VMEM((ROWS, C2), BF),
            pltpu.VMEM((ROWS, C2), BF),
            pltpu.VMEM((2, ROWS, 2 * CAP * N_DEV), BF),
            pltpu.VMEM((SLOT_ROWS, ROWS), BF),
            pltpu.VMEM((SLOT_ROWS, 1), I32),
            pltpu.VMEM((N_DEV, 1, 128), F32),
            pltpu.VMEM((N_DEV, 1, 128), F32),
            pltpu.VMEM((N_DEV, 2 * CAP, C), BF),
            pltpu.VMEM((N_DEV, 2 * CAP, C), BF),
            pltpu.VMEM((N_FAR, 2 * CAP, C), BF),
            pltpu.VMEM((N_DEV, 2 * CAP, C), BF),
            pltpu.VMEM((N_DEV, 2 * CAP, C), BF),
            pltpu.VMEM((N_FAR, 2 * CAP, C), BF),
            pltpu.VMEM((N_ENC, SLOTS, RIM, C), BF),
            pltpu.VMEM((N_ENC, SLOTS, RIM, C), BF),
            dma((9,)),
            dma((2,)),
            dma((4,)),
            dma((4,)),
            dma((8,)),
            dma((8,)),
            dma((8,)),
            dma((8,)),
        ],
        compiler_params=pltpu.CompilerParams(
            collective_id=0, has_side_effects=True, vmem_limit_bytes=62 * 1024 * 1024
        ),
    )(
        frame_tiles,
        tile_ids,
        partner_slot,
        mix_kernel,
        mix_bias,
        down_weight,
        down_bias,
        token_pos,
        grad_rows,
        *transforms(),
    )
    return llm, gout[None, None]


def solution(mesh):
    return jax.shard_map(
        on_device,
        mesh=mesh,
        in_specs=(
            P("enc", "seq", None, None, None, None),
            P("enc", "seq", None),
            P("enc", "seq", None),
            P(),
            P(),
            P(),
            P(),
            P("enc", "seq", None, None),
            P(("enc", "seq"), None),
        ),
        out_specs=(P(("enc", "seq"), None), P("enc", "seq", None, None, None, None)),
        check_vma=False,
    )
```

```python
import functools

import itertools

import jax
import jax.numpy as jnp
import numpy as np
from jax import lax
from jax.experimental import pallas as pl
from jax.experimental.pallas import tpu as pltpu
from jax.sharding import PartitionSpec as P

C = 768
C2 = 1536
KS = 7
TH = 16
GW = 32
SLOTS = 2
ROWS = 256
N_ENC = 8
N_SEQ = 16
N_DEV = 128
CAP = 8
SLOT_ROWS = CAP * N_DEV

def orbit(o):
    turned = [o, o[2:] + o[:2], o[1:] + o[:1]]
    return [p for q in turned for p in (q, tuple(-d % 4 for d in q))]


ALL_OFFSETS = sorted(itertools.product((0, 1, 3, 2), repeat=3), key=lambda o: -sum(min(d, 4 - d) for d in o))
ORDERED = list(dict.fromkeys(p for o in ALL_OFFSETS for p in orbit(o)))


def relayed(off, f):
    return 2 in off


def first_leg(off, f):
    return tuple(way if d == 2 else 0 for d, way in zip(off, (1 + 2 * f, 3 - 2 * f, 1 + 2 * f)))


PLACES = [(o, f) for o in ORDERED for f in (0, 1) if any(o)] + [((0, 0, 0), 1), ((0, 0, 0), 0)]
DESTS = [p for p in PLACES if relayed(*p)] + [p for p in PLACES if not relayed(*p)]
N_FAR = sum(relayed(*p) for p in PLACES)
OWN = N_DEV - 1
HALF_DEV = N_DEV // 2


def packed(values):
    words = []
    for n in range(0, N_DEV, 16):
        word = sum(v << (2 * i) for i, v in enumerate(values[n : n + 16]))
        words.append(word - (1 << 32) if word >> 31 else word)
    return words


WORDS = [packed([o[axis] for o, f in DESTS]) for axis in range(3)] + [packed([f for o, f in DESTS])]
HALO = 3
CELLS = TH * GW
RIM = HALO * GW
FR, FC = TH + 2 * HALO, GW + HALO
N_FREQ = FR * (FC // 2 + 1)
HALF_F = 400
ALL_F = 2 * HALF_F
TAPS = 8 * KS
SQRT_HALF = 0.7071067811865476
INV_ROOT = 0.3989422804014327
BF = jnp.bfloat16
F32 = jnp.float32
I32 = jnp.int32


def transforms():
    kr, kc = [v.reshape(-1, 1) for v in np.meshgrid(np.arange(FR), np.arange(FC // 2 + 1), indexing="ij")]

    def wave(r, c):
        return np.exp(2j * np.pi * (kr * r / FR + kc * c / FC))

    def rows_of(z):
        out = np.zeros((ALL_F, z.shape[1]))
        out[:N_FREQ], out[HALF_F : HALF_F + N_FREQ] = z.real, z.imag
        return out

    r, c = [v.ravel() for v in np.meshgrid(np.arange(TH), np.arange(GW), indexing="ij")]
    by_patch = np.argsort(((r % 2) * 2 + c % 2) * 128 + (r // 2) * 16 + c // 2)
    rr, rc = [v.ravel() for v in np.meshgrid(np.arange(HALO), np.arange(GW), indexing="ij")]
    rim_patch = np.argsort(rr * GW + (rc % 2) * 16 + rc // 2)
    there = rows_of(np.conj(wave(r, c)))
    rims = [rows_of(np.conj(wave(rr + at, rc))) for at in (-HALO, TH)]
    rim_cells = np.concatenate(rims, axis=1)
    rim_patches = np.concatenate([m[:, rim_patch] for m in rims], axis=1)
    share = np.where(kc == 0, 1.0, 2.0) / (FR * FC)
    back = wave(r, c) * share
    back = (rows_of(np.conj(back))).T
    a, b = np.arange(TAPS) // 8, np.arange(TAPS) % 8
    taps = rows_of(wave(a - HALO, b - HALO) * (b < KS))
    high = taps.astype(BF)
    low = (taps - high.astype(np.float64)).astype(BF)
    return [
        m.astype(BF)
        for m in (there, there[:, by_patch], rim_cells, rim_patches, back[by_patch], back, high, low)
    ]


def iota(shape, axis):
    return lax.broadcasted_iota(I32, shape, axis)


def dot(a, b):
    return jnp.dot(a, b, preferred_element_type=F32)


def kernel(
    tiles_hbm, ids_ref, partner_ref, mixk_ref, mixb_ref, w_hbm, downb_ref, pos_ref, grad_hbm,
    to_f_hbm, to_b_hbm, rim_f_hbm, rim_b_hbm, from_f_hbm, from_b_hbm, tap_high, tap_low,
    llm_hbm, gout_hbm,
    to_f, to_b, rim_f, rim_b, from_f, from_b, taps, wave, field, edge, mg, to_patch, to_cell, llm_ref, gout_ref, osem,
    tiles, w, grads, mixb, downb, A, slope, tok, pg, sel, hot, owner,
    msg, rmsg, gsend, grecv, grel, tsend, trecv, trel, rimf, rimb,
    lsem, msem, gsem, tsem, fsend, frecv, bsend, brecv,
):
    enc = lax.axis_index("enc")
    seq = lax.axis_index("seq")
    me = enc * N_SEQ + seq
    cy, core = enc // 2, enc % 2

    ld_tiles = pltpu.make_async_copy(tiles_hbm.at[0, 0], tiles, lsem.at[0])
    ld_grads = pltpu.make_async_copy(grad_hbm, grads, lsem.at[1])
    ld_w = pltpu.make_async_copy(w_hbm, w, lsem.at[2])
    ld_tiles.start()
    ld_grads.start()
    ld_consts = [
        pltpu.make_async_copy(src, dst, lsem.at[3 + n])
        for n, (src, dst) in enumerate(
            ((to_f_hbm, to_f), (rim_f_hbm, rim_f), (from_f_hbm, from_f), (to_b_hbm, to_b), (rim_b_hbm, rim_b), (from_b_hbm, from_b))
        )
    ]
    for n in range(3):
        ld_consts[n].start()
    ld_w.start()
    for n in range(3, 6):
        ld_consts[n].start()

    cx, cz = seq >> 2, seq & 3
    at_x = [((cx + d) & 3) * 4 for d in range(4)]
    at_y = [((cy + d) & 3) * 2 for d in range(4)]
    at_z = [(cz + d) & 3 for d in range(4)]
    at_core = [core, 1 - core]

    def device(off, f):
        dx, dy, dz = off
        return at_y[dy] + at_core[f], at_x[dx] + at_z[dz]

    others = range(OWN)
    barrier = pltpu.get_barrier_semaphore()
    for q in others:
        pl.semaphore_signal(barrier, inc=1, device_id=device(*DESTS[q]), device_id_type=pl.DeviceIdType.MESH)


    pos = pos_ref[0, 0]
    prow = jnp.concatenate([pos[0:1, :], pos[1:2, :]], axis=1)
    pcol = jnp.concatenate(
        [jnp.transpose(jnp.broadcast_to(pos[i : i + 1, :].astype(F32), (128, 128))) for i in range(2)], axis=0
    ).astype(I32)[:, 0:1]
    orow, ocol = prow // ROWS, pcol // ROWS
    lcol = pcol - ocol * ROWS
    same = jnp.broadcast_to(ocol, (ROWS, ROWS)) == jnp.broadcast_to(orow, (ROWS, ROWS))
    at0, at1 = iota((ROWS, ROWS), 0), iota((ROWS, ROWS), 1)
    rank_row = jnp.sum(jnp.where(same & (at0 < at1), 1.0, 0.0), axis=0, keepdims=True).astype(I32)
    rank_col = jnp.sum(jnp.where(same & (at1 < at0), 1.0, 0.0), axis=1, keepdims=True).astype(I32)
    slot_row = orow * CAP + rank_row
    to_owner = jnp.where(iota((N_DEV, ROWS), 0) == orow, 1.0, 0.0).astype(BF)
    ranked = jnp.where(iota((ROWS, 128), 1) == rank_col, (lcol + 1).astype(F32), 0.0).astype(BF)
    msg[...] = dot(to_owner, ranked).reshape(N_DEV, 1, 128)
    rmsg[pl.ds(me, 1)] = msg[pl.ds(me, 1)]

    def lower(k):
        return lax.rem(ids_ref[0, 0, k], 2)

    up = lax.rem(cy + 1, 4) * 2 + core
    down = lax.rem(cy + 3, 4) * 2 + core
    across = lax.rem(cy + 2, 4) * 2 + core
    sib = cy * 2 + 1 - core

    def rim_copies(rims, ssem, rsem):
        def copy(n, ref, to):
            return pltpu.make_async_remote_copy(
                src_ref=ref, dst_ref=ref, send_sem=ssem.at[n], recv_sem=rsem.at[n],
                device_id=(to, seq), device_id_type=pl.DeviceIdType.MESH,
            )

        def landed(n, ref):
            return pltpu.make_async_copy(ref, ref, rsem.at[n])

        sends = [
            copy(0, rims.at[enc], up),
            copy(1, rims.at[enc], down),
            copy(2, rims.at[enc], sib),
            copy(3, rims.at[down, 0], up),
            copy(4, rims.at[up, 1], down),
            copy(5, rims.at[down], sib),
            copy(6, rims.at[up], sib),
            copy(7, rims.at[across], sib),
        ]
        other = 1 - 2 * core
        arrivals = [
            landed(0, rims.at[down]),
            landed(1, rims.at[up]),
            landed(2, rims.at[sib]),
            landed(3, rims.at[across, 0]),
            landed(4, rims.at[across, 1]),
            landed(5, rims.at[down + other]),
            landed(6, rims.at[up + other]),
            landed(7, rims.at[across + other]),
        ]
        return sends, arrivals

    def place_rims(rims):
        for k in range(SLOTS):
            want = partner_ref[0, 0, k]
            rim = jnp.zeros((RIM, C), BF)
            for q in range(N_ENC * SLOTS):
                rim = jnp.where(want == q, rims[q // 2, q % 2], rim)
            none = jnp.zeros((RIM, C), BF)
            below = lower(k) == 1
            edge[k, 0:RIM, :] = jnp.where(below, rim, none)
            edge[k, RIM : 2 * RIM, :] = jnp.where(below, none, rim)

    def columns(n):
        return pl.ds(pl.multiple_of(n * 256, 256), 256)

    def spectrum(there, cells):
        @pl.loop(0, SLOTS * 3)
        def _(i):
            k, cols = i // 3, columns(lax.rem(i, 3))
            field[k, :, cols] = dot(there, cells(k, cols))

    def depthwise(there, back, way, turn, cells, store):
        @pl.loop(0, SLOTS * 3)
        def _(i):
            k, cols = i // 3, columns(lax.rem(i, 3))
            z = field[k, :, cols] + dot(there[...], edge[k, :, cols])
            re, im = z[0:HALF_F], z[HALF_F:ALL_F]
            wr, wi = wave[0:HALF_F, cols], way * wave[HALF_F:ALL_F, cols]
            product = jnp.concatenate([re * wr - im * wi, re * wi + im * wr], axis=0).astype(BF)
            store(k, cols, dot(turn[...], cells(k, cols)) + dot(back[...], product))

    def owner_of_row():
        place = iota((SLOT_ROWS, 1), 0) // CAP
        block, shift = place // 16, 2 * (place % 16)
        d = []
        for words in WORDS:
            word = jnp.full(place.shape, words[0])
            for n in range(1, 8):
                word = jnp.where(block == n, words[n], word)
            d.append(jnp.right_shift(word, shift) & 3)
        c = core + d[3] - 2 * core * d[3]
        return (((cy + d[1]) & 3) * 2 + c) * N_SEQ + ((cx + d[0]) & 3) * 4 + ((cz + d[2]) & 3)

    def fill_rows(buf, rows_ref, part):
        slots = slice(part * SLOT_ROWS // 2, (part + 1) * SLOT_ROWS // 2)
        dests = slice(part * HALF_DEV, (part + 1) * HALF_DEV)

        @pl.loop(0, C // 256)
        def _(n):
            c0 = pl.multiple_of(n * 256, 256)
            y0 = dot(hot[slots, :], rows_ref[:, pl.ds(c0, 256)]).reshape(HALF_DEV, CAP, 256)
            y1 = dot(hot[slots, :], rows_ref[:, pl.ds(c0 + C, 256)]).reshape(HALF_DEV, CAP, 256)
            buf[dests, :, pl.ds(c0, 256)] = jnp.concatenate([y0, y1], axis=1).astype(BF)

    def send_rows(buf, rel, got, sems, chosen):
        for q in chosen:
            off, f = DESTS[q]
            far = q < N_FAR
            pltpu.make_async_remote_copy(
                src_ref=buf.at[q], dst_ref=rel.at[q] if far else got.at[me],
                send_sem=sems.at[0], recv_sem=sems.at[2 if far else 1],
                device_id=device(first_leg(off, f), 0) if far else device(off, f),
                device_id_type=pl.DeviceIdType.MESH,
            ).start()

    def forward(rel, got, sems):
        part = rel.at[pl.ds(0, N_FAR)]
        pltpu.make_async_copy(part, part, sems.at[2]).wait()
        for q in range(N_FAR):
            off, f = DESTS[q]
            leg = first_leg(off, f)
            e0, s0 = device([-d % 4 for d in leg], 0)
            pltpu.make_async_remote_copy(
                src_ref=rel.at[q], dst_ref=got.at[e0 * N_SEQ + s0],
                send_sem=sems.at[3], recv_sem=sems.at[1],
                device_id=device([(o - d) % 4 for o, d in zip(off, leg)], f), device_id_type=pl.DeviceIdType.MESH,
            ).start()

    def keep_own(buf, got):
        got[pl.ds(me, 1)] = buf[OWN : OWN + 1]

    def wait_rows(buf, sem):
        part = buf.at[pl.ds(0, N_DEV - 1)]
        pltpu.make_async_copy(part, part, sem).wait()

    ld_tiles.wait()
    for k in range(SLOTS):
        high, low = tiles[k, TH - HALO : TH].reshape(RIM, C), tiles[k, 0:HALO].reshape(RIM, C)
        rimf[enc, k] = jnp.where(lower(k) == 0, high, low)
    pl.semaphore_wait(barrier, N_DEV - 1)
    for q in others:
        e, s = device(*DESTS[q])
        pltpu.make_async_remote_copy(
            src_ref=msg.at[e * N_SEQ + s], dst_ref=rmsg.at[me],
            send_sem=msem.at[0], recv_sem=msem.at[1],
            device_id=(e, s), device_id_type=pl.DeviceIdType.MESH,
        ).start()
    f_send, f_got = rim_copies(rimf, fsend, frecv)
    for n in range(3):
        f_send[n].start()
    owner[...] = owner_of_row()

    def tile_cells(k, cols):
        return tiles[k, :, :, cols].reshape(CELLS, 256)

    def grad_cells(k, cols):
        return mg[k, :, cols]

    ld_grads.wait()
    wait_rows(rmsg, msem.at[1])

    asked = rmsg[...].reshape(N_DEV, 128)
    asked_t = jnp.transpose(asked)[0:CAP, :].astype(BF)
    asked = asked.astype(BF)

    shape = (SLOT_ROWS, 128)
    rows = dot(jnp.where(iota(shape, 1) == owner[...], 1.0, 0.0).astype(BF), asked)
    want = jnp.sum(jnp.where(iota(shape, 1) == iota(shape, 0) % CAP, rows, 0.0), axis=1, keepdims=True).astype(I32)
    hot[...] = jnp.where(iota((SLOT_ROWS, ROWS), 1) == want - 1, 1.0, 0.0).astype(BF)
    for part in range(2):
        fill_rows(gsend, grads, part)
    send_rows(gsend, grel, grecv, gsem, [q for q in others if DESTS[q][0][1] == 0])
    f_got[0].wait()
    f_send[3].start()
    f_send[5].start()
    f_got[1].wait()
    f_send[4].start()
    f_send[6].start()
    send_rows(gsend, grel, grecv, gsem, [q for q in others if DESTS[q][0][1] != 0])
    keep_own(gsend, grecv)

    mixb[...] = mixb_ref[...].reshape(1, C)
    downb[...] = downb_ref[...].reshape(1, C2)

    def cell_of(m):
        return ((m % 128) // 16 * 2 + m // 256) * GW + m % 16 * 2 + m // 128 % 2

    p0, p1 = iota((CELLS, CELLS), 0), iota((CELLS, CELLS), 1)
    to_patch[...] = jnp.where(p1 == cell_of(p0), 1.0, 0.0).astype(BF)
    to_cell[...] = jnp.where(p0 == cell_of(p1), 1.0, 0.0).astype(BF)

    taps[...] = jnp.zeros((TAPS, C), F32)
    for a in range(KS):
        taps[8 * a : 8 * a + KS, :] = mixk_ref[a].astype(F32)
    flat_taps = taps[...].astype(BF)
    wave[...] = dot(tap_high[...], flat_taps) + dot(tap_low[...], flat_taps)

    ld_consts[0].wait()
    spectrum(to_f[...], tile_cells)
    forward(grel, grecv, gsem)
    f_got[3].wait()
    f_got[4].wait()
    f_send[7].start()
    for n in (2, 5, 6, 7):
        f_got[n].wait()
    place_rims(rimf)
    ld_consts[1].wait()
    ld_consts[2].wait()

    def store_mixed(k, cols, cells):
        mixed = (cells + mixb[:, cols]).astype(BF)
        A[:, pl.ds(pl.multiple_of(k * 128, 128), 128), cols] = mixed.reshape(4, 128, 256)

    depthwise(rim_f, from_f, 1.0, to_patch, tile_cells, store_mixed)
    ld_w.wait()

    @pl.loop(0, C2 // 256)
    def _(n):
        cols = pl.ds(pl.multiple_of(n * 256, 256), 256)
        pre = jnp.zeros((ROWS, 256), F32) + downb[:, cols]
        for j in range(4):
            pre = pre + dot(A[j], w[j * C : (j + 1) * C, cols])
        phi = 0.5 * (1.0 + lax.erf(pre * SQRT_HALF))
        tok[:, cols] = (pre * phi).astype(BF)
        slope[:, cols] = phi + pre * INV_ROOT * jnp.exp(-0.5 * pre * pre)

    at = owner[...] * CAP + iota((SLOT_ROWS, 1), 0) % CAP
    hot[...] = jnp.where(at == slot_row, 1.0, 0.0).astype(BF)
    for part in range(2):
        fill_rows(tsend, tok, part)
        if part == 0:
            send_rows(tsend, trel, trecv, tsem, others[:HALF_DEV])
    send_rows(tsend, trel, trecv, tsem, others[HALF_DEV:N_FAR])
    keep_own(tsend, trecv)

    back_at = ocol * (2 * CAP) + rank_col
    for h in range(2):
        sel[h] = jnp.where(iota((ROWS, 2 * CAP * N_DEV), 1) == back_at + h * CAP, 1.0, 0.0).astype(BF)
    wait_rows(grecv, gsem.at[1])

    def picked(got, h, c0):
        part = got[:, :, pl.ds(pl.multiple_of(c0, 256), 256)].reshape(2 * CAP * N_DEV, 256)
        return dot(sel[h], part)

    @pl.loop(0, C2 // 256)
    def _(n):
        h = n // 3
        cols = pl.ds(pl.multiple_of(n * 256, 256), 256)
        pg[:, cols] = (picked(grecv, h, (n - 3 * h) * 256) * slope[:, cols]).astype(BF)

    @pl.loop(0, 4 * (C // 256))
    def _(m):
        j, n = m // 3, lax.rem(m, 3)
        part = w[pl.ds(pl.multiple_of(m * 256, 256), 256), :]
        g = lax.dot_general(pg[...], part, (((1,), (1,)), ((), ())), preferred_element_type=F32)
        mg[:, pl.ds(pl.multiple_of(j * 128, 128), 128), columns(n)] = g.astype(BF).reshape(SLOTS, 128, 256)

    def rim_rows(k, rows):
        at = [((r % 2) * 2 + dx) * 128 + (r // 2) * 16 for r in rows for dx in range(2)]
        return jnp.concatenate([mg[k, a : a + 16, :] for a in at], axis=0)

    for k in range(SLOTS):
        rimb[enc, k] = jnp.where(lower(k) == 0, rim_rows(k, range(TH - HALO, TH)), rim_rows(k, range(HALO)))
    b_send, b_got = rim_copies(rimb, bsend, brecv)
    for n in range(3):
        b_send[n].start()
    forward(trel, trecv, tsem)
    ld_consts[3].wait()
    spectrum(to_b[...], grad_cells)

    for g in range(N_DEV // N_SEQ):
        shape = (N_DEV, 256)
        at1 = iota(shape, 1)
        over = jnp.where(iota(shape, 0) == g * N_SEQ + at1 // (2 * CAP), 1.0, 0.0).astype(BF)
        rows = dot(asked_t, over)
        k8 = iota((CAP, 256), 1)
        put = jnp.sum(jnp.where(iota((CAP, 256), 0) == k8 % CAP, rows, 0.0), axis=0, keepdims=True).astype(I32)
        hit = iota((ROWS, 256), 0) == put - 1
        part = (iota((ROWS, 256), 1) // CAP) % 2
        for h in range(2):
            sel[h, :, g * 256 : (g + 1) * 256] = jnp.where(hit & (part == h), 1.0, 0.0).astype(BF)

    b_got[0].wait()
    b_send[3].start()
    b_send[5].start()
    b_got[1].wait()
    b_send[4].start()
    b_send[6].start()
    send_rows(tsend, trel, trecv, tsem, others[N_FAR:])
    b_got[3].wait()
    b_got[4].wait()
    b_send[7].start()
    for n in (2, 5, 6, 7):
        b_got[n].wait()
    place_rims(rimb)
    ld_consts[4].wait()
    ld_consts[5].wait()

    def store_grad(k, cols, cells):
        gout_ref[k, :, :, cols] = cells.astype(BF).reshape(TH, GW, 256)

    depthwise(rim_b, from_b, -1.0, to_cell, grad_cells, store_grad)
    put_gout = pltpu.make_async_copy(gout_ref, gout_hbm, osem.at[6])
    put_gout.start()

    wait_rows(trecv, tsem.at[1])

    @pl.loop(0, C2 // 256)
    def _(n):
        h = n // 3
        cols = pl.ds(pl.multiple_of(n * 256, 256), 256)
        llm_ref[:, cols] = picked(trecv, h, (n - 3 * h) * 256).astype(BF)
        pltpu.make_async_copy(llm_ref.at[:, cols], llm_hbm.at[:, cols], osem.at[n]).start()

    for n in range(C2 // 256):
        cols = pl.ds(n * 256, 256)
        pltpu.make_async_copy(llm_ref.at[:, cols], llm_hbm.at[:, cols], osem.at[n]).wait()
    put_gout.wait()
    for n in range(8):
        f_send[n].wait_send()
        b_send[n].wait_send()
    wait_rows(msg, msem.at[0])
    for buf, rel, sems in ((gsend, grel, gsem), (tsend, trel, tsem)):
        wait_rows(buf, sems.at[0])
        part = rel.at[pl.ds(0, N_FAR)]
        pltpu.make_async_copy(part, part, sems.at[3]).wait()


def on_device(frame_tiles, tile_ids, partner_slot, mix_kernel, mix_bias, down_weight, down_bias, token_pos, grad_rows):
    vmem = pl.BlockSpec(memory_space=pltpu.VMEM)
    smem = pl.BlockSpec(memory_space=pltpu.SMEM)
    anyw = pl.BlockSpec(memory_space=pl.ANY)
    dma = pltpu.SemaphoreType.DMA
    llm, gout = pl.pallas_call(
        kernel,
        out_shape=(
            jax.ShapeDtypeStruct((ROWS, C2), BF),
            jax.ShapeDtypeStruct((SLOTS, TH, GW, C), BF),
        ),
        in_specs=[anyw, smem, smem, vmem, vmem, anyw, vmem, vmem, anyw] + [anyw] * 6 + [vmem] * 2,
        out_specs=(anyw, anyw),
        scratch_shapes=[
            pltpu.VMEM((ALL_F, CELLS), BF),
            pltpu.VMEM((ALL_F, CELLS), BF),
            pltpu.VMEM((ALL_F, 2 * RIM), BF),
            pltpu.VMEM((ALL_F, 2 * RIM), BF),
            pltpu.VMEM((CELLS, ALL_F), BF),
            pltpu.VMEM((CELLS, ALL_F), BF),
            pltpu.VMEM((TAPS, C), F32),
            pltpu.VMEM((ALL_F, C), F32),
            pltpu.VMEM((SLOTS, ALL_F, C), F32),
            pltpu.VMEM((SLOTS, 2 * RIM, C), BF),
            pltpu.VMEM((SLOTS, CELLS, C), BF),
            pltpu.VMEM((CELLS, CELLS), BF),
            pltpu.VMEM((CELLS, CELLS), BF),
            pltpu.VMEM((ROWS, C2), BF),
            pltpu.VMEM((SLOTS, TH, GW, C), BF),
            dma((7,)),
            pltpu.VMEM((SLOTS, TH, GW, C), BF),
            pltpu.VMEM((4 * C, C2), BF),
            pltpu.VMEM((ROWS, C2), BF),
            pltpu.VMEM((1, C), F32),
            pltpu.VMEM((1, C2), F32),
            pltpu.VMEM((4, ROWS, C), BF),
            pltpu.VMEM((ROWS, C2), F32),
            pltpu.VMEM((ROWS, C2), BF),
            pltpu.VMEM((ROWS, C2), BF),
            pltpu.VMEM((2, ROWS, 2 * CAP * N_DEV), BF),
            pltpu.VMEM((SLOT_ROWS, ROWS), BF),
            pltpu.VMEM((SLOT_ROWS, 1), I32),
            pltpu.VMEM((N_DEV, 1, 128), F32),
            pltpu.VMEM((N_DEV, 1, 128), F32),
            pltpu.VMEM((N_DEV, 2 * CAP, C), BF),
            pltpu.VMEM((N_DEV, 2 * CAP, C), BF),
            pltpu.VMEM((N_FAR, 2 * CAP, C), BF),
            pltpu.VMEM((N_DEV, 2 * CAP, C), BF),
            pltpu.VMEM((N_DEV, 2 * CAP, C), BF),
            pltpu.VMEM((N_FAR, 2 * CAP, C), BF),
            pltpu.VMEM((N_ENC, SLOTS, RIM, C), BF),
            pltpu.VMEM((N_ENC, SLOTS, RIM, C), BF),
            dma((9,)),
            dma((2,)),
            dma((4,)),
            dma((4,)),
            dma((8,)),
            dma((8,)),
            dma((8,)),
            dma((8,)),
        ],
        compiler_params=pltpu.CompilerParams(
            collective_id=0, has_side_effects=True, vmem_limit_bytes=62 * 1024 * 1024
        ),
    )(
        frame_tiles,
        tile_ids,
        partner_slot,
        mix_kernel,
        mix_bias,
        down_weight,
        down_bias,
        token_pos,
        grad_rows,
        *transforms(),
    )
    return llm, gout[None, None]


def solution(mesh):
    return jax.shard_map(
        on_device,
        mesh=mesh,
        in_specs=(
            P("enc", "seq", None, None, None, None),
            P("enc", "seq", None),
            P("enc", "seq", None),
            P(),
            P(),
            P(),
            P(),
            P("enc", "seq", None, None),
            P(("enc", "seq"), None),
        ),
        out_specs=(P(("enc", "seq"), None), P("enc", "seq", None, None, None, None)),
        check_vma=False,
    )
```

```python
import functools

import itertools

import jax
import jax.numpy as jnp
import numpy as np
from jax import lax
from jax.experimental import pallas as pl
from jax.experimental.pallas import tpu as pltpu
from jax.sharding import PartitionSpec as P

C = 768
C2 = 1536
KS = 7
TH = 16
GW = 32
SLOTS = 2
ROWS = 256
N_ENC = 8
N_SEQ = 16
N_DEV = 128
CAP = 8
SLOT_ROWS = CAP * N_DEV

def orbit(o):
    turned = [o, o[2:] + o[:2], o[1:] + o[:1]]
    return [p for q in turned for p in (q, tuple(-d % 4 for d in q))]


ALL_OFFSETS = sorted(itertools.product((0, 1, 3, 2), repeat=3), key=lambda o: -sum(min(d, 4 - d) for d in o))
ORDERED = list(dict.fromkeys(p for o in ALL_OFFSETS for p in orbit(o)))


def relayed(off, f):
    return 2 in off


def first_leg(off, f):
    return tuple(way if d == 2 else 0 for d, way in zip(off, (1 + 2 * f, 3 - 2 * f, 1 + 2 * f)))


PLACES = [(o, f) for o in ORDERED for f in (0, 1) if any(o)] + [((0, 0, 0), 1), ((0, 0, 0), 0)]
DESTS = [p for p in PLACES if relayed(*p)] + [p for p in PLACES if not relayed(*p)]
N_FAR = sum(relayed(*p) for p in PLACES)
OWN = N_DEV - 1
HALF_DEV = N_DEV // 2


def packed(values):
    words = []
    for n in range(0, N_DEV, 16):
        word = sum(v << (2 * i) for i, v in enumerate(values[n : n + 16]))
        words.append(word - (1 << 32) if word >> 31 else word)
    return words


WORDS = [packed([o[axis] for o, f in DESTS]) for axis in range(3)] + [packed([f for o, f in DESTS])]
HALO = 3
CELLS = TH * GW
RIM = HALO * GW
FR, FC = TH + 2 * HALO, GW + HALO
N_FREQ = FR * (FC // 2 + 1)
HALF_F = 400
ALL_F = 2 * HALF_F
TAPS = 8 * KS
SQRT_HALF = 0.7071067811865476
INV_ROOT = 0.3989422804014327
BF = jnp.bfloat16
F32 = jnp.float32
I32 = jnp.int32


def transforms():
    kr, kc = [v.reshape(-1, 1) for v in np.meshgrid(np.arange(FR), np.arange(FC // 2 + 1), indexing="ij")]

    def wave(r, c):
        return np.exp(2j * np.pi * (kr * r / FR + kc * c / FC))

    def rows_of(z):
        out = np.zeros((ALL_F, z.shape[1]))
        out[:N_FREQ], out[HALF_F : HALF_F + N_FREQ] = z.real, z.imag
        return out

    r, c = [v.ravel() for v in np.meshgrid(np.arange(TH), np.arange(GW), indexing="ij")]
    by_patch = np.argsort(((r % 2) * 2 + c % 2) * 128 + (r // 2) * 16 + c // 2)
    rr, rc = [v.ravel() for v in np.meshgrid(np.arange(HALO), np.arange(GW), indexing="ij")]
    rim_patch = np.argsort(rr * GW + (rc % 2) * 16 + rc // 2)
    there = rows_of(np.conj(wave(r, c)))
    rims = [rows_of(np.conj(wave(rr + at, rc))) for at in (-HALO, TH)]
    rim_cells = np.concatenate(rims, axis=1)
    rim_patches = np.concatenate([m[:, rim_patch] for m in rims], axis=1)
    share = np.where(kc == 0, 1.0, 2.0) / (FR * FC)
    back = wave(r, c) * share
    back = (rows_of(np.conj(back))).T
    a, b = np.arange(TAPS) // 8, np.arange(TAPS) % 8
    taps = rows_of(wave(a - HALO, b - HALO) * (b < KS))
    high = taps.astype(BF)
    low = (taps - high.astype(np.float64)).astype(BF)
    return [
        m.astype(BF)
        for m in (there, there[:, by_patch], rim_cells, rim_patches, back[by_patch], back, high, low)
    ]


def iota(shape, axis):
    return lax.broadcasted_iota(I32, shape, axis)


def dot(a, b):
    return jnp.dot(a, b, preferred_element_type=F32)


def kernel(
    tiles_hbm, ids_ref, partner_ref, mixk_ref, mixb_ref, w_hbm, downb_ref, pos_ref, grad_hbm,
    to_f_hbm, to_b_hbm, rim_f_hbm, rim_b_hbm, from_f_hbm, from_b_hbm, tap_high, tap_low,
    llm_hbm, gout_hbm,
    to_f, to_b, rim_f, rim_b, from_f, from_b, taps, wave, field, edge, mg, to_patch, to_cell, llm_ref, gout_ref, osem,
    tiles, w, grads, mixb, downb, A, slope, tok, pg, sel, hot, owner,
    msg, rmsg, gsend, grecv, grel, tsend, trecv, trel, rimf, rimb,
    lsem, msem, gsem, tsem, fsend, frecv, bsend, brecv,
):
    enc = lax.axis_index("enc")
    seq = lax.axis_index("seq")
    me = enc * N_SEQ + seq
    cy, core = enc // 2, enc % 2

    ld_tiles = pltpu.make_async_copy(tiles_hbm.at[0, 0], tiles, lsem.at[0])
    ld_grads = pltpu.make_async_copy(grad_hbm, grads, lsem.at[1])
    ld_w = pltpu.make_async_copy(w_hbm, w, lsem.at[2])
    ld_tiles.start()
    ld_grads.start()
    ld_consts = [
        pltpu.make_async_copy(src, dst, lsem.at[3 + n])
        for n, (src, dst) in enumerate(
            ((to_f_hbm, to_f), (rim_f_hbm, rim_f), (from_f_hbm, from_f), (to_b_hbm, to_b), (rim_b_hbm, rim_b), (from_b_hbm, from_b))
        )
    ]
    for n in range(3):
        ld_consts[n].start()
    ld_w.start()
    for n in range(3, 6):
        ld_consts[n].start()

    cx, cz = seq >> 2, seq & 3
    at_x = [((cx + d) & 3) * 4 for d in range(4)]
    at_y = [((cy + d) & 3) * 2 for d in range(4)]
    at_z = [(cz + d) & 3 for d in range(4)]
    at_core = [core, 1 - core]

    def device(off, f):
        dx, dy, dz = off
        return at_y[dy] + at_core[f], at_x[dx] + at_z[dz]

    others = range(OWN)
    barrier = pltpu.get_barrier_semaphore()
    for q in others:
        pl.semaphore_signal(barrier, inc=1, device_id=device(*DESTS[q]), device_id_type=pl.DeviceIdType.MESH)


    pos = pos_ref[0, 0]
    prow = jnp.concatenate([pos[0:1, :], pos[1:2, :]], axis=1)
    pcol = jnp.concatenate(
        [jnp.transpose(jnp.broadcast_to(pos[i : i + 1, :].astype(F32), (128, 128))) for i in range(2)], axis=0
    ).astype(I32)[:, 0:1]
    orow, ocol = prow // ROWS, pcol // ROWS
    lcol = pcol - ocol * ROWS
    same = jnp.broadcast_to(ocol, (ROWS, ROWS)) == jnp.broadcast_to(orow, (ROWS, ROWS))
    at0, at1 = iota((ROWS, ROWS), 0), iota((ROWS, ROWS), 1)
    rank_row = jnp.sum(jnp.where(same & (at0 < at1), 1.0, 0.0), axis=0, keepdims=True).astype(I32)
    rank_col = jnp.sum(jnp.where(same & (at1 < at0), 1.0, 0.0), axis=1, keepdims=True).astype(I32)
    slot_row = orow * CAP + rank_row
    to_owner = jnp.where(iota((N_DEV, ROWS), 0) == orow, 1.0, 0.0).astype(BF)
    ranked = jnp.where(iota((ROWS, 128), 1) == rank_col, (lcol + 1).astype(F32), 0.0).astype(BF)
    msg[...] = dot(to_owner, ranked).reshape(N_DEV, 1, 128)
    rmsg[pl.ds(me, 1)] = msg[pl.ds(me, 1)]

    def lower(k):
        return lax.rem(ids_ref[0, 0, k], 2)

    up = lax.rem(cy + 1, 4) * 2 + core
    down = lax.rem(cy + 3, 4) * 2 + core
    across = lax.rem(cy + 2, 4) * 2 + core
    sib = cy * 2 + 1 - core

    def rim_copies(rims, ssem, rsem):
        def copy(n, ref, to):
            return pltpu.make_async_remote_copy(
                src_ref=ref, dst_ref=ref, send_sem=ssem.at[n], recv_sem=rsem.at[n],
                device_id=(to, seq), device_id_type=pl.DeviceIdType.MESH,
            )

        def landed(n, ref):
            return pltpu.make_async_copy(ref, ref, rsem.at[n])

        sends = [
            copy(0, rims.at[enc], up),
            copy(1, rims.at[enc], down),
            copy(2, rims.at[enc], sib),
            copy(3, rims.at[down, 0], up),
            copy(4, rims.at[up, 1], down),
            copy(5, rims.at[down], sib),
            copy(6, rims.at[up], sib),
            copy(7, rims.at[across], sib),
        ]
        other = 1 - 2 * core
        arrivals = [
            landed(0, rims.at[down]),
            landed(1, rims.at[up]),
            landed(2, rims.at[sib]),
            landed(3, rims.at[across, 0]),
            landed(4, rims.at[across, 1]),
            landed(5, rims.at[down + other]),
            landed(6, rims.at[up + other]),
            landed(7, rims.at[across + other]),
        ]
        return sends, arrivals

    def place_rims(rims):
        for k in range(SLOTS):
            want = partner_ref[0, 0, k]
            rim = jnp.zeros((RIM, C), BF)
            for q in range(N_ENC * SLOTS):
                rim = jnp.where(want == q, rims[q // 2, q % 2], rim)
            none = jnp.zeros((RIM, C), BF)
            below = lower(k) == 1
            edge[k, 0:RIM, :] = jnp.where(below, rim, none)
            edge[k, RIM : 2 * RIM, :] = jnp.where(below, none, rim)

    def columns(n):
        return pl.ds(pl.multiple_of(n * 256, 256), 256)

    def spectrum(there, cells):
        @pl.loop(0, SLOTS * 3)
        def _(i):
            k, cols = i // 3, columns(lax.rem(i, 3))
            field[k, :, cols] = dot(there, cells(k, cols))

    def depthwise(there, back, way, turn, cells, store):
        @pl.loop(0, SLOTS * 3)
        def _(i):
            k, cols = i // 3, columns(lax.rem(i, 3))
            z = field[k, :, cols] + dot(there[...], edge[k, :, cols])
            re, im = z[0:HALF_F], z[HALF_F:ALL_F]
            wr, wi = wave[0:HALF_F, cols], way * wave[HALF_F:ALL_F, cols]
            product = jnp.concatenate([re * wr - im * wi, re * wi + im * wr], axis=0).astype(BF)
            store(k, cols, dot(turn[...], cells(k, cols)) + dot(back[...], product))

    def owner_of_row():
        place = iota((SLOT_ROWS, 1), 0) // CAP
        block, shift = place // 16, 2 * (place % 16)
        d = []
        for words in WORDS:
            word = jnp.full(place.shape, words[0])
            for n in range(1, 8):
                word = jnp.where(block == n, words[n], word)
            d.append(jnp.right_shift(word, shift) & 3)
        c = core + d[3] - 2 * core * d[3]
        return (((cy + d[1]) & 3) * 2 + c) * N_SEQ + ((cx + d[0]) & 3) * 4 + ((cz + d[2]) & 3)

    def fill_rows(buf, rows_ref, part):
        slots = slice(part * SLOT_ROWS // 2, (part + 1) * SLOT_ROWS // 2)
        dests = slice(part * HALF_DEV, (part + 1) * HALF_DEV)

        @pl.loop(0, C // 256)
        def _(n):
            c0 = pl.multiple_of(n * 256, 256)
            y0 = dot(hot[slots, :], rows_ref[:, pl.ds(c0, 256)]).reshape(HALF_DEV, CAP, 256)
            y1 = dot(hot[slots, :], rows_ref[:, pl.ds(c0 + C, 256)]).reshape(HALF_DEV, CAP, 256)
            buf[dests, :, pl.ds(c0, 256)] = jnp.concatenate([y0, y1], axis=1).astype(BF)

    def send_rows(buf, rel, got, sems, chosen):
        for q in chosen:
            off, f = DESTS[q]
            far = q < N_FAR
            pltpu.make_async_remote_copy(
                src_ref=buf.at[q], dst_ref=rel.at[q] if far else got.at[me],
                send_sem=sems.at[0], recv_sem=sems.at[2 if far else 1],
                device_id=device(first_leg(off, f), 0) if far else device(off, f),
                device_id_type=pl.DeviceIdType.MESH,
            ).start()

    def forward(rel, got, sems):
        part = rel.at[pl.ds(0, N_FAR)]
        pltpu.make_async_copy(part, part, sems.at[2]).wait()
        for q in range(N_FAR):
            off, f = DESTS[q]
            leg = first_leg(off, f)
            e0, s0 = device([-d % 4 for d in leg], 0)
            pltpu.make_async_remote_copy(
                src_ref=rel.at[q], dst_ref=got.at[e0 * N_SEQ + s0],
                send_sem=sems.at[3], recv_sem=sems.at[1],
                device_id=device([(o - d) % 4 for o, d in zip(off, leg)], f), device_id_type=pl.DeviceIdType.MESH,
            ).start()

    def keep_own(buf, got):
        got[pl.ds(me, 1)] = buf[OWN : OWN + 1]

    def wait_rows(buf, sem):
        part = buf.at[pl.ds(0, N_DEV - 1)]
        pltpu.make_async_copy(part, part, sem).wait()

    ld_tiles.wait()
    for k in range(SLOTS):
        high, low = tiles[k, TH - HALO : TH].reshape(RIM, C), tiles[k, 0:HALO].reshape(RIM, C)
        rimf[enc, k] = jnp.where(lower(k) == 0, high, low)
    pl.semaphore_wait(barrier, N_DEV - 1)
    for q in others:
        e, s = device(*DESTS[q])
        pltpu.make_async_remote_copy(
            src_ref=msg.at[e * N_SEQ + s], dst_ref=rmsg.at[me],
            send_sem=msem.at[0], recv_sem=msem.at[1],
            device_id=(e, s), device_id_type=pl.DeviceIdType.MESH,
        ).start()
    f_send, f_got = rim_copies(rimf, fsend, frecv)
    for n in range(3):
        f_send[n].start()
    owner[...] = owner_of_row()

    def tile_cells(k, cols):
        return tiles[k, :, :, cols].reshape(CELLS, 256)

    def grad_cells(k, cols):
        return mg[k, :, cols]

    ld_grads.wait()
    wait_rows(rmsg, msem.at[1])

    asked = rmsg[...].reshape(N_DEV, 128)
    asked_t = jnp.transpose(asked)[0:CAP, :].astype(BF)
    asked = asked.astype(BF)

    shape = (SLOT_ROWS, 128)
    rows = dot(jnp.where(iota(shape, 1) == owner[...], 1.0, 0.0).astype(BF), asked)
    want = jnp.sum(jnp.where(iota(shape, 1) == iota(shape, 0) % CAP, rows, 0.0), axis=1, keepdims=True).astype(I32)
    hot[...] = jnp.where(iota((SLOT_ROWS, ROWS), 1) == want - 1, 1.0, 0.0).astype(BF)
    for part in range(2):
        fill_rows(gsend, grads, part)
    send_rows(gsend, grel, grecv, gsem, [q for q in others if DESTS[q][0][1] == 0])
    f_got[0].wait()
    f_send[3].start()
    f_send[5].start()
    f_got[1].wait()
    f_send[4].start()
    f_send[6].start()
    send_rows(gsend, grel, grecv, gsem, [q for q in others if DESTS[q][0][1] != 0])
    keep_own(gsend, grecv)

    mixb[...] = mixb_ref[...].reshape(1, C)
    downb[...] = downb_ref[...].reshape(1, C2)

    def cell_of(m):
        return ((m % 128) // 16 * 2 + m // 256) * GW + m % 16 * 2 + m // 128 % 2

    p0, p1 = iota((CELLS, CELLS), 0), iota((CELLS, CELLS), 1)
    to_patch[...] = jnp.where(p1 == cell_of(p0), 1.0, 0.0).astype(BF)
    to_cell[...] = jnp.where(p0 == cell_of(p1), 1.0, 0.0).astype(BF)

    taps[...] = jnp.zeros((TAPS, C), F32)
    for a in range(KS):
        taps[8 * a : 8 * a + KS, :] = mixk_ref[a].astype(F32)
    flat_taps = taps[...].astype(BF)
    wave[...] = dot(tap_high[...], flat_taps) + dot(tap_low[...], flat_taps)

    ld_consts[0].wait()
    spectrum(to_f[...], tile_cells)
    forward(grel, grecv, gsem)
    f_got[3].wait()
    f_got[4].wait()
    f_send[7].start()
    for n in (2, 5, 6, 7):
        f_got[n].wait()
    place_rims(rimf)
    ld_consts[1].wait()
    ld_consts[2].wait()

    def store_mixed(k, cols, cells):
        mixed = (cells + mixb[:, cols]).astype(BF)
        A[:, pl.ds(pl.multiple_of(k * 128, 128), 128), cols] = mixed.reshape(4, 128, 256)

    depthwise(rim_f, from_f, 1.0, to_patch, tile_cells, store_mixed)
    ld_w.wait()

    @pl.loop(0, C2 // 256)
    def _(n):
        cols = pl.ds(pl.multiple_of(n * 256, 256), 256)
        pre = jnp.zeros((ROWS, 256), F32) + downb[:, cols]
        for j in range(4):
            pre = pre + dot(A[j], w[j * C : (j + 1) * C, cols])
        phi = 0.5 * (1.0 + lax.erf(pre * SQRT_HALF))
        tok[:, cols] = (pre * phi).astype(BF)
        slope[:, cols] = phi + pre * INV_ROOT * jnp.exp(-0.5 * pre * pre)

    at = owner[...] * CAP + iota((SLOT_ROWS, 1), 0) % CAP
    hot[...] = jnp.where(at == slot_row, 1.0, 0.0).astype(BF)
    for part in range(2):
        fill_rows(tsend, tok, part)
        if part == 0:
            send_rows(tsend, trel, trecv, tsem, others[:HALF_DEV])
    send_rows(tsend, trel, trecv, tsem, others[HALF_DEV:N_FAR])
    keep_own(tsend, trecv)

    back_at = ocol * (2 * CAP) + rank_col
    for h in range(2):
        sel[h] = jnp.where(iota((ROWS, 2 * CAP * N_DEV), 1) == back_at + h * CAP, 1.0, 0.0).astype(BF)
    wait_rows(grecv, gsem.at[1])

    def picked(got, h, c0):
        part = got[:, :, pl.ds(pl.multiple_of(c0, 256), 256)].reshape(2 * CAP * N_DEV, 256)
        return dot(sel[h], part)

    @pl.loop(0, C2 // 256)
    def _(n):
        h = n // 3
        cols = pl.ds(pl.multiple_of(n * 256, 256), 256)
        pg[:, cols] = (picked(grecv, h, (n - 3 * h) * 256) * slope[:, cols]).astype(BF)

    @pl.loop(0, 4 * (C // 256))
    def _(m):
        j, n = m // 3, lax.rem(m, 3)
        part = w[pl.ds(pl.multiple_of(m * 256, 256), 256), :]
        g = lax.dot_general(pg[...], part, (((1,), (1,)), ((), ())), preferred_element_type=F32)
        mg[:, pl.ds(pl.multiple_of(j * 128, 128), 128), columns(n)] = g.astype(BF).reshape(SLOTS, 128, 256)

    def rim_rows(k, rows):
        at = [((r % 2) * 2 + dx) * 128 + (r // 2) * 16 for r in rows for dx in range(2)]
        return jnp.concatenate([mg[k, a : a + 16, :] for a in at], axis=0)

    for k in range(SLOTS):
        rimb[enc, k] = jnp.where(lower(k) == 0, rim_rows(k, range(TH - HALO, TH)), rim_rows(k, range(HALO)))
    b_send, b_got = rim_copies(rimb, bsend, brecv)
    for n in range(3):
        b_send[n].start()
    forward(trel, trecv, tsem)
    ld_consts[3].wait()
    spectrum(to_b[...], grad_cells)

    for g in range(N_DEV // N_SEQ):
        shape = (N_DEV, 256)
        at1 = iota(shape, 1)
        over = jnp.where(iota(shape, 0) == g * N_SEQ + at1 // (2 * CAP), 1.0, 0.0).astype(BF)
        rows = dot(asked_t, over)
        k8 = iota((CAP, 256), 1)
        put = jnp.sum(jnp.where(iota((CAP, 256), 0) == k8 % CAP, rows, 0.0), axis=0, keepdims=True).astype(I32)
        hit = iota((ROWS, 256), 0) == put - 1
        part = (iota((ROWS, 256), 1) // CAP) % 2
        for h in range(2):
            sel[h, :, g * 256 : (g + 1) * 256] = jnp.where(hit & (part == h), 1.0, 0.0).astype(BF)

    b_got[0].wait()
    b_send[3].start()
    b_send[5].start()
    b_got[1].wait()
    b_send[4].start()
    b_send[6].start()
    send_rows(tsend, trel, trecv, tsem, others[N_FAR:])
    b_got[3].wait()
    b_got[4].wait()
    b_send[7].start()
    for n in (2, 5, 6, 7):
        b_got[n].wait()
    place_rims(rimb)
    ld_consts[4].wait()
    ld_consts[5].wait()

    def store_grad(k, cols, cells):
        gout_ref[k, :, :, cols] = cells.astype(BF).reshape(TH, GW, 256)

    depthwise(rim_b, from_b, -1.0, to_cell, grad_cells, store_grad)
    put_gout = pltpu.make_async_copy(gout_ref, gout_hbm, osem.at[6])
    put_gout.start()

    wait_rows(trecv, tsem.at[1])

    @pl.loop(0, C2 // 256)
    def _(n):
        h = n // 3
        cols = pl.ds(pl.multiple_of(n * 256, 256), 256)
        llm_ref[:, cols] = picked(trecv, h, (n - 3 * h) * 256).astype(BF)
        pltpu.make_async_copy(llm_ref.at[:, cols], llm_hbm.at[:, cols], osem.at[n]).start()

    for n in range(C2 // 256):
        cols = pl.ds(n * 256, 256)
        pltpu.make_async_copy(llm_ref.at[:, cols], llm_hbm.at[:, cols], osem.at[n]).wait()
    put_gout.wait()
    for n in range(8):
        f_send[n].wait_send()
        b_send[n].wait_send()
    wait_rows(msg, msem.at[0])
    for buf, rel, sems in ((gsend, grel, gsem), (tsend, trel, tsem)):
        wait_rows(buf, sems.at[0])
        part = rel.at[pl.ds(0, N_FAR)]
        pltpu.make_async_copy(part, part, sems.at[3]).wait()


def hand_over(llm_ref, gout_ref, llm_out, gout_out, sems):
    copies = [
        pltpu.make_async_copy(llm_ref.at[pl.ds(n * 128, 128)], llm_out.at[pl.ds(n * 128, 128)], sems.at[n])
        for n in range(2)
    ] + [
        pltpu.make_async_copy(gout_ref.at[n // 2, pl.ds(n % 2 * 8, 8)], gout_out.at[n // 2, pl.ds(n % 2 * 8, 8)], sems.at[2 + n])
        for n in range(4)
    ]
    for copy in copies:
        copy.start()
    for copy in copies:
        copy.wait()


def on_device(frame_tiles, tile_ids, partner_slot, mix_kernel, mix_bias, down_weight, down_bias, token_pos, grad_rows):
    vmem = pl.BlockSpec(memory_space=pltpu.VMEM)
    smem = pl.BlockSpec(memory_space=pltpu.SMEM)
    anyw = pl.BlockSpec(memory_space=pl.ANY)
    dma = pltpu.SemaphoreType.DMA
    llm, gout = pl.pallas_call(
        kernel,
        out_shape=(
            jax.ShapeDtypeStruct((ROWS, C2), BF),
            jax.ShapeDtypeStruct((SLOTS, TH, GW, C), BF),
        ),
        in_specs=[anyw, smem, smem, vmem, vmem, anyw, vmem, vmem, anyw] + [anyw] * 6 + [vmem] * 2,
        out_specs=(anyw, anyw),
        scratch_shapes=[
            pltpu.VMEM((ALL_F, CELLS), BF),
            pltpu.VMEM((ALL_F, CELLS), BF),
            pltpu.VMEM((ALL_F, 2 * RIM), BF),
            pltpu.VMEM((ALL_F, 2 * RIM), BF),
            pltpu.VMEM((CELLS, ALL_F), BF),
            pltpu.VMEM((CELLS, ALL_F), BF),
            pltpu.VMEM((TAPS, C), F32),
            pltpu.VMEM((ALL_F, C), F32),
            pltpu.VMEM((SLOTS, ALL_F, C), F32),
            pltpu.VMEM((SLOTS, 2 * RIM, C), BF),
            pltpu.VMEM((SLOTS, CELLS, C), BF),
            pltpu.VMEM((CELLS, CELLS), BF),
            pltpu.VMEM((CELLS, CELLS), BF),
            pltpu.VMEM((ROWS, C2), BF),
            pltpu.VMEM((SLOTS, TH, GW, C), BF),
            dma((7,)),
            pltpu.VMEM((SLOTS, TH, GW, C), BF),
            pltpu.VMEM((4 * C, C2), BF),
            pltpu.VMEM((ROWS, C2), BF),
            pltpu.VMEM((1, C), F32),
            pltpu.VMEM((1, C2), F32),
            pltpu.VMEM((4, ROWS, C), BF),
            pltpu.VMEM((ROWS, C2), F32),
            pltpu.VMEM((ROWS, C2), BF),
            pltpu.VMEM((ROWS, C2), BF),
            pltpu.VMEM((2, ROWS, 2 * CAP * N_DEV), BF),
            pltpu.VMEM((SLOT_ROWS, ROWS), BF),
            pltpu.VMEM((SLOT_ROWS, 1), I32),
            pltpu.VMEM((N_DEV, 1, 128), F32),
            pltpu.VMEM((N_DEV, 1, 128), F32),
            pltpu.VMEM((N_DEV, 2 * CAP, C), BF),
            pltpu.VMEM((N_DEV, 2 * CAP, C), BF),
            pltpu.VMEM((N_FAR, 2 * CAP, C), BF),
            pltpu.VMEM((N_DEV, 2 * CAP, C), BF),
            pltpu.VMEM((N_DEV, 2 * CAP, C), BF),
            pltpu.VMEM((N_FAR, 2 * CAP, C), BF),
            pltpu.VMEM((N_ENC, SLOTS, RIM, C), BF),
            pltpu.VMEM((N_ENC, SLOTS, RIM, C), BF),
            dma((9,)),
            dma((2,)),
            dma((4,)),
            dma((4,)),
            dma((8,)),
            dma((8,)),
            dma((8,)),
            dma((8,)),
        ],
        compiler_params=pltpu.CompilerParams(
            collective_id=0, has_side_effects=True, vmem_limit_bytes=62 * 1024 * 1024
        ),
    )(
        frame_tiles,
        tile_ids,
        partner_slot,
        mix_kernel,
        mix_bias,
        down_weight,
        down_bias,
        token_pos,
        grad_rows,
        *transforms(),
    )
    llm, gout = pl.pallas_call(
        hand_over,
        out_shape=(
            jax.ShapeDtypeStruct((ROWS, C2), BF),
            jax.ShapeDtypeStruct((SLOTS, TH, GW, C), BF),
        ),
        in_specs=[vmem, vmem],
        out_specs=(anyw, anyw),
        scratch_shapes=[dma((6,))],
    )(llm, gout)
    return llm, gout[None, None]


def solution(mesh):
    return jax.shard_map(
        on_device,
        mesh=mesh,
        in_specs=(
            P("enc", "seq", None, None, None, None),
            P("enc", "seq", None),
            P("enc", "seq", None),
            P(),
            P(),
            P(),
            P(),
            P("enc", "seq", None, None),
            P(("enc", "seq"), None),
        ),
        out_specs=(P(("enc", "seq"), None), P("enc", "seq", None, None, None, None)),
        check_vma=False,
    )
```

```python
import functools

import itertools

import jax
import jax.numpy as jnp
import numpy as np
from jax import lax
from jax.experimental import pallas as pl
from jax.experimental.pallas import tpu as pltpu
from jax.sharding import PartitionSpec as P

C = 768
C2 = 1536
KS = 7
TH = 16
GW = 32
SLOTS = 2
ROWS = 256
N_ENC = 8
N_SEQ = 16
N_DEV = 128
CAP = 8
SLOT_ROWS = CAP * N_DEV

def orbit(o):
    turned = [o, o[2:] + o[:2], o[1:] + o[:1]]
    return [p for q in turned for p in (q, tuple(-d % 4 for d in q))]


ALL_OFFSETS = sorted(itertools.product((0, 1, 3, 2), repeat=3), key=lambda o: -sum(min(d, 4 - d) for d in o))
ORDERED = list(dict.fromkeys(p for o in ALL_OFFSETS for p in orbit(o)))


def relayed(off, f):
    return 2 in off


def first_leg(off, f):
    return tuple(way if d == 2 else 0 for d, way in zip(off, (1 + 2 * f, 3 - 2 * f, 1 + 2 * f)))


PLACES = [(o, f) for o in ORDERED for f in (0, 1) if any(o)] + [((0, 0, 0), 1), ((0, 0, 0), 0)]
DESTS = [p for p in PLACES if relayed(*p)] + [p for p in PLACES if not relayed(*p)]
N_FAR = sum(relayed(*p) for p in PLACES)
OWN = N_DEV - 1
HALF_DEV = N_DEV // 2


def packed(values):
    words = []
    for n in range(0, N_DEV, 16):
        word = sum(v << (2 * i) for i, v in enumerate(values[n : n + 16]))
        words.append(word - (1 << 32) if word >> 31 else word)
    return words


WORDS = [packed([o[axis] for o, f in DESTS]) for axis in range(3)] + [packed([f for o, f in DESTS])]
HALO = 3
CELLS = TH * GW
RIM = HALO * GW
FR, FC = TH + 2 * HALO, GW + HALO
N_FREQ = FR * (FC // 2 + 1)
HALF_F = 400
ALL_F = 2 * HALF_F
TAPS = 8 * KS
SQRT_HALF = 0.7071067811865476
INV_ROOT = 0.3989422804014327
BF = jnp.bfloat16
F32 = jnp.float32
I32 = jnp.int32


def transforms():
    kr, kc = [v.reshape(-1, 1) for v in np.meshgrid(np.arange(FR), np.arange(FC // 2 + 1), indexing="ij")]

    def wave(r, c):
        return np.exp(2j * np.pi * (kr * r / FR + kc * c / FC))

    def rows_of(z):
        out = np.zeros((ALL_F, z.shape[1]))
        out[:N_FREQ], out[HALF_F : HALF_F + N_FREQ] = z.real, z.imag
        return out

    r, c = [v.ravel() for v in np.meshgrid(np.arange(TH), np.arange(GW), indexing="ij")]
    by_patch = np.argsort(((r % 2) * 2 + c % 2) * 128 + (r // 2) * 16 + c // 2)
    rr, rc = [v.ravel() for v in np.meshgrid(np.arange(HALO), np.arange(GW), indexing="ij")]
    rim_patch = np.argsort(rr * GW + (rc % 2) * 16 + rc // 2)
    there = rows_of(np.conj(wave(r, c)))
    rims = [rows_of(np.conj(wave(rr + at, rc))) for at in (-HALO, TH)]
    rim_cells = np.concatenate(rims, axis=1)
    rim_patches = np.concatenate([m[:, rim_patch] for m in rims], axis=1)
    share = np.where(kc == 0, 1.0, 2.0) / (FR * FC)
    back = wave(r, c) * share
    back = (rows_of(np.conj(back))).T
    a, b = np.arange(TAPS) // 8, np.arange(TAPS) % 8
    taps = rows_of(wave(a - HALO, b - HALO) * (b < KS))
    high = taps.astype(BF)
    low = (taps - high.astype(np.float64)).astype(BF)
    return [
        m.astype(BF)
        for m in (there, there[:, by_patch], rim_cells, rim_patches, back[by_patch], back, high, low)
    ]


def iota(shape, axis):
    return lax.broadcasted_iota(I32, shape, axis)


def dot(a, b):
    return jnp.dot(a, b, preferred_element_type=F32)


def kernel(
    tiles_hbm, ids_ref, partner_ref, mixk_ref, mixb_ref, w_hbm, downb_ref, pos_ref, grad_hbm,
    to_f_hbm, to_b_hbm, rim_f_hbm, rim_b_hbm, from_f_hbm, from_b_hbm, tap_high, tap_low,
    llm_hbm, gout_hbm,
    to_f, to_b, rim_f, rim_b, from_f, from_b, taps, wave, field, edge, mg, to_patch, to_cell, llm_ref, gout_ref, osem,
    tiles, w, grads, mixb, downb, A, slope, tok, pg, sel, hot, owner,
    msg, rmsg, gsend, grecv, grel, tsend, trecv, trel, rimf, rimb,
    lsem, msem, gsem, tsem, fsend, frecv, bsend, brecv,
):
    enc = lax.axis_index("enc")
    seq = lax.axis_index("seq")
    me = enc * N_SEQ + seq
    cy, core = enc // 2, enc % 2

    ld_tiles = pltpu.make_async_copy(tiles_hbm.at[0, 0], tiles, lsem.at[0])
    ld_grads = pltpu.make_async_copy(grad_hbm, grads, lsem.at[1])
    ld_w = pltpu.make_async_copy(w_hbm, w, lsem.at[2])
    ld_tiles.start()
    ld_grads.start()
    ld_consts = [
        pltpu.make_async_copy(src, dst, lsem.at[3 + n])
        for n, (src, dst) in enumerate(
            ((to_f_hbm, to_f), (rim_f_hbm, rim_f), (from_f_hbm, from_f), (to_b_hbm, to_b), (rim_b_hbm, rim_b), (from_b_hbm, from_b))
        )
    ]
    for n in range(3):
        ld_consts[n].start()
    ld_w.start()
    for n in range(3, 6):
        ld_consts[n].start()

    cx, cz = seq >> 2, seq & 3
    at_x = [((cx + d) & 3) * 4 for d in range(4)]
    at_y = [((cy + d) & 3) * 2 for d in range(4)]
    at_z = [(cz + d) & 3 for d in range(4)]
    at_core = [core, 1 - core]

    def device(off, f):
        dx, dy, dz = off
        return at_y[dy] + at_core[f], at_x[dx] + at_z[dz]

    others = range(OWN)
    barrier = pltpu.get_barrier_semaphore()
    for q in others:
        pl.semaphore_signal(barrier, inc=1, device_id=device(*DESTS[q]), device_id_type=pl.DeviceIdType.MESH)


    pos = pos_ref[0, 0]
    prow = jnp.concatenate([pos[0:1, :], pos[1:2, :]], axis=1)
    pcol = jnp.concatenate(
        [jnp.transpose(jnp.broadcast_to(pos[i : i + 1, :].astype(F32), (128, 128))) for i in range(2)], axis=0
    ).astype(I32)[:, 0:1]
    orow, ocol = prow // ROWS, pcol // ROWS
    lcol = pcol - ocol * ROWS
    same = jnp.broadcast_to(ocol, (ROWS, ROWS)) == jnp.broadcast_to(orow, (ROWS, ROWS))
    at0, at1 = iota((ROWS, ROWS), 0), iota((ROWS, ROWS), 1)
    rank_row = jnp.sum(jnp.where(same & (at0 < at1), 1.0, 0.0), axis=0, keepdims=True).astype(I32)
    rank_col = jnp.sum(jnp.where(same & (at1 < at0), 1.0, 0.0), axis=1, keepdims=True).astype(I32)
    slot_row = orow * CAP + rank_row
    to_owner = jnp.where(iota((N_DEV, ROWS), 0) == orow, 1.0, 0.0).astype(BF)
    ranked = jnp.where(iota((ROWS, 128), 1) == rank_col, (lcol + 1).astype(F32), 0.0).astype(BF)
    msg[...] = dot(to_owner, ranked).reshape(N_DEV, 1, 128)
    rmsg[pl.ds(me, 1)] = msg[pl.ds(me, 1)]

    def lower(k):
        return lax.rem(ids_ref[0, 0, k], 2)

    up = lax.rem(cy + 1, 4) * 2 + core
    down = lax.rem(cy + 3, 4) * 2 + core
    across = lax.rem(cy + 2, 4) * 2 + core
    sib = cy * 2 + 1 - core

    def rim_copies(rims, ssem, rsem):
        def copy(n, ref, to):
            return pltpu.make_async_remote_copy(
                src_ref=ref, dst_ref=ref, send_sem=ssem.at[n], recv_sem=rsem.at[n],
                device_id=(to, seq), device_id_type=pl.DeviceIdType.MESH,
            )

        def landed(n, ref):
            return pltpu.make_async_copy(ref, ref, rsem.at[n])

        sends = [
            copy(0, rims.at[enc], up),
            copy(1, rims.at[enc], down),
            copy(2, rims.at[enc], sib),
            copy(3, rims.at[down, 0], up),
            copy(4, rims.at[up, 1], down),
            copy(5, rims.at[down], sib),
            copy(6, rims.at[up], sib),
            copy(7, rims.at[across], sib),
        ]
        other = 1 - 2 * core
        arrivals = [
            landed(0, rims.at[down]),
            landed(1, rims.at[up]),
            landed(2, rims.at[sib]),
            landed(3, rims.at[across, 0]),
            landed(4, rims.at[across, 1]),
            landed(5, rims.at[down + other]),
            landed(6, rims.at[up + other]),
            landed(7, rims.at[across + other]),
        ]
        return sends, arrivals

    def place_rims(rims):
        for k in range(SLOTS):
            want = partner_ref[0, 0, k]
            rim = jnp.zeros((RIM, C), BF)
            for q in range(N_ENC * SLOTS):
                rim = jnp.where(want == q, rims[q // 2, q % 2], rim)
            none = jnp.zeros((RIM, C), BF)
            below = lower(k) == 1
            edge[k, 0:RIM, :] = jnp.where(below, rim, none)
            edge[k, RIM : 2 * RIM, :] = jnp.where(below, none, rim)

    def columns(n):
        return pl.ds(pl.multiple_of(n * 256, 256), 256)

    def spectrum(there, cells):
        @pl.loop(0, SLOTS * 3)
        def _(i):
            k, cols = i // 3, columns(lax.rem(i, 3))
            field[k, :, cols] = dot(there, cells(k, cols))

    def depthwise(there, back, way, turn, cells, store):
        @pl.loop(0, SLOTS * 3)
        def _(i):
            k, cols = i // 3, columns(lax.rem(i, 3))
            z = field[k, :, cols] + dot(there[...], edge[k, :, cols])
            re, im = z[0:HALF_F], z[HALF_F:ALL_F]
            wr, wi = wave[0:HALF_F, cols], way * wave[HALF_F:ALL_F, cols]
            product = jnp.concatenate([re * wr - im * wi, re * wi + im * wr], axis=0).astype(BF)
            store(k, cols, dot(turn[...], cells(k, cols)) + dot(back[...], product))

    def owner_of_row():
        place = iota((SLOT_ROWS, 1), 0) // CAP
        block, shift = place // 16, 2 * (place % 16)
        d = []
        for words in WORDS:
            word = jnp.full(place.shape, words[0])
            for n in range(1, 8):
                word = jnp.where(block == n, words[n], word)
            d.append(jnp.right_shift(word, shift) & 3)
        c = core + d[3] - 2 * core * d[3]
        return (((cy + d[1]) & 3) * 2 + c) * N_SEQ + ((cx + d[0]) & 3) * 4 + ((cz + d[2]) & 3)

    def fill_rows(buf, rows_ref, part):
        slots = slice(part * SLOT_ROWS // 2, (part + 1) * SLOT_ROWS // 2)
        dests = slice(part * HALF_DEV, (part + 1) * HALF_DEV)

        @pl.loop(0, C // 256)
        def _(n):
            c0 = pl.multiple_of(n * 256, 256)
            y0 = dot(hot[slots, :], rows_ref[:, pl.ds(c0, 256)]).reshape(HALF_DEV, CAP, 256)
            y1 = dot(hot[slots, :], rows_ref[:, pl.ds(c0 + C, 256)]).reshape(HALF_DEV, CAP, 256)
            buf[dests, :, pl.ds(c0, 256)] = jnp.concatenate([y0, y1], axis=1).astype(BF)

    def send_rows(buf, rel, got, sems, chosen):
        for q in chosen:
            off, f = DESTS[q]
            far = q < N_FAR
            pltpu.make_async_remote_copy(
                src_ref=buf.at[q], dst_ref=rel.at[q] if far else got.at[me],
                send_sem=sems.at[0], recv_sem=sems.at[2 if far else 1],
                device_id=device(first_leg(off, f), 0) if far else device(off, f),
                device_id_type=pl.DeviceIdType.MESH,
            ).start()

    def forward(rel, got, sems):
        part = rel.at[pl.ds(0, N_FAR)]
        pltpu.make_async_copy(part, part, sems.at[2]).wait()
        for q in range(N_FAR):
            off, f = DESTS[q]
            leg = first_leg(off, f)
            e0, s0 = device([-d % 4 for d in leg], 0)
            pltpu.make_async_remote_copy(
                src_ref=rel.at[q], dst_ref=got.at[e0 * N_SEQ + s0],
                send_sem=sems.at[3], recv_sem=sems.at[1],
                device_id=device([(o - d) % 4 for o, d in zip(off, leg)], f), device_id_type=pl.DeviceIdType.MESH,
            ).start()

    def keep_own(buf, got):
        got[pl.ds(me, 1)] = buf[OWN : OWN + 1]

    def wait_rows(buf, sem):
        part = buf.at[pl.ds(0, N_DEV - 1)]
        pltpu.make_async_copy(part, part, sem).wait()

    ld_tiles.wait()
    for k in range(SLOTS):
        high, low = tiles[k, TH - HALO : TH].reshape(RIM, C), tiles[k, 0:HALO].reshape(RIM, C)
        rimf[enc, k] = jnp.where(lower(k) == 0, high, low)
    pl.semaphore_wait(barrier, N_DEV - 1)
    for q in others:
        e, s = device(*DESTS[q])
        pltpu.make_async_remote_copy(
            src_ref=msg.at[e * N_SEQ + s], dst_ref=rmsg.at[me],
            send_sem=msem.at[0], recv_sem=msem.at[1],
            device_id=(e, s), device_id_type=pl.DeviceIdType.MESH,
        ).start()
    f_send, f_got = rim_copies(rimf, fsend, frecv)
    for n in range(3):
        f_send[n].start()
    owner[...] = owner_of_row()

    def tile_cells(k, cols):
        return tiles[k, :, :, cols].reshape(CELLS, 256)

    def grad_cells(k, cols):
        return mg[k, :, cols]

    mixb[...] = mixb_ref[...].reshape(1, C)
    downb[...] = downb_ref[...].reshape(1, C2)

    def cell_of(m):
        return ((m % 128) // 16 * 2 + m // 256) * GW + m % 16 * 2 + m // 128 % 2

    p0, p1 = iota((CELLS, CELLS), 0), iota((CELLS, CELLS), 1)
    to_patch[...] = jnp.where(p1 == cell_of(p0), 1.0, 0.0).astype(BF)
    to_cell[...] = jnp.where(p0 == cell_of(p1), 1.0, 0.0).astype(BF)

    taps[...] = jnp.zeros((TAPS, C), F32)
    for a in range(KS):
        taps[8 * a : 8 * a + KS, :] = mixk_ref[a].astype(F32)
    flat_taps = taps[...].astype(BF)
    wave[...] = dot(tap_high[...], flat_taps) + dot(tap_low[...], flat_taps)

    ld_grads.wait()
    wait_rows(rmsg, msem.at[1])

    asked = rmsg[...].reshape(N_DEV, 128)
    asked_t = jnp.transpose(asked)[0:CAP, :].astype(BF)
    asked = asked.astype(BF)

    shape = (SLOT_ROWS, 128)
    rows = dot(jnp.where(iota(shape, 1) == owner[...], 1.0, 0.0).astype(BF), asked)
    want = jnp.sum(jnp.where(iota(shape, 1) == iota(shape, 0) % CAP, rows, 0.0), axis=1, keepdims=True).astype(I32)
    hot[...] = jnp.where(iota((SLOT_ROWS, ROWS), 1) == want - 1, 1.0, 0.0).astype(BF)
    for part in range(2):
        fill_rows(gsend, grads, part)
    send_rows(gsend, grel, grecv, gsem, [q for q in others if DESTS[q][0][1] == 0])
    f_got[0].wait()
    f_send[3].start()
    f_send[5].start()
    f_got[1].wait()
    f_send[4].start()
    f_send[6].start()
    send_rows(gsend, grel, grecv, gsem, [q for q in others if DESTS[q][0][1] != 0])
    keep_own(gsend, grecv)

    ld_consts[0].wait()
    spectrum(to_f[...], tile_cells)
    forward(grel, grecv, gsem)
    f_got[3].wait()
    f_got[4].wait()
    f_send[7].start()
    for n in (2, 5, 6, 7):
        f_got[n].wait()
    place_rims(rimf)
    ld_consts[1].wait()
    ld_consts[2].wait()

    def store_mixed(k, cols, cells):
        mixed = (cells + mixb[:, cols]).astype(BF)
        A[:, pl.ds(pl.multiple_of(k * 128, 128), 128), cols] = mixed.reshape(4, 128, 256)

    depthwise(rim_f, from_f, 1.0, to_patch, tile_cells, store_mixed)
    ld_w.wait()

    @pl.loop(0, C2 // 256)
    def _(n):
        cols = pl.ds(pl.multiple_of(n * 256, 256), 256)
        pre = jnp.zeros((ROWS, 256), F32) + downb[:, cols]
        for j in range(4):
            pre = pre + dot(A[j], w[j * C : (j + 1) * C, cols])
        phi = 0.5 * (1.0 + lax.erf(pre * SQRT_HALF))
        tok[:, cols] = (pre * phi).astype(BF)
        slope[:, cols] = phi + pre * INV_ROOT * jnp.exp(-0.5 * pre * pre)

    at = owner[...] * CAP + iota((SLOT_ROWS, 1), 0) % CAP
    hot[...] = jnp.where(at == slot_row, 1.0, 0.0).astype(BF)
    for part in range(2):
        fill_rows(tsend, tok, part)
        if part == 0:
            send_rows(tsend, trel, trecv, tsem, others[:HALF_DEV])
    send_rows(tsend, trel, trecv, tsem, others[HALF_DEV:N_FAR])
    keep_own(tsend, trecv)

    back_at = ocol * (2 * CAP) + rank_col
    for h in range(2):
        sel[h] = jnp.where(iota((ROWS, 2 * CAP * N_DEV), 1) == back_at + h * CAP, 1.0, 0.0).astype(BF)
    wait_rows(grecv, gsem.at[1])

    def picked(got, h, c0):
        part = got[:, :, pl.ds(pl.multiple_of(c0, 256), 256)].reshape(2 * CAP * N_DEV, 256)
        return dot(sel[h], part)

    @pl.loop(0, C2 // 256)
    def _(n):
        h = n // 3
        cols = pl.ds(pl.multiple_of(n * 256, 256), 256)
        pg[:, cols] = (picked(grecv, h, (n - 3 * h) * 256) * slope[:, cols]).astype(BF)

    @pl.loop(0, 4 * (C // 256))
    def _(m):
        j, n = m // 3, lax.rem(m, 3)
        part = w[pl.ds(pl.multiple_of(m * 256, 256), 256), :]
        g = lax.dot_general(pg[...], part, (((1,), (1,)), ((), ())), preferred_element_type=F32)
        mg[:, pl.ds(pl.multiple_of(j * 128, 128), 128), columns(n)] = g.astype(BF).reshape(SLOTS, 128, 256)

    def rim_rows(k, rows):
        at = [((r % 2) * 2 + dx) * 128 + (r // 2) * 16 for r in rows for dx in range(2)]
        return jnp.concatenate([mg[k, a : a + 16, :] for a in at], axis=0)

    for k in range(SLOTS):
        rimb[enc, k] = jnp.where(lower(k) == 0, rim_rows(k, range(TH - HALO, TH)), rim_rows(k, range(HALO)))
    b_send, b_got = rim_copies(rimb, bsend, brecv)
    for n in range(3):
        b_send[n].start()
    forward(trel, trecv, tsem)
    ld_consts[3].wait()
    spectrum(to_b[...], grad_cells)

    for g in range(N_DEV // N_SEQ):
        shape = (N_DEV, 256)
        at1 = iota(shape, 1)
        over = jnp.where(iota(shape, 0) == g * N_SEQ + at1 // (2 * CAP), 1.0, 0.0).astype(BF)
        rows = dot(asked_t, over)
        k8 = iota((CAP, 256), 1)
        put = jnp.sum(jnp.where(iota((CAP, 256), 0) == k8 % CAP, rows, 0.0), axis=0, keepdims=True).astype(I32)
        hit = iota((ROWS, 256), 0) == put - 1
        part = (iota((ROWS, 256), 1) // CAP) % 2
        for h in range(2):
            sel[h, :, g * 256 : (g + 1) * 256] = jnp.where(hit & (part == h), 1.0, 0.0).astype(BF)

    b_got[0].wait()
    b_send[3].start()
    b_send[5].start()
    b_got[1].wait()
    b_send[4].start()
    b_send[6].start()
    send_rows(tsend, trel, trecv, tsem, others[N_FAR:])
    b_got[3].wait()
    b_got[4].wait()
    b_send[7].start()
    for n in (2, 5, 6, 7):
        b_got[n].wait()
    place_rims(rimb)
    ld_consts[4].wait()
    ld_consts[5].wait()

    def store_grad(k, cols, cells):
        gout_ref[k, :, :, cols] = cells.astype(BF).reshape(TH, GW, 256)

    depthwise(rim_b, from_b, -1.0, to_cell, grad_cells, store_grad)
    put_gout = pltpu.make_async_copy(gout_ref, gout_hbm, osem.at[6])
    put_gout.start()

    wait_rows(trecv, tsem.at[1])

    @pl.loop(0, C2 // 256)
    def _(n):
        h = n // 3
        cols = pl.ds(pl.multiple_of(n * 256, 256), 256)
        llm_ref[:, cols] = picked(trecv, h, (n - 3 * h) * 256).astype(BF)
        pltpu.make_async_copy(llm_ref.at[:, cols], llm_hbm.at[:, cols], osem.at[n]).start()

    for n in range(C2 // 256):
        cols = pl.ds(n * 256, 256)
        pltpu.make_async_copy(llm_ref.at[:, cols], llm_hbm.at[:, cols], osem.at[n]).wait()
    put_gout.wait()
    for n in range(8):
        f_send[n].wait_send()
        b_send[n].wait_send()
    wait_rows(msg, msem.at[0])
    for buf, rel, sems in ((gsend, grel, gsem), (tsend, trel, tsem)):
        wait_rows(buf, sems.at[0])
        part = rel.at[pl.ds(0, N_FAR)]
        pltpu.make_async_copy(part, part, sems.at[3]).wait()


def hand_over(llm_ref, gout_ref, llm_out, gout_out, sems):
    copies = [
        pltpu.make_async_copy(llm_ref.at[pl.ds(n * 128, 128)], llm_out.at[pl.ds(n * 128, 128)], sems.at[n])
        for n in range(2)
    ] + [
        pltpu.make_async_copy(gout_ref.at[n // 2, pl.ds(n % 2 * 8, 8)], gout_out.at[n // 2, pl.ds(n % 2 * 8, 8)], sems.at[2 + n])
        for n in range(4)
    ]
    for copy in copies:
        copy.start()
    for copy in copies:
        copy.wait()


def on_device(frame_tiles, tile_ids, partner_slot, mix_kernel, mix_bias, down_weight, down_bias, token_pos, grad_rows):
    vmem = pl.BlockSpec(memory_space=pltpu.VMEM)
    smem = pl.BlockSpec(memory_space=pltpu.SMEM)
    anyw = pl.BlockSpec(memory_space=pl.ANY)
    dma = pltpu.SemaphoreType.DMA
    llm, gout = pl.pallas_call(
        kernel,
        out_shape=(
            jax.ShapeDtypeStruct((ROWS, C2), BF),
            jax.ShapeDtypeStruct((SLOTS, TH, GW, C), BF),
        ),
        in_specs=[anyw, smem, smem, vmem, vmem, anyw, vmem, vmem, anyw] + [anyw] * 6 + [vmem] * 2,
        out_specs=(anyw, anyw),
        scratch_shapes=[
            pltpu.VMEM((ALL_F, CELLS), BF),
            pltpu.VMEM((ALL_F, CELLS), BF),
            pltpu.VMEM((ALL_F, 2 * RIM), BF),
            pltpu.VMEM((ALL_F, 2 * RIM), BF),
            pltpu.VMEM((CELLS, ALL_F), BF),
            pltpu.VMEM((CELLS, ALL_F), BF),
            pltpu.VMEM((TAPS, C), F32),
            pltpu.VMEM((ALL_F, C), F32),
            pltpu.VMEM((SLOTS, ALL_F, C), F32),
            pltpu.VMEM((SLOTS, 2 * RIM, C), BF),
            pltpu.VMEM((SLOTS, CELLS, C), BF),
            pltpu.VMEM((CELLS, CELLS), BF),
            pltpu.VMEM((CELLS, CELLS), BF),
            pltpu.VMEM((ROWS, C2), BF),
            pltpu.VMEM((SLOTS, TH, GW, C), BF),
            dma((7,)),
            pltpu.VMEM((SLOTS, TH, GW, C), BF),
            pltpu.VMEM((4 * C, C2), BF),
            pltpu.VMEM((ROWS, C2), BF),
            pltpu.VMEM((1, C), F32),
            pltpu.VMEM((1, C2), F32),
            pltpu.VMEM((4, ROWS, C), BF),
            pltpu.VMEM((ROWS, C2), F32),
            pltpu.VMEM((ROWS, C2), BF),
            pltpu.VMEM((ROWS, C2), BF),
            pltpu.VMEM((2, ROWS, 2 * CAP * N_DEV), BF),
            pltpu.VMEM((SLOT_ROWS, ROWS), BF),
            pltpu.VMEM((SLOT_ROWS, 1), I32),
            pltpu.VMEM((N_DEV, 1, 128), F32),
            pltpu.VMEM((N_DEV, 1, 128), F32),
            pltpu.VMEM((N_DEV, 2 * CAP, C), BF),
            pltpu.VMEM((N_DEV, 2 * CAP, C), BF),
            pltpu.VMEM((N_FAR, 2 * CAP, C), BF),
            pltpu.VMEM((N_DEV, 2 * CAP, C), BF),
            pltpu.VMEM((N_DEV, 2 * CAP, C), BF),
            pltpu.VMEM((N_FAR, 2 * CAP, C), BF),
            pltpu.VMEM((N_ENC, SLOTS, RIM, C), BF),
            pltpu.VMEM((N_ENC, SLOTS, RIM, C), BF),
            dma((9,)),
            dma((2,)),
            dma((4,)),
            dma((4,)),
            dma((8,)),
            dma((8,)),
            dma((8,)),
            dma((8,)),
        ],
        compiler_params=pltpu.CompilerParams(
            collective_id=0, has_side_effects=True, vmem_limit_bytes=62 * 1024 * 1024
        ),
    )(
        frame_tiles,
        tile_ids,
        partner_slot,
        mix_kernel,
        mix_bias,
        down_weight,
        down_bias,
        token_pos,
        grad_rows,
        *transforms(),
    )
    llm, gout = pl.pallas_call(
        hand_over,
        out_shape=(
            jax.ShapeDtypeStruct((ROWS, C2), BF),
            jax.ShapeDtypeStruct((SLOTS, TH, GW, C), BF),
        ),
        in_specs=[vmem, vmem],
        out_specs=(anyw, anyw),
        scratch_shapes=[dma((6,))],
    )(llm, gout)
    return llm, gout[None, None]


def solution(mesh):
    return jax.shard_map(
        on_device,
        mesh=mesh,
        in_specs=(
            P("enc", "seq", None, None, None, None),
            P("enc", "seq", None),
            P("enc", "seq", None),
            P(),
            P(),
            P(),
            P(),
            P("enc", "seq", None, None),
            P(("enc", "seq"), None),
        ),
        out_specs=(P(("enc", "seq"), None), P("enc", "seq", None, None, None, None)),
        check_vma=False,
    )
```
